32 devices in a mesh: jobs: 2 (over x), clus: 16 (over z, y, core).
Axes of the slice: x: 2, y: 2, z: 4, core: 2. Of those that a mesh axis runs over, the one named last changes fastest.
Arguments:
- vertices: float32 [3, 65536], P(None, ('jobs', 'clus')), parts along dimension 1, may hold values from 0 to 17
- panel_vertices: int32 [3, 131072], P(None, ('jobs', 'clus')), parts along dimension 1, may hold values from 0 to 32767, as said below
- near_pairs: int32 [512, 4], P(('jobs', 'clus')), parts along dimension 0, may hold values from -1 to 255, as said below
- far_pairs: int32 [512, 32], P(('jobs', 'clus')), parts along dimension 0, may hold values from 0 to 255, as said below
- basis: float32 [32, 131072], P(None, ('jobs', 'clus')), parts along dimension 1, may hold values from -0.75 to 0.75
- krylov: float32 [16, 131072], P(None, ('jobs', 'clus')), parts along dimension 1, may hold values from -12 to 12
Outputs:
- next_basis: float32 [16, 131072], P(None, ('jobs', 'clus')), parts along dimension 1
- second_image: float32 [16, 131072], P(None, ('jobs', 'clus')), parts along dimension 1
The draws below stay inside these ranges and needn't reach their ends.
There are 2 independent parts, one for each index of `jobs`. The reference program is written for one: setup_inputs(seed, part) draws one part's arguments, and reference() takes and returns one part's arrays. A program takes and returns all parts, laid end to end along the dimension named above; each array names one. Nothing has to cross between parts.
Inputs may be any that keep to these rules, and one draw needn't show every extreme that they name: `panel_vertices`: the vertices of a panel of cluster c are among vertices c * 128 to (c + 1) * 128 - 1. `near_pairs`: row c starts with c itself, then distinct clusters j with |j // 16 - c // 16| <= 1; live entries come first and -1 fills the rest; some row has all 4 slots live. `far_pairs`: row c holds 32 distinct clusters j with 2 <= |j // 16 - c // 16| <= 4.
All inputs are finite; a program needn't handle non-finite values.
Results may differ from the reference program's by a relative error of at most 0.0003.
Values sent between devices are 32-bit elements; how exact they have to be, the bound alone decides.
No kernel may reach another device: no remote copies, remote signals or barrier semaphores. Data moves between devices by JAX's collectives and lax.ppermute only.
A program may use at most 128 MiB of HBM per device.

```python
import jax
import jax.numpy as jnp
from jax import lax

CL = 256
RANK = 32
CD = 16
NRHS = 16
NMAX = 4
FMAX = 32
REACH = 4
VCL = 128
CLUSTERS = 256
PANELS = 65536
VERTS = 32768
N_CLUS = 16


def draw_vertices(key, part):
    key = jax.random.fold_in(key, 11)
    subkeys = jax.random.split(key, 3)
    vertex_index = jnp.arange(VERTS)
    cluster = vertex_index // VCL
    owner_block = (cluster // CD).astype(jnp.float32)
    layer_index = (cluster % CD).astype(jnp.float32)
    across = jax.random.uniform(subkeys[0], (VERTS,), jnp.float32)
    along = jax.random.uniform(subkeys[1], (VERTS,), jnp.float32)
    height = jax.random.uniform(subkeys[2], (VERTS,), jnp.float32)
    return jnp.stack([2.0 * across, owner_block + along, 0.05 * layer_index + 0.02 * height])


def draw_krylov(key, part):
    key = jax.random.fold_in(key, 13)
    position_share = jnp.arange(PANELS).astype(jnp.float32) / (PANELS - 1)
    values = jnp.clip(jax.random.normal(key, (NRHS, PANELS), jnp.float32), -4.0, 4.0)
    profile = 1.0 + 2.0 * position_share
    return values * profile[None, :]


def draw_panel_vertices(key, part):
    key = jax.random.fold_in(key, 17)
    cluster = jnp.arange(PANELS) // CL
    offsets = jax.random.randint(key, (3, PANELS), 0, VCL)
    return (cluster[None, :] * VCL + offsets).astype(jnp.int32)


def ranked(key, candidates, invalid, leading):
    window_width = candidates.shape[1]
    scores = jax.random.randint(key, candidates.shape, 0, 2 ** 18) * window_width + jnp.arange(window_width)[None, :]
    scores = jnp.where(invalid, 2 ** 30, scores)
    scores = jnp.where(leading, -1, scores)
    ranking = jnp.argsort(scores, axis=1, stable=True)
    return jnp.take_along_axis(candidates, ranking, axis=1)


def draw_near_pairs(key, part):
    key = jax.random.fold_in(key, 19)
    subkeys = jax.random.split(key, 4)
    cluster = jnp.arange(CLUSTERS)
    owner_block = cluster // CD
    candidates = (owner_block[:, None] - 1) * CD + jnp.arange(3 * CD)[None, :]
    invalid = (candidates < 0) | (candidates >= CLUSTERS)
    picked = ranked(subkeys[0], candidates, invalid, candidates == cluster[:, None])[:, :NMAX]
    blocks = CLUSTERS // CD
    chosen = jax.random.randint(subkeys[1], (), 0, blocks)
    count_caps = jax.random.randint(subkeys[2], (blocks,), max(NMAX // 2, 1), NMAX + 1)
    count_caps = jnp.where(jnp.arange(blocks) == chosen, NMAX, count_caps)
    counts = 1 + jax.random.randint(subkeys[3], (CLUSTERS,), 0, count_caps[owner_block])
    counts = jnp.where((owner_block == chosen) & (cluster % CD == 0), NMAX, counts)
    return jnp.where(jnp.arange(NMAX)[None, :] < counts[:, None], picked, -1).astype(jnp.int32)


def draw_far_pairs(key, part):
    key = jax.random.fold_in(key, 23)
    cluster = jnp.arange(CLUSTERS)
    owner_block = cluster // CD
    candidates = (owner_block[:, None] - REACH) * CD + jnp.arange((2 * REACH + 1) * CD)[None, :]
    distance = jnp.abs(candidates // CD - owner_block[:, None])
    invalid = (candidates < 0) | (candidates >= CLUSTERS) | (distance <= 1)
    picked = ranked(key, candidates, invalid, jnp.zeros(candidates.shape, jnp.bool_))
    return picked[:, :FMAX].astype(jnp.int32)


def shard_levels(key, extent, pieces, low, top_value):
    gain, own = 1.0, jax.random.fold_in(key, 6)
    for dim, blocks in pieces:
        heights = jnp.exp(jax.random.uniform(jax.random.fold_in(own, dim), (blocks,), jnp.float32, low / len(pieces), top_value / len(pieces)))
        gain = gain * jnp.repeat(heights, extent[dim] // blocks).reshape([-1 if axis == dim else 1 for axis in range(len(extent))])
    return gain


def noise(key, shape, width, most, shards=(), kind=jnp.bfloat16):
    factor_of = shard_levels(key, shape, shards, -0.22, 0.18) if shards else 1.0
    values = jax.random.normal(key, shape, jnp.float32) * width * factor_of
    return jnp.minimum(jnp.maximum(values, -most), most).astype(kind)


def setup_inputs(seed: int = 0, part: int = 0) -> dict:
    key_list = jax.random.split(jax.random.key(seed), 7)
    part_keys = jax.random.split(jax.random.fold_in(key_list[6], part), 7)
    vertices = draw_vertices(jax.random.fold_in(jax.random.fold_in(key_list[6], part), 71), part)
    panel_vertices = draw_panel_vertices(jax.random.fold_in(jax.random.fold_in(key_list[6], part), 71), part)
    near_pairs = draw_near_pairs(jax.random.fold_in(jax.random.fold_in(key_list[6], part), 71), part)
    far_pairs = draw_far_pairs(jax.random.fold_in(jax.random.fold_in(key_list[6], part), 71), part)
    basis = noise(part_keys[4], (RANK, PANELS), 0.125, 0.75, ((1, 16),), jnp.float32)
    krylov = draw_krylov(jax.random.fold_in(jax.random.fold_in(key_list[6], part), 71), part)
    return {"vertices": vertices, "panel_vertices": panel_vertices, "near_pairs": near_pairs, "far_pairs": far_pairs, "basis": basis, "krylov": krylov}


SMOOTHING = 0.04
COULOMB = 2.0
PROXY_RADIUS = 0.6
HIGHEST_PRECISION = lax.Precision.HIGHEST

def proxy_directions(points):
    counter = jnp.arange(points).astype(jnp.float32)
    height = 1.0 - (2.0 * counter + 1.0) / points
    radial = jnp.sqrt(1.0 - height * height)
    azimuth = counter * 2.399963
    return jnp.stack([radial * jnp.cos(azimuth), radial * jnp.sin(azimuth), height])

def geometry(vertices, corner_index):
    corners = vertices[:, corner_index]
    centroid = (corners[:, 0] + corners[:, 1] + corners[:, 2]) / 3.0
    edge_one = corners[:, 1] - corners[:, 0]
    edge_two = corners[:, 2] - corners[:, 0]
    normal = jnp.stack([edge_one[1] * edge_two[2] - edge_one[2] * edge_two[1], edge_one[2] * edge_two[0] - edge_one[0] * edge_two[2], edge_one[0] * edge_two[1] - edge_one[1] * edge_two[0]])
    panel_area = 0.5 * jnp.sqrt(lax.optimization_barrier(jnp.sum(normal * normal, axis=0)))
    return (centroid, panel_area)

def near_term(target, source, charges, live_mask):
    offsets = target[:, :, :, None] - source[:, :, None, :]
    kernel = 1.0 / jnp.sqrt(lax.optimization_barrier(jnp.sum(offsets * offsets, axis=0)) + SMOOTHING)
    masked = charges * live_mask[None, :, None]
    return jnp.einsum('cpq,rcq->rcp', kernel, masked, precision=HIGHEST_PRECISION)

def coupling(target_proxy, source_proxy):
    offsets = target_proxy[:, :, None, :, None] - source_proxy[:, :, :, None, :]
    return 1.0 / jnp.sqrt(lax.optimization_barrier(jnp.sum(offsets * offsets, axis=0)) + SMOOTHING)

def operate(centroid, panel_area, centers, basis, near_pairs, far_pairs, charges):
    directions = proxy_directions(RANK)
    weighted = panel_area[None, :] * charges
    blocks = weighted.reshape(NRHS, CLUSTERS, CL)
    centroid_blocks = centroid.reshape(3, CLUSTERS, CL)
    basis_blocks = basis.reshape(RANK, CLUSTERS, CL)
    area_blocks = panel_area.reshape(CLUSTERS, CL)
    moments = jnp.einsum('acp,rcp->rac', basis_blocks, blocks, precision=HIGHEST_PRECISION)

    def one_group(inputs):
        cluster_ids, near_list, far_list = inputs
        target = centroid_blocks[:, cluster_ids]
        running = jnp.zeros((NRHS, CD, CL), jnp.float32)
        for slot_index in range(NMAX):
            column = near_list[:, slot_index]
            chosen = jnp.maximum(column, 0)
            running = running + near_term(target, centroid_blocks[:, chosen], blocks[:, chosen], (column >= 0).astype(jnp.float32))
        target_proxy = centers[:, cluster_ids][:, :, None] + PROXY_RADIUS * directions[:, None, :]
        source_proxy = centers[:, far_list][:, :, :, None] + PROXY_RADIUS * directions[:, None, None, :]
        coupler = coupling(target_proxy, source_proxy)
        far_field = jnp.einsum('cfab,rbcf->rca', coupler, moments[:, :, far_list], precision=HIGHEST_PRECISION)
        far_potential = jnp.einsum('acp,rca->rcp', basis_blocks[:, cluster_ids], far_field, precision=HIGHEST_PRECISION)
        return COULOMB * area_blocks[cluster_ids][None] * (running + far_potential)
    cluster_ids = jnp.arange(CLUSTERS).reshape(N_CLUS, CD)
    result = lax.map(one_group, (cluster_ids, near_pairs.reshape(N_CLUS, CD, NMAX), far_pairs.reshape(N_CLUS, CD, FMAX)))
    return jnp.transpose(result, (1, 0, 2, 3)).reshape(NRHS, PANELS)

def reference(vertices, panel_vertices, near_pairs, far_pairs, basis, krylov):
    centroid, panel_area = geometry(vertices, panel_vertices)
    centers = lax.optimization_barrier(jnp.mean(centroid.reshape(3, CLUSTERS, CL), axis=2))
    image = operate(centroid, panel_area, centers, basis, near_pairs, far_pairs, krylov)
    correlation = lax.optimization_barrier(jnp.sum(krylov * image, axis=1))
    squared = lax.optimization_barrier(jnp.sum(krylov * krylov, axis=1))
    projection = correlation / (squared + 1e-06)
    residual = image - projection[:, None] * krylov
    scaling = jnp.sqrt(lax.optimization_barrier(jnp.sum(residual * residual, axis=1)) / PANELS + 1e-06)
    next_basis = residual / scaling[:, None]
    second_image = operate(centroid, panel_area, centers, basis, near_pairs, far_pairs, next_basis)
    return (next_basis, second_image)
```

```python
import functools

import jax
import jax.numpy as jnp
import numpy as np
from jax import lax
from jax.experimental import pallas as pl
from jax.experimental.pallas import tpu as pltpu
from jax.sharding import PartitionSpec as P

REACH = 4
SMOOTHING = 0.04
COULOMB = 2.0
PROXY_RADIUS = 0.6
LANES = 128
F32 = jnp.float32
BF16 = jnp.bfloat16


def proxy_offsets(points):
    counter = np.arange(points, dtype=np.float32)
    height = 1.0 - (2.0 * counter + 1.0) / points
    radial = np.sqrt(1.0 - height * height)
    azimuth = counter * 2.399963
    return PROXY_RADIUS * np.stack([radial * np.cos(azimuth), radial * np.sin(azimuth), height]).astype(np.float32)


def split(value):
    high = value.astype(BF16)
    return high, (value - high.astype(F32)).astype(BF16)


def stacked(value):
    return jnp.concatenate(split(value), axis=0)


def folded(value):
    half = value.shape[0] // 2
    return value[:half] + value[half:]


def dot_nt(left, right):
    return lax.dot_general(left, right, (((1,), (1,)), ((), ())), preferred_element_type=F32)


def dot_nn(left, right):
    return lax.dot_general(left, right, (((1,), (0,)), ((), ())), preferred_element_type=F32)


def moments_of(weighted, basis_block):
    pieces = stacked(weighted)
    high, low = split(basis_block)
    return folded(dot_nt(pieces, high) + dot_nt(pieces, low))


def prepare_kernel(cl, vcl, rank, base_ref, vertices_ref, corners_ref, krylov_ref, basis_ref, charges_ref, centroid_ref, table_ref, area_ref):
    clusters = krylov_ref.shape[1] // cl
    rhs = krylov_ref.shape[0]
    base = base_ref[0]
    table_ref[rhs:, :] = jnp.zeros_like(table_ref[rhs:, :])
    for c in range(clusters):
        mesh = vertices_ref[:, c * vcl:(c + 1) * vcl]
        tables = [jnp.broadcast_to(mesh[k:k + 1, :], (8, vcl)) for k in range(3)]
        sums = [jnp.zeros((1, 1), F32)] * 3
        for h in range(cl // LANES):
            lanes = slice(c * cl + h * LANES, c * cl + (h + 1) * LANES)
            local = corners_ref[:, lanes] - (base + c * vcl)
            local = jnp.concatenate([local, local, local[:2]], axis=0)
            first, edge_one, edge_two = [], [], []
            for k in range(3):
                corner = jnp.take_along_axis(tables[k], local, axis=1, mode="promise_in_bounds")
                middle = (corner[0:1] + corner[1:2] + corner[2:3]) / 3.0
                centroid_ref[c:c + 1, k * cl + h * LANES:k * cl + (h + 1) * LANES] = middle
                sums[k] = sums[k] + jnp.sum(middle, axis=1, keepdims=True)
                edge_one.append(corner[1:2] - corner[0:1])
                edge_two.append(corner[2:3] - corner[0:1])
            normal = [
                edge_one[1] * edge_two[2] - edge_one[2] * edge_two[1],
                edge_one[2] * edge_two[0] - edge_one[0] * edge_two[2],
                edge_one[0] * edge_two[1] - edge_one[1] * edge_two[0],
            ]
            area = 0.5 * jnp.sqrt(normal[0] * normal[0] + normal[1] * normal[1] + normal[2] * normal[2])
            area_ref[:, lanes] = jnp.broadcast_to(area, (8, LANES))
            charges_ref[:, lanes] = area * krylov_ref[:, lanes]
        for k in range(3):
            table_ref[rhs + k:rhs + k + 1, c * rank:(c + 1) * rank] = jnp.broadcast_to(sums[k] / cl, (1, rank))
        panels = slice(c * cl, (c + 1) * cl)
        table_ref[0:rhs, c * rank:(c + 1) * rank] = moments_of(charges_ref[:, panels], basis_ref[:, panels])


def columns_of(centroid_ref, row, cl, columns_ref, at):
    rows = jnp.concatenate([centroid_ref[row:row + 1, k * cl:(k + 1) * cl] for k in range(3)] * 2 + [centroid_ref[row:row + 1, 0:cl]] * 2, axis=0)
    upright = jnp.transpose(rows)
    for k in range(3):
        columns_ref[at, k] = jnp.broadcast_to(upright[:, k:k + 1], (cl, LANES))


def near_block(columns, source, cl, out_ref, at):
    for h in range(cl // LANES):
        lanes = slice(h * LANES, (h + 1) * LANES)
        gap = [columns[k] - source(k, h) for k in range(3)]
        square = gap[0] * gap[0] + gap[1] * gap[1] + gap[2] * gap[2]
        high, low = split(lax.rsqrt(square + SMOOTHING))
        out_ref[at, 0:cl, lanes] = high
        out_ref[at, cl:2 * cl, lanes] = low


def near_product(pieces, block_ref, at, cl):
    return dot_nt(pieces, block_ref[at, 0:cl, :]) + dot_nt(pieces, block_ref[at, cl:2 * cl, :])


def self_kernel(cl, charges_ref, centroid_ref, blocks_ref, near_ref, columns_ref):
    clusters = charges_ref.shape[1] // cl
    for c in range(clusters):
        columns_of(centroid_ref, c, cl, columns_ref, c % 2)
        source = lambda k, h: centroid_ref[c:c + 1, k * cl + h * LANES:k * cl + (h + 1) * LANES]
        near_block([columns_ref[c % 2, k] for k in range(3)], source, cl, blocks_ref, c)
        panels = slice(c * cl, (c + 1) * cl)
        near_ref[:, panels] = folded(near_product(stacked(charges_ref[:, panels]), blocks_ref, c, cl))


def fill_charges(pieces_ref, blocks, clusters, cl):
    for b, ref in enumerate(blocks):
        for c in range(clusters):
            pieces_ref[b * clusters + c] = stacked(ref[:, c * cl:(c + 1) * cl])
    pieces_ref[3 * clusters] = jnp.zeros_like(pieces_ref[3 * clusters])


def list_pairs(near_ref, base, clusters, list_ref):
    slots = near_ref.shape[1]

    def put(n, c, j):
        list_ref[0, n] = c
        list_ref[1, n] = j

    def step(i, n):
        c = i // (slots - 1)
        j = near_ref[c, 1 + i % (slots - 1)]
        put(n, c, j - base)
        return n + (j >= 0).astype(jnp.int32)

    count = lax.fori_loop(0, clusters * (slots - 1), step, jnp.int32(0))
    put(count, 0, 3 * clusters)
    return count


def remote_kernel(cl, base_ref, near_ref, own_ref, left_ref, right_ref, own_centroid_ref, left_centroid_ref, right_centroid_ref, start_ref,
                  blocks_ref, near_out_ref, pieces_ref, sources_ref, columns_ref, even_ref, odd_ref, total_ref, list_ref, sems):
    clusters = own_ref.shape[1] // cl
    rhs = own_ref.shape[0]
    count = list_pairs(near_ref, base_ref[0], clusters, list_ref)
    for b, ref in enumerate((left_centroid_ref, own_centroid_ref, right_centroid_ref)):
        for c in range(clusters):
            for k in range(3):
                sources_ref[b * clusters + c, k:k + 1, :] = ref[c:c + 1, k * cl:(k + 1) * cl]
    sources_ref[3 * clusters] = jnp.zeros_like(sources_ref[3 * clusters])
    fill_charges(pieces_ref, (left_ref, own_ref, right_ref), clusters, cl)
    for c in range(clusters):
        columns_of(own_centroid_ref, c, cl, columns_ref, c)
        total_ref[c] = jnp.zeros_like(total_ref[c])
    steps = (count + 1) // 2

    def build(ref, m, which):
        c, j = list_ref[0, 2 * m + which], list_ref[1, 2 * m + which]
        source = lambda k, h: sources_ref[j, k:k + 1, h * LANES:(h + 1) * LANES]
        near_block([columns_ref[c, k] for k in range(3)], source, cl, ref, m)

    def apply(ref, m, which):
        c, j = list_ref[0, 2 * m + which], list_ref[1, 2 * m + which]
        total_ref[c] += near_product(pieces_ref[j], ref, m, cl)

    def send(ref, m, which):
        return pltpu.make_async_copy(ref.at[m], blocks_ref.at[2 * m + which], sems.at[which])

    def step(m, _):
        build(even_ref, m, 0)
        send(even_ref, m, 0).start()
        apply(even_ref, m, 0)
        build(odd_ref, m, 1)
        send(odd_ref, m, 1).start()
        apply(odd_ref, m, 1)
        return 0

    lax.fori_loop(0, steps, step, 0)
    for c in range(clusters):
        panels = slice(c * cl, (c + 1) * cl)
        near_out_ref[:, panels] = start_ref[:, panels] + folded(total_ref[c])

    def drain(m, _):
        send(even_ref, m, 0).wait()
        send(odd_ref, m, 1).wait()
        return 0

    lax.fori_loop(0, steps, drain, 0)


def gather_tables(position, far_ref, table_ref, rank, pieces_ref, middle_ref, each):
    devices, _, span = table_ref.shape
    rhs = pieces_ref.shape[1] // 2
    per = LANES // rank
    groups = span // LANES
    clusters = far_ref.shape[0]
    window = 2 * REACH + 1

    def load(b, _):
        block = jnp.clip(position - REACH + b, 0, devices - 1)
        for g in range(groups):
            tile = table_ref[block, :, g * LANES:(g + 1) * LANES]
            for s in range(per):
                turned = pltpu.roll(tile, s * rank, 1) if s else tile
                at = (s * window + b) * groups + g
                pieces_ref[at] = stacked(turned[:rhs])
                if middle_ref is not None:
                    middle_ref[at] = turned[rhs:]
        return 0

    lax.fori_loop(0, window, load, 0)
    lane = lax.broadcasted_iota(jnp.int32, (1, LANES), 1) // rank
    base = (position - REACH) * clusters

    def cluster(c, _):
        rows, centers = [], []
        for g in range(far_ref.shape[1] // per):
            row = center = None
            for u in range(per):
                j = far_ref[c, g * per + u] - base
                at = lax.rem(u - j + 4 * per * window * clusters, per) * (window * groups) + j // per
                take = pieces_ref[at]
                row = take if row is None else jnp.where(lane == u, take, row)
                if middle_ref is not None:
                    take = middle_ref[at]
                    center = take if center is None else jnp.where(lane == u, take, center)
            rows.append(row)
            centers.append(center)
        each(c, jnp.concatenate(rows, axis=1), centers)
        return 0

    lax.fori_loop(0, clusters, cluster, 0)


def far_potential(gathered, coupling, basis_block, rank):
    field = folded(dot_nt(gathered, coupling))
    field = stacked(field[:, 0:rank] + field[:, rank:2 * rank])
    high, low = split(basis_block)
    return folded(dot_nn(field, high) + dot_nn(field, low))


def image_kernel(cl, rank, position_ref, far_ref, table_ref, own_table_ref, basis_ref, area_ref, near_ref, krylov_ref, upright_ref, flat_ref,
                 image_ref, charges_ref, moments_ref, coupling_ref, pieces_ref, middle_ref):
    rhs = krylov_ref.shape[0]
    clusters = krylov_ref.shape[1] // cl
    span = clusters * rank

    def each(c, gathered, centers):
        panels = pl.ds(pl.multiple_of(c * cl, cl), cl)
        mine = [jnp.broadcast_to(own_table_ref[c, k:k + 1, :], (1, LANES)) for k in range(3)]
        for g, center in enumerate(centers):
            square = SMOOTHING
            for k in range(3):
                gap = (center[k:k + 1] - mine[k] + flat_ref[k:k + 1, :]) - upright_ref[k]
                square = square + gap * gap
            high, low = split(lax.rsqrt(square))
            coupling_ref[c, 0:rank, g * LANES:(g + 1) * LANES] = high
            coupling_ref[c, rank:2 * rank, g * LANES:(g + 1) * LANES] = low
        far = far_potential(gathered, coupling_ref[c], basis_ref[:, panels], rank)
        area = area_ref[0:1, panels]
        image = COULOMB * area * (near_ref[:, panels] + far)
        image_ref[:, panels] = image
        charges_ref[:, panels] = area * image

    gather_tables(position_ref[0], far_ref, table_ref, rank, pieces_ref, middle_ref, each)
    for c in range(clusters):
        panels = slice(c * cl, (c + 1) * cl)
        moments_ref[:, c * rank:(c + 1) * rank] = moments_of(charges_ref[:, panels], basis_ref[:, panels])
    image, krylov = image_ref[...], krylov_ref[...]
    squared = jnp.sum(krylov * krylov, axis=1, keepdims=True)
    correlation = jnp.sum(krylov * image, axis=1, keepdims=True)
    local = jnp.where(squared > 0, correlation / jnp.where(squared > 0, squared, 1.0), 0.0)
    residual = image - local * krylov
    energy = jnp.sum(residual * residual, axis=1, keepdims=True)
    lane = lax.broadcasted_iota(jnp.int32, (rhs, LANES), 1)
    moments_ref[:, span:] = jnp.where(lane == 0, squared, jnp.where(lane == 1, local, jnp.where(lane == 2, energy, correlation)))


def self_again_kernel(cl, charges_ref, blocks_ref, near_ref):
    clusters = charges_ref.shape[1] // cl
    for c in range(clusters):
        panels = slice(c * cl, (c + 1) * cl)
        near_ref[:, panels] = folded(near_product(stacked(charges_ref[:, panels]), blocks_ref, c, cl))


def finish_kernel(cl, rank, position_ref, base_ref, near_ref, far_ref, blocks_ref, own_ref, left_ref, right_ref, start_ref, table_ref, coupling_ref,
                  basis_ref, area_ref, image_ref, krylov_ref, next_ref, second_ref, held_ref, charge_ref, pieces_ref, total_ref, list_ref, sems):
    rhs = krylov_ref.shape[0]
    clusters = krylov_ref.shape[1] // cl
    span = clusters * rank
    devices = table_ref.shape[0]
    count = list_pairs(near_ref, base_ref[0], clusters, list_ref)
    steps = (count + 1) // 2

    def fetch(i):
        return pltpu.make_async_copy(blocks_ref.at[i], held_ref.at[i], sems.at[i])

    def begin(m, _):
        fetch(2 * m).start()
        fetch(2 * m + 1).start()
        return 0

    lax.fori_loop(0, steps, begin, 0)

    def add(d, sums):
        return sums[0] + table_ref[d, :, span:], sums[1]

    squared = correlation = jnp.zeros((rhs, 1), F32)
    for d in range(devices):
        squared = squared + table_ref[d, :, span:span + 1]
        correlation = correlation + table_ref[d, :, span + 3:span + 4]
    projection = correlation / (squared + 1e-06)
    energy = jnp.zeros((rhs, 1), F32)
    for d in range(devices):
        gap = projection - table_ref[d, :, span + 1:span + 2]
        energy = energy + table_ref[d, :, span + 2:span + 3] + gap * gap * table_ref[d, :, span:span + 1]
    scaling = jnp.sqrt(energy / (krylov_ref.shape[1] * devices) + 1e-06)
    next_ref[...] = (image_ref[...] - projection * krylov_ref[...]) / scaling
    fill_charges(charge_ref, (left_ref, own_ref, right_ref), clusters, cl)
    for c in range(clusters):
        total_ref[c] = jnp.zeros_like(total_ref[c])

    def step(m, _):
        for which in range(2):
            i = 2 * m + which
            fetch(i).wait()
            c, j = list_ref[0, i], list_ref[1, i]
            total_ref[c] += near_product(charge_ref[j], held_ref, i, cl)
        return 0

    lax.fori_loop(0, steps, step, 0)

    def each(c, gathered, _):
        panels = pl.ds(pl.multiple_of(c * cl, cl), cl)
        far = far_potential(gathered, coupling_ref[c], basis_ref[:, panels], rank)
        image = COULOMB * area_ref[0:1, panels] * (start_ref[:, panels] + folded(total_ref[c]) + far)
        second_ref[:, panels] = (image - projection * image_ref[:, panels]) / scaling

    gather_tables(position_ref[0], far_ref, table_ref.at[:, :, 0:span], rank, pieces_ref, None, each)


def call(kernel, outs, scratch, memory, *args, limit=48):
    spaces = {"s": pltpu.SMEM, "v": pltpu.VMEM, "a": pl.ANY}
    ins, out_spaces = memory.split(">")
    return pl.pallas_call(
        kernel,
        out_shape=[jax.ShapeDtypeStruct(*out) for out in outs],
        in_specs=[pl.BlockSpec(memory_space=spaces[m]) for m in ins],
        out_specs=[pl.BlockSpec(memory_space=spaces[m]) for m in out_spaces],
        scratch_shapes=scratch,
        compiler_params=pltpu.CompilerParams(vmem_limit_bytes=limit * 2 ** 20),
    )(*args)


def body(vertices, panel_vertices, near_pairs, far_pairs, basis, krylov):
    clusters, slots = near_pairs.shape
    partners = far_pairs.shape[1]
    rhs, panels = krylov.shape
    rank = basis.shape[0]
    cl = panels // clusters
    vcl = vertices.shape[1] // clusters
    span = clusters * rank
    devices = lax.axis_size("clus")
    position = lax.axis_index("clus")
    place = position.reshape(1).astype(jnp.int32)
    base = ((position - 1) * clusters).reshape(1).astype(jnp.int32)
    corner_base = (position * vertices.shape[1]).reshape(1).astype(jnp.int32)
    offsets = proxy_offsets(rank)
    upright = jnp.asarray(np.ascontiguousarray(np.broadcast_to(offsets[:, :, None], (3, rank, LANES))))
    flat = jnp.asarray(np.concatenate([np.tile(offsets, (1, LANES // rank)), np.zeros((5, LANES), np.float32)]))
    live = clusters * (slots - 1) + 2
    window = (2 * REACH + 1) * (LANES // rank) * (span // LANES)
    bf_block = (2 * cl, cl)

    charges, centroid, table, area = call(
        functools.partial(prepare_kernel, cl, vcl, rank),
        [((rhs, panels), F32), ((clusters, 3 * cl), F32), ((rhs + 8, span), F32), ((8, panels), F32)],
        [],
        "svvvv>vvvv",
        corner_base, vertices, panel_vertices, krylov, basis,
    )

    def shifted(value, steps):
        return lax.ppermute(value, "clus", [(i, i + steps) for i in range(devices) if 0 <= i + steps < devices])

    packed = jnp.concatenate([charges, centroid], axis=1)
    left, right = shifted(packed, 1), shifted(packed, -1)
    tables = lax.all_gather(table, "clus", axis=0)
    own_blocks, near = call(
        functools.partial(self_kernel, cl),
        [((clusters,) + bf_block, BF16), ((rhs, panels), F32)],
        [pltpu.VMEM((2, 3, cl, LANES), F32)],
        "vv>vv",
        charges, centroid,
    )
    blocks, near = call(
        functools.partial(remote_kernel, cl),
        [((live,) + bf_block, BF16), ((rhs, panels), F32)],
        [
            pltpu.VMEM((3 * clusters + 1, 2 * rhs, cl), BF16),
            pltpu.VMEM((3 * clusters + 1, 8, cl), F32),
            pltpu.VMEM((clusters, 3, cl, LANES), F32),
            pltpu.VMEM((live // 2,) + bf_block, BF16),
            pltpu.VMEM((live // 2,) + bf_block, BF16),
            pltpu.VMEM((clusters, 2 * rhs, cl), F32),
            pltpu.SMEM((2, live), jnp.int32),
            pltpu.SemaphoreType.DMA((2,)),
        ],
        "ssvvvvvvv>av",
        base, near_pairs, charges, left[:, :panels], right[:, :panels], centroid, left[:, panels:], right[:, panels:], near,
    )
    centers = jnp.transpose(table[rhs:].reshape(8, clusters, rank), (1, 0, 2))[:, :, 0:1]
    image, second_charges, moments, coupling = call(
        functools.partial(image_kernel, cl, rank),
        [((rhs, panels), F32), ((rhs, panels), F32), ((rhs, span + LANES), F32), ((clusters, 2 * rank, partners * rank), BF16)],
        [pltpu.VMEM((window, 2 * rhs, LANES), BF16), pltpu.VMEM((window, 8, LANES), F32)],
        "ssvvvvvvvv>vvvv",
        place, far_pairs, tables, centers, basis, area, near, krylov, upright, flat,
    )
    left, right = shifted(second_charges, 1), shifted(second_charges, -1)
    tables = lax.all_gather(moments, "clus", axis=0)
    (near,) = call(
        functools.partial(self_again_kernel, cl),
        [((rhs, panels), F32)],
        [],
        "vv>v",
        second_charges, own_blocks,
    )
    return tuple(call(
        functools.partial(finish_kernel, cl, rank),
        [((rhs, panels), F32), ((rhs, panels), F32)],
        [
            pltpu.VMEM((live,) + bf_block, BF16),
            pltpu.VMEM((3 * clusters + 1, 2 * rhs, cl), BF16),
            pltpu.VMEM((window, 2 * rhs, LANES), BF16),
            pltpu.VMEM((clusters, 2 * rhs, cl), F32),
            pltpu.SMEM((2, live), jnp.int32),
            pltpu.SemaphoreType.DMA((live,)),
        ],
        "ssssavvvvvvvvvv>vv",
        place, base, near_pairs, far_pairs, blocks, second_charges, left, right, near, tables, coupling, basis, area, image, krylov,
    ))


def solution(mesh):
    whole = P(None, ("jobs", "clus"))
    rows = P(("jobs", "clus"), None)
    return jax.shard_map(
        body,
        mesh=mesh,
        in_specs=(whole, whole, rows, rows, whole, whole),
        out_specs=(whole, whole),
        check_vma=False,
    )
```

```python
import functools

import jax
import jax.numpy as jnp
import numpy as np
from jax import lax
from jax.experimental import pallas as pl
from jax.experimental.pallas import tpu as pltpu
from jax.sharding import PartitionSpec as P

REACH = 4
SMOOTHING = 0.04
COULOMB = 2.0
PROXY_RADIUS = 0.6
LANES = 128
F32 = jnp.float32
BF16 = jnp.bfloat16


def proxy_offsets(points):
    counter = np.arange(points, dtype=np.float32)
    height = 1.0 - (2.0 * counter + 1.0) / points
    radial = np.sqrt(1.0 - height * height)
    azimuth = counter * 2.399963
    return PROXY_RADIUS * np.stack([radial * np.cos(azimuth), radial * np.sin(azimuth), height]).astype(np.float32)


def split(value):
    high = value.astype(BF16)
    return high, (value - high.astype(F32)).astype(BF16)


def stacked(value):
    return jnp.concatenate(split(value), axis=0)


def folded(value):
    half = value.shape[0] // 2
    return value[:half] + value[half:]


def dot_nt(left, right):
    return lax.dot_general(left, right, (((1,), (1,)), ((), ())), preferred_element_type=F32)


def dot_nn(left, right):
    return lax.dot_general(left, right, (((1,), (0,)), ((), ())), preferred_element_type=F32)


def moments_of(weighted, basis_block):
    pieces = stacked(weighted)
    high, low = split(basis_block)
    return folded(dot_nt(pieces, high) + dot_nt(pieces, low))


def prepare_kernel(cl, vcl, rank, base_ref, vertices_hbm, corners_hbm, krylov_hbm, basis_hbm, payload_ref, area_ref, center_ref,
                   vertices_ref, corners_ref, krylov_ref, basis_ref, mesh_ref, local_ref, sems):
    moves = [
        pltpu.make_async_copy(source, target, sems.at[i])
        for i, (source, target) in enumerate(((vertices_hbm, vertices_ref), (corners_hbm, corners_ref), (krylov_hbm, krylov_ref), (basis_hbm, basis_ref)))
    ]
    for move in moves:
        move.start()
    rhs, panels = krylov_ref.shape
    clusters = panels // cl
    parts = cl // LANES
    moves[0].wait()
    for c in range(clusters):
        mesh_ref[3 * c:3 * c + 3, :] = vertices_ref[:, c * vcl:(c + 1) * vcl]
    moves[1].wait()
    for i in range(clusters * parts):
        local_ref[3 * i:3 * i + 3, :] = corners_ref[:, i * LANES:(i + 1) * LANES]
    first = base_ref[0] + vcl * lax.broadcasted_iota(jnp.int32, (clusters, LANES), 0)
    tables = [mesh_ref[pl.ds(k, clusters, stride=3), :] for k in range(3)]
    sums = [None] * 3
    for h in range(parts):
        local = [local_ref[pl.ds(3 * h + m, clusters, stride=3 * parts), :] - first for m in range(3)]
        corner = [[jnp.take_along_axis(tables[k], local[m], axis=1, mode="promise_in_bounds") for k in range(3)] for m in range(3)]
        for k in range(3):
            middle = (corner[0][k] + corner[1][k] + corner[2][k]) / 3.0
            payload_ref[:, panels + k * cl + h * LANES:panels + k * cl + (h + 1) * LANES] = middle
            sums[k] = middle if h == 0 else sums[k] + middle
        one = [corner[1][k] - corner[0][k] for k in range(3)]
        two = [corner[2][k] - corner[0][k] for k in range(3)]
        normal = [one[1] * two[2] - one[2] * two[1], one[2] * two[0] - one[0] * two[2], one[0] * two[1] - one[1] * two[0]]
        area_ref[:, h * LANES:(h + 1) * LANES] = 0.5 * jnp.sqrt(normal[0] * normal[0] + normal[1] * normal[1] + normal[2] * normal[2])
    table = panels + 3 * cl
    span = clusters * rank
    mine = lax.broadcasted_iota(jnp.int32, (clusters, span), 1) // rank == lax.broadcasted_iota(jnp.int32, (clusters, span), 0)
    half = span // 2
    payload_ref[:, table + span:] = jnp.zeros_like(payload_ref[:, table + span:])
    for k in range(3):
        center = jnp.sum(sums[k], axis=1, keepdims=True) / cl
        center_ref[:, k * LANES:(k + 1) * LANES] = jnp.broadcast_to(center, (clusters, LANES))
        row = jnp.sum(jnp.where(mine, center, 0.0), axis=0, keepdims=True)
        payload_ref[k:k + 1, table + span:] = row[:, 0:half]
        payload_ref[8 + k:9 + k, table + span:] = row[:, half:]
    moves[2].wait()
    moves[3].wait()
    for c in range(clusters):
        lanes = slice(c * cl, (c + 1) * cl)
        charges = area_ref[c:c + 1, :] * krylov_ref[:, lanes]
        payload_ref[:, lanes] = charges
        payload_ref[:, table + c * rank:table + (c + 1) * rank] = moments_of(charges, basis_ref[:, lanes])


def columns_of(payload_ref, panels, c, cl, columns_ref, at):
    rows = [payload_ref[c:c + 1, panels + k * cl:panels + (k + 1) * cl] for k in range(3)]
    upright = jnp.transpose(jnp.concatenate(rows * 2 + rows[:2], axis=0))
    for k in range(3):
        columns_ref[at, k] = jnp.broadcast_to(upright[:, k:k + 1], (cl, LANES))


def near_block(columns, source, cl, out_ref, at):
    for h in range(cl // LANES):
        lanes = slice(h * LANES, (h + 1) * LANES)
        gap = [columns[k] - source(k, h) for k in range(3)]
        square = gap[0] * gap[0] + gap[1] * gap[1] + gap[2] * gap[2]
        high, low = split(lax.rsqrt(square + SMOOTHING))
        out_ref[at, 0:cl, lanes] = high
        out_ref[at, cl:2 * cl, lanes] = low


def near_product(pieces, block_ref, at, cl):
    return dot_nt(pieces, block_ref[at, 0:cl, :]) + dot_nt(pieces, block_ref[at, cl:2 * cl, :])


def self_kernel(cl, payload_ref, blocks_ref, near_ref, columns_ref):
    panels = near_ref.shape[1]
    for c in range(panels // cl):
        columns_of(payload_ref, panels, c, cl, columns_ref, c % 2)
        source = lambda k, h: payload_ref[c:c + 1, panels + k * cl + h * LANES:panels + k * cl + (h + 1) * LANES]
        near_block([columns_ref[c % 2, k] for k in range(3)], source, cl, blocks_ref, c)
        lanes = slice(c * cl, (c + 1) * cl)
        near_ref[:, lanes] = folded(near_product(stacked(payload_ref[:, lanes]), blocks_ref, c, cl))


def self_again_kernel(cl, payload_ref, blocks_ref, near_ref):
    for c in range(near_ref.shape[1] // cl):
        lanes = slice(c * cl, (c + 1) * cl)
        near_ref[:, lanes] = folded(near_product(stacked(payload_ref[:, lanes]), blocks_ref, c, cl))


def fill_charges(pieces_ref, blocks, clusters, cl):
    for b, ref in enumerate(blocks):
        for c in range(clusters):
            pieces_ref[b * clusters + c] = stacked(ref[:, c * cl:(c + 1) * cl])
    pieces_ref[3 * clusters] = jnp.zeros_like(pieces_ref[3 * clusters])


def list_pairs(near_ref, base, list_ref, pad):
    slots, clusters = near_ref.shape
    n = jnp.int32(0)
    for c in range(clusters):
        for k in range(1, slots):
            j = near_ref[k, c]
            list_ref[0, n] = jnp.int32(c)
            list_ref[1, n] = j - base
            list_ref[2, n] = n
            n = n + (j >= 0).astype(jnp.int32)
    for i in range(pad):
        list_ref[0, n + i] = jnp.int32(0)
        list_ref[1, n + i] = jnp.int32(3 * clusters)
        list_ref[2, n + i] = jnp.int32(0)
    return n


def remote_kernel(cl, base_ref, near_ref, own_ref, left_ref, right_ref, start_ref, even_ref, odd_ref, near_out_ref,
                  pieces_ref, sources_ref, columns_ref, total_ref, list_ref):
    panels = start_ref.shape[1]
    clusters = panels // cl
    count = list_pairs(near_ref, base_ref[0], list_ref, 2)
    sources_ref[3 * clusters] = jnp.zeros_like(sources_ref[3 * clusters])
    for b, ref in enumerate((left_ref, own_ref, right_ref)):
        for c in range(clusters):
            for k in range(3):
                sources_ref[b * clusters + c, k:k + 1, :] = ref[c:c + 1, panels + k * cl:panels + (k + 1) * cl]
    fill_charges(pieces_ref, (left_ref, own_ref, right_ref), clusters, cl)
    for c in range(clusters):
        columns_of(own_ref, panels, c, cl, columns_ref, c)
        total_ref[c] = jnp.zeros_like(total_ref[c])
    odd_ref[0] = jnp.zeros_like(odd_ref[0])
    steps = (count + 1) // 2

    def build(ref, at, i):
        c, j = list_ref[0, i], list_ref[1, i]
        source = lambda k, h: sources_ref[j, k:k + 1, h * LANES:(h + 1) * LANES]
        near_block([columns_ref[c, k] for k in range(3)], source, cl, ref, at)

    def product(ref, at, i):
        return near_product(pieces_ref[list_ref[1, i]], ref, at, cl)

    def step(m, _):
        before = jnp.maximum(2 * m - 1, 0)
        part = product(odd_ref, m, before)
        build(even_ref, m, 2 * m)
        total_ref[list_ref[0, before]] += part
        part = product(even_ref, m, 2 * m)
        build(odd_ref, m + 1, 2 * m + 1)
        total_ref[list_ref[0, 2 * m]] += part
        return 0

    lax.fori_loop(0, steps, step, 0)
    last = jnp.maximum(2 * steps - 1, 0)
    total_ref[list_ref[0, last]] += product(odd_ref, steps, last)
    for c in range(clusters):
        lanes = slice(c * cl, (c + 1) * cl)
        near_out_ref[:, lanes] = start_ref[:, lanes] + folded(total_ref[c])


def remote_again_kernel(cl, base_ref, near_ref, own_ref, left_ref, right_ref, start_ref, even_ref, odd_ref, near_out_ref, pieces_ref, total_ref, list_ref):
    clusters = start_ref.shape[1] // cl
    count = list_pairs(near_ref, base_ref[0], list_ref, 4)
    fill_charges(pieces_ref, (left_ref, own_ref, right_ref), clusters, cl)
    for c in range(clusters):
        total_ref[c] = jnp.zeros_like(total_ref[c])

    def step(m, _):
        parts = []
        for w in range(4):
            i = 4 * m + w
            at = list_ref[2, i]
            parts.append(near_product(pieces_ref[list_ref[1, i]], (even_ref, odd_ref)[w % 2], at // 2 + w % 2, cl))
        for w in range(4):
            total_ref[list_ref[0, 4 * m + w]] += parts[w]
        return 0

    lax.fori_loop(0, (count + 3) // 4, step, 0)
    for c in range(clusters):
        lanes = slice(c * cl, (c + 1) * cl)
        near_out_ref[:, lanes] = start_ref[:, lanes] + folded(total_ref[c])


def window_tiles(tables, clusters, rank):
    groups = clusters * rank // LANES
    width = tables[0].shape[1] // 3
    for side, ref in enumerate(tables):
        for b in range(3):
            for g in range(groups):
                yield (side * 3 + b) * groups + g, ref, b * width, g


def load_window(tables, clusters, rank, pieces_ref, middle_ref):
    rhs = pieces_ref.shape[1] // 2
    per = LANES // rank
    span = clusters * rank
    count = pieces_ref.shape[0] // per
    for at, ref, first, g in window_tiles(tables, clusters, rank):
        tile = ref[:, first + g * LANES:first + (g + 1) * LANES]
        for s in range(per):
            pieces_ref[s * count + at] = stacked(pltpu.roll(tile, s * rank, 1) if s else tile)
        if middle_ref is not None:
            half = span // 2 // LANES
            row, lane = 8 * (g // half), first + span + g % half * LANES
            tile = ref[row:row + 8, lane:lane + LANES]
            for s in range(per):
                middle_ref[s * count + at] = pltpu.roll(tile, s * rank, 1) if s else tile


def pick(source_ref, at_ref, c, g, per, lane):
    row = None
    for u in range(per):
        take = source_ref[at_ref[c, g * per + u]]
        row = take if row is None else jnp.where(lane == u, take, row)
    return row


def far_fields(gathered_ref, coupling_ref, fields_ref, rank):
    for c in range(gathered_ref.shape[0]):
        field = folded(dot_nt(gathered_ref[c], coupling_ref[c]))
        fields_ref[c] = stacked(field[:, 0:rank] + field[:, rank:2 * rank])


def far_potential(field, basis_block):
    high, low = split(basis_block)
    return folded(dot_nn(field, high) + dot_nn(field, low))


def image_kernel(cl, rank, at_ref, below_ref, above_ref, center_ref, basis_ref, area_ref, near_ref, krylov_ref, upright_ref, flat_ref,
                 image_ref, payload_ref, coupling_ref, pieces_ref, middle_ref, gathered_ref, fields_ref):
    rhs, panels = krylov_ref.shape
    clusters = panels // cl
    span = clusters * rank
    per = LANES // rank
    load_window((below_ref, above_ref), clusters, rank, pieces_ref, middle_ref)
    lane = lax.broadcasted_iota(jnp.int32, (1, LANES), 1) // rank
    for c in range(clusters):
        mine = [flat_ref[k:k + 1, :] - center_ref[c:c + 1, k * LANES:(k + 1) * LANES] for k in range(3)]
        for g in range(at_ref.shape[1] // per):
            lanes = slice(g * LANES, (g + 1) * LANES)
            gathered_ref[c, :, lanes] = pick(pieces_ref, at_ref, c, g, per, lane)
            center = pick(middle_ref, at_ref, c, g, per, lane)
            gap = [(center[k:k + 1] + mine[k]) - upright_ref[k] for k in range(3)]
            high, low = split(lax.rsqrt(gap[0] * gap[0] + gap[1] * gap[1] + gap[2] * gap[2] + SMOOTHING))
            coupling_ref[c, 0:rank, lanes] = high
            coupling_ref[c, rank:2 * rank, lanes] = low
    far_fields(gathered_ref, coupling_ref, fields_ref, rank)
    squared = correlation = jnp.zeros((rhs, cl), F32)
    for c in range(clusters):
        lanes = slice(c * cl, (c + 1) * cl)
        area = area_ref[c:c + 1, :]
        image = COULOMB * area * (near_ref[:, lanes] + far_potential(fields_ref[c], basis_ref[:, lanes]))
        image_ref[:, lanes] = image
        payload_ref[:, lanes] = area * image
        krylov = krylov_ref[:, lanes]
        squared = squared + krylov * krylov
        correlation = correlation + krylov * image
    for c in range(clusters):
        lanes = slice(c * cl, (c + 1) * cl)
        payload_ref[:, panels + c * rank:panels + (c + 1) * rank] = moments_of(payload_ref[:, lanes], basis_ref[:, lanes])
    squared = jnp.sum(squared, axis=1, keepdims=True)
    correlation = jnp.sum(correlation, axis=1, keepdims=True)
    local = ratio(correlation, squared)
    residual = image_ref[...] - local * krylov_ref[...]
    payload_ref[:, panels + span:] = in_lanes(squared, correlation, jnp.sum(residual * residual, axis=1, keepdims=True), local)


def ratio(correlation, squared):
    return jnp.where(squared > 0, correlation / jnp.where(squared > 0, squared, 1.0), 0.0)


def in_lanes(*columns):
    lane = lax.broadcasted_iota(jnp.int32, (columns[0].shape[0], LANES), 1)
    out = columns[-1]
    for i, column in enumerate(columns[:-1]):
        out = jnp.where(lane == i, column, out)
    return out


def merged(groups):
    squared = sum(group[:, 0:1] for group in groups)
    correlation = sum(group[:, 1:2] for group in groups)
    local = ratio(correlation, squared)
    energy = 0.0
    for group in groups:
        gap = local - group[:, 3:4]
        energy = energy + (group[:, 2:3] + gap * gap * group[:, 0:1])
    return squared, correlation, energy, local


def window_sums_kernel(at, *refs):
    own_ref, left_ref, right_ref, below_ref, above_ref, out_ref = refs
    width = below_ref.shape[1] // 3
    groups = [ref[:, ref.shape[1] - LANES:] for ref in (own_ref, left_ref, right_ref)]
    groups += [below_ref[:, (b + 1) * width - LANES:(b + 1) * width] for b in range(3)]
    groups += [above_ref[:, (b + 1) * width - LANES:(b + 1) * width] for b in range(2)]
    out_ref[...] = in_lanes(*merged(groups))


def double_sums_kernel(one_ref, two_ref, out_ref):
    out_ref[...] = in_lanes(*merged([one_ref[...], two_ref[...]]))


def far_again_kernel(cl, rank, at_ref, below_ref, above_ref, coupling_ref, basis_ref, area_ref, near_ref, image_ref, pieces_ref, gathered_ref, fields_ref):
    clusters = near_ref.shape[1] // cl
    per = LANES // rank
    load_window((below_ref, above_ref), clusters, rank, pieces_ref, None)
    lane = lax.broadcasted_iota(jnp.int32, (1, LANES), 1) // rank
    for c in range(clusters):
        for g in range(at_ref.shape[1] // per):
            gathered_ref[c, :, g * LANES:(g + 1) * LANES] = pick(pieces_ref, at_ref, c, g, per, lane)
    far_fields(gathered_ref, coupling_ref, fields_ref, rank)
    for c in range(clusters):
        lanes = slice(c * cl, (c + 1) * cl)
        image_ref[:, lanes] = COULOMB * area_ref[c:c + 1, :] * (near_ref[:, lanes] + far_potential(fields_ref[c], basis_ref[:, lanes]))


def finish_kernel(total, one_ref, two_ref, krylov_ref, image_ref, again_ref, next_ref, second_ref):
    squared, correlation, energy, local = merged([one_ref[...], two_ref[...]])
    projection = correlation / (squared + 1e-06)
    gap = projection - local
    scaling = 1.0 / jnp.sqrt((energy + gap * gap * squared) / total + 1e-06)
    image = image_ref[...]
    next_ref[...] = (image - projection * krylov_ref[...]) * scaling
    second_ref[...] = (again_ref[...] - projection * image) * scaling


def call(kernel, outs, scratch, memory, *args, limit=24):
    spaces = {"s": pltpu.SMEM, "v": pltpu.VMEM, "a": pl.ANY, "h": pltpu.HBM}
    ins, out_spaces = memory.split(">")
    return pl.pallas_call(
        kernel,
        out_shape=[jax.ShapeDtypeStruct(*out) for out in outs],
        in_specs=[pl.BlockSpec(memory_space=spaces[m]) for m in ins],
        out_specs=[pl.BlockSpec(memory_space=spaces[m]) for m in out_spaces],
        scratch_shapes=scratch,
        compiler_params=pltpu.CompilerParams(vmem_limit_bytes=limit * 2 ** 20),
    )(*args)


def body(vertices, panel_vertices, near_pairs, far_pairs, basis, krylov):
    clusters, slots = near_pairs.shape
    partners = far_pairs.shape[1]
    rhs, panels = krylov.shape
    rank = basis.shape[0]
    cl = panels // clusters
    vcl = vertices.shape[1] // clusters
    span = clusters * rank
    per = LANES // rank
    devices = lax.axis_size("clus")
    position = lax.axis_index("clus")
    base = ((position - 1) * clusters).reshape(1).astype(jnp.int32)
    corner_base = (position * vertices.shape[1]).reshape(1).astype(jnp.int32)
    offsets = proxy_offsets(rank)
    upright = jnp.asarray(np.ascontiguousarray(np.broadcast_to(offsets[:, :, None], (3, rank, LANES))))
    flat = jnp.asarray(np.concatenate([np.tile(offsets, (1, per)), np.zeros((5, LANES), np.float32)]))
    live = clusters * (slots - 1)
    half = ((live + 1) // 2 + 1, 2 * cl, cl)
    near_lists = near_pairs.T
    step = far_pairs // clusters - position
    block = jnp.where(step < 0, step + REACH, step + REACH - 3)
    turn = (jnp.arange(partners, dtype=jnp.int32) - far_pairs) % per
    tiles = 6 * span // LANES
    at = turn * tiles + block * (span // LANES) + far_pairs % clusters // per

    def shifted(value, steps):
        return lax.ppermute(value, "clus", [(i, (i + steps) % devices) for i in range(devices)])

    def relayed(own, left, right, first):
        triple = jnp.concatenate([value[:, first:] for value in (left, own, right)], axis=1)
        return shifted(triple, 3), shifted(triple, -3)

    table = panels + 3 * cl
    payload, area, centers = call(
        functools.partial(prepare_kernel, cl, vcl, rank),
        [((rhs, table + span + span // 2), F32), ((clusters, cl), F32), ((clusters, 3 * LANES), F32)],
        [
            pltpu.VMEM(vertices.shape, F32),
            pltpu.VMEM(panel_vertices.shape, jnp.int32),
            pltpu.VMEM(krylov.shape, F32),
            pltpu.VMEM(basis.shape, F32),
            pltpu.VMEM((3 * clusters, vcl), F32),
            pltpu.VMEM((3 * panels // LANES, LANES), jnp.int32),
            pltpu.SemaphoreType.DMA((4,)),
        ],
        "shhhh>vvv",
        corner_base, vertices, panel_vertices, krylov, basis,
    )
    left, right = shifted(payload, 1), shifted(payload, -1)
    own_blocks, near = call(
        functools.partial(self_kernel, cl),
        [((clusters, 2 * cl, cl), BF16), ((rhs, panels), F32)],
        [pltpu.VMEM((2, 3, cl, LANES), F32)],
        "v>vv",
        payload,
    )
    below, above = relayed(payload, left, right, table)
    pieces = pltpu.VMEM((3 * clusters + 1, 2 * rhs, cl), BF16)
    total = pltpu.VMEM((clusters, 2 * rhs, cl), F32)
    pairs = pltpu.SMEM((3, live + 4), jnp.int32)
    even, odd, near = call(
        functools.partial(remote_kernel, cl),
        [(half, BF16), (half, BF16), ((rhs, panels), F32)],
        [pieces, pltpu.VMEM((3 * clusters + 1, 8, cl), F32), pltpu.VMEM((clusters, 3, cl, LANES), F32), total, pairs],
        "ssvvvv>vvv",
        base, near_lists, payload, left, right, near,
    )
    window = pltpu.VMEM((per * tiles, 2 * rhs, LANES), BF16)
    gathered = pltpu.VMEM((clusters, 2 * rhs, partners * rank), BF16)
    fields = pltpu.VMEM((clusters, 2 * rhs, rank), BF16)
    image, payload, coupling = call(
        functools.partial(image_kernel, cl, rank),
        [((rhs, panels), F32), ((rhs, panels + span + LANES), F32), ((clusters, 2 * rank, partners * rank), BF16)],
        [window, pltpu.VMEM((per * tiles, 8, LANES), F32), gathered, fields],
        "svvvvvvvvv>vvv",
        at, below, above, centers, basis, area, near, krylov, upright, flat,
    )
    left, right = shifted(payload, 1), shifted(payload, -1)
    (near,) = call(functools.partial(self_again_kernel, cl), [((rhs, panels), F32)], [], "vv>v", payload, own_blocks)
    below, above = relayed(payload, left, right, panels)
    (near,) = call(
        functools.partial(remote_again_kernel, cl),
        [((rhs, panels), F32)],
        [pieces, total, pairs],
        "ssvvvvvv>v",
        base, near_lists, payload, left, right, near, even, odd,
    )
    sums_shape = [((rhs, LANES), F32)]
    (sums,) = call(functools.partial(window_sums_kernel, panels), sums_shape, [], "vvvvv>v", payload, left, right, below, above)
    size = 2 * REACH
    other = shifted(sums, size)
    while 2 * size < devices:
        (sums,) = call(double_sums_kernel, sums_shape, [], "vv>v", sums, other)
        size = 2 * size
        other = shifted(sums, size)
    (again,) = call(
        functools.partial(far_again_kernel, cl, rank),
        [((rhs, panels), F32)],
        [window, gathered, fields],
        "svvvvvv>v",
        at, below, above, coupling, basis, area, near,
    )
    return tuple(call(
        functools.partial(finish_kernel, panels * devices),
        [((rhs, panels), F32), ((rhs, panels), F32)],
        [],
        "vvvvv>vv",
        sums, other, krylov, image, again,
    ))


def solution(mesh):
    whole = P(None, ("jobs", "clus"))
    rows = P(("jobs", "clus"), None)
    return jax.shard_map(
        body,
        mesh=mesh,
        in_specs=(whole, whole, rows, rows, whole, whole),
        out_specs=(whole, whole),
        check_vma=False,
    )
```

```python
import functools

import jax
import jax.numpy as jnp
import numpy as np
from jax import lax
from jax.experimental import pallas as pl
from jax.experimental.pallas import tpu as pltpu
from jax.sharding import PartitionSpec as P

REACH = 4
SMOOTHING = 0.04
COULOMB = 2.0
PROXY_RADIUS = 0.6
LANES = 128
F32 = jnp.float32
BF16 = jnp.bfloat16


def proxy_offsets(points):
    counter = np.arange(points, dtype=np.float32)
    height = 1.0 - (2.0 * counter + 1.0) / points
    radial = np.sqrt(1.0 - height * height)
    azimuth = counter * 2.399963
    return PROXY_RADIUS * np.stack([radial * np.cos(azimuth), radial * np.sin(azimuth), height]).astype(np.float32)


def split(value):
    high = value.astype(BF16)
    return high, (value - high.astype(F32)).astype(BF16)


def stacked(value):
    return jnp.concatenate(split(value), axis=0)


def folded(value):
    half = value.shape[0] // 2
    return value[:half] + value[half:]


def dot_nt(left, right):
    return lax.dot_general(left, right, (((1,), (1,)), ((), ())), preferred_element_type=F32)


def dot_nn(left, right):
    return lax.dot_general(left, right, (((1,), (0,)), ((), ())), preferred_element_type=F32)


def moments_of(weighted, basis_block):
    pieces = stacked(weighted)
    high, low = split(basis_block)
    return folded(dot_nt(pieces, high) + dot_nt(pieces, low))


def copies(pairs, sems):
    moves = [pltpu.make_async_copy(source, target, sems.at[i]) for i, (source, target) in enumerate(pairs)]
    for move in moves:
        move.start()
    return moves


def prepare_kernel(cl, vcl, rank, position_ref, vertices_hbm, corners_hbm, krylov_hbm, basis_hbm, far_hbm, payload_ref, table_ref, area_ref, center_ref, at_ref,
                   vertices_ref, corners_ref, krylov_ref, basis_ref, far_ref, mesh_ref, local_ref, sems):
    moves = copies(((vertices_hbm, vertices_ref), (corners_hbm, corners_ref), (krylov_hbm, krylov_ref), (basis_hbm, basis_ref), (far_hbm, far_ref)), sems)
    rhs, panels = krylov_ref.shape
    clusters = panels // cl
    parts = cl // LANES
    moves[0].wait()
    for c in range(clusters):
        mesh_ref[3 * c:3 * c + 3, :] = vertices_ref[:, c * vcl:(c + 1) * vcl]
    moves[1].wait()
    for i in range(clusters * parts):
        local_ref[3 * i:3 * i + 3, :] = corners_ref[:, i * LANES:(i + 1) * LANES]
    first = position_ref[0] * (vcl * clusters) + vcl * lax.broadcasted_iota(jnp.int32, (clusters, LANES), 0)
    tables = [mesh_ref[pl.ds(k, clusters, stride=3), :] for k in range(3)]
    sums = [None] * 3
    for h in range(parts):
        local = [local_ref[pl.ds(3 * h + m, clusters, stride=3 * parts), :] - first for m in range(3)]
        corner = [[jnp.take_along_axis(tables[k], local[m], axis=1, mode="promise_in_bounds") for k in range(3)] for m in range(3)]
        for k in range(3):
            middle = (corner[0][k] + corner[1][k] + corner[2][k]) / 3.0
            payload_ref[:, panels + k * cl + h * LANES:panels + k * cl + (h + 1) * LANES] = middle
            sums[k] = middle if h == 0 else sums[k] + middle
        one = [corner[1][k] - corner[0][k] for k in range(3)]
        two = [corner[2][k] - corner[0][k] for k in range(3)]
        normal = [one[1] * two[2] - one[2] * two[1], one[2] * two[0] - one[0] * two[2], one[0] * two[1] - one[1] * two[0]]
        area_ref[:, h * LANES:(h + 1) * LANES] = 0.5 * jnp.sqrt(normal[0] * normal[0] + normal[1] * normal[1] + normal[2] * normal[2])
    span = clusters * rank
    mine = lax.broadcasted_iota(jnp.int32, (clusters, span), 1) // rank == lax.broadcasted_iota(jnp.int32, (clusters, span), 0)
    half = span // 2
    table_ref[:, span:] = jnp.zeros_like(table_ref[:, span:])
    for k in range(3):
        center = jnp.sum(sums[k], axis=1, keepdims=True) / cl
        center_ref[:, k * LANES:(k + 1) * LANES] = jnp.broadcast_to(center, (clusters, LANES))
        row = jnp.sum(jnp.where(mine, center, 0.0), axis=0, keepdims=True)
        table_ref[k:k + 1, span:] = row[:, 0:half]
        table_ref[8 + k:9 + k, span:] = row[:, half:]
    moves[2].wait()
    moves[3].wait()
    for c in range(clusters):
        lanes = slice(c * cl, (c + 1) * cl)
        charges = area_ref[c:c + 1, :] * krylov_ref[:, lanes]
        payload_ref[:, lanes] = charges
        table_ref[:, c * rank:(c + 1) * rank] = moments_of(charges, basis_ref[:, lanes])
    moves[4].wait()
    far = far_ref[...]
    step = lax.div(far, clusters) - position_ref[0]
    block = jnp.where(step < 0, step + REACH, step + REACH - 3)
    per = LANES // rank
    turn = lax.rem(lax.broadcasted_iota(jnp.int32, far.shape, 1) - far + per * clusters * 2 ** 16, per)
    at_ref[...] = (turn * 6 + block) * (span // LANES) + lax.div(lax.rem(far, clusters), per)


def columns_of(payload_ref, panels, c, cl, columns_ref, at):
    rows = [payload_ref[c:c + 1, panels + k * cl:panels + (k + 1) * cl] for k in range(3)]
    upright = jnp.transpose(jnp.concatenate(rows * 2 + rows[:2], axis=0))
    for k in range(3):
        columns_ref[at, k] = jnp.broadcast_to(upright[:, k:k + 1], (cl, LANES))


def near_block(columns, source, cl, out_ref, at):
    for h in range(cl // LANES):
        lanes = slice(h * LANES, (h + 1) * LANES)
        gap = [columns[k] - source(k, h) for k in range(3)]
        square = gap[0] * gap[0] + gap[1] * gap[1] + gap[2] * gap[2]
        high, low = split(lax.rsqrt(square + SMOOTHING))
        out_ref[at, 0:cl, lanes] = high
        out_ref[at, cl:2 * cl, lanes] = low


def near_product(pieces, block_ref, at, cl):
    return dot_nt(pieces, block_ref[at, 0:cl, :]) + dot_nt(pieces, block_ref[at, cl:2 * cl, :])


def self_kernel(cl, position_ref, pairs_ref, payload_ref, blocks_ref, near_ref, list_ref, columns_ref):
    panels = near_ref.shape[1]
    list_pairs(pairs_ref, (position_ref[0] - 1) * (panels // cl), list_ref, 4)
    for c in range(panels // cl):
        columns_of(payload_ref, panels, c, cl, columns_ref, c % 2)
        source = lambda k, h: payload_ref[c:c + 1, panels + k * cl + h * LANES:panels + k * cl + (h + 1) * LANES]
        near_block([columns_ref[c % 2, k] for k in range(3)], source, cl, blocks_ref, c)
        lanes = slice(c * cl, (c + 1) * cl)
        near_ref[:, lanes] = folded(near_product(stacked(payload_ref[:, lanes]), blocks_ref, c, cl))


def self_again_kernel(cl, payload_ref, blocks_ref, near_ref):
    for c in range(near_ref.shape[1] // cl):
        lanes = slice(c * cl, (c + 1) * cl)
        near_ref[:, lanes] = folded(near_product(stacked(payload_ref[:, lanes]), blocks_ref, c, cl))


def fill_charges(pieces_ref, blocks, clusters, cl):
    for b, ref in enumerate(blocks):
        for c in range(clusters):
            pieces_ref[b * clusters + c] = stacked(ref[:, c * cl:(c + 1) * cl])
    pieces_ref[3 * clusters] = jnp.zeros_like(pieces_ref[3 * clusters])


def list_pairs(near_ref, base, list_ref, pad):
    slots, clusters = near_ref.shape
    n = jnp.int32(0)
    for c in range(clusters):
        for k in range(1, slots):
            j = near_ref[k, c]
            list_ref[0, n] = jnp.int32(c)
            list_ref[1, n] = j - base
            list_ref[2, n] = n
            n = n + (j >= 0).astype(jnp.int32)
    for i in range(pad):
        list_ref[0, n + i] = jnp.int32(0)
        list_ref[1, n + i] = jnp.int32(3 * clusters)
        list_ref[2, n + i] = jnp.int32(0)
    list_ref[3, 0] = n


def remote_kernel(cl, list_ref, own_ref, left_ref, right_ref, start_ref, even_ref, odd_ref, near_out_ref,
                  pieces_ref, sources_ref, columns_ref, total_ref):
    panels = start_ref.shape[1]
    clusters = panels // cl
    count = list_ref[3, 0]
    sources_ref[3 * clusters] = jnp.zeros_like(sources_ref[3 * clusters])
    for b, ref in enumerate((left_ref, own_ref, right_ref)):
        for c in range(clusters):
            for k in range(3):
                sources_ref[b * clusters + c, k:k + 1, :] = ref[c:c + 1, panels + k * cl:panels + (k + 1) * cl]
    fill_charges(pieces_ref, (left_ref, own_ref, right_ref), clusters, cl)
    for c in range(clusters):
        columns_of(own_ref, panels, c, cl, columns_ref, c)
        total_ref[c] = jnp.zeros_like(total_ref[c])
    odd_ref[0] = jnp.zeros_like(odd_ref[0])
    steps = (count + 1) // 2

    def build(ref, at, i):
        c, j = list_ref[0, i], list_ref[1, i]
        source = lambda k, h: sources_ref[j, k:k + 1, h * LANES:(h + 1) * LANES]
        near_block([columns_ref[c, k] for k in range(3)], source, cl, ref, at)

    def product(ref, at, i):
        return near_product(pieces_ref[list_ref[1, i]], ref, at, cl)

    def step(m, _):
        before = jnp.maximum(2 * m - 1, 0)
        part = product(odd_ref, m, before)
        build(even_ref, m, 2 * m)
        total_ref[list_ref[0, before]] += part
        part = product(even_ref, m, 2 * m)
        build(odd_ref, m + 1, 2 * m + 1)
        total_ref[list_ref[0, 2 * m]] += part
        return 0

    lax.fori_loop(0, steps, step, 0)
    last = jnp.maximum(2 * steps - 1, 0)
    total_ref[list_ref[0, last]] += product(odd_ref, steps, last)
    for c in range(clusters):
        lanes = slice(c * cl, (c + 1) * cl)
        near_out_ref[:, lanes] = start_ref[:, lanes] + folded(total_ref[c])


def remote_again_kernel(cl, list_ref, own_ref, left_ref, right_ref, start_ref, area_ref, even_ref, odd_ref, image_ref, pieces_ref, total_ref):
    clusters = start_ref.shape[1] // cl
    count = list_ref[3, 0]
    fill_charges(pieces_ref, (left_ref, own_ref, right_ref), clusters, cl)
    for c in range(clusters):
        total_ref[c] = jnp.zeros_like(total_ref[c])

    def step(m, _):
        parts = []
        for w in range(4):
            i = 4 * m + w
            at = list_ref[2, i]
            parts.append(near_product(pieces_ref[list_ref[1, i]], (even_ref, odd_ref)[w % 2], at // 2 + w % 2, cl))
        for w in range(4):
            total_ref[list_ref[0, 4 * m + w]] += parts[w]
        return 0

    lax.fori_loop(0, (count + 3) // 4, step, 0)
    for c in range(clusters):
        lanes = slice(c * cl, (c + 1) * cl)
        image_ref[:, lanes] = COULOMB * area_ref[c:c + 1, :] * (start_ref[:, lanes] + folded(total_ref[c]))


def load_window(tables, clusters, rank, pieces_ref, middle_ref):
    rhs = pieces_ref.shape[1] // 2
    per = LANES // rank
    span = clusters * rank
    count = pieces_ref.shape[0] // per
    groups = span // LANES
    for at in range(count):
        ref, g = tables[at // groups], at % groups
        tile = ref[:, g * LANES:(g + 1) * LANES]
        for s in range(per):
            pieces_ref[s * count + at] = stacked(pltpu.roll(tile, s * rank, 1) if s else tile)
        if middle_ref is not None:
            half = groups // 2
            row, lane = 8 * (g // half), span + g % half * LANES
            tile = ref[row:row + 8, lane:lane + LANES]
            for s in range(per):
                middle_ref[s * count + at] = pltpu.roll(tile, s * rank, 1) if s else tile


def pick(source_ref, at_ref, c, g, per, lane):
    row = None
    for u in range(per):
        take = source_ref[at_ref[c, g * per + u]]
        row = take if row is None else jnp.where(lane == u, take, row)
    return row


def far_fields(gathered_ref, coupling_ref, fields_ref, rank):
    for c in range(gathered_ref.shape[0]):
        field = folded(dot_nt(gathered_ref[c], coupling_ref[c]))
        fields_ref[c] = stacked(field[:, 0:rank] + field[:, rank:2 * rank])


def far_potential(field, basis_block):
    high, low = split(basis_block)
    return folded(dot_nn(field, high) + dot_nn(field, low))


def image_kernel(cl, rank, at_ref, *refs):
    tables = refs[:6]
    (center_ref, area_ref, near_ref, basis_hbm, krylov_hbm, offsets_hbm, image_ref, payload_ref, table_ref, sums_ref, coupling_ref,
     pieces_ref, middle_ref, gathered_ref, fields_ref, basis_ref, krylov_ref, offsets_ref, sems) = refs[6:]
    moves = copies(((offsets_hbm, offsets_ref), (basis_hbm, basis_ref), (krylov_hbm, krylov_ref)), sems)
    rhs, panels = krylov_ref.shape
    clusters = panels // cl
    span = clusters * rank
    per = LANES // rank
    load_window(tables, clusters, rank, pieces_ref, middle_ref)
    lane = lax.broadcasted_iota(jnp.int32, (1, LANES), 1) // rank
    moves[0].wait()
    for c in range(clusters):
        mine = [offsets_ref[3, k:k + 1, :] - center_ref[c:c + 1, k * LANES:(k + 1) * LANES] for k in range(3)]
        for g in range(at_ref.shape[1] // per):
            lanes = slice(g * LANES, (g + 1) * LANES)
            gathered_ref[c, :, lanes] = pick(pieces_ref, at_ref, c, g, per, lane)
            center = pick(middle_ref, at_ref, c, g, per, lane)
            gap = [(center[k:k + 1] + mine[k]) - offsets_ref[k] for k in range(3)]
            high, low = split(lax.rsqrt(gap[0] * gap[0] + gap[1] * gap[1] + gap[2] * gap[2] + SMOOTHING))
            coupling_ref[c, 0:rank, lanes] = high
            coupling_ref[c, rank:2 * rank, lanes] = low
    far_fields(gathered_ref, coupling_ref, fields_ref, rank)
    moves[1].wait()
    moves[2].wait()
    squared = correlation = jnp.zeros((rhs, cl), F32)
    for c in range(clusters):
        lanes = slice(c * cl, (c + 1) * cl)
        area = area_ref[c:c + 1, :]
        image = COULOMB * area * (near_ref[:, lanes] + far_potential(fields_ref[c], basis_ref[:, lanes]))
        image_ref[:, lanes] = image
        payload_ref[:, lanes] = area * image
        krylov = krylov_ref[:, lanes]
        squared = squared + krylov * krylov
        correlation = correlation + krylov * image
    for c in range(clusters):
        lanes = slice(c * cl, (c + 1) * cl)
        table_ref[:, c * rank:(c + 1) * rank] = moments_of(payload_ref[:, lanes], basis_ref[:, lanes])
    squared = jnp.sum(squared, axis=1, keepdims=True)
    correlation = jnp.sum(correlation, axis=1, keepdims=True)
    local = ratio(correlation, squared)
    residual = image_ref[...] - local * krylov_ref[...]
    sums_ref[...] = in_lanes(squared, correlation, jnp.sum(residual * residual, axis=1, keepdims=True), local)


def ratio(correlation, squared):
    return jnp.where(squared > 0, correlation / jnp.where(squared > 0, squared, 1.0), 0.0)


def in_lanes(*columns):
    lane = lax.broadcasted_iota(jnp.int32, (columns[0].shape[0], LANES), 1)
    out = columns[-1]
    for i, column in enumerate(columns[:-1]):
        out = jnp.where(lane == i, column, out)
    return out


def merged(groups):
    squared = sum(group[:, 0:1] for group in groups)
    correlation = sum(group[:, 1:2] for group in groups)
    local = ratio(correlation, squared)
    energy = 0.0
    for group in groups:
        gap = local - group[:, 3:4]
        energy = energy + (group[:, 2:3] + gap * gap * group[:, 0:1])
    return squared, correlation, energy, local


def double_sums_kernel(one_ref, two_ref, out_ref):
    out_ref[...] = in_lanes(*merged([one_ref[...], two_ref[...]]))


def far_again_kernel(cl, rank, at_ref, *refs):
    tables = refs[:6]
    coupling_ref, near_ref, basis_hbm, out_ref, pieces_ref, gathered_ref, fields_ref, basis_ref, sems = refs[6:]
    moves = copies(((basis_hbm, basis_ref),), sems)
    clusters = near_ref.shape[1] // cl
    per = LANES // rank
    load_window(tables, clusters, rank, pieces_ref, None)
    lane = lax.broadcasted_iota(jnp.int32, (1, LANES), 1) // rank
    for c in range(clusters):
        for g in range(at_ref.shape[1] // per):
            gathered_ref[c, :, g * LANES:(g + 1) * LANES] = pick(pieces_ref, at_ref, c, g, per, lane)
    far_fields(gathered_ref, coupling_ref, fields_ref, rank)
    moves[0].wait()
    for c in range(clusters):
        lanes = slice(c * cl, (c + 1) * cl)
        out_ref[:, lanes] = near_ref[:, lanes] + far_potential(fields_ref[c], basis_ref[:, lanes])


def finish_kernel(total, one_ref, two_ref, image_ref, again_ref, krylov_hbm, next_ref, second_ref, krylov_ref, sems):
    moves = copies(((krylov_hbm, krylov_ref),), sems)
    squared, correlation, energy, local = merged([one_ref[...], two_ref[...]])
    projection = correlation / (squared + 1e-06)
    gap = projection - local
    scaling = 1.0 / jnp.sqrt((energy + gap * gap * squared) / total + 1e-06)
    image = image_ref[...]
    second_ref[...] = (again_ref[...] - projection * image) * scaling
    moves[0].wait()
    next_ref[...] = (image - projection * krylov_ref[...]) * scaling


def call(kernel, outs, scratch, memory, *args, limit=4, us=1.0):
    spaces = {"s": pltpu.SMEM, "v": pltpu.VMEM, "p": pltpu.VMEM, "h": pltpu.HBM}
    ins, out_spaces = memory.split(">")
    pinned = {"h": pltpu.HBM, "p": pltpu.VMEM}
    return pl.pallas_call(
        kernel,
        out_shape=[pltpu.VMEM(*out) if m == "p" else jax.ShapeDtypeStruct(*out) for m, out in zip(out_spaces, outs)],
        in_specs=[pl.BlockSpec(memory_space=spaces[m]) for m in ins],
        out_specs=[pl.BlockSpec(memory_space=spaces[m]) for m in out_spaces],
        scratch_shapes=scratch,
        compiler_params=pltpu.CompilerParams(vmem_limit_bytes=limit * 2 ** 20),
        cost_estimate=pl.CostEstimate(flops=int(us * 5e8), bytes_accessed=int(us * 3.6e6), transcendentals=0),
    )(*(pltpu.with_memory_space_constraint(a, pinned[m]) if m in pinned else a for m, a in zip(ins, args)))


def body(vertices, panel_vertices, near_pairs, far_pairs, basis, krylov):
    clusters, slots = near_pairs.shape
    partners = far_pairs.shape[1]
    rhs, panels = krylov.shape
    rank = basis.shape[0]
    cl = panels // clusters
    vcl = vertices.shape[1] // clusters
    span = clusters * rank
    per = LANES // rank
    devices = lax.axis_size("clus")
    position = lax.axis_index("clus").reshape(1).astype(jnp.int32)
    offsets = proxy_offsets(rank)
    flat = np.concatenate([np.tile(offsets, (1, per)), np.zeros((rank - 3, LANES), np.float32)])
    offsets = jnp.asarray(np.concatenate([np.broadcast_to(offsets[:, :, None], (3, rank, LANES)), flat[None]]))
    live = clusters * (slots - 1)
    half = ((live + 1) // 2 + 1, 2 * cl, cl)
    reach = [step for step in range(-REACH, REACH + 1) if abs(step) > 1]

    def shifted(value, steps):
        return lax.ppermute(value, "clus", [(i, i + steps) for i in range(devices) if 0 <= i + steps < devices])

    def around(value, steps):
        return lax.ppermute(value, "clus", [(i, (i + steps) % devices) for i in range(devices)])

    whole = ((rhs, panels), F32)
    basis_here = pltpu.VMEM(basis.shape, F32)
    krylov_here = pltpu.VMEM(krylov.shape, F32)
    payload, table, area, centers, at = call(
        functools.partial(prepare_kernel, cl, vcl, rank),
        [((rhs, panels + 3 * cl), F32), ((rhs, span + span // 2), F32), ((clusters, cl), F32), ((clusters, 3 * LANES), F32), (far_pairs.shape, jnp.int32)],
        [
            pltpu.VMEM(vertices.shape, F32),
            pltpu.VMEM(panel_vertices.shape, jnp.int32),
            krylov_here,
            basis_here,
            pltpu.VMEM(far_pairs.shape, jnp.int32),
            pltpu.VMEM((3 * clusters, vcl), F32),
            pltpu.VMEM((3 * panels // LANES, LANES), jnp.int32),
            pltpu.SemaphoreType.DMA((5,)),
        ],
        "shhhhh>vvvvv",
        position, vertices, panel_vertices, krylov, basis, far_pairs,
        us=2.0,
    )
    left, right = shifted(payload, 1), shifted(payload, -1)
    tables = [shifted(table, -step) for step in reach]
    own_blocks, near, pairs = call(
        functools.partial(self_kernel, cl),
        [((clusters, 2 * cl, cl), BF16), whole, ((4, live + 4), jnp.int32)],
        [pltpu.VMEM((2, 3, cl, LANES), F32)],
        "ssv>pvs",
        position, near_pairs.T, payload,
        us=3.0,
    )
    pieces = pltpu.VMEM((3 * clusters + 1, 2 * rhs, cl), BF16)
    total = pltpu.VMEM((clusters, 2 * rhs, cl), F32)
    even, odd, near = call(
        functools.partial(remote_kernel, cl),
        [(half, BF16), (half, BF16), whole],
        [pieces, pltpu.VMEM((3 * clusters + 1, 8, cl), F32), pltpu.VMEM((clusters, 3, cl, LANES), F32), total],
        "svvvv>ppv",
        pairs, payload, left, right, near,
        limit=12,
        us=8.0,
    )
    tiles = per * len(reach) * span // LANES
    window = pltpu.VMEM((tiles, 2 * rhs, LANES), BF16)
    gathered = pltpu.VMEM((clusters, 2 * rhs, partners * rank), BF16)
    fields = pltpu.VMEM((clusters, 2 * rhs, rank), BF16)
    image, payload, table, sums, coupling = call(
        functools.partial(image_kernel, cl, rank),
        [whole, whole, ((rhs, span), F32), ((rhs, LANES), F32), ((clusters, 2 * rank, partners * rank), BF16)],
        [window, pltpu.VMEM((tiles, 8, LANES), F32), gathered, fields, basis_here, krylov_here, pltpu.VMEM(offsets.shape, F32), pltpu.SemaphoreType.DMA((3,))],
        "s" + "v" * 9 + "hhh>vvvvp",
        at, *tables, centers, area, near, basis, krylov, offsets,
        limit=8,
        us=3.5,
    )
    left, right = shifted(payload, 1), shifted(payload, -1)
    tables = [shifted(table, -step) for step in reach]
    other = around(sums, 1)
    (near,) = call(functools.partial(self_again_kernel, cl), [whole], [], "vp>v", payload, own_blocks, us=1.3)
    size = 1
    while 2 * size < devices:
        (sums,) = call(double_sums_kernel, [((rhs, LANES), F32)], [], "vv>v", sums, other, us=0.3)
        size = 2 * size
        other = around(sums, size)
    (near,) = call(
        functools.partial(far_again_kernel, cl, rank),
        [whole],
        [window, gathered, fields, basis_here, pltpu.SemaphoreType.DMA((1,))],
        "s" + "v" * 6 + "pvh>v",
        at, *tables, coupling, near, basis,
        limit=8,
        us=2.0,
    )
    (again,) = call(
        functools.partial(remote_again_kernel, cl),
        [whole],
        [pieces, total],
        "svvvvvpp>v",
        pairs, payload, left, right, near, area, even, odd,
        us=3.0,
    )
    return tuple(call(
        functools.partial(finish_kernel, panels * devices),
        [whole, whole],
        [krylov_here, pltpu.SemaphoreType.DMA((1,))],
        "vvvvh>vv",
        sums, other, image, again, krylov,
    ))


def solution(mesh):
    whole = P(None, ("jobs", "clus"))
    rows = P(("jobs", "clus"), None)
    return jax.shard_map(
        body,
        mesh=mesh,
        in_specs=(whole, whole, rows, rows, whole, whole),
        out_specs=(whole, whole),
        check_vma=False,
    )
```

```python
import functools

import jax
import jax.numpy as jnp
import numpy as np
from jax import lax
from jax.experimental import pallas as pl
from jax.experimental.pallas import tpu as pltpu
from jax.sharding import PartitionSpec as P

REACH = 4
SMOOTHING = 0.04
COULOMB = 2.0
PROXY_RADIUS = 0.6
LANES = 128
F32 = jnp.float32
BF16 = jnp.bfloat16


def proxy_offsets(points):
    counter = np.arange(points, dtype=np.float32)
    height = 1.0 - (2.0 * counter + 1.0) / points
    radial = np.sqrt(1.0 - height * height)
    azimuth = counter * 2.399963
    return PROXY_RADIUS * np.stack([radial * np.cos(azimuth), radial * np.sin(azimuth), height]).astype(np.float32)


def split(value):
    high = value.astype(BF16)
    return high, (value - high.astype(F32)).astype(BF16)


def stacked(value):
    return jnp.concatenate(split(value), axis=0)


def folded(value):
    half = value.shape[0] // 2
    return value[:half] + value[half:]


def dot_nt(left, right):
    return lax.dot_general(left, right, (((1,), (1,)), ((), ())), preferred_element_type=F32)


def dot_nn(left, right):
    return lax.dot_general(left, right, (((1,), (0,)), ((), ())), preferred_element_type=F32)


def quartered(value):
    half = value.shape[1] // 2
    value = folded(value)
    return value[:, 0:half] + value[:, half:]


def moments_of(weighted, basis_pieces):
    return quartered(dot_nt(stacked(weighted), basis_pieces))


def copies(pairs, sems):
    moves = [pltpu.make_async_copy(source, target, sems.at[i]) for i, (source, target) in enumerate(pairs)]
    for move in moves:
        move.start()
    return moves


def pair_list(near, position, clusters):
    sides = near.astype(F32)
    block = lax.div(near, clusters) - position
    place = (1 - block * (1 - 2 * lax.rem(position, 2))) * clusters + lax.rem(near, clusters)
    across = lax.broadcasted_iota(jnp.int32, (clusters, clusters), 1)
    down = lax.broadcasted_iota(jnp.int32, (clusters, clusters), 0)
    live = [(sides[k:k + 1] >= 0).astype(F32) for k in range(near.shape[0])]
    counts = sum(live[1:])
    first = jnp.sum(jnp.where(across < down, counts, 0.0), axis=1, keepdims=True)
    row = lax.broadcasted_iota(jnp.int32, (clusters, LANES), 1).astype(F32)
    target = lax.broadcasted_iota(jnp.int32, (clusters, 1), 0).astype(F32)
    found = jnp.zeros((clusters, LANES), F32)
    for k in range(1, near.shape[0]):
        upright = lambda value: jnp.sum(jnp.where(across == down, value, 0.0), axis=1, keepdims=True)
        hit = jnp.where(row == first + (k - 1), upright(live[k]), 0.0)
        found = found + hit * (target * 64 + upright(place[k:k + 1].astype(F32)))
    count = jnp.sum(counts, axis=1, keepdims=True)
    found = jnp.where(row[0:1] < count, jnp.sum(found, axis=0, keepdims=True), 3.0 * clusters)
    rows = lax.broadcasted_iota(jnp.int32, (8, LANES), 0)
    return jnp.where(rows == 0, found, count).astype(jnp.int32)


def prepare_kernel(cl, vcl, rank, position_ref, vertices_hbm, corners_hbm, krylov_hbm, basis_hbm, far_hbm, near_hbm, offsets_hbm,
                   payload_ref, table_ref, area_ref, center_ref, at_ref, pairs_ref, basis_ref, krylov_ref, offsets_ref,
                   vertices_ref, corners_ref, raw_ref, far_ref, near_ref, mesh_ref, local_ref, sems):
    moves = copies((
        (vertices_hbm, vertices_ref), (corners_hbm, corners_ref), (krylov_hbm, krylov_ref), (basis_hbm, raw_ref),
        (far_hbm, far_ref), (near_hbm, near_ref), (offsets_hbm, offsets_ref),
    ), sems)
    rhs, panels = krylov_ref.shape
    clusters = panels // cl
    parts = cl // LANES
    moves[0].wait()
    for c in range(clusters):
        mesh_ref[3 * c:3 * c + 3, :] = vertices_ref[:, c * vcl:(c + 1) * vcl]
    moves[1].wait()
    for i in range(clusters * parts):
        local_ref[3 * i:3 * i + 3, :] = corners_ref[:, i * LANES:(i + 1) * LANES]
    first = position_ref[0] * (vcl * clusters) + vcl * lax.broadcasted_iota(jnp.int32, (clusters, LANES), 0)
    tables = [mesh_ref[pl.ds(k, clusters, stride=3), :] for k in range(3)]
    sums = [None] * 3
    for h in range(parts):
        local = [local_ref[pl.ds(3 * h + m, clusters, stride=3 * parts), :] - first for m in range(3)]
        corner = [[jnp.take_along_axis(tables[k], local[m], axis=1, mode="promise_in_bounds") for k in range(3)] for m in range(3)]
        for k in range(3):
            middle = (corner[0][k] + corner[1][k] + corner[2][k]) / 3.0
            payload_ref[:, panels + k * cl + h * LANES:panels + k * cl + (h + 1) * LANES] = middle
            sums[k] = middle if h == 0 else sums[k] + middle
        one = [corner[1][k] - corner[0][k] for k in range(3)]
        two = [corner[2][k] - corner[0][k] for k in range(3)]
        normal = [one[1] * two[2] - one[2] * two[1], one[2] * two[0] - one[0] * two[2], one[0] * two[1] - one[1] * two[0]]
        area_ref[:, h * LANES:(h + 1) * LANES] = 0.5 * jnp.sqrt(normal[0] * normal[0] + normal[1] * normal[1] + normal[2] * normal[2])
    span = clusters * rank
    mine = lax.broadcasted_iota(jnp.int32, (clusters, span), 1) // rank == lax.broadcasted_iota(jnp.int32, (clusters, span), 0)
    half = span // 2
    table_ref[:, span:] = jnp.zeros_like(table_ref[:, span:])
    for k in range(3):
        center = jnp.sum(sums[k], axis=1, keepdims=True) / cl
        center_ref[:, k * LANES:(k + 1) * LANES] = jnp.broadcast_to(center, (clusters, LANES))
        row = jnp.sum(jnp.where(mine, center, 0.0), axis=0, keepdims=True)
        table_ref[k:k + 1, span:] = row[:, 0:half]
        table_ref[8 + k:9 + k, span:] = row[:, half:]
    moves[2].wait()
    moves[3].wait()
    for c in range(clusters):
        lanes = slice(c * cl, (c + 1) * cl)
        basis_ref[:, lanes] = stacked(raw_ref[:, lanes])
        charges = area_ref[c:c + 1, :] * krylov_ref[:, lanes]
        payload_ref[:, lanes] = charges
        table_ref[:, c * rank:(c + 1) * rank] = moments_of(charges, basis_ref[:, lanes])
    moves[4].wait()
    far = far_ref[...]
    step = lax.div(far, clusters) - position_ref[0]
    block = jnp.where(step < 0, step + REACH, step + REACH - 3)
    per = LANES // rank
    turn = lax.rem(lax.broadcasted_iota(jnp.int32, far.shape, 1) - far + per * clusters * 2 ** 16, per)
    at_ref[...] = (turn * 6 + block) * (span // LANES) + lax.div(lax.rem(far, clusters), per)
    moves[5].wait()
    pairs_ref[...] = pair_list(near_ref[...], position_ref[0], clusters)
    moves[6].wait()


def columns_of(payload_ref, panels, c, cl, columns_ref, at):
    rows = [payload_ref[c:c + 1, panels + k * cl:panels + (k + 1) * cl] for k in range(3)]
    upright = jnp.transpose(jnp.concatenate(rows * 2 + rows[:2], axis=0))
    for k in range(3):
        columns_ref[at, k] = jnp.broadcast_to(upright[:, k:k + 1], (cl, LANES))


def near_block(columns, source, cl, out_ref, at):
    for h in range(cl // LANES):
        lanes = slice(h * LANES, (h + 1) * LANES)
        gap = [columns[k] - source(k, h) for k in range(3)]
        square = gap[0] * gap[0] + gap[1] * gap[1] + gap[2] * gap[2]
        high, low = split(lax.rsqrt(square + SMOOTHING))
        out_ref[at, 0:cl, lanes] = high
        out_ref[at, cl:2 * cl, lanes] = low


def near_product(pieces, block_ref, at, cl):
    return dot_nt(pieces, block_ref[at, 0:cl, :]) + dot_nt(pieces, block_ref[at, cl:2 * cl, :])


def self_kernel(cl, payload_ref, blocks_ref, near_ref, columns_ref):
    panels = near_ref.shape[1]
    for c in range(panels // cl):
        columns_of(payload_ref, panels, c, cl, columns_ref, c % 2)
        source = lambda k, h: payload_ref[c:c + 1, panels + k * cl + h * LANES:panels + k * cl + (h + 1) * LANES]
        near_block([columns_ref[c % 2, k] for k in range(3)], source, cl, blocks_ref, c)
        lanes = slice(c * cl, (c + 1) * cl)
        near_ref[:, lanes] = folded(near_product(stacked(payload_ref[:, lanes]), blocks_ref, c, cl))


def self_again_kernel(cl, payload_ref, blocks_ref, near_ref):
    for c in range(near_ref.shape[1] // cl):
        lanes = slice(c * cl, (c + 1) * cl)
        near_ref[:, lanes] = folded(near_product(stacked(payload_ref[:, lanes]), blocks_ref, c, cl))


def fill_charges(pieces_ref, blocks, clusters, cl):
    for b, ref in enumerate(blocks):
        for c in range(clusters):
            pieces_ref[b * clusters + c] = stacked(ref[:, c * cl:(c + 1) * cl])
    pieces_ref[3 * clusters] = jnp.zeros_like(pieces_ref[3 * clusters])


def pair_at(pairs_ref, i):
    pair = pairs_ref[0, i]
    return lax.shift_right_logical(pair, 6), lax.bitwise_and(pair, 63)


def remote_kernel(cl, rank, pairs_ref, partner_ref, own_ref, other_ref, start_ref, area_ref, krylov_ref, basis_ref,
                  even_ref, odd_ref, image_ref, charges_ref, table_ref, sums_ref, pieces_ref, sources_ref, columns_ref, total_ref):
    rhs, panels = start_ref.shape
    clusters = panels // cl
    steps = (pairs_ref[1, 0] + 1) // 2
    sources_ref[3 * clusters] = jnp.zeros_like(sources_ref[3 * clusters])
    for b, ref in enumerate((partner_ref, own_ref, other_ref)):
        for c in range(clusters):
            for k in range(3):
                sources_ref[b * clusters + c, k:k + 1, :] = ref[c:c + 1, panels + k * cl:panels + (k + 1) * cl]
    fill_charges(pieces_ref, (partner_ref, own_ref, other_ref), clusters, cl)
    for c in range(clusters):
        columns_of(own_ref, panels, c, cl, columns_ref, c)
        total_ref[c] = jnp.zeros_like(total_ref[c])
    odd_ref[0] = jnp.zeros_like(odd_ref[0])

    def build(ref, at, i):
        c, j = pair_at(pairs_ref, i)
        source = lambda k, h: sources_ref[j, k:k + 1, h * LANES:(h + 1) * LANES]
        near_block([columns_ref[c, k] for k in range(3)], source, cl, ref, at)

    def product(ref, at, i):
        return near_product(pieces_ref[pair_at(pairs_ref, i)[1]], ref, at, cl)

    def add(i, part):
        total_ref[pair_at(pairs_ref, i)[0]] += part

    def step(m, _):
        before = jnp.maximum(2 * m - 1, 0)
        part = product(odd_ref, m, before)
        build(even_ref, m, 2 * m)
        add(before, part)
        part = product(even_ref, m, 2 * m)
        build(odd_ref, m + 1, 2 * m + 1)
        add(2 * m, part)
        return 0

    lax.fori_loop(0, steps, step, 0)
    last = jnp.maximum(2 * steps - 1, 0)
    add(last, product(odd_ref, steps, last))
    squared = correlation = jnp.zeros((rhs, cl), F32)
    for c in range(clusters):
        lanes = slice(c * cl, (c + 1) * cl)
        area = area_ref[c:c + 1, :]
        image = COULOMB * area * (start_ref[:, lanes] + folded(total_ref[c]))
        charges = area * image
        image_ref[:, lanes] = image
        charges_ref[:, lanes] = charges
        table_ref[:, c * rank:(c + 1) * rank] = moments_of(charges, basis_ref[:, lanes])
        krylov = krylov_ref[:, lanes]
        squared = squared + krylov * krylov
        correlation = correlation + krylov * image
    squared = jnp.sum(squared, axis=1, keepdims=True)
    correlation = jnp.sum(correlation, axis=1, keepdims=True)
    local = ratio(correlation, squared)
    residual = image_ref[...] - local * krylov_ref[...]
    sums_ref[...] = in_lanes(squared, correlation, jnp.sum(residual * residual, axis=1, keepdims=True), local)


def finish_kernel(cl, total, groups, pairs_ref, *refs):
    sums = refs[:groups]
    (partner_ref, own_ref, other_ref, start_ref, area_ref, even_ref, odd_ref, image_ref, krylov_ref, next_hbm, second_hbm,
     pieces_ref, total_ref, next_ref, second_ref, sems) = refs[groups:]
    panels = start_ref.shape[1]
    clusters = panels // cl
    squared, correlation, energy, local = merged([ref[...] for ref in sums])
    projection = correlation / (squared + 1e-06)
    gap = projection - local
    scaling = 1.0 / jnp.sqrt((energy + gap * gap * squared) / total + 1e-06)
    next_ref[...] = (image_ref[...] - projection * krylov_ref[...]) * scaling
    moves = copies(((next_ref, next_hbm),), sems)
    fill_charges(pieces_ref, (partner_ref, own_ref, other_ref), clusters, cl)
    for c in range(clusters):
        total_ref[c] = jnp.zeros_like(total_ref[c])
    count = pairs_ref[1, 0]

    def step(m, _):
        parts = []
        for w in range(4):
            i = 4 * m + w
            at = jnp.where(i < count, i // 2, 0) + w % 2
            parts.append(near_product(pieces_ref[pair_at(pairs_ref, i)[1]], (even_ref, odd_ref)[w % 2], at, cl))
        for w in range(4):
            total_ref[pair_at(pairs_ref, 4 * m + w)[0]] += parts[w]
        return 0

    lax.fori_loop(0, (count + 3) // 4, step, 0)
    for c in range(clusters):
        lanes = slice(c * cl, (c + 1) * cl)
        image = COULOMB * area_ref[c:c + 1, :] * (start_ref[:, lanes] + folded(total_ref[c]))
        second_ref[:, lanes] = (image - projection * image_ref[:, lanes]) * scaling
    moves.append(pltpu.make_async_copy(second_ref, second_hbm, sems.at[1]))
    moves[1].start()
    moves[0].wait()
    moves[1].wait()


def load_window(tables, clusters, rank, pieces_ref, middle_ref):
    rhs = pieces_ref.shape[1] // 2
    per = LANES // rank
    span = clusters * rank
    count = pieces_ref.shape[0] // per
    groups = span // LANES
    for at in range(count):
        ref, g = tables[at // groups], at % groups
        tile = ref[:, g * LANES:(g + 1) * LANES]
        for s in range(per):
            pieces_ref[s * count + at] = stacked(pltpu.roll(tile, s * rank, 1) if s else tile)
        if middle_ref is not None:
            half = groups // 2
            row, lane = 8 * (g // half), span + g % half * LANES
            tile = ref[row:row + 8, lane:lane + LANES]
            for s in range(per):
                middle_ref[s * count + at] = pltpu.roll(tile, s * rank, 1) if s else tile


def pick(source_ref, at_ref, c, g, per, lane):
    row = None
    for u in range(per):
        take = source_ref[at_ref[c, g * per + u]]
        row = take if row is None else jnp.where(lane == u, take, row)
    return row


def far_fields(gathered_ref, coupling_ref, fields_ref):
    for c in range(gathered_ref.shape[0]):
        field = quartered(dot_nt(gathered_ref[c], coupling_ref[c]))
        fields_ref[c] = stacked(jnp.concatenate([field, field], axis=1))


def add_far(cl, near_ref, fields_ref, basis_ref, out_ref):
    for c in range(fields_ref.shape[0]):
        lanes = slice(c * cl, (c + 1) * cl)
        out_ref[:, lanes] = near_ref[:, lanes] + folded(dot_nn(fields_ref[c], basis_ref[:, lanes]))


def far_kernel(cl, rank, at_ref, *refs):
    tables = refs[:6]
    center_ref, near_ref, basis_ref, offsets_ref, out_ref, coupling_ref, pieces_ref, middle_ref, gathered_ref, fields_ref = refs[6:]
    clusters = near_ref.shape[1] // cl
    per = LANES // rank
    load_window(tables, clusters, rank, pieces_ref, middle_ref)
    lane = lax.broadcasted_iota(jnp.int32, (1, LANES), 1) // rank
    for c in range(clusters):
        mine = [offsets_ref[3, k:k + 1, :] - center_ref[c:c + 1, k * LANES:(k + 1) * LANES] for k in range(3)]
        for g in range(at_ref.shape[1] // per):
            lanes = slice(g * LANES, (g + 1) * LANES)
            gathered_ref[c, :, lanes] = pick(pieces_ref, at_ref, c, g, per, lane)
            center = pick(middle_ref, at_ref, c, g, per, lane)
            gap = [(center[k:k + 1] + mine[k]) - offsets_ref[k] for k in range(3)]
            high, low = split(lax.rsqrt(gap[0] * gap[0] + gap[1] * gap[1] + gap[2] * gap[2] + SMOOTHING))
            coupling_ref[c, 0:rank, lanes] = high
            coupling_ref[c, rank:2 * rank, lanes] = low
    far_fields(gathered_ref, coupling_ref, fields_ref)
    add_far(cl, near_ref, fields_ref, basis_ref, out_ref)


def far_again_kernel(cl, rank, at_ref, *refs):
    tables = refs[:6]
    coupling_ref, near_ref, basis_ref, out_ref, pieces_ref, gathered_ref, fields_ref = refs[6:]
    clusters = near_ref.shape[1] // cl
    per = LANES // rank
    load_window(tables, clusters, rank, pieces_ref, None)
    lane = lax.broadcasted_iota(jnp.int32, (1, LANES), 1) // rank
    for c in range(clusters):
        for g in range(at_ref.shape[1] // per):
            gathered_ref[c, :, g * LANES:(g + 1) * LANES] = pick(pieces_ref, at_ref, c, g, per, lane)
    far_fields(gathered_ref, coupling_ref, fields_ref)
    add_far(cl, near_ref, fields_ref, basis_ref, out_ref)


def ratio(correlation, squared):
    return jnp.where(squared > 0, correlation / jnp.where(squared > 0, squared, 1.0), 0.0)


def in_lanes(*columns):
    lane = lax.broadcasted_iota(jnp.int32, (columns[0].shape[0], LANES), 1)
    out = columns[-1]
    for i, column in enumerate(columns[:-1]):
        out = jnp.where(lane == i, column, out)
    return out


def merged(groups):
    squared = sum(group[:, 0:1] for group in groups)
    correlation = sum(group[:, 1:2] for group in groups)
    local = ratio(correlation, squared)
    energy = 0.0
    for group in groups:
        gap = local - group[:, 3:4]
        energy = energy + (group[:, 2:3] + gap * gap * group[:, 0:1])
    return squared, correlation, energy, local


def merge_kernel(*refs):
    refs[-1][...] = in_lanes(*merged([ref[...] for ref in refs[:-1]]))


def call(kernel, outs, scratch, memory, *args, limit=6, us=1.0):
    spaces = {"s": pltpu.SMEM, "v": pltpu.VMEM, "p": pltpu.VMEM, "h": pltpu.HBM}
    ins, out_spaces = memory.split(">")
    pinned = {"h": pltpu.HBM, "p": pltpu.VMEM}
    return pl.pallas_call(
        kernel,
        out_shape=[pltpu.VMEM(*out) if m == "p" else jax.ShapeDtypeStruct(*out) for m, out in zip(out_spaces, outs)],
        in_specs=[pl.BlockSpec(memory_space=spaces[m]) for m in ins],
        out_specs=[pl.BlockSpec(memory_space=spaces[m]) for m in out_spaces],
        scratch_shapes=scratch,
        compiler_params=pltpu.CompilerParams(vmem_limit_bytes=limit * 2 ** 20),
        cost_estimate=pl.CostEstimate(flops=int(us * 5e8), bytes_accessed=int(us * 3.6e6), transcendentals=0),
    )(*(pltpu.with_memory_space_constraint(a, pinned[m]) if m in pinned else a for m, a in zip(ins, args)))


def body(vertices, panel_vertices, near_pairs, far_pairs, basis, krylov):
    clusters, slots = near_pairs.shape
    partners = far_pairs.shape[1]
    rhs, panels = krylov.shape
    rank = basis.shape[0]
    cl = panels // clusters
    vcl = vertices.shape[1] // clusters
    span = clusters * rank
    per = LANES // rank
    devices = lax.axis_size("clus")
    position = lax.axis_index("clus").reshape(1).astype(jnp.int32)
    offsets = proxy_offsets(rank)
    flat = np.concatenate([np.tile(offsets, (1, per)), np.zeros((rank - 3, LANES), np.float32)])
    offsets = jnp.asarray(np.concatenate([np.broadcast_to(offsets[:, :, None], (3, rank, LANES)), flat[None]]))
    live = clusters * (slots - 1)
    half = ((live + 1) // 2 + 1, 2 * cl, cl)
    reach = [step for step in range(-REACH, REACH + 1) if abs(step) > 1]
    pairing = [(i, i + 1 - 2 * (i % 2)) for i in range(devices)]
    bridging = [(i, i - 1 + 2 * (i % 2)) for i in range(1, devices - 1)] + [(0, 0), (devices - 1, devices - 1)]

    def around(value, steps):
        return lax.ppermute(value, "clus", [(i, (i + steps) % devices) for i in range(devices)])

    def neighbours(value):
        other = lax.ppermute(value, "clus", bridging)
        return lax.ppermute(value, "clus", pairing), other

    def tables_of(value):
        return [around(value, -step) for step in reach]

    whole = ((rhs, panels), F32)
    payload, table, area, centers, at, pairs, basis, krylov, offsets = call(
        functools.partial(prepare_kernel, cl, vcl, rank),
        [
            ((rhs, panels + 3 * cl), F32), ((rhs, span + span // 2), F32), ((clusters, cl), F32), ((clusters, 3 * LANES), F32),
            (far_pairs.shape, jnp.int32), ((8, LANES), jnp.int32), ((2 * rank, panels), BF16), whole, (offsets.shape, F32),
        ],
        [
            pltpu.VMEM(vertices.shape, F32),
            pltpu.VMEM(panel_vertices.shape, jnp.int32),
            pltpu.VMEM(basis.shape, F32),
            pltpu.VMEM(far_pairs.shape, jnp.int32),
            pltpu.VMEM((slots, clusters), jnp.int32),
            pltpu.VMEM((3 * clusters, vcl), F32),
            pltpu.VMEM((3 * panels // LANES, LANES), jnp.int32),
            pltpu.SemaphoreType.DMA((7,)),
        ],
        "shhhhhhh>vvvvvvppp",
        position, vertices, panel_vertices, krylov, basis, far_pairs, near_pairs.T, offsets,
        us=1.5,
    )
    partner, other = neighbours(payload)
    tables = tables_of(table)
    own_blocks, near = call(
        functools.partial(self_kernel, cl),
        [((clusters, 2 * cl, cl), BF16), whole],
        [pltpu.VMEM((2, 3, cl, LANES), F32)],
        "v>pv",
        payload,
        us=3.0,
    )
    tiles = per * len(reach) * span // LANES
    window = pltpu.VMEM((tiles, 2 * rhs, LANES), BF16)
    gathered = pltpu.VMEM((clusters, 2 * rhs, partners * rank), BF16)
    fields = pltpu.VMEM((clusters, 2 * rhs, 2 * rank), BF16)
    near, coupling = call(
        functools.partial(far_kernel, cl, rank),
        [whole, ((clusters, 2 * rank, partners * rank), BF16)],
        [window, pltpu.VMEM((tiles, 8, LANES), F32), gathered, fields],
        "s" + "v" * 8 + "pp>vp",
        at, *tables, centers, near, basis, offsets,
        us=3.0,
    )
    pieces = pltpu.VMEM((3 * clusters + 1, 2 * rhs, cl), BF16)
    total = pltpu.VMEM((clusters, 2 * rhs, cl), F32)
    even, odd, image, charges, table, sums = call(
        functools.partial(remote_kernel, cl, rank),
        [(half, BF16), (half, BF16), whole, whole, ((rhs, span), F32), ((rhs, LANES), F32)],
        [pieces, pltpu.VMEM((3 * clusters + 1, 8, cl), F32), pltpu.VMEM((clusters, 3, cl, LANES), F32), total],
        "svvvvvpp>ppvvvv",
        pairs, partner, payload, other, near, area, krylov, basis,
        limit=12,
        us=8.0,
    )
    partner, other = neighbours(charges)
    tables = tables_of(table)
    (near,) = call(functools.partial(self_again_kernel, cl), [whole], [], "vp>v", charges, own_blocks, us=1.3)
    sums, near = lax.optimization_barrier((sums, near))
    size = 1
    while size < devices:
        groups = [sums] + [around(sums, k * size) for k in range(1, min(4, devices // size))]
        size = size * len(groups)
        if size < devices:
            (sums,) = call(merge_kernel, [((rhs, LANES), F32)], [], "v" * len(groups) + ">v", *groups, us=0.3)
    (near,) = call(
        functools.partial(far_again_kernel, cl, rank),
        [whole],
        [window, gathered, fields],
        "s" + "v" * 6 + "pvp>v",
        at, *tables, coupling, near, basis,
        us=2.0,
    )
    return tuple(call(
        functools.partial(finish_kernel, cl, panels * devices, len(groups)),
        [whole, whole],
        [pieces, total, pltpu.VMEM(krylov.shape, F32), pltpu.VMEM(krylov.shape, F32), pltpu.SemaphoreType.DMA((2,))],
        "s" + "v" * (len(groups) + 5) + "ppvp>hh",
        pairs, *groups, partner, charges, other, near, area, even, odd, image, krylov,
        us=3.0,
    ))


def solution(mesh):
    whole = P(None, ("jobs", "clus"))
    rows = P(("jobs", "clus"), None)
    return jax.shard_map(
        body,
        mesh=mesh,
        in_specs=(whole, whole, rows, rows, whole, whole),
        out_specs=(whole, whole),
        check_vma=False,
    )
```

```python
import functools

import jax
import jax.numpy as jnp
import numpy as np
from jax import lax
from jax.experimental import pallas as pl
from jax.experimental.pallas import tpu as pltpu
from jax.sharding import PartitionSpec as P

REACH = 4
SMOOTHING = 0.04
COULOMB = 2.0
PROXY_RADIUS = 0.6
LANES = 128
F32 = jnp.float32
BF16 = jnp.bfloat16


def proxy_offsets(points):
    counter = np.arange(points, dtype=np.float32)
    height = 1.0 - (2.0 * counter + 1.0) / points
    radial = np.sqrt(1.0 - height * height)
    azimuth = counter * 2.399963
    return PROXY_RADIUS * np.stack([radial * np.cos(azimuth), radial * np.sin(azimuth), height]).astype(np.float32)


def split(value):
    high = value.astype(BF16)
    return high, (value - high.astype(F32)).astype(BF16)


def stacked(value):
    return jnp.concatenate(split(value), axis=0)


def folded(value):
    half = value.shape[0] // 2
    return value[:half] + value[half:]


def dot_nt(left, right):
    return lax.dot_general(left, right, (((1,), (1,)), ((), ())), preferred_element_type=F32)


def dot_nn(left, right):
    return lax.dot_general(left, right, (((1,), (0,)), ((), ())), preferred_element_type=F32)


def quartered(value):
    half = value.shape[1] // 2
    value = folded(value)
    return value[:, 0:half] + value[:, half:]


def moments_of(weighted, basis_pieces):
    return quartered(dot_nt(stacked(weighted), basis_pieces))


def copies(pairs, sems):
    moves = [pltpu.make_async_copy(source, target, sems.at[i]) for i, (source, target) in enumerate(pairs)]
    for move in moves:
        move.start()
    return moves


def pair_list(near, position, clusters):
    block = lax.div(near, clusters) - position
    place = (1 - block * (1 - 2 * lax.rem(position, 2))) * clusters + lax.rem(near, clusters)
    place = place.astype(F32)
    across = lax.broadcasted_iota(jnp.int32, (clusters, clusters), 1)
    down = lax.broadcasted_iota(jnp.int32, (clusters, clusters), 0)
    upright = lambda value: jnp.sum(jnp.where(across == down, value, 0.0), axis=1, keepdims=True)
    row = lax.broadcasted_iota(jnp.int32, (clusters, LANES), 1).astype(F32)
    target = lax.broadcasted_iota(jnp.int32, (clusters, 1), 0).astype(F32)
    rows = lax.broadcasted_iota(jnp.int32, (8, LANES), 0)
    out = jnp.zeros((8, LANES), F32)
    for which in range(2):
        here = place >= 2.0 * clusters if which else place < 2.0 * clusters
        live = jnp.where(here & (near >= 0), 1.0, 0.0)
        counts = sum(live[k:k + 1] for k in range(near.shape[0]))
        first = jnp.sum(jnp.where(across < down, counts, 0.0), axis=1, keepdims=True)
        found = jnp.zeros((clusters, LANES), F32)
        for k in range(near.shape[0]):
            alive = upright(live[k:k + 1])
            hit = jnp.where(row == first, alive, 0.0)
            found = found + hit * (target * 64 + upright(place[k:k + 1]) - 2.0 * clusters * which)
            first = first + alive
        count = jnp.sum(counts, axis=1, keepdims=True)
        found = jnp.where(row[0:1] < count, jnp.sum(found, axis=0, keepdims=True), (2.0 - which) * clusters)
        out = jnp.where(rows == which, found, jnp.where(rows == 2 + which, count, out))
    return out.astype(jnp.int32)


def prepare_kernel(cl, vcl, rank, position_ref, vertices_hbm, corners_hbm, krylov_hbm, basis_hbm, far_hbm, near_hbm, offsets_hbm,
                   payload_ref, area_ref, center_ref, at_ref, pairs_ref, basis_ref, krylov_ref, offsets_ref,
                   vertices_ref, corners_ref, raw_ref, far_ref, near_ref, mesh_ref, local_ref, sems):
    moves = copies((
        (vertices_hbm, vertices_ref), (corners_hbm, corners_ref), (krylov_hbm, krylov_ref), (basis_hbm, raw_ref),
        (far_hbm, far_ref), (near_hbm, near_ref), (offsets_hbm, offsets_ref),
    ), sems)
    rhs, panels = krylov_ref.shape
    clusters = panels // cl
    parts = cl // LANES
    moves[0].wait()
    for c in range(clusters):
        mesh_ref[3 * c:3 * c + 3, :] = vertices_ref[:, c * vcl:(c + 1) * vcl]
    moves[1].wait()
    for i in range(clusters * parts):
        local_ref[3 * i:3 * i + 3, :] = corners_ref[:, i * LANES:(i + 1) * LANES]
    first = position_ref[0] * (vcl * clusters) + vcl * lax.broadcasted_iota(jnp.int32, (clusters, LANES), 0)
    tables = [mesh_ref[pl.ds(k, clusters, stride=3), :] for k in range(3)]
    sums = [None] * 3
    for h in range(parts):
        local = [local_ref[pl.ds(3 * h + m, clusters, stride=3 * parts), :] - first for m in range(3)]
        corner = [[jnp.take_along_axis(tables[k], local[m], axis=1, mode="promise_in_bounds") for k in range(3)] for m in range(3)]
        for k in range(3):
            middle = (corner[0][k] + corner[1][k] + corner[2][k]) / 3.0
            payload_ref[:, panels + k * cl + h * LANES:panels + k * cl + (h + 1) * LANES] = middle
            sums[k] = middle if h == 0 else sums[k] + middle
        one = [corner[1][k] - corner[0][k] for k in range(3)]
        two = [corner[2][k] - corner[0][k] for k in range(3)]
        normal = [one[1] * two[2] - one[2] * two[1], one[2] * two[0] - one[0] * two[2], one[0] * two[1] - one[1] * two[0]]
        area_ref[:, h * LANES:(h + 1) * LANES] = 0.5 * jnp.sqrt(normal[0] * normal[0] + normal[1] * normal[1] + normal[2] * normal[2])
    span = clusters * rank
    table = panels + 3 * cl
    mine = lax.broadcasted_iota(jnp.int32, (clusters, span), 1) // rank == lax.broadcasted_iota(jnp.int32, (clusters, span), 0)
    half = span // 2
    payload_ref[:, table + span:] = jnp.zeros_like(payload_ref[:, table + span:])
    for k in range(3):
        center = jnp.sum(sums[k], axis=1, keepdims=True) / cl
        center_ref[:, k * LANES:(k + 1) * LANES] = jnp.broadcast_to(center, (clusters, LANES))
        row = jnp.sum(jnp.where(mine, center, 0.0), axis=0, keepdims=True)
        payload_ref[k:k + 1, table + span:] = row[:, 0:half]
        payload_ref[8 + k:9 + k, table + span:] = row[:, half:]
    moves[2].wait()
    moves[3].wait()
    for c in range(clusters):
        lanes = slice(c * cl, (c + 1) * cl)
        basis_ref[:, lanes] = stacked(raw_ref[:, lanes])
        charges = area_ref[c:c + 1, :] * krylov_ref[:, lanes]
        payload_ref[:, lanes] = charges
        payload_ref[:, table + c * rank:table + (c + 1) * rank] = moments_of(charges, basis_ref[:, lanes])
    moves[4].wait()
    far = far_ref[...]
    step = (lax.div(far, clusters) - position_ref[0]) * (1 - 2 * lax.rem(position_ref[0], 2))
    block = jnp.where(step < 0, step + REACH, step + REACH - 3)
    per = LANES // rank
    turn = lax.rem(lax.broadcasted_iota(jnp.int32, far.shape, 1) - far + per * clusters * 2 ** 16, per)
    at_ref[...] = (turn * 6 + block) * (span // LANES) + lax.div(lax.rem(far, clusters), per)
    moves[5].wait()
    pairs_ref[...] = pair_list(near_ref[...], position_ref[0], clusters)
    moves[6].wait()


def columns_of(payload_ref, panels, c, cl, columns_ref, at):
    rows = [payload_ref[c:c + 1, panels + k * cl:panels + (k + 1) * cl] for k in range(3)]
    upright = jnp.transpose(jnp.concatenate(rows * 2 + rows[:2], axis=0))
    for k in range(3):
        columns_ref[at, k] = jnp.broadcast_to(upright[:, k:k + 1], (cl, LANES))


def near_block(columns, source, cl, out_ref, at):
    for h in range(cl // LANES):
        lanes = slice(h * LANES, (h + 1) * LANES)
        gap = [columns[k] - source(k, h) for k in range(3)]
        square = gap[0] * gap[0] + gap[1] * gap[1] + gap[2] * gap[2]
        high, low = split(lax.rsqrt(square + SMOOTHING))
        out_ref[at, 0:cl, lanes] = high
        out_ref[at, cl:2 * cl, lanes] = low


def near_product(pieces, block_ref, at, cl):
    return dot_nt(pieces, block_ref[at, 0:cl, :]) + dot_nt(pieces, block_ref[at, cl:2 * cl, :])


def fill_charges(pieces_ref, blocks, clusters, cl):
    for b, ref in enumerate(blocks):
        for c in range(clusters):
            pieces_ref[b * clusters + c] = stacked(ref[:, c * cl:(c + 1) * cl])
    pieces_ref[len(blocks) * clusters] = jnp.zeros_like(pieces_ref[0])


def pair_at(pairs_ref, which, i):
    pair = pairs_ref[which, i]
    return lax.shift_right_logical(pair, 6), lax.bitwise_and(pair, 63)


def near_kernel(cl, which, number, pairs_ref, *refs):
    blocks = refs[:number]
    if which:
        columns_ref, start_ref, even_ref, odd_ref, near_out_ref, pieces_ref, sources_ref, total_ref = refs[number:]
    else:
        even_ref, odd_ref, near_out_ref, columns_ref, tail_ref, pieces_ref, sources_ref, total_ref = refs[number:]
        tail_ref[...] = blocks[1][:, blocks[1].shape[1] - tail_ref.shape[1]:]
    panels = near_out_ref.shape[1]
    clusters = panels // cl
    steps = (pairs_ref[2 + which, 0] + 1) // 2
    sources_ref[number * clusters] = jnp.zeros_like(sources_ref[0])
    for b, ref in enumerate(blocks):
        for c in range(clusters):
            for k in range(3):
                sources_ref[b * clusters + c, k:k + 1, :] = ref[c:c + 1, panels + k * cl:panels + (k + 1) * cl]
    fill_charges(pieces_ref, blocks, clusters, cl)
    for c in range(clusters):
        if not which:
            columns_of(blocks[1], panels, c, cl, columns_ref, c)
        total_ref[c] = jnp.zeros_like(total_ref[c])
    odd_ref[0] = jnp.zeros_like(odd_ref[0])

    def build(ref, at, i):
        c, j = pair_at(pairs_ref, which, i)
        source = lambda k, h: sources_ref[j, k:k + 1, h * LANES:(h + 1) * LANES]
        near_block([columns_ref[c, k] for k in range(3)], source, cl, ref, at)

    def product(ref, at, i):
        return near_product(pieces_ref[pair_at(pairs_ref, which, i)[1]], ref, at, cl)

    def add(i, part):
        total_ref[pair_at(pairs_ref, which, i)[0]] += part

    def step(m, _):
        before = jnp.maximum(2 * m - 1, 0)
        part = product(odd_ref, m, before)
        build(even_ref, m, 2 * m)
        add(before, part)
        part = product(even_ref, m, 2 * m)
        build(odd_ref, m + 1, 2 * m + 1)
        add(2 * m, part)
        return 0

    lax.fori_loop(0, steps, step, 0)
    last = jnp.maximum(2 * steps - 1, 0)
    add(last, product(odd_ref, steps, last))
    for c in range(clusters):
        lanes = slice(c * cl, (c + 1) * cl)
        near = folded(total_ref[c])
        near_out_ref[:, lanes] = start_ref[:, lanes] + near if which else near


def near_again_kernel(cl, which, number, pairs_ref, *refs):
    blocks = refs[:number]
    if which:
        start_ref, even_ref, odd_ref, near_out_ref, pieces_ref, total_ref = refs[number:]
    else:
        even_ref, odd_ref, near_out_ref, tail_ref, pieces_ref, total_ref = refs[number:]
        tail_ref[...] = blocks[1][:, blocks[1].shape[1] - tail_ref.shape[1]:]
    clusters = near_out_ref.shape[1] // cl
    fill_charges(pieces_ref, blocks, clusters, cl)
    for c in range(clusters):
        total_ref[c] = jnp.zeros_like(total_ref[c])
    count = pairs_ref[2 + which, 0]

    def step(m, _):
        parts = []
        for w in range(4):
            i = 4 * m + w
            at = jnp.where(i < count, i // 2, 0) + w % 2
            parts.append(near_product(pieces_ref[pair_at(pairs_ref, which, i)[1]], (even_ref, odd_ref)[w % 2], at, cl))
        for w in range(4):
            total_ref[pair_at(pairs_ref, which, 4 * m + w)[0]] += parts[w]
        return 0

    lax.fori_loop(0, (count + 3) // 4, step, 0)
    for c in range(clusters):
        lanes = slice(c * cl, (c + 1) * cl)
        near = folded(total_ref[c])
        near_out_ref[:, lanes] = start_ref[:, lanes] + near if which else near


def load_window(tables, clusters, rank, pieces_ref, middle_ref):
    per = LANES // rank
    span = clusters * rank
    count = pieces_ref.shape[0] // per
    groups = span // LANES
    for at in range(count):
        (ref, first), g = tables[at // groups], at % groups
        tile = ref[:, first + g * LANES:first + (g + 1) * LANES]
        for s in range(per):
            pieces_ref[s * count + at] = stacked(pltpu.roll(tile, s * rank, 1) if s else tile)
        if middle_ref is not None:
            half = groups // 2
            row, lane = 8 * (g // half), first + span + g % half * LANES
            tile = ref[row:row + 8, lane:lane + LANES]
            for s in range(per):
                middle_ref[s * count + at] = pltpu.roll(tile, s * rank, 1) if s else tile


def six_tables(width, second_ref, other_ref, third_ref):
    return (second_ref, width), (second_ref, 0), (other_ref, other_ref.shape[1] - width), (third_ref, 2 * width), (third_ref, width), (third_ref, 0)


def pick(source_ref, at_ref, c, g, per, lane):
    row = None
    for u in range(per):
        take = source_ref[at_ref[c, g * per + u]]
        row = take if row is None else jnp.where(lane == u, take, row)
    return row


def far_fields(gathered_ref, coupling_ref, fields_ref):
    for c in range(gathered_ref.shape[0]):
        field = quartered(dot_nt(gathered_ref[c], coupling_ref[c]))
        fields_ref[c] = stacked(jnp.concatenate([field, field], axis=1))


def far_potential(fields_ref, c, basis):
    return folded(dot_nn(fields_ref[c], basis))


def image_kernel(cl, rank, at_ref, second_ref, other_ref, third_ref, center_ref, area_ref, near_ref, basis_ref, krylov_ref, offsets_ref,
                 image_ref, payload_ref, coupling_ref, pieces_ref, middle_ref, gathered_ref, fields_ref):
    rhs, panels = near_ref.shape
    clusters = panels // cl
    per = LANES // rank
    span = clusters * rank
    load_window(six_tables(span + span // 2, second_ref, other_ref, third_ref), clusters, rank, pieces_ref, middle_ref)
    lane = lax.broadcasted_iota(jnp.int32, (1, LANES), 1) // rank
    for c in range(clusters):
        mine = [offsets_ref[3, k:k + 1, :] - center_ref[c:c + 1, k * LANES:(k + 1) * LANES] for k in range(3)]
        for g in range(at_ref.shape[1] // per):
            lanes = slice(g * LANES, (g + 1) * LANES)
            gathered_ref[c, :, lanes] = pick(pieces_ref, at_ref, c, g, per, lane)
            center = pick(middle_ref, at_ref, c, g, per, lane)
            gap = [(center[k:k + 1] + mine[k]) - offsets_ref[k] for k in range(3)]
            high, low = split(lax.rsqrt(gap[0] * gap[0] + gap[1] * gap[1] + gap[2] * gap[2] + SMOOTHING))
            coupling_ref[c, 0:rank, lanes] = high
            coupling_ref[c, rank:2 * rank, lanes] = low
    far_fields(gathered_ref, coupling_ref, fields_ref)
    squared = correlation = jnp.zeros((rhs, cl), F32)
    for c in range(clusters):
        lanes = slice(c * cl, (c + 1) * cl)
        basis = basis_ref[:, lanes]
        area = area_ref[c:c + 1, :]
        image = COULOMB * area * (near_ref[:, lanes] + far_potential(fields_ref, c, basis))
        charges = area * image
        image_ref[:, lanes] = image
        payload_ref[:, lanes] = charges
        payload_ref[:, panels + c * rank:panels + (c + 1) * rank] = moments_of(charges, basis)
        krylov = krylov_ref[:, lanes]
        squared = squared + krylov * krylov
        correlation = correlation + krylov * image
    squared = jnp.sum(squared, axis=1, keepdims=True)
    correlation = jnp.sum(correlation, axis=1, keepdims=True)
    local = ratio(correlation, squared)
    residual = image_ref[...] - local * krylov_ref[...]
    payload_ref[:, panels + span:] = in_lanes(squared, correlation, jnp.sum(residual * residual, axis=1, keepdims=True), local)


def finish_kernel(cl, rank, total, at_ref, one_ref, two_ref, second_table_ref, other_ref, third_ref, near_ref, area_ref, image_ref, coupling_ref, basis_ref, krylov_ref,
                  next_hbm, second_hbm, pieces_ref, gathered_ref, fields_ref, next_ref, second_ref, sems):
    clusters = near_ref.shape[1] // cl
    per = LANES // rank
    squared, correlation, energy, local = merged([one_ref[...], two_ref[...]])
    projection = correlation / (squared + 1e-06)
    gap = projection - local
    scaling = 1.0 / jnp.sqrt((energy + gap * gap * squared) / total + 1e-06)
    next_ref[...] = (image_ref[...] - projection * krylov_ref[...]) * scaling
    moves = copies(((next_ref, next_hbm),), sems)
    load_window(six_tables(clusters * rank, second_table_ref, other_ref, third_ref), clusters, rank, pieces_ref, None)
    lane = lax.broadcasted_iota(jnp.int32, (1, LANES), 1) // rank
    for c in range(clusters):
        for g in range(at_ref.shape[1] // per):
            gathered_ref[c, :, g * LANES:(g + 1) * LANES] = pick(pieces_ref, at_ref, c, g, per, lane)
    far_fields(gathered_ref, coupling_ref, fields_ref)
    for c in range(clusters):
        lanes = slice(c * cl, (c + 1) * cl)
        image = COULOMB * area_ref[c:c + 1, :] * (near_ref[:, lanes] + far_potential(fields_ref, c, basis_ref[:, lanes]))
        second_ref[:, lanes] = (image - projection * image_ref[:, lanes]) * scaling
    moves.append(pltpu.make_async_copy(second_ref, second_hbm, sems.at[1]))
    moves[1].start()
    moves[0].wait()
    moves[1].wait()


def ratio(correlation, squared):
    return jnp.where(squared > 0, correlation / jnp.where(squared > 0, squared, 1.0), 0.0)


def in_lanes(*columns):
    lane = lax.broadcasted_iota(jnp.int32, (columns[0].shape[0], LANES), 1)
    out = columns[-1]
    for i, column in enumerate(columns[:-1]):
        out = jnp.where(lane == i, column, out)
    return out


def merged(groups):
    squared = sum(group[:, 0:1] for group in groups)
    correlation = sum(group[:, 1:2] for group in groups)
    local = ratio(correlation, squared)
    energy = 0.0
    for group in groups:
        gap = local - group[:, 3:4]
        energy = energy + (group[:, 2:3] + gap * gap * group[:, 0:1])
    return squared, correlation, energy, local


def merge_kernel(one_ref, two_ref, out_ref):
    out_ref[...] = in_lanes(*merged([ref[:, ref.shape[1] - LANES:] for ref in (one_ref, two_ref)]))


def call(kernel, outs, scratch, memory, *args, limit=6, us=1.0):
    spaces = {"s": pltpu.SMEM, "v": pltpu.VMEM, "p": pltpu.VMEM, "h": pltpu.HBM}
    ins, out_spaces = memory.split(">")
    pinned = {"h": pltpu.HBM, "p": pltpu.VMEM}
    return pl.pallas_call(
        kernel,
        out_shape=[pltpu.VMEM(*out) if m == "p" else jax.ShapeDtypeStruct(*out) for m, out in zip(out_spaces, outs)],
        in_specs=[pl.BlockSpec(memory_space=spaces[m]) for m in ins],
        out_specs=[pl.BlockSpec(memory_space=spaces[m]) for m in out_spaces],
        scratch_shapes=scratch,
        compiler_params=pltpu.CompilerParams(vmem_limit_bytes=limit * 2 ** 20),
        cost_estimate=pl.CostEstimate(flops=int(us * 5e8), bytes_accessed=int(us * 3.6e6), transcendentals=0),
    )(*(pltpu.with_memory_space_constraint(a, pinned[m]) if m in pinned else a for m, a in zip(ins, args)))


def body(vertices, panel_vertices, near_pairs, far_pairs, basis, krylov):
    clusters, slots = near_pairs.shape
    partners = far_pairs.shape[1]
    rhs, panels = krylov.shape
    rank = basis.shape[0]
    cl = panels // clusters
    vcl = vertices.shape[1] // clusters
    span = clusters * rank
    per = LANES // rank
    devices = lax.axis_size("clus")
    position = lax.axis_index("clus").reshape(1).astype(jnp.int32)
    offsets = proxy_offsets(rank)
    flat = np.concatenate([np.tile(offsets, (1, per)), np.zeros((rank - 3, LANES), np.float32)])
    offsets = jnp.asarray(np.concatenate([np.broadcast_to(offsets[:, :, None], (3, rank, LANES)), flat[None]]))
    width = span + span // 2
    pairing = [(i, i + 1 - 2 * (i % 2)) for i in range(devices)]
    bridging = [(i, i - 1 + 2 * (i % 2)) for i in range(1, devices - 1)] + [(0, 0), (devices - 1, devices - 1)]
    second = [(i, (i + 3 * (2 * (i % 2) - 1)) % devices) for i in range(devices)]
    third = [(i, i + 4 * (2 * (i % 2) - 1)) for i in range(1, devices - 1)] + [(0, 3), (devices - 1, devices - 4)]
    third = [(i, j % devices) for i, j in third]

    def move(value, pairs):
        return lax.ppermute(value, "clus", pairs)

    def exchange(value, first, width):
        mine = value[:, first:first + width]
        partner = move(value, pairing)
        pair = jnp.concatenate([mine, partner[:, first:first + width]], axis=1)
        other = move(jnp.concatenate([value[:, :first], pair], axis=1), bridging)
        return partner, other, move(pair, second)

    def last_exchange(tail, other, width):
        return move(jnp.concatenate([tail[:, :width], other[:, other.shape[1] - 2 * width:]], axis=1), third)

    whole = ((rhs, panels), F32)
    payload, area, centers, at, pairs, basis, krylov, offsets = call(
        functools.partial(prepare_kernel, cl, vcl, rank),
        [
            ((rhs, panels + 3 * cl + width), F32), ((clusters, cl), F32), ((clusters, 3 * LANES), F32),
            (far_pairs.shape, jnp.int32), ((8, LANES), jnp.int32), ((2 * rank, panels), BF16), whole, (offsets.shape, F32),
        ],
        [
            pltpu.VMEM(vertices.shape, F32),
            pltpu.VMEM(panel_vertices.shape, jnp.int32),
            pltpu.VMEM(basis.shape, F32),
            pltpu.VMEM(far_pairs.shape, jnp.int32),
            pltpu.VMEM((slots, clusters), jnp.int32),
            pltpu.VMEM((3 * clusters, vcl), F32),
            pltpu.VMEM((3 * panels // LANES, LANES), jnp.int32),
            pltpu.SemaphoreType.DMA((7,)),
        ],
        "shhhhhhh>vvvvvppp",
        position, vertices, panel_vertices, krylov, basis, far_pairs, near_pairs.T, offsets,
        us=1.5,
    )
    partner, other, two = exchange(payload, panels + 3 * cl, width)
    total = pltpu.VMEM((clusters, 2 * rhs, cl), F32)

    def kept(most):
        return [(((most + 1) // 2 + 1, 2 * cl, cl), BF16)] * 2

    def pieces(number):
        return pltpu.VMEM((number * clusters + 1, 2 * rhs, cl), BF16)

    def sources(number):
        return pltpu.VMEM((number * clusters + 1, 8, cl), F32)

    even, odd, near, columns, tail = call(
        functools.partial(near_kernel, cl, 0, 2),
        [*kept(clusters * slots), whole, ((clusters, 3, cl, LANES), F32), ((rhs, width), F32)],
        [pieces(2), sources(2), total],
        "svv>ppvpv",
        pairs, partner, payload,
        us=8.0,
    )
    three = last_exchange(tail, other, width)
    even_other, odd_other, near = call(
        functools.partial(near_kernel, cl, 1, 1),
        [*kept(clusters * (slots - 1)), whole],
        [pieces(1), sources(1), total],
        "svpv>ppv",
        pairs, other, columns, near,
        us=3.0,
    )
    tiles = 6 * per * span // LANES
    window = pltpu.VMEM((tiles, 2 * rhs, LANES), BF16)
    gathered = pltpu.VMEM((clusters, 2 * rhs, partners * rank), BF16)
    fields = pltpu.VMEM((clusters, 2 * rhs, 2 * rank), BF16)
    image, payload, coupling = call(
        functools.partial(image_kernel, cl, rank),
        [whole, ((rhs, panels + span + LANES), F32), ((clusters, 2 * rank, partners * rank), BF16)],
        [window, pltpu.VMEM((tiles, 8, LANES), F32), gathered, fields],
        "svvvvvvppp>vvp",
        at, two, other, three, centers, area, near, basis, krylov, offsets,
        us=4.5,
    )
    partner, other, two = exchange(payload, panels, span)
    near, one = call(
        functools.partial(near_again_kernel, cl, 0, 2),
        [whole, ((rhs, span + LANES), F32)],
        [pieces(2), total],
        "svvpp>vv",
        pairs, partner, payload, even, odd,
        us=2.5,
    )
    three = last_exchange(one, other, span)
    many = partner
    size = 2
    while size < devices:
        (one,) = call(merge_kernel, [((rhs, LANES), F32)], [], "vv>v", one, many, us=0.3)
        many = move(one, [(i, (i + size) % devices) for i in range(devices)])
        size = 2 * size
    (near,) = call(
        functools.partial(near_again_kernel, cl, 1, 1),
        [whole],
        [pieces(1), total],
        "svvpp>v",
        pairs, other, near, even_other, odd_other,
        us=2.0,
    )
    here = pltpu.VMEM((rhs, panels), F32)
    return tuple(call(
        functools.partial(finish_kernel, cl, rank, panels * devices),
        [whole, whole],
        [window, gathered, fields, here, here, pltpu.SemaphoreType.DMA((2,))],
        "svvvvvvvvppp>hh",
        at, one, many, two, other, three, near, area, image, coupling, basis, krylov,
        us=3.0,
    ))


def solution(mesh):
    whole = P(None, ("jobs", "clus"))
    rows = P(("jobs", "clus"), None)
    return jax.shard_map(
        body,
        mesh=mesh,
        in_specs=(whole, whole, rows, rows, whole, whole),
        out_specs=(whole, whole),
        check_vma=False,
    )
```

```python
import functools

import jax
import jax.numpy as jnp
import numpy as np
from jax import lax
from jax.experimental import pallas as pl
from jax.experimental.pallas import tpu as pltpu
from jax.sharding import PartitionSpec as P

REACH = 4
SMOOTHING = 0.04
COULOMB = 2.0
PROXY_RADIUS = 0.6
LANES = 128
F32 = jnp.float32
BF16 = jnp.bfloat16


def proxy_offsets(points):
    counter = np.arange(points, dtype=np.float32)
    height = 1.0 - (2.0 * counter + 1.0) / points
    radial = np.sqrt(1.0 - height * height)
    azimuth = counter * 2.399963
    return PROXY_RADIUS * np.stack([radial * np.cos(azimuth), radial * np.sin(azimuth), height]).astype(np.float32)


def split(value):
    high = value.astype(BF16)
    return high, (value - high.astype(F32)).astype(BF16)


def stacked(value):
    return jnp.concatenate(split(value), axis=0)


def folded(value):
    half = value.shape[0] // 2
    return value[:half] + value[half:]


def dot_nt(left, right):
    return lax.dot_general(left, right, (((1,), (1,)), ((), ())), preferred_element_type=F32)


def dot_nn(left, right):
    return lax.dot_general(left, right, (((1,), (0,)), ((), ())), preferred_element_type=F32)


def quartered(value):
    half = value.shape[1] // 2
    value = folded(value)
    return value[:, 0:half] + value[:, half:]


def moments_of(weighted, basis_pieces):
    return quartered(dot_nt(stacked(weighted), basis_pieces))


def copies(pairs, sems):
    moves = [pltpu.make_async_copy(source, target, sems.at[i]) for i, (source, target) in enumerate(pairs)]
    for move in moves:
        move.start()
    return moves


def pair_list(near, position, clusters):
    block = lax.div(near, clusters) - position
    partner = block * (1 - 2 * lax.rem(position, 2)) > 0
    place = (lax.rem(near, clusters) + jnp.where((block != 0) & ~partner, clusters, 0)).astype(F32)
    across = lax.broadcasted_iota(jnp.int32, (clusters, clusters), 1)
    down = lax.broadcasted_iota(jnp.int32, (clusters, clusters), 0)
    upright = lambda value: jnp.sum(jnp.where(across == down, value, 0.0), axis=1, keepdims=True)
    row = lax.broadcasted_iota(jnp.int32, (clusters, LANES), 1).astype(F32)
    target = lax.broadcasted_iota(jnp.int32, (clusters, 1), 0).astype(F32)
    rows = lax.broadcasted_iota(jnp.int32, (8, LANES), 0)
    out = jnp.zeros((8, LANES), F32)
    for which in range(2):
        here = block != 0 if which else block == 0
        live = jnp.where(here & (near >= 0), 1.0, 0.0)
        counts = sum(live[k:k + 1] for k in range(near.shape[0]))
        first = jnp.sum(jnp.where(across < down, counts, 0.0), axis=1, keepdims=True)
        found = jnp.zeros((clusters, LANES), F32)
        for k in range(near.shape[0]):
            alive = upright(live[k:k + 1])
            hit = jnp.where(row == first, alive, 0.0)
            found = found + hit * (target * 64 + upright(place[k:k + 1]))
            first = first + alive
        count = jnp.sum(counts, axis=1, keepdims=True)
        found = jnp.where(row[0:1] < count, jnp.sum(found, axis=0, keepdims=True), (1.0 + which) * clusters)
        out = jnp.where(rows == which, found, jnp.where(rows == 2 + which, count, out))
    return out.astype(jnp.int32)


def prepare_kernel(cl, vcl, rank, position_ref, vertices_hbm, corners_hbm, krylov_hbm, basis_hbm, far_hbm, near_hbm, offsets_hbm, weights_hbm,
                   payload_ref, area_ref, center_ref, at_ref, pairs_ref, basis_ref, krylov_ref, offsets_ref, weights_ref,
                   vertices_ref, corners_ref, raw_ref, far_ref, near_ref, mesh_ref, local_ref, sems):
    moves = copies((
        (vertices_hbm, vertices_ref), (corners_hbm, corners_ref), (krylov_hbm, krylov_ref), (basis_hbm, raw_ref),
        (far_hbm, far_ref), (near_hbm, near_ref), (offsets_hbm, offsets_ref), (weights_hbm.at[position_ref[0]], weights_ref),
    ), sems)
    rhs, panels = krylov_ref.shape
    clusters = panels // cl
    parts = cl // LANES
    moves[0].wait()
    for c in range(clusters):
        mesh_ref[3 * c:3 * c + 3, :] = vertices_ref[:, c * vcl:(c + 1) * vcl]
    moves[1].wait()
    for i in range(clusters * parts):
        local_ref[3 * i:3 * i + 3, :] = corners_ref[:, i * LANES:(i + 1) * LANES]
    first = position_ref[0] * (vcl * clusters) + vcl * lax.broadcasted_iota(jnp.int32, (clusters, LANES), 0)
    tables = [mesh_ref[pl.ds(k, clusters, stride=3), :] for k in range(3)]
    sums = [None] * 3
    for h in range(parts):
        local = [local_ref[pl.ds(3 * h + m, clusters, stride=3 * parts), :] - first for m in range(3)]
        corner = [[jnp.take_along_axis(tables[k], local[m], axis=1, mode="promise_in_bounds") for k in range(3)] for m in range(3)]
        for k in range(3):
            middle = (corner[0][k] + corner[1][k] + corner[2][k]) / 3.0
            payload_ref[:, panels + k * cl + h * LANES:panels + k * cl + (h + 1) * LANES] = middle
            sums[k] = middle if h == 0 else sums[k] + middle
        one = [corner[1][k] - corner[0][k] for k in range(3)]
        two = [corner[2][k] - corner[0][k] for k in range(3)]
        normal = [one[1] * two[2] - one[2] * two[1], one[2] * two[0] - one[0] * two[2], one[0] * two[1] - one[1] * two[0]]
        area_ref[:, h * LANES:(h + 1) * LANES] = 0.5 * jnp.sqrt(normal[0] * normal[0] + normal[1] * normal[1] + normal[2] * normal[2])
    span = clusters * rank
    table = panels + 3 * cl
    mine = lax.broadcasted_iota(jnp.int32, (clusters, span), 1) // rank == lax.broadcasted_iota(jnp.int32, (clusters, span), 0)
    half = span // 2
    payload_ref[:, table + span:] = jnp.zeros_like(payload_ref[:, table + span:])
    for k in range(3):
        center = jnp.sum(sums[k], axis=1, keepdims=True) / cl
        center_ref[:, k * LANES:(k + 1) * LANES] = jnp.broadcast_to(center, (clusters, LANES))
        row = jnp.sum(jnp.where(mine, center, 0.0), axis=0, keepdims=True)
        payload_ref[k:k + 1, table + span:] = row[:, 0:half]
        payload_ref[8 + k:9 + k, table + span:] = row[:, half:]
    moves[2].wait()
    moves[3].wait()
    for c in range(clusters):
        lanes = slice(c * cl, (c + 1) * cl)
        basis_ref[:, lanes] = stacked(raw_ref[:, lanes])
        charges = area_ref[c:c + 1, :] * krylov_ref[:, lanes]
        payload_ref[:, lanes] = charges
        payload_ref[:, table + c * rank:table + (c + 1) * rank] = moments_of(charges, basis_ref[:, lanes])
    moves[4].wait()
    far = far_ref[...]
    step = (lax.div(far, clusters) - position_ref[0]) * (1 - 2 * lax.rem(position_ref[0], 2))
    block = jnp.where(step < 0, step + REACH, step + REACH - 3)
    per = LANES // rank
    turn = lax.rem(lax.broadcasted_iota(jnp.int32, far.shape, 1) - far + per * clusters * 2 ** 16, per)
    at_ref[...] = (turn * 6 + block) * (span // LANES) + lax.div(lax.rem(far, clusters), per)
    moves[5].wait()
    pairs_ref[...] = pair_list(near_ref[...], position_ref[0], clusters)
    moves[6].wait()
    moves[7].wait()


def columns_of(payload_ref, panels, c, cl, columns_ref, at):
    rows = [payload_ref[c:c + 1, panels + k * cl:panels + (k + 1) * cl] for k in range(3)]
    upright = jnp.transpose(jnp.concatenate(rows * 2 + rows[:2], axis=0))
    for k in range(3):
        columns_ref[at, k] = jnp.broadcast_to(upright[:, k:k + 1], (cl, LANES))


def near_block(columns, source, cl, out_ref, at):
    for h in range(cl // LANES):
        lanes = slice(h * LANES, (h + 1) * LANES)
        gap = [columns[k] - source(k, h) for k in range(3)]
        square = gap[0] * gap[0] + gap[1] * gap[1] + gap[2] * gap[2]
        high, low = split(lax.rsqrt(square + SMOOTHING))
        out_ref[at, 0:cl, lanes] = high
        out_ref[at, cl:2 * cl, lanes] = low


def near_product(pieces, block_ref, at, cl):
    return dot_nt(pieces, block_ref[at, 0:cl, :]) + dot_nt(pieces, block_ref[at, cl:2 * cl, :])


def fill_charges(pieces_ref, blocks, clusters, cl):
    for b, ref in enumerate(blocks):
        for c in range(clusters):
            pieces_ref[b * clusters + c] = stacked(ref[:, c * cl:(c + 1) * cl])
    pieces_ref[len(blocks) * clusters] = jnp.zeros_like(pieces_ref[0])


def pair_at(pairs_ref, which, i):
    pair = pairs_ref[which, i]
    return lax.shift_right_logical(pair, 6), lax.bitwise_and(pair, 63)


def near_kernel(cl, which, number, pairs_ref, *refs):
    blocks = refs[:number]
    if which:
        columns_ref, start_ref, even_ref, odd_ref, near_out_ref, pieces_ref, sources_ref, total_ref = refs[number:]
    else:
        _, even_ref, odd_ref, near_out_ref, columns_ref, tail_ref, pieces_ref, sources_ref, total_ref = refs[number:]
        tail_ref[...] = blocks[0][:, blocks[0].shape[1] - tail_ref.shape[1]:]
    panels = near_out_ref.shape[1]
    clusters = panels // cl
    steps = (pairs_ref[2 + which, 0] + 1) // 2
    sources_ref[number * clusters] = jnp.zeros_like(sources_ref[0])
    for b, ref in enumerate(blocks):
        for c in range(clusters):
            for k in range(3):
                sources_ref[b * clusters + c, k:k + 1, :] = ref[c:c + 1, panels + k * cl:panels + (k + 1) * cl]
    fill_charges(pieces_ref, blocks, clusters, cl)
    for c in range(clusters):
        if not which:
            columns_of(blocks[0], panels, c, cl, columns_ref, c)
        total_ref[c] = jnp.zeros_like(total_ref[c])
    odd_ref[0] = jnp.zeros_like(odd_ref[0])

    def build(ref, at, i):
        c, j = pair_at(pairs_ref, which, i)
        source = lambda k, h: sources_ref[j, k:k + 1, h * LANES:(h + 1) * LANES]
        near_block([columns_ref[c, k] for k in range(3)], source, cl, ref, at)

    def product(ref, at, i):
        return near_product(pieces_ref[pair_at(pairs_ref, which, i)[1]], ref, at, cl)

    def add(i, part):
        total_ref[pair_at(pairs_ref, which, i)[0]] += part

    def step(m, _):
        before = jnp.maximum(2 * m - 1, 0)
        part = product(odd_ref, m, before)
        build(even_ref, m, 2 * m)
        add(before, part)
        part = product(even_ref, m, 2 * m)
        build(odd_ref, m + 1, 2 * m + 1)
        add(2 * m, part)
        return 0

    lax.fori_loop(0, steps, step, 0)
    last = jnp.maximum(2 * steps - 1, 0)
    add(last, product(odd_ref, steps, last))
    for c in range(clusters):
        lanes = slice(c * cl, (c + 1) * cl)
        near = folded(total_ref[c])
        near_out_ref[:, lanes] = start_ref[:, lanes] + near if which else near


def near_again_kernel(cl, which, number, pairs_ref, *refs):
    blocks = refs[:number]
    if which:
        start_ref, even_ref, odd_ref, near_out_ref, pieces_ref, total_ref = refs[number:]
    else:
        _, even_ref, odd_ref, near_out_ref, tail_ref, pieces_ref, total_ref = refs[number:]
        tail_ref[...] = blocks[0][:, blocks[0].shape[1] - tail_ref.shape[1]:]
    clusters = near_out_ref.shape[1] // cl
    fill_charges(pieces_ref, blocks, clusters, cl)
    for c in range(clusters):
        total_ref[c] = jnp.zeros_like(total_ref[c])
    count = pairs_ref[2 + which, 0]

    def step(m, _):
        parts = []
        for w in range(4):
            i = 4 * m + w
            at = jnp.where(i < count, i // 2, 0) + w % 2
            parts.append(near_product(pieces_ref[pair_at(pairs_ref, which, i)[1]], (even_ref, odd_ref)[w % 2], at, cl))
        for w in range(4):
            total_ref[pair_at(pairs_ref, which, 4 * m + w)[0]] += parts[w]
        return 0

    lax.fori_loop(0, (count + 3) // 4, step, 0)
    for c in range(clusters):
        lanes = slice(c * cl, (c + 1) * cl)
        near = folded(total_ref[c])
        near_out_ref[:, lanes] = start_ref[:, lanes] + near if which else near


def load_window(tables, clusters, rank, pieces_ref, middle_ref):
    per = LANES // rank
    span = clusters * rank
    count = pieces_ref.shape[0] // per
    groups = span // LANES
    for at in range(count):
        (ref, first), g = tables[at // groups], at % groups
        tile = ref[:, first + g * LANES:first + (g + 1) * LANES]
        for s in range(per):
            pieces_ref[s * count + at] = stacked(pltpu.roll(tile, s * rank, 1) if s else tile)
        if middle_ref is not None:
            half = groups // 2
            row, lane = 8 * (g // half), first + span + g % half * LANES
            tile = ref[row:row + 8, lane:lane + LANES]
            for s in range(per):
                middle_ref[s * count + at] = pltpu.roll(tile, s * rank, 1) if s else tile


def six_tables(width, second_ref, other_ref, third_ref):
    gap = third_ref.shape[1] - 3 * width
    return (
        (second_ref, width), (second_ref, 0), (other_ref, other_ref.shape[1] - width),
        (third_ref, 2 * width + gap), (third_ref, width + gap), (third_ref, 0),
    )


def pick(source_ref, at_ref, c, g, per, lane):
    row = None
    for u in range(per):
        take = source_ref[at_ref[c, g * per + u]]
        row = take if row is None else jnp.where(lane == u, take, row)
    return row


def far_fields(gathered_ref, coupling_ref, fields_ref):
    for c in range(gathered_ref.shape[0]):
        field = quartered(dot_nt(gathered_ref[c], coupling_ref[c]))
        fields_ref[c] = stacked(jnp.concatenate([field, field], axis=1))


def far_potential(fields_ref, c, basis):
    return folded(dot_nn(fields_ref[c], basis))


def image_kernel(cl, rank, at_ref, second_ref, other_ref, third_ref, center_ref, area_ref, near_ref, basis_ref, krylov_ref, offsets_ref,
                 image_ref, payload_ref, coupling_ref, pieces_ref, middle_ref, gathered_ref, fields_ref):
    rhs, panels = near_ref.shape
    clusters = panels // cl
    per = LANES // rank
    span = clusters * rank
    load_window(six_tables(span + span // 2, second_ref, other_ref, third_ref), clusters, rank, pieces_ref, middle_ref)
    lane = lax.broadcasted_iota(jnp.int32, (1, LANES), 1) // rank
    for c in range(clusters):
        mine = [offsets_ref[3, k:k + 1, :] - center_ref[c:c + 1, k * LANES:(k + 1) * LANES] for k in range(3)]
        for g in range(at_ref.shape[1] // per):
            lanes = slice(g * LANES, (g + 1) * LANES)
            gathered_ref[c, :, lanes] = pick(pieces_ref, at_ref, c, g, per, lane)
            center = pick(middle_ref, at_ref, c, g, per, lane)
            gap = [(center[k:k + 1] + mine[k]) - offsets_ref[k] for k in range(3)]
            high, low = split(lax.rsqrt(gap[0] * gap[0] + gap[1] * gap[1] + gap[2] * gap[2] + SMOOTHING))
            coupling_ref[c, 0:rank, lanes] = high
            coupling_ref[c, rank:2 * rank, lanes] = low
    far_fields(gathered_ref, coupling_ref, fields_ref)
    squared = correlation = jnp.zeros((rhs, cl), F32)
    for c in range(clusters):
        lanes = slice(c * cl, (c + 1) * cl)
        basis = basis_ref[:, lanes]
        area = area_ref[c:c + 1, :]
        image = COULOMB * area * (near_ref[:, lanes] + far_potential(fields_ref, c, basis))
        charges = area * image
        image_ref[:, lanes] = image
        payload_ref[:, lanes] = charges
        payload_ref[:, panels + c * rank:panels + (c + 1) * rank] = moments_of(charges, basis)
        krylov = krylov_ref[:, lanes]
        squared = squared + krylov * krylov
        correlation = correlation + krylov * image
    squared = jnp.sum(squared, axis=1, keepdims=True)
    correlation = jnp.sum(correlation, axis=1, keepdims=True)
    local = ratio(correlation, squared)
    residual = image_ref[...] - local * krylov_ref[...]
    payload_ref[:, panels + span:] = in_lanes(squared, correlation, jnp.sum(residual * residual, axis=1, keepdims=True), local)


def far_again_kernel(cl, rank, at_ref, second_ref, other_ref, third_ref, near_ref, area_ref, coupling_ref, basis_ref,
                     image_ref, pieces_ref, gathered_ref, fields_ref):
    clusters = near_ref.shape[1] // cl
    per = LANES // rank
    load_window(six_tables(clusters * rank + LANES, second_ref, other_ref, third_ref), clusters, rank, pieces_ref, None)
    lane = lax.broadcasted_iota(jnp.int32, (1, LANES), 1) // rank
    for c in range(clusters):
        for g in range(at_ref.shape[1] // per):
            gathered_ref[c, :, g * LANES:(g + 1) * LANES] = pick(pieces_ref, at_ref, c, g, per, lane)
    far_fields(gathered_ref, coupling_ref, fields_ref)
    for c in range(clusters):
        lanes = slice(c * cl, (c + 1) * cl)
        image_ref[:, lanes] = COULOMB * area_ref[c:c + 1, :] * (near_ref[:, lanes] + far_potential(fields_ref, c, basis_ref[:, lanes]))


def finish_kernel(total, one_ref, two_ref, image_ref, again_ref, krylov_ref, next_hbm, second_hbm, next_ref, second_ref, sems):
    squared, correlation, energy, local = merged([one_ref[...], two_ref[...]])
    projection = correlation / (squared + 1e-06)
    gap = projection - local
    scaling = 1.0 / jnp.sqrt((energy + gap * gap * squared) / total + 1e-06)
    moves = []
    half = next_ref.shape[1] // 2
    for h in range(2):
        lanes = slice(h * half, (h + 1) * half)
        image = image_ref[:, lanes]
        next_ref[:, lanes] = (image - projection * krylov_ref[:, lanes]) * scaling
        second_ref[:, lanes] = (again_ref[:, lanes] - projection * image) * scaling
        for held, hbm in ((next_ref, next_hbm), (second_ref, second_hbm)):
            moves.append(pltpu.make_async_copy(held.at[:, lanes], hbm.at[:, lanes], sems.at[len(moves)]))
            moves[-1].start()
    for move in moves:
        move.wait()


def ratio(correlation, squared):
    return jnp.where(squared > 0, correlation / jnp.where(squared > 0, squared, 1.0), 0.0)


def in_lanes(*columns):
    lane = lax.broadcasted_iota(jnp.int32, (columns[0].shape[0], LANES), 1)
    out = columns[-1]
    for i, column in enumerate(columns[:-1]):
        out = jnp.where(lane == i, column, out)
    return out


def merged(groups, weights=None):
    weights = weights or [1.0] * len(groups)
    squared = sum(weight * group[:, 0:1] for group, weight in zip(groups, weights))
    correlation = sum(weight * group[:, 1:2] for group, weight in zip(groups, weights))
    local = ratio(correlation, squared)
    energy = 0.0
    for group, weight in zip(groups, weights):
        gap = local - group[:, 3:4]
        energy = energy + weight * (group[:, 2:3] + gap * gap * group[:, 0:1])
    return squared, correlation, energy, local


def known_sums(tail_ref, partner_ref, other_ref, second_ref, third_ref):
    width = tail_ref.shape[1]
    ends = [(tail_ref, width), (partner_ref, partner_ref.shape[1]), (other_ref, other_ref.shape[1] - width), (other_ref, other_ref.shape[1])]
    ends += [(second_ref, width), (second_ref, 2 * width)]
    ends += [(third_ref, width), (third_ref, width + LANES), (third_ref, 2 * width + LANES), (third_ref, 3 * width + LANES)]
    return [ref[:, end - LANES:end] for ref, end in ends]


def known_sums_kernel(weights_ref, *refs):
    groups = known_sums(*refs[:5])
    for side, out_ref in enumerate(refs[5:]):
        weights = [weights_ref[0:1, 16 * side + i:16 * side + i + 1] for i in range(len(groups))]
        out_ref[...] = in_lanes(*merged(groups, weights))


def completing(devices, *moves):
    partner, other, second, third = ({target: source for source, target in move} for move in moves)
    slots = []
    for i in range(devices):
        two, three = second[i], third[i]
        slots.append([i, partner[i], other[i], partner[other[i]], two, partner[two], three, partner[three], other[three], partner[other[three]]])
    known = [set(slot) for slot in slots]
    everyone = set(range(devices))
    target_of = {}

    def matched(target, seen):
        for source in range(devices):
            if source not in seen and known[target] | known[source] == everyone:
                seen.add(source)
                if source not in target_of or matched(target_of[source], seen):
                    target_of[source] = target
                    return True
        return False

    if not all(matched(i, set()) for i in range(devices)):
        return None
    weights = np.zeros((devices, 8, LANES), np.float32)
    for i in range(devices):
        for at, device in enumerate(slots[i]):
            if device not in slots[i][:at]:
                weights[i, :, at] = 1.0
                weights[i, :, 16 + at] = device not in known[target_of[i]]
    return sorted(target_of.items()), weights


def merge_kernel(one_ref, two_ref, out_ref):
    out_ref[...] = in_lanes(*merged([ref[:, ref.shape[1] - LANES:] for ref in (one_ref, two_ref)]))


def call(kernel, outs, scratch, memory, *args, limit=6, us=1.0):
    spaces = {"s": pltpu.SMEM, "v": pltpu.VMEM, "p": pltpu.VMEM, "h": pltpu.HBM}
    ins, out_spaces = memory.split(">")
    pinned = {"h": pltpu.HBM, "p": pltpu.VMEM}
    return pl.pallas_call(
        kernel,
        out_shape=[pltpu.VMEM(*out) if m == "p" else jax.ShapeDtypeStruct(*out) for m, out in zip(out_spaces, outs)],
        in_specs=[pl.BlockSpec(memory_space=spaces[m]) for m in ins],
        out_specs=[pl.BlockSpec(memory_space=spaces[m]) for m in out_spaces],
        scratch_shapes=scratch,
        compiler_params=pltpu.CompilerParams(vmem_limit_bytes=limit * 2 ** 20),
        cost_estimate=pl.CostEstimate(flops=int(us * 5e8), bytes_accessed=int(us * 3.6e6), transcendentals=0),
    )(*(pltpu.with_memory_space_constraint(a, pinned[m]) if m in pinned else a for m, a in zip(ins, args)))


def body(vertices, panel_vertices, near_pairs, far_pairs, basis, krylov):
    clusters, slots = near_pairs.shape
    partners = far_pairs.shape[1]
    rhs, panels = krylov.shape
    rank = basis.shape[0]
    cl = panels // clusters
    vcl = vertices.shape[1] // clusters
    span = clusters * rank
    per = LANES // rank
    devices = lax.axis_size("clus")
    position = lax.axis_index("clus").reshape(1).astype(jnp.int32)
    offsets = proxy_offsets(rank)
    flat = np.concatenate([np.tile(offsets, (1, per)), np.zeros((rank - 3, LANES), np.float32)])
    offsets = jnp.asarray(np.concatenate([np.broadcast_to(offsets[:, :, None], (3, rank, LANES)), flat[None]]))
    width = span + span // 2
    pairing = [(i, i + 1 - 2 * (i % 2)) for i in range(devices)]
    bridging = [(i, i - 1 + 2 * (i % 2)) for i in range(1, devices - 1)] + [(0, 0), (devices - 1, devices - 1)]
    second = [(i, (i + 3 * (2 * (i % 2) - 1)) % devices) for i in range(devices)]
    third = [(i, i + 4 * (2 * (i % 2) - 1)) for i in range(1, devices - 1)] + [(0, 3), (devices - 1, devices - 4)]
    third = [(i, j % devices) for i, j in third]

    completion = completing(devices, pairing, bridging, second, third)
    weights = completion[1] if completion else np.zeros((devices, 8, LANES), np.float32)

    def move(value, pairs):
        return lax.ppermute(value, "clus", pairs)

    def exchange(value, first, width):
        mine = value[:, first:first + width]
        partner = move(value, pairing)
        pair = jnp.concatenate([mine, partner[:, first:first + width]], axis=1)
        other = move(jnp.concatenate([value[:, :first], pair], axis=1), bridging)
        return partner, other, move(pair, second)

    def last_exchange(tail, between, other):
        pair = other[:, other.shape[1] - 2 * tail.shape[1]:]
        return move(jnp.concatenate([tail, *between, pair], axis=1), third)

    whole = ((rhs, panels), F32)
    payload, area, centers, at, pairs, basis, krylov, offsets, weights = call(
        functools.partial(prepare_kernel, cl, vcl, rank),
        [
            ((rhs, panels + 3 * cl + width), F32), ((clusters, cl), F32), ((clusters, 3 * LANES), F32),
            (far_pairs.shape, jnp.int32), ((8, LANES), jnp.int32), ((2 * rank, panels), BF16), whole, (offsets.shape, F32), ((8, LANES), F32),
        ],
        [
            pltpu.VMEM(vertices.shape, F32),
            pltpu.VMEM(panel_vertices.shape, jnp.int32),
            pltpu.VMEM(basis.shape, F32),
            pltpu.VMEM(far_pairs.shape, jnp.int32),
            pltpu.VMEM((slots, clusters), jnp.int32),
            pltpu.VMEM((3 * clusters, vcl), F32),
            pltpu.VMEM((3 * panels // LANES, LANES), jnp.int32),
            pltpu.SemaphoreType.DMA((8,)),
        ],
        "shhhhhhhh>vvvvvpppp",
        position, vertices, panel_vertices, krylov, basis, far_pairs, near_pairs.T, offsets, jnp.asarray(weights),
        us=1.5,
    )
    partner, other, two = exchange(payload, panels + 3 * cl, width)
    total = pltpu.VMEM((clusters, 2 * rhs, cl), F32)

    def kept(most):
        return [(((most + 1) // 2 + 1, 2 * cl, cl), BF16)] * 2

    def pieces(number):
        return pltpu.VMEM((number * clusters + 1, 2 * rhs, cl), BF16)

    def sources(number):
        return pltpu.VMEM((number * clusters + 1, 8, cl), F32)

    even, odd, near, columns, tail = call(
        functools.partial(near_kernel, cl, 0, 1),
        [*kept(clusters * slots), whole, ((clusters, 3, cl, LANES), F32), ((rhs, width), F32)],
        [pieces(1), sources(1), total],
        "svv>ppvpv",
        pairs, payload, partner,
        us=6.0,
    )
    three = last_exchange(tail, [], other)
    even_other, odd_other, near = call(
        functools.partial(near_kernel, cl, 1, 2),
        [*kept(clusters * (slots - 1)), whole],
        [pieces(2), sources(2), total],
        "svvpv>ppv",
        pairs, partner, other, columns, near,
        us=4.0,
    )
    tiles = 6 * per * span // LANES
    window = pltpu.VMEM((tiles, 2 * rhs, LANES), BF16)
    gathered = pltpu.VMEM((clusters, 2 * rhs, partners * rank), BF16)
    fields = pltpu.VMEM((clusters, 2 * rhs, 2 * rank), BF16)
    image, payload, coupling = call(
        functools.partial(image_kernel, cl, rank),
        [whole, ((rhs, panels + span + LANES), F32), ((clusters, 2 * rank, partners * rank), BF16)],
        [window, pltpu.VMEM((tiles, 8, LANES), F32), gathered, fields],
        "svvvvvvppp>vvp",
        at, two, other, three, centers, area, near, basis, krylov, offsets,
        us=4.5,
    )
    partner, other, two = exchange(payload, panels, span + LANES)
    near, tail = call(
        functools.partial(near_again_kernel, cl, 0, 1),
        [whole, ((rhs, span + LANES), F32)],
        [pieces(1), total],
        "svvpp>vv",
        pairs, payload, partner, even, odd,
        us=2.5,
    )
    three = last_exchange(tail, [partner[:, panels + span:]], other)
    (near,) = call(
        functools.partial(near_again_kernel, cl, 1, 2),
        [whole],
        [pieces(2), total],
        "svvvpp>v",
        pairs, partner, other, near, even_other, odd_other,
        us=2.0,
    )
    sums_shape = ((rhs, LANES), F32)
    if completion:
        one, many = call(known_sums_kernel, [sums_shape] * 2, [], "pvvvvv>vv", weights, tail, partner, other, two, three, us=0.3)
        many = move(many, completion[0])
    else:
        one, many, size = tail, partner, 2
        while size < devices:
            (one,) = call(merge_kernel, [sums_shape], [], "vv>v", one, many, us=0.3)
            many = move(one, [(i, (i + size) % devices) for i in range(devices)])
            size = 2 * size
    (again,) = call(
        functools.partial(far_again_kernel, cl, rank),
        [whole],
        [window, gathered, fields],
        "svvvvvpp>v",
        at, two, other, three, near, area, coupling, basis,
        us=2.0,
    )
    here = pltpu.VMEM((rhs, panels), F32)
    return tuple(call(
        functools.partial(finish_kernel, panels * devices),
        [whole, whole],
        [here, here, pltpu.SemaphoreType.DMA((4,))],
        "vvvvp>hh",
        one, many, image, again, krylov,
    ))


def solution(mesh):
    whole = P(None, ("jobs", "clus"))
    rows = P(("jobs", "clus"), None)
    return jax.shard_map(
        body,
        mesh=mesh,
        in_specs=(whole, whole, rows, rows, whole, whole),
        out_specs=(whole, whole),
        check_vma=False,
    )
```

```python
import functools

import jax
import jax.numpy as jnp
import numpy as np
from jax import lax
from jax.experimental import pallas as pl
from jax.experimental.pallas import tpu as pltpu
from jax.sharding import PartitionSpec as P

REACH = 4
SMOOTHING = 0.04
COULOMB = 2.0
PROXY_RADIUS = 0.6
LANES = 128
F32 = jnp.float32
BF16 = jnp.bfloat16


def proxy_offsets(points):
    counter = np.arange(points, dtype=np.float32)
    height = 1.0 - (2.0 * counter + 1.0) / points
    radial = np.sqrt(1.0 - height * height)
    azimuth = counter * 2.399963
    return PROXY_RADIUS * np.stack([radial * np.cos(azimuth), radial * np.sin(azimuth), height]).astype(np.float32)


def split(value):
    high = value.astype(BF16)
    return high, (value - high.astype(F32)).astype(BF16)


def stacked(value):
    return jnp.concatenate(split(value), axis=0)


def folded(value):
    half = value.shape[0] // 2
    return value[:half] + value[half:]


def dot_nt(left, right):
    return lax.dot_general(left, right, (((1,), (1,)), ((), ())), preferred_element_type=F32)


def dot_nn(left, right):
    return lax.dot_general(left, right, (((1,), (0,)), ((), ())), preferred_element_type=F32)


def quartered(value):
    half = value.shape[1] // 2
    value = folded(value)
    return value[:, 0:half] + value[:, half:]


def moments_of(weighted, basis_pieces):
    return quartered(dot_nt(stacked(weighted), basis_pieces))


def copies(pairs, sems):
    moves = [pltpu.make_async_copy(source, target, sems.at[i]) for i, (source, target) in enumerate(pairs)]
    for move in moves:
        move.start()
    return moves


def pair_list(near, position, clusters):
    block = lax.div(near, clusters) - position
    partner = block * (1 - 2 * lax.rem(position, 2)) > 0
    place = (lax.rem(near, clusters) + jnp.where((block != 0) & ~partner, clusters, 0)).astype(F32)
    across = lax.broadcasted_iota(jnp.int32, (clusters, clusters), 1)
    down = lax.broadcasted_iota(jnp.int32, (clusters, clusters), 0)
    upright = lambda value: jnp.sum(jnp.where(across == down, value, 0.0), axis=1, keepdims=True)
    row = lax.broadcasted_iota(jnp.int32, (clusters, LANES), 1).astype(F32)
    target = lax.broadcasted_iota(jnp.int32, (clusters, 1), 0).astype(F32)
    rows = lax.broadcasted_iota(jnp.int32, (8, LANES), 0)
    out = jnp.zeros((8, LANES), F32)
    for which in range(2):
        here = block != 0 if which else block == 0
        live = jnp.where(here & (near >= 0), 1.0, 0.0)
        counts = sum(live[k:k + 1] for k in range(1, near.shape[0]))
        first = jnp.sum(jnp.where(across < down, counts, 0.0), axis=1, keepdims=True)
        found = jnp.zeros((clusters, LANES), F32)
        for k in range(1, near.shape[0]):
            alive = upright(live[k:k + 1])
            hit = jnp.where(row == first, alive, 0.0)
            found = found + hit * (target * 64 + upright(place[k:k + 1]))
            first = first + alive
        count = jnp.sum(counts, axis=1, keepdims=True)
        found = jnp.where(row[0:1] < count, jnp.sum(found, axis=0, keepdims=True), (1.0 + which) * clusters)
        out = jnp.where(rows == which, found, jnp.where(rows == 2 + which, count, out))
    return out.astype(jnp.int32)


def prepare_kernel(cl, vcl, rank, position_ref, vertices_hbm, corners_hbm, krylov_hbm, basis_hbm, far_hbm, near_hbm, offsets_hbm, weights_hbm,
                   payload_ref, area_ref, center_ref, at_ref, pairs_ref, basis_ref, krylov_ref, offsets_ref, weights_ref,
                   vertices_ref, corners_ref, raw_ref, far_ref, near_ref, mesh_ref, local_ref, sems):
    moves = copies((
        (vertices_hbm, vertices_ref), (corners_hbm, corners_ref), (krylov_hbm, krylov_ref), (basis_hbm, raw_ref),
        (far_hbm, far_ref), (near_hbm, near_ref), (offsets_hbm, offsets_ref), (weights_hbm.at[position_ref[0]], weights_ref),
    ), sems)
    rhs, panels = krylov_ref.shape
    clusters = panels // cl
    parts = cl // LANES
    moves[0].wait()
    for c in range(clusters):
        mesh_ref[3 * c:3 * c + 3, :] = vertices_ref[:, c * vcl:(c + 1) * vcl]
    moves[1].wait()
    for i in range(clusters * parts):
        local_ref[3 * i:3 * i + 3, :] = corners_ref[:, i * LANES:(i + 1) * LANES]
    first = position_ref[0] * (vcl * clusters) + vcl * lax.broadcasted_iota(jnp.int32, (clusters, LANES), 0)
    tables = [mesh_ref[pl.ds(k, clusters, stride=3), :] for k in range(3)]
    sums = [None] * 3
    for h in range(parts):
        local = [local_ref[pl.ds(3 * h + m, clusters, stride=3 * parts), :] - first for m in range(3)]
        corner = [[jnp.take_along_axis(tables[k], local[m], axis=1, mode="promise_in_bounds") for k in range(3)] for m in range(3)]
        for k in range(3):
            middle = (corner[0][k] + corner[1][k] + corner[2][k]) / 3.0
            payload_ref[:, panels + k * cl + h * LANES:panels + k * cl + (h + 1) * LANES] = middle
            sums[k] = middle if h == 0 else sums[k] + middle
        one = [corner[1][k] - corner[0][k] for k in range(3)]
        two = [corner[2][k] - corner[0][k] for k in range(3)]
        normal = [one[1] * two[2] - one[2] * two[1], one[2] * two[0] - one[0] * two[2], one[0] * two[1] - one[1] * two[0]]
        area_ref[:, h * LANES:(h + 1) * LANES] = 0.5 * jnp.sqrt(normal[0] * normal[0] + normal[1] * normal[1] + normal[2] * normal[2])
    span = clusters * rank
    table = panels + 3 * cl
    mine = lax.broadcasted_iota(jnp.int32, (clusters, span), 1) // rank == lax.broadcasted_iota(jnp.int32, (clusters, span), 0)
    half = span // 2
    payload_ref[:, table + span:] = jnp.zeros_like(payload_ref[:, table + span:])
    for k in range(3):
        center = jnp.sum(sums[k], axis=1, keepdims=True) / cl
        center_ref[:, k * LANES:(k + 1) * LANES] = jnp.broadcast_to(center, (clusters, LANES))
        row = jnp.sum(jnp.where(mine, center, 0.0), axis=0, keepdims=True)
        payload_ref[k:k + 1, table + span:] = row[:, 0:half]
        payload_ref[8 + k:9 + k, table + span:] = row[:, half:]
    moves[2].wait()
    moves[3].wait()
    for c in range(clusters):
        lanes = slice(c * cl, (c + 1) * cl)
        basis_ref[:, lanes] = stacked(raw_ref[:, lanes])
        charges = area_ref[c:c + 1, :] * krylov_ref[:, lanes]
        payload_ref[:, lanes] = charges
        payload_ref[:, table + c * rank:table + (c + 1) * rank] = moments_of(charges, basis_ref[:, lanes])
    moves[4].wait()
    far = far_ref[...]
    step = (lax.div(far, clusters) - position_ref[0]) * (1 - 2 * lax.rem(position_ref[0], 2))
    block = jnp.where(step < 0, step + REACH, step + REACH - 3)
    per = LANES // rank
    turn = lax.rem(lax.broadcasted_iota(jnp.int32, far.shape, 1) - far + per * clusters * 2 ** 16, per)
    at_ref[...] = (turn * 6 + block) * (span // LANES) + lax.div(lax.rem(far, clusters), per)
    moves[5].wait()
    pairs_ref[...] = pair_list(near_ref[...], position_ref[0], clusters)
    moves[6].wait()
    moves[7].wait()


def columns_of(payload_ref, panels, c, cl, columns_ref, at):
    rows = [payload_ref[c:c + 1, panels + k * cl:panels + (k + 1) * cl] for k in range(3)]
    upright = jnp.transpose(jnp.concatenate(rows * 2 + rows[:2], axis=0))
    for k in range(3):
        columns_ref[at, k] = jnp.broadcast_to(upright[:, k:k + 1], (cl, LANES))


def near_block(columns, source, cl, out_ref):
    for h in range(cl // LANES):
        lanes = slice(h * LANES, (h + 1) * LANES)
        gap = [columns[k] - source(k, h) for k in range(3)]
        square = gap[0] * gap[0] + gap[1] * gap[1] + gap[2] * gap[2]
        high, low = split(lax.rsqrt(square + SMOOTHING))
        out_ref[0:cl, lanes] = high
        out_ref[cl:2 * cl, lanes] = low


def near_product(pieces, block_ref, cl):
    return dot_nt(pieces, block_ref[0:cl, :]) + dot_nt(pieces, block_ref[cl:2 * cl, :])


def fill_charges(pieces_ref, blocks, clusters, cl):
    for b, ref in enumerate(blocks):
        for c in range(clusters):
            pieces_ref[b * clusters + c] = stacked(ref[:, c * cl:(c + 1) * cl])
    pieces_ref[len(blocks) * clusters] = jnp.zeros_like(pieces_ref[0])


def pair_at(pairs_ref, which, i):
    pair = pairs_ref[which, i]
    return lax.shift_right_logical(pair, 6), lax.bitwise_and(pair, 63)


def near_kernel(cl, which, number, pairs_ref, *refs):
    blocks = refs[:number]
    if which:
        columns_ref, start_ref, kept_ref, near_out_ref, pieces_ref, sources_ref, total_ref = refs[number:]
    else:
        _, own_ref, kept_ref, near_out_ref, columns_ref, tail_ref, pieces_ref, sources_ref, total_ref = refs[number:]
        tail_ref[...] = blocks[0][:, blocks[0].shape[1] - tail_ref.shape[1]:]
    panels = near_out_ref.shape[1]
    clusters = panels // cl
    group = kept_ref.shape[1]
    fill_charges(pieces_ref, blocks, clusters, cl)
    if which:
        total_ref[...] = jnp.zeros_like(total_ref)
    else:
        for c in range(clusters):
            columns_of(blocks[0], panels, c, cl, columns_ref, c)
            source = lambda k, h: blocks[0][c:c + 1, panels + k * cl + h * LANES:panels + k * cl + (h + 1) * LANES]
            near_block([columns_ref[c, k] for k in range(3)], source, cl, own_ref.at[c])
            total_ref[c] = near_product(pieces_ref[c], own_ref.at[c], cl)
    sources_ref[number * clusters] = jnp.zeros_like(sources_ref[0])
    for b, ref in enumerate(blocks):
        for c in range(clusters):
            for k in range(3):
                sources_ref[b * clusters + c, k:k + 1, :] = ref[c:c + 1, panels + k * cl:panels + (k + 1) * cl]

    def step(m, _):
        pairs = [pair_at(pairs_ref, which, group * m + w) for w in range(group)]
        parts = []
        for w, (c, j) in enumerate(pairs):
            source = lambda k, h: sources_ref[j, k:k + 1, h * LANES:(h + 1) * LANES]
            near_block([columns_ref[c, k] for k in range(3)], source, cl, kept_ref.at[m, w])
            parts.append(near_product(pieces_ref[j], kept_ref.at[m, w], cl))
        for (c, j), part in zip(pairs, parts):
            total_ref[c] += part
        return 0

    lax.fori_loop(0, (pairs_ref[2 + which, 0] + group - 1) // group, step, 0)
    for c in range(clusters):
        lanes = slice(c * cl, (c + 1) * cl)
        near = folded(total_ref[c])
        near_out_ref[:, lanes] = start_ref[:, lanes] + near if which else near


def near_again_kernel(cl, which, number, pairs_ref, *refs):
    blocks = refs[:number]
    if which:
        start_ref, kept_ref, near_out_ref, pieces_ref, total_ref = refs[number:]
    else:
        _, own_ref, kept_ref, near_out_ref, tail_ref, pieces_ref, total_ref = refs[number:]
        tail_ref[...] = blocks[0][:, blocks[0].shape[1] - tail_ref.shape[1]:]
    clusters = near_out_ref.shape[1] // cl
    group = kept_ref.shape[1]
    fill_charges(pieces_ref, blocks, clusters, cl)
    if which:
        total_ref[...] = jnp.zeros_like(total_ref)
    else:
        for c in range(clusters):
            total_ref[c] = near_product(pieces_ref[c], own_ref.at[c], cl)

    def step(m, _):
        pairs = [pair_at(pairs_ref, which, group * m + w) for w in range(group)]
        parts = [near_product(pieces_ref[j], kept_ref.at[m, w], cl) for w, (c, j) in enumerate(pairs)]
        for (c, j), part in zip(pairs, parts):
            total_ref[c] += part
        return 0

    lax.fori_loop(0, (pairs_ref[2 + which, 0] + group - 1) // group, step, 0)
    for c in range(clusters):
        lanes = slice(c * cl, (c + 1) * cl)
        near = folded(total_ref[c])
        near_out_ref[:, lanes] = start_ref[:, lanes] + near if which else near


def load_window(tables, clusters, rank, pieces_ref, middle_ref):
    per = LANES // rank
    span = clusters * rank
    count = pieces_ref.shape[0] // per
    groups = span // LANES
    for at in range(count):
        (ref, first), g = tables[at // groups], at % groups
        tile = ref[:, first + g * LANES:first + (g + 1) * LANES]
        for s in range(per):
            pieces_ref[s * count + at] = stacked(pltpu.roll(tile, s * rank, 1) if s else tile)
        if middle_ref is not None:
            half = groups // 2
            row, lane = 8 * (g // half), first + span + g % half * LANES
            tile = ref[row:row + 8, lane:lane + LANES]
            for s in range(per):
                middle_ref[s * count + at] = pltpu.roll(tile, s * rank, 1) if s else tile


def six_tables(width, second_ref, other_ref, third_ref):
    gap = third_ref.shape[1] - 3 * width
    return (
        (second_ref, width), (second_ref, 0), (other_ref, other_ref.shape[1] - width),
        (third_ref, 2 * width + gap), (third_ref, width + gap), (third_ref, 0),
    )


def pick(source_ref, at_ref, c, g, per, lane):
    row = None
    for u in range(per):
        take = source_ref[at_ref[c, g * per + u]]
        row = take if row is None else jnp.where(lane == u, take, row)
    return row


def far_fields(gathered_ref, coupling_ref, fields_ref):
    for c in range(gathered_ref.shape[0]):
        field = quartered(dot_nt(gathered_ref[c], coupling_ref[c]))
        fields_ref[c] = stacked(jnp.concatenate([field, field], axis=1))


def far_potential(fields_ref, c, basis):
    return folded(dot_nn(fields_ref[c], basis))


def image_kernel(cl, rank, at_ref, second_ref, other_ref, third_ref, center_ref, area_ref, near_ref, basis_ref, krylov_ref, offsets_ref,
                 image_ref, payload_ref, coupling_ref, pieces_ref, middle_ref, gathered_ref, fields_ref):
    rhs, panels = near_ref.shape
    clusters = panels // cl
    per = LANES // rank
    span = clusters * rank
    load_window(six_tables(span + span // 2, second_ref, other_ref, third_ref), clusters, rank, pieces_ref, middle_ref)
    lane = lax.broadcasted_iota(jnp.int32, (1, LANES), 1) // rank
    for c in range(clusters):
        mine = [offsets_ref[3, k:k + 1, :] - center_ref[c:c + 1, k * LANES:(k + 1) * LANES] for k in range(3)]
        for g in range(at_ref.shape[1] // per):
            lanes = slice(g * LANES, (g + 1) * LANES)
            gathered_ref[c, :, lanes] = pick(pieces_ref, at_ref, c, g, per, lane)
            center = pick(middle_ref, at_ref, c, g, per, lane)
            gap = [(center[k:k + 1] + mine[k]) - offsets_ref[k] for k in range(3)]
            high, low = split(lax.rsqrt(gap[0] * gap[0] + gap[1] * gap[1] + gap[2] * gap[2] + SMOOTHING))
            coupling_ref[c, 0:rank, lanes] = high
            coupling_ref[c, rank:2 * rank, lanes] = low
    far_fields(gathered_ref, coupling_ref, fields_ref)
    squared = correlation = jnp.zeros((rhs, cl), F32)
    for c in range(clusters):
        lanes = slice(c * cl, (c + 1) * cl)
        basis = basis_ref[:, lanes]
        area = area_ref[c:c + 1, :]
        image = COULOMB * area * (near_ref[:, lanes] + far_potential(fields_ref, c, basis))
        charges = area * image
        image_ref[:, lanes] = image
        payload_ref[:, lanes] = charges
        payload_ref[:, panels + c * rank:panels + (c + 1) * rank] = moments_of(charges, basis)
        krylov = krylov_ref[:, lanes]
        squared = squared + krylov * krylov
        correlation = correlation + krylov * image
    squared = jnp.sum(squared, axis=1, keepdims=True)
    correlation = jnp.sum(correlation, axis=1, keepdims=True)
    local = ratio(correlation, squared)
    residual = image_ref[...] - local * krylov_ref[...]
    payload_ref[:, panels + span:] = in_lanes(squared, correlation, jnp.sum(residual * residual, axis=1, keepdims=True), local)


def far_again_kernel(cl, rank, at_ref, second_ref, other_ref, third_ref, near_ref, area_ref, coupling_ref, basis_ref,
                     image_ref, pieces_ref, gathered_ref, fields_ref):
    clusters = near_ref.shape[1] // cl
    per = LANES // rank
    load_window(six_tables(clusters * rank + LANES, second_ref, other_ref, third_ref), clusters, rank, pieces_ref, None)
    lane = lax.broadcasted_iota(jnp.int32, (1, LANES), 1) // rank
    for c in range(clusters):
        for g in range(at_ref.shape[1] // per):
            gathered_ref[c, :, g * LANES:(g + 1) * LANES] = pick(pieces_ref, at_ref, c, g, per, lane)
    far_fields(gathered_ref, coupling_ref, fields_ref)
    for c in range(clusters):
        lanes = slice(c * cl, (c + 1) * cl)
        image_ref[:, lanes] = COULOMB * area_ref[c:c + 1, :] * (near_ref[:, lanes] + far_potential(fields_ref, c, basis_ref[:, lanes]))


def finish_kernel(total, one_ref, two_ref, image_ref, again_ref, krylov_ref, next_hbm, second_hbm, next_ref, second_ref, sems):
    squared, correlation, energy, local = merged([one_ref[...], two_ref[...]])
    projection = correlation / (squared + 1e-06)
    gap = projection - local
    scaling = 1.0 / jnp.sqrt((energy + gap * gap * squared) / total + 1e-06)
    moves = []
    half = next_ref.shape[1] // 2
    for h in range(2):
        lanes = slice(h * half, (h + 1) * half)
        image = image_ref[:, lanes]
        next_ref[:, lanes] = (image - projection * krylov_ref[:, lanes]) * scaling
        second_ref[:, lanes] = (again_ref[:, lanes] - projection * image) * scaling
        for held, hbm in ((next_ref, next_hbm), (second_ref, second_hbm)):
            moves.append(pltpu.make_async_copy(held.at[:, lanes], hbm.at[:, lanes], sems.at[len(moves)]))
            moves[-1].start()
    for move in moves:
        move.wait()


def ratio(correlation, squared):
    return jnp.where(squared > 0, correlation / jnp.where(squared > 0, squared, 1.0), 0.0)


def in_lanes(*columns):
    lane = lax.broadcasted_iota(jnp.int32, (columns[0].shape[0], LANES), 1)
    out = columns[-1]
    for i, column in enumerate(columns[:-1]):
        out = jnp.where(lane == i, column, out)
    return out


def merged(groups, weights=None):
    weights = weights or [1.0] * len(groups)
    squared = sum(weight * group[:, 0:1] for group, weight in zip(groups, weights))
    correlation = sum(weight * group[:, 1:2] for group, weight in zip(groups, weights))
    local = ratio(correlation, squared)
    energy = 0.0
    for group, weight in zip(groups, weights):
        gap = local - group[:, 3:4]
        energy = energy + weight * (group[:, 2:3] + gap * gap * group[:, 0:1])
    return squared, correlation, energy, local


def known_sums(tail_ref, partner_ref, other_ref, second_ref, third_ref):
    width = tail_ref.shape[1]
    ends = [(tail_ref, width), (partner_ref, partner_ref.shape[1]), (other_ref, other_ref.shape[1] - width), (other_ref, other_ref.shape[1])]
    ends += [(second_ref, width), (second_ref, 2 * width)]
    ends += [(third_ref, width), (third_ref, width + LANES), (third_ref, 2 * width + LANES), (third_ref, 3 * width + LANES)]
    return [ref[:, end - LANES:end] for ref, end in ends]


def known_sums_kernel(weights_ref, *refs):
    groups = known_sums(*refs[:5])
    for side, out_ref in enumerate(refs[5:]):
        weights = [weights_ref[0:1, 16 * side + i:16 * side + i + 1] for i in range(len(groups))]
        out_ref[...] = in_lanes(*merged(groups, weights))


def completing(devices, *moves):
    partner, other, second, third = ({target: source for source, target in move} for move in moves)
    slots = []
    for i in range(devices):
        two, three = second[i], third[i]
        slots.append([i, partner[i], other[i], partner[other[i]], two, partner[two], three, partner[three], other[three], partner[other[three]]])
    known = [set(slot) for slot in slots]
    everyone = set(range(devices))
    target_of = {}

    def matched(target, seen):
        for source in range(devices):
            if source not in seen and known[target] | known[source] == everyone:
                seen.add(source)
                if source not in target_of or matched(target_of[source], seen):
                    target_of[source] = target
                    return True
        return False

    if not all(matched(i, set()) for i in range(devices)):
        return None
    weights = np.zeros((devices, 8, LANES), np.float32)
    for i in range(devices):
        for at, device in enumerate(slots[i]):
            if device not in slots[i][:at]:
                weights[i, :, at] = 1.0
                weights[i, :, 16 + at] = device not in known[target_of[i]]
    return sorted(target_of.items()), weights


def merge_kernel(one_ref, two_ref, out_ref):
    out_ref[...] = in_lanes(*merged([ref[:, ref.shape[1] - LANES:] for ref in (one_ref, two_ref)]))


def call(kernel, outs, scratch, memory, *args, limit=6, us=1.0):
    spaces = {"s": pltpu.SMEM, "v": pltpu.VMEM, "p": pltpu.VMEM, "h": pltpu.HBM}
    ins, out_spaces = memory.split(">")
    pinned = {"h": pltpu.HBM, "p": pltpu.VMEM}
    return pl.pallas_call(
        kernel,
        out_shape=[pltpu.VMEM(*out) if m == "p" else jax.ShapeDtypeStruct(*out) for m, out in zip(out_spaces, outs)],
        in_specs=[pl.BlockSpec(memory_space=spaces[m]) for m in ins],
        out_specs=[pl.BlockSpec(memory_space=spaces[m]) for m in out_spaces],
        scratch_shapes=scratch,
        compiler_params=pltpu.CompilerParams(vmem_limit_bytes=limit * 2 ** 20),
        cost_estimate=pl.CostEstimate(flops=int(us * 5e8), bytes_accessed=int(us * 3.6e6), transcendentals=0),
    )(*(pltpu.with_memory_space_constraint(a, pinned[m]) if m in pinned else a for m, a in zip(ins, args)))


def body(vertices, panel_vertices, near_pairs, far_pairs, basis, krylov):
    clusters, slots = near_pairs.shape
    partners = far_pairs.shape[1]
    rhs, panels = krylov.shape
    rank = basis.shape[0]
    cl = panels // clusters
    vcl = vertices.shape[1] // clusters
    span = clusters * rank
    per = LANES // rank
    devices = lax.axis_size("clus")
    position = lax.axis_index("clus").reshape(1).astype(jnp.int32)
    offsets = proxy_offsets(rank)
    flat = np.concatenate([np.tile(offsets, (1, per)), np.zeros((rank - 3, LANES), np.float32)])
    offsets = jnp.asarray(np.concatenate([np.broadcast_to(offsets[:, :, None], (3, rank, LANES)), flat[None]]))
    width = span + span // 2
    pairing = [(i, i + 1 - 2 * (i % 2)) for i in range(devices)]
    bridging = [(i, i - 1 + 2 * (i % 2)) for i in range(1, devices - 1)] + [(0, 0), (devices - 1, devices - 1)]
    second = [(i, (i + 3 * (2 * (i % 2) - 1)) % devices) for i in range(devices)]
    third = [(i, i + 4 * (2 * (i % 2) - 1)) for i in range(1, devices - 1)] + [(0, 3), (devices - 1, devices - 4)]
    third = [(i, j % devices) for i, j in third]

    completion = completing(devices, pairing, bridging, second, third)
    weights = completion[1] if completion else np.zeros((devices, 8, LANES), np.float32)

    def move(value, pairs):
        return lax.ppermute(value, "clus", pairs)

    def exchange(value, first, width):
        mine = value[:, first:first + width]
        partner = move(value, pairing)
        pair = jnp.concatenate([mine, partner[:, first:first + width]], axis=1)
        other = move(jnp.concatenate([value[:, :first], pair], axis=1), bridging)
        return partner, other, move(pair, second)

    def last_exchange(tail, between, other):
        pair = other[:, other.shape[1] - 2 * tail.shape[1]:]
        return move(jnp.concatenate([tail, *between, pair], axis=1), third)

    whole = ((rhs, panels), F32)
    payload, area, centers, at, pairs, basis, krylov, offsets, weights = call(
        functools.partial(prepare_kernel, cl, vcl, rank),
        [
            ((rhs, panels + 3 * cl + width), F32), ((clusters, cl), F32), ((clusters, 3 * LANES), F32),
            (far_pairs.shape, jnp.int32), ((8, LANES), jnp.int32), ((2 * rank, panels), BF16), whole, (offsets.shape, F32), ((8, LANES), F32),
        ],
        [
            pltpu.VMEM(vertices.shape, F32),
            pltpu.VMEM(panel_vertices.shape, jnp.int32),
            pltpu.VMEM(basis.shape, F32),
            pltpu.VMEM(far_pairs.shape, jnp.int32),
            pltpu.VMEM((slots, clusters), jnp.int32),
            pltpu.VMEM((3 * clusters, vcl), F32),
            pltpu.VMEM((3 * panels // LANES, LANES), jnp.int32),
            pltpu.SemaphoreType.DMA((8,)),
        ],
        "shhhhhhhh>vvvvvpppp",
        position, vertices, panel_vertices, krylov, basis, far_pairs, near_pairs.T, offsets, jnp.asarray(weights),
        us=1.5,
    )
    partner, other, two = exchange(payload, panels + 3 * cl, width)
    total = pltpu.VMEM((clusters, 2 * rhs, cl), F32)

    group = 4
    own = ((clusters, 2 * cl, cl), BF16)
    kept = ((clusters * (slots - 1) // group, group, 2 * cl, cl), BF16)

    def pieces(number):
        return pltpu.VMEM((number * clusters + 1, 2 * rhs, cl), BF16)

    def sources(number):
        return pltpu.VMEM((number * clusters + 1, 8, cl), F32)

    own_blocks, blocks, near, columns, tail = call(
        functools.partial(near_kernel, cl, 0, 1),
        [own, kept, whole, ((clusters, 3, cl, LANES), F32), ((rhs, width), F32)],
        [pieces(1), sources(1), total],
        "svv>ppvpv",
        pairs, payload, partner,
        us=6.0,
    )
    three = last_exchange(tail, [], other)
    blocks_other, near = call(
        functools.partial(near_kernel, cl, 1, 2),
        [kept, whole],
        [pieces(2), sources(2), total],
        "svvpv>pv",
        pairs, partner, other, columns, near,
        us=4.0,
    )
    tiles = 6 * per * span // LANES
    window = pltpu.VMEM((tiles, 2 * rhs, LANES), BF16)
    gathered = pltpu.VMEM((clusters, 2 * rhs, partners * rank), BF16)
    fields = pltpu.VMEM((clusters, 2 * rhs, 2 * rank), BF16)
    image, payload, coupling = call(
        functools.partial(image_kernel, cl, rank),
        [whole, ((rhs, panels + span + LANES), F32), ((clusters, 2 * rank, partners * rank), BF16)],
        [window, pltpu.VMEM((tiles, 8, LANES), F32), gathered, fields],
        "svvvvvvppp>vvp",
        at, two, other, three, centers, area, near, basis, krylov, offsets,
        us=4.5,
    )
    partner, other, two = exchange(payload, panels, span + LANES)
    near, tail = call(
        functools.partial(near_again_kernel, cl, 0, 1),
        [whole, ((rhs, span + LANES), F32)],
        [pieces(1), total],
        "svvpp>vv",
        pairs, payload, partner, own_blocks, blocks,
        us=2.5,
    )
    three = last_exchange(tail, [partner[:, panels + span:]], other)
    (near,) = call(
        functools.partial(near_again_kernel, cl, 1, 2),
        [whole],
        [pieces(2), total],
        "svvvp>v",
        pairs, partner, other, near, blocks_other,
        us=2.0,
    )
    sums_shape = ((rhs, LANES), F32)
    if completion:
        one, many = call(known_sums_kernel, [sums_shape] * 2, [], "pvvvvv>vv", weights, tail, partner, other, two, three, us=0.3)
        many = move(many, completion[0])
    else:
        one, many, size = tail, partner, 2
        while size < devices:
            (one,) = call(merge_kernel, [sums_shape], [], "vv>v", one, many, us=0.3)
            many = move(one, [(i, (i + size) % devices) for i in range(devices)])
            size = 2 * size
    (again,) = call(
        functools.partial(far_again_kernel, cl, rank),
        [whole],
        [window, gathered, fields],
        "svvvvvpp>v",
        at, two, other, three, near, area, coupling, basis,
        us=2.0,
    )
    here = pltpu.VMEM((rhs, panels), F32)
    return tuple(call(
        functools.partial(finish_kernel, panels * devices),
        [whole, whole],
        [here, here, pltpu.SemaphoreType.DMA((4,))],
        "vvvvp>hh",
        one, many, image, again, krylov,
    ))


def solution(mesh):
    whole = P(None, ("jobs", "clus"))
    rows = P(("jobs", "clus"), None)
    return jax.shard_map(
        body,
        mesh=mesh,
        in_specs=(whole, whole, rows, rows, whole, whole),
        out_specs=(whole, whole),
        check_vma=False,
    )
```

```python
import functools

import jax
import jax.numpy as jnp
import numpy as np
from jax import lax
from jax.experimental import pallas as pl
from jax.experimental.pallas import tpu as pltpu
from jax.sharding import PartitionSpec as P

REACH = 4
SMOOTHING = 0.04
COULOMB = 2.0
PROXY_RADIUS = 0.6
LANES = 128
F32 = jnp.float32
BF16 = jnp.bfloat16


def proxy_offsets(points):
    counter = np.arange(points, dtype=np.float32)
    height = 1.0 - (2.0 * counter + 1.0) / points
    radial = np.sqrt(1.0 - height * height)
    azimuth = counter * 2.399963
    return PROXY_RADIUS * np.stack([radial * np.cos(azimuth), radial * np.sin(azimuth), height]).astype(np.float32)


def split(value):
    high = value.astype(BF16)
    return high, (value - high.astype(F32)).astype(BF16)


def stacked(value):
    return jnp.concatenate(split(value), axis=0)


def folded(value):
    half = value.shape[0] // 2
    return value[:half] + value[half:]


def dot_nt(left, right):
    return lax.dot_general(left, right, (((1,), (1,)), ((), ())), preferred_element_type=F32)


def dot_nn(left, right):
    return lax.dot_general(left, right, (((1,), (0,)), ((), ())), preferred_element_type=F32)


def quartered(value):
    half = value.shape[1] // 2
    value = folded(value)
    return value[:, 0:half] + value[:, half:]


def moments_of(weighted, basis_pieces):
    return quartered(dot_nt(stacked(weighted), basis_pieces))


def copies(pairs, sems):
    moves = [pltpu.make_async_copy(source, target, sems.at[i]) for i, (source, target) in enumerate(pairs)]
    for move in moves:
        move.start()
    return moves


def pair_list(near, position, clusters):
    block = lax.div(near, clusters) - position
    partner = block * (1 - 2 * lax.rem(position, 2)) > 0
    place = (lax.rem(near, clusters) + jnp.where((block != 0) & ~partner, clusters, 0)).astype(F32)
    across = lax.broadcasted_iota(jnp.int32, (clusters, clusters), 1)
    down = lax.broadcasted_iota(jnp.int32, (clusters, clusters), 0)
    upright = lambda value: jnp.sum(jnp.where(across == down, value, 0.0), axis=1, keepdims=True)
    row = lax.broadcasted_iota(jnp.int32, (clusters, LANES), 1).astype(F32)
    target = lax.broadcasted_iota(jnp.int32, (clusters, 1), 0).astype(F32)
    rows = lax.broadcasted_iota(jnp.int32, (8, LANES), 0)
    out = jnp.zeros((8, LANES), F32)
    for which in range(2):
        here = block != 0 if which else block == 0
        live = jnp.where(here & (near >= 0), 1.0, 0.0)
        counts = sum(live[k:k + 1] for k in range(1, near.shape[0]))
        first = jnp.sum(jnp.where(across < down, counts, 0.0), axis=1, keepdims=True)
        found = jnp.zeros((clusters, LANES), F32)
        for k in range(1, near.shape[0]):
            alive = upright(live[k:k + 1])
            hit = jnp.where(row == first, alive, 0.0)
            found = found + hit * (target * 64 + upright(place[k:k + 1]))
            first = first + alive
        count = jnp.sum(counts, axis=1, keepdims=True)
        found = jnp.where(row[0:1] < count, jnp.sum(found, axis=0, keepdims=True), (1.0 + which) * clusters)
        out = jnp.where(rows == which, found, jnp.where(rows == 2 + which, count, out))
    return out.astype(jnp.int32)


def prepare_kernel(cl, vcl, rank, position_ref, vertices_hbm, corners_hbm, krylov_hbm, basis_hbm, far_hbm, near_hbm, offsets_hbm,
                   payload_ref, heavy_ref, area_ref, center_ref, at_ref, pairs_ref, basis_ref, krylov_ref, offsets_ref,
                   vertices_ref, corners_ref, raw_ref, far_ref, near_ref, mesh_ref, local_ref, sems):
    moves = copies((
        (vertices_hbm, vertices_ref), (corners_hbm, corners_ref), (krylov_hbm, krylov_ref), (basis_hbm, raw_ref),
        (far_hbm, far_ref), (near_hbm, near_ref), (offsets_hbm, offsets_ref),
    ), sems)
    rhs, panels = krylov_ref.shape
    clusters = panels // cl
    parts = cl // LANES
    moves[0].wait()
    for c in range(clusters):
        mesh_ref[3 * c:3 * c + 3, :] = vertices_ref[:, c * vcl:(c + 1) * vcl]
    moves[1].wait()
    for i in range(clusters * parts):
        local_ref[3 * i:3 * i + 3, :] = corners_ref[:, i * LANES:(i + 1) * LANES]
    first = position_ref[0] * (vcl * clusters) + vcl * lax.broadcasted_iota(jnp.int32, (clusters, LANES), 0)
    tables = [mesh_ref[pl.ds(k, clusters, stride=3), :] for k in range(3)]
    sums = [None] * 3
    for h in range(parts):
        local = [local_ref[pl.ds(3 * h + m, clusters, stride=3 * parts), :] - first for m in range(3)]
        corner = [[jnp.take_along_axis(tables[k], local[m], axis=1, mode="promise_in_bounds") for k in range(3)] for m in range(3)]
        for k in range(3):
            middle = (corner[0][k] + corner[1][k] + corner[2][k]) / 3.0
            lanes = slice(panels + k * cl + h * LANES, panels + k * cl + (h + 1) * LANES)
            payload_ref[:, lanes] = middle
            heavy_ref[:, lanes] = middle
            sums[k] = middle if h == 0 else sums[k] + middle
        one = [corner[1][k] - corner[0][k] for k in range(3)]
        two = [corner[2][k] - corner[0][k] for k in range(3)]
        normal = [one[1] * two[2] - one[2] * two[1], one[2] * two[0] - one[0] * two[2], one[0] * two[1] - one[1] * two[0]]
        area_ref[:, h * LANES:(h + 1) * LANES] = 0.5 * jnp.sqrt(normal[0] * normal[0] + normal[1] * normal[1] + normal[2] * normal[2])
    span = clusters * rank
    table = panels + 3 * cl
    mine = lax.broadcasted_iota(jnp.int32, (clusters, span), 1) // rank == lax.broadcasted_iota(jnp.int32, (clusters, span), 0)
    half = span // 2
    payload_ref[:, table + span:] = jnp.zeros_like(payload_ref[:, table + span:])
    for k in range(3):
        center = jnp.sum(sums[k], axis=1, keepdims=True) / cl
        center_ref[:, k * LANES:(k + 1) * LANES] = jnp.broadcast_to(center, (clusters, LANES))
        row = jnp.sum(jnp.where(mine, center, 0.0), axis=0, keepdims=True)
        payload_ref[k:k + 1, table + span:] = row[:, 0:half]
        payload_ref[8 + k:9 + k, table + span:] = row[:, half:]
    moves[2].wait()
    moves[3].wait()
    for c in range(clusters):
        lanes = slice(c * cl, (c + 1) * cl)
        basis_ref[:, lanes] = stacked(raw_ref[:, lanes])
        charges = area_ref[c:c + 1, :] * krylov_ref[:, lanes]
        payload_ref[:, lanes] = charges
        heavy_ref[:, lanes] = charges
        payload_ref[:, table + c * rank:table + (c + 1) * rank] = moments_of(charges, basis_ref[:, lanes])
    moves[4].wait()
    far = far_ref[...]
    step = (lax.div(far, clusters) - position_ref[0]) * (1 - 2 * lax.rem(position_ref[0], 2))
    block = jnp.where(step < 0, step + REACH, step + REACH - 3)
    per = LANES // rank
    turn = lax.rem(lax.broadcasted_iota(jnp.int32, far.shape, 1) - far + per * clusters * 2 ** 16, per)
    at_ref[...] = (turn * 6 + block) * (span // LANES) + lax.div(lax.rem(far, clusters), per)
    moves[5].wait()
    pairs_ref[...] = pair_list(near_ref[...], position_ref[0], clusters)
    moves[6].wait()


def columns_of(payload_ref, panels, c, cl, columns_ref, at):
    rows = [payload_ref[c:c + 1, panels + k * cl:panels + (k + 1) * cl] for k in range(3)]
    upright = jnp.transpose(jnp.concatenate(rows * 2 + rows[:2], axis=0))
    for k in range(3):
        columns_ref[at, k] = jnp.broadcast_to(upright[:, k:k + 1], (cl, LANES))


def near_block(columns, source, cl, out_ref):
    for h in range(cl // LANES):
        lanes = slice(h * LANES, (h + 1) * LANES)
        gap = [columns[k] - source(k, h) for k in range(3)]
        square = gap[0] * gap[0] + gap[1] * gap[1] + gap[2] * gap[2]
        high, low = split(lax.rsqrt(square + SMOOTHING))
        out_ref[0:cl, lanes] = high
        out_ref[cl:2 * cl, lanes] = low


def near_product(pieces, block_ref, cl):
    return dot_nt(pieces, block_ref[0:cl, :]) + dot_nt(pieces, block_ref[cl:2 * cl, :])


def fill_charges(pieces_ref, blocks, clusters, cl):
    for b, ref in enumerate(blocks):
        for c in range(clusters):
            pieces_ref[b * clusters + c] = stacked(ref[:, c * cl:(c + 1) * cl])
    pieces_ref[len(blocks) * clusters] = jnp.zeros_like(pieces_ref[0])


def pair_at(pairs_ref, which, i):
    pair = pairs_ref[which, i]
    return lax.shift_right_logical(pair, 6), lax.bitwise_and(pair, 63)


def near_kernel(cl, which, number, pairs_ref, *refs):
    blocks = refs[:number]
    if which:
        columns_ref, start_ref, kept_ref, near_out_ref, pieces_ref, sources_ref, total_ref = refs[number:]
    else:
        _, own_ref, kept_ref, near_out_ref, columns_ref, tail_ref, pieces_ref, sources_ref, total_ref = refs[number:]
        tail_ref[...] = blocks[0][:, blocks[0].shape[1] - tail_ref.shape[1]:]
    panels = near_out_ref.shape[1]
    clusters = panels // cl
    group = kept_ref.shape[1]
    fill_charges(pieces_ref, blocks, clusters, cl)
    if which:
        total_ref[...] = jnp.zeros_like(total_ref)
    else:
        for c in range(clusters):
            columns_of(blocks[0], panels, c, cl, columns_ref, c)
            source = lambda k, h: blocks[0][c:c + 1, panels + k * cl + h * LANES:panels + k * cl + (h + 1) * LANES]
            near_block([columns_ref[c, k] for k in range(3)], source, cl, own_ref.at[c])
            total_ref[c] = near_product(pieces_ref[c], own_ref.at[c], cl)
    sources_ref[number * clusters] = jnp.zeros_like(sources_ref[0])
    for b, ref in enumerate(blocks):
        for c in range(clusters):
            for k in range(3):
                sources_ref[b * clusters + c, k:k + 1, :] = ref[c:c + 1, panels + k * cl:panels + (k + 1) * cl]

    def step(m, _):
        pairs = [pair_at(pairs_ref, which, group * m + w) for w in range(group)]
        parts = []
        for w, (c, j) in enumerate(pairs):
            source = lambda k, h: sources_ref[j, k:k + 1, h * LANES:(h + 1) * LANES]
            near_block([columns_ref[c, k] for k in range(3)], source, cl, kept_ref.at[m, w])
            parts.append(near_product(pieces_ref[j], kept_ref.at[m, w], cl))
        for (c, j), part in zip(pairs, parts):
            total_ref[c] += part
        return 0

    lax.fori_loop(0, (pairs_ref[2 + which, 0] + group - 1) // group, step, 0)
    for c in range(clusters):
        lanes = slice(c * cl, (c + 1) * cl)
        near = folded(total_ref[c])
        near_out_ref[:, lanes] = start_ref[:, lanes] + near if which else near


def near_again_kernel(cl, which, number, pairs_ref, *refs):
    blocks = refs[:number]
    if which:
        start_ref, kept_ref, near_out_ref, pieces_ref, total_ref = refs[number:]
    else:
        _, own_ref, kept_ref, near_out_ref, tail_ref, pieces_ref, total_ref = refs[number:]
        tail_ref[...] = blocks[0][:, blocks[0].shape[1] - tail_ref.shape[1]:]
    clusters = near_out_ref.shape[1] // cl
    group = kept_ref.shape[1]
    fill_charges(pieces_ref, blocks, clusters, cl)
    if which:
        total_ref[...] = jnp.zeros_like(total_ref)
    else:
        for c in range(clusters):
            total_ref[c] = near_product(pieces_ref[c], own_ref.at[c], cl)

    def step(m, _):
        pairs = [pair_at(pairs_ref, which, group * m + w) for w in range(group)]
        parts = [near_product(pieces_ref[j], kept_ref.at[m, w], cl) for w, (c, j) in enumerate(pairs)]
        for (c, j), part in zip(pairs, parts):
            total_ref[c] += part
        return 0

    lax.fori_loop(0, (pairs_ref[2 + which, 0] + group - 1) // group, step, 0)
    for c in range(clusters):
        lanes = slice(c * cl, (c + 1) * cl)
        near = folded(total_ref[c])
        near_out_ref[:, lanes] = start_ref[:, lanes] + near if which else near


def load_window(tables, clusters, rank, pieces_ref, middle_ref):
    per = LANES // rank
    span = clusters * rank
    count = pieces_ref.shape[0] // per
    groups = span // LANES
    for at in range(count):
        (ref, first), g = tables[at // groups], at % groups
        tile = ref[:, first + g * LANES:first + (g + 1) * LANES]
        for s in range(per):
            pieces_ref[s * count + at] = stacked(pltpu.roll(tile, s * rank, 1) if s else tile)
        if middle_ref is not None:
            half = groups // 2
            row, lane = 8 * (g // half), first + span + g % half * LANES
            tile = ref[row:row + 8, lane:lane + LANES]
            for s in range(per):
                middle_ref[s * count + at] = pltpu.roll(tile, s * rank, 1) if s else tile


def six_tables(near_ref, far_ref, swapped_ref):
    width = near_ref.shape[1] // 2
    return (far_ref, 0), (far_ref, width), (near_ref, 0), (swapped_ref, width), (swapped_ref, 0), (swapped_ref, 3 * width)


def pick(source_ref, at_ref, c, g, per, lane):
    row = None
    for u in range(per):
        take = source_ref[at_ref[c, g * per + u]]
        row = take if row is None else jnp.where(lane == u, take, row)
    return row


def far_fields(gathered_ref, coupling_ref, fields_ref):
    for c in range(gathered_ref.shape[0]):
        field = quartered(dot_nt(gathered_ref[c], coupling_ref[c]))
        fields_ref[c] = stacked(jnp.concatenate([field, field], axis=1))


def far_potential(fields_ref, c, basis):
    return folded(dot_nn(fields_ref[c], basis))


def image_kernel(cl, rank, at_ref, near_pair_ref, far_pair_ref, swapped_ref, center_ref, area_ref, near_ref, basis_ref, krylov_ref, offsets_ref,
                 image_ref, payload_ref, heavy_ref, coupling_ref, pieces_ref, middle_ref, gathered_ref, fields_ref):
    rhs, panels = near_ref.shape
    clusters = panels // cl
    per = LANES // rank
    span = clusters * rank
    load_window(six_tables(near_pair_ref, far_pair_ref, swapped_ref), clusters, rank, pieces_ref, middle_ref)
    lane = lax.broadcasted_iota(jnp.int32, (1, LANES), 1) // rank
    for c in range(clusters):
        mine = [offsets_ref[3, k:k + 1, :] - center_ref[c:c + 1, k * LANES:(k + 1) * LANES] for k in range(3)]
        for g in range(at_ref.shape[1] // per):
            lanes = slice(g * LANES, (g + 1) * LANES)
            gathered_ref[c, :, lanes] = pick(pieces_ref, at_ref, c, g, per, lane)
            center = pick(middle_ref, at_ref, c, g, per, lane)
            gap = [(center[k:k + 1] + mine[k]) - offsets_ref[k] for k in range(3)]
            high, low = split(lax.rsqrt(gap[0] * gap[0] + gap[1] * gap[1] + gap[2] * gap[2] + SMOOTHING))
            coupling_ref[c, 0:rank, lanes] = high
            coupling_ref[c, rank:2 * rank, lanes] = low
    far_fields(gathered_ref, coupling_ref, fields_ref)
    squared = correlation = jnp.zeros((rhs, cl), F32)
    for c in range(clusters):
        lanes = slice(c * cl, (c + 1) * cl)
        basis = basis_ref[:, lanes]
        area = area_ref[c:c + 1, :]
        image = COULOMB * area * (near_ref[:, lanes] + far_potential(fields_ref, c, basis))
        charges = area * image
        image_ref[:, lanes] = image
        payload_ref[:, lanes] = charges
        heavy_ref[:, lanes] = charges
        payload_ref[:, panels + c * rank:panels + (c + 1) * rank] = moments_of(charges, basis)
        krylov = krylov_ref[:, lanes]
        squared = squared + krylov * krylov
        correlation = correlation + krylov * image
    squared = jnp.sum(squared, axis=1, keepdims=True)
    correlation = jnp.sum(correlation, axis=1, keepdims=True)
    local = ratio(correlation, squared)
    residual = image_ref[...] - local * krylov_ref[...]
    payload_ref[:, panels + span:] = in_lanes(squared, correlation, jnp.sum(residual * residual, axis=1, keepdims=True), local)


def far_again_kernel(cl, rank, at_ref, near_pair_ref, far_pair_ref, swapped_ref, near_ref, area_ref, coupling_ref, basis_ref,
                     image_ref, pieces_ref, gathered_ref, fields_ref):
    clusters = near_ref.shape[1] // cl
    per = LANES // rank
    load_window(six_tables(near_pair_ref, far_pair_ref, swapped_ref), clusters, rank, pieces_ref, None)
    lane = lax.broadcasted_iota(jnp.int32, (1, LANES), 1) // rank
    for c in range(clusters):
        for g in range(at_ref.shape[1] // per):
            gathered_ref[c, :, g * LANES:(g + 1) * LANES] = pick(pieces_ref, at_ref, c, g, per, lane)
    far_fields(gathered_ref, coupling_ref, fields_ref)
    for c in range(clusters):
        lanes = slice(c * cl, (c + 1) * cl)
        image_ref[:, lanes] = COULOMB * area_ref[c:c + 1, :] * (near_ref[:, lanes] + far_potential(fields_ref, c, basis_ref[:, lanes]))


def finish_kernel(total, one_ref, two_ref, image_ref, again_ref, krylov_ref, next_hbm, second_hbm, next_ref, second_ref, sems):
    squared, correlation, energy, local = merged([one_ref[...], two_ref[...]])
    projection = correlation / (squared + 1e-06)
    gap = projection - local
    scaling = 1.0 / jnp.sqrt((energy + gap * gap * squared) / total + 1e-06)
    moves = []
    half = next_ref.shape[1] // 2
    for h in range(2):
        lanes = slice(h * half, (h + 1) * half)
        image = image_ref[:, lanes]
        next_ref[:, lanes] = (image - projection * krylov_ref[:, lanes]) * scaling
        second_ref[:, lanes] = (again_ref[:, lanes] - projection * image) * scaling
        for held, hbm in ((next_ref, next_hbm), (second_ref, second_hbm)):
            moves.append(pltpu.make_async_copy(held.at[:, lanes], hbm.at[:, lanes], sems.at[len(moves)]))
            moves[-1].start()
    for move in moves:
        move.wait()


def ratio(correlation, squared):
    return jnp.where(squared > 0, correlation / jnp.where(squared > 0, squared, 1.0), 0.0)


def in_lanes(*columns):
    lane = lax.broadcasted_iota(jnp.int32, (columns[0].shape[0], LANES), 1)
    out = columns[-1]
    for i, column in enumerate(columns[:-1]):
        out = jnp.where(lane == i, column, out)
    return out


def merged(groups):
    squared = sum(group[:, 0:1] for group in groups)
    correlation = sum(group[:, 1:2] for group in groups)
    local = ratio(correlation, squared)
    energy = 0.0
    for group in groups:
        gap = local - group[:, 3:4]
        energy = energy + (group[:, 2:3] + gap * gap * group[:, 0:1])
    return squared, correlation, energy, local


def window_sums_kernel(payload_ref, partner_ref, near_pair_ref, far_pair_ref, swapped_ref, out_ref):
    width = near_pair_ref.shape[1] // 2
    ends = [(payload_ref, payload_ref.shape[1]), (partner_ref, partner_ref.shape[1])]
    ends += [(ref, end) for ref in (near_pair_ref, far_pair_ref, swapped_ref) for end in (width, 2 * width)]
    out_ref[...] = in_lanes(*merged([ref[:, end - LANES:end] for ref, end in ends]))


def merge_kernel(one_ref, two_ref, out_ref):
    out_ref[...] = in_lanes(*merged([one_ref[...], two_ref[...]]))


def call(kernel, outs, scratch, memory, *args, limit=6, us=1.0):
    spaces = {"s": pltpu.SMEM, "v": pltpu.VMEM, "p": pltpu.VMEM, "h": pltpu.HBM}
    ins, out_spaces = memory.split(">")
    pinned = {"h": pltpu.HBM, "p": pltpu.VMEM}
    return pl.pallas_call(
        kernel,
        out_shape=[pltpu.VMEM(*out) if m == "p" else jax.ShapeDtypeStruct(*out) for m, out in zip(out_spaces, outs)],
        in_specs=[pl.BlockSpec(memory_space=spaces[m]) for m in ins],
        out_specs=[pl.BlockSpec(memory_space=spaces[m]) for m in out_spaces],
        scratch_shapes=scratch,
        compiler_params=pltpu.CompilerParams(vmem_limit_bytes=limit * 2 ** 20),
        cost_estimate=pl.CostEstimate(flops=int(us * 5e8), bytes_accessed=int(us * 3.6e6), transcendentals=0),
    )(*(pltpu.with_memory_space_constraint(a, pinned[m]) if m in pinned else a for m, a in zip(ins, args)))


def body(vertices, panel_vertices, near_pairs, far_pairs, basis, krylov):
    clusters, slots = near_pairs.shape
    partners = far_pairs.shape[1]
    rhs, panels = krylov.shape
    rank = basis.shape[0]
    cl = panels // clusters
    vcl = vertices.shape[1] // clusters
    span = clusters * rank
    per = LANES // rank
    devices = lax.axis_size("clus")
    position = lax.axis_index("clus").reshape(1).astype(jnp.int32)
    offsets = proxy_offsets(rank)
    flat = np.concatenate([np.tile(offsets, (1, per)), np.zeros((rank - 3, LANES), np.float32)])
    offsets = jnp.asarray(np.concatenate([np.broadcast_to(offsets[:, :, None], (3, rank, LANES)), flat[None]]))
    width = span + span // 2
    pairing = [(i, i + 1 - 2 * (i % 2)) for i in range(devices)]
    bridging = [(i, i - 1 + 2 * (i % 2)) for i in range(1, devices - 1)] + [(0, 0), (devices - 1, devices - 1)]

    def move(value, pairs):
        return lax.ppermute(value, "clus", pairs)

    def outward(value, steps):
        return move(value, [(i, (i + steps * (1 - 2 * (i % 2))) % devices) for i in range(devices)])

    def exchange(payload, heavy):
        other = move(heavy, bridging)
        partner = move(payload, pairing)
        pair = jnp.concatenate([value[:, heavy.shape[1]:] for value in (payload, partner)], axis=1)
        return partner, other, outward(pair, 2), outward(pair, 4)

    def swapped(near_pair, far_pair, tail):
        return move(jnp.concatenate([near_pair, far_pair, tail], axis=1), pairing)

    whole = ((rhs, panels), F32)
    payload, heavy, area, centers, at, pairs, basis, krylov, offsets = call(
        functools.partial(prepare_kernel, cl, vcl, rank),
        [
            ((rhs, panels + 3 * cl + width), F32), ((rhs, panels + 3 * cl), F32), ((clusters, cl), F32), ((clusters, 3 * LANES), F32),
            (far_pairs.shape, jnp.int32), ((8, LANES), jnp.int32), ((2 * rank, panels), BF16), whole, (offsets.shape, F32),
        ],
        [
            pltpu.VMEM(vertices.shape, F32),
            pltpu.VMEM(panel_vertices.shape, jnp.int32),
            pltpu.VMEM(basis.shape, F32),
            pltpu.VMEM(far_pairs.shape, jnp.int32),
            pltpu.VMEM((slots, clusters), jnp.int32),
            pltpu.VMEM((3 * clusters, vcl), F32),
            pltpu.VMEM((3 * panels // LANES, LANES), jnp.int32),
            pltpu.SemaphoreType.DMA((7,)),
        ],
        "shhhhhhh>vvvvvvppp",
        position, vertices, panel_vertices, krylov, basis, far_pairs, near_pairs.T, offsets,
        us=1.5,
    )
    partner, other, near_pair, far_pair = exchange(payload, heavy)
    total = pltpu.VMEM((clusters, 2 * rhs, cl), F32)

    group = 4
    own = ((clusters, 2 * cl, cl), BF16)
    kept = ((clusters * (slots - 1) // group, group, 2 * cl, cl), BF16)

    def pieces(number):
        return pltpu.VMEM((number * clusters + 1, 2 * rhs, cl), BF16)

    def sources(number):
        return pltpu.VMEM((number * clusters + 1, 8, cl), F32)

    own_blocks, blocks, near, columns, tail = call(
        functools.partial(near_kernel, cl, 0, 1),
        [own, kept, whole, ((clusters, 3, cl, LANES), F32), ((rhs, LANES), F32)],
        [pieces(1), sources(1), total],
        "svv>ppvpv",
        pairs, payload, partner,
        us=8.0,
    )
    swap = swapped(near_pair, far_pair, tail)
    blocks_other, near = call(
        functools.partial(near_kernel, cl, 1, 2),
        [kept, whole],
        [pieces(2), sources(2), total],
        "svvpv>pv",
        pairs, partner, other, columns, near,
        us=4.0,
    )
    tiles = 6 * per * span // LANES
    window = pltpu.VMEM((tiles, 2 * rhs, LANES), BF16)
    gathered = pltpu.VMEM((clusters, 2 * rhs, partners * rank), BF16)
    fields = pltpu.VMEM((clusters, 2 * rhs, 2 * rank), BF16)
    image, payload, heavy, coupling = call(
        functools.partial(image_kernel, cl, rank),
        [whole, ((rhs, panels + span + LANES), F32), whole, ((clusters, 2 * rank, partners * rank), BF16)],
        [window, pltpu.VMEM((tiles, 8, LANES), F32), gathered, fields],
        "svvvvvvppp>vvvp",
        at, near_pair, far_pair, swap, centers, area, near, basis, krylov, offsets,
        us=4.5,
    )
    partner, other, near_pair, far_pair = exchange(payload, heavy)
    near, tail = call(
        functools.partial(near_again_kernel, cl, 0, 1),
        [whole, ((rhs, LANES), F32)],
        [pieces(1), total],
        "svvpp>vv",
        pairs, payload, partner, own_blocks, blocks,
        us=8.0,
    )
    swap = swapped(near_pair, far_pair, tail)
    (near,) = call(
        functools.partial(near_again_kernel, cl, 1, 2),
        [whole],
        [pieces(2), total],
        "svvvp>v",
        pairs, partner, other, near, blocks_other,
        us=2.0,
    )
    sums_shape = ((rhs, LANES), F32)
    (one,) = call(window_sums_kernel, [sums_shape], [], "vvvvv>v", payload, partner, near_pair, far_pair, swap, us=0.3)
    size = 8
    many = outward(one, size)
    while 2 * size < devices:
        (one,) = call(merge_kernel, [sums_shape], [], "vv>v", one, many, us=0.3)
        size = 2 * size
        many = outward(one, size)
    (again,) = call(
        functools.partial(far_again_kernel, cl, rank),
        [whole],
        [window, gathered, fields],
        "svvvvvpp>v",
        at, near_pair, far_pair, swap, near, area, coupling, basis,
        us=2.0,
    )
    here = pltpu.VMEM((rhs, panels), F32)
    return tuple(call(
        functools.partial(finish_kernel, panels * devices),
        [whole, whole],
        [here, here, pltpu.SemaphoreType.DMA((4,))],
        "vvvvp>hh",
        one, many, image, again, krylov,
    ))


def solution(mesh):
    whole = P(None, ("jobs", "clus"))
    rows = P(("jobs", "clus"), None)
    return jax.shard_map(
        body,
        mesh=mesh,
        in_specs=(whole, whole, rows, rows, whole, whole),
        out_specs=(whole, whole),
        check_vma=False,
    )
```

```python
import functools

import jax
import jax.numpy as jnp
import numpy as np
from jax import lax
from jax.experimental import pallas as pl
from jax.experimental.pallas import tpu as pltpu
from jax.sharding import PartitionSpec as P

REACH = 4
SMOOTHING = 0.04
COULOMB = 2.0
PROXY_RADIUS = 0.6
LANES = 128
F32 = jnp.float32
BF16 = jnp.bfloat16


def proxy_offsets(points):
    counter = np.arange(points, dtype=np.float32)
    height = 1.0 - (2.0 * counter + 1.0) / points
    radial = np.sqrt(1.0 - height * height)
    azimuth = counter * 2.399963
    return PROXY_RADIUS * np.stack([radial * np.cos(azimuth), radial * np.sin(azimuth), height]).astype(np.float32)


def split(value):
    high = value.astype(BF16)
    return high, (value - high.astype(F32)).astype(BF16)


def stacked(value):
    return jnp.concatenate(split(value), axis=0)


def folded(value):
    half = value.shape[0] // 2
    return value[:half] + value[half:]


def dot_nt(left, right):
    return lax.dot_general(left, right, (((1,), (1,)), ((), ())), preferred_element_type=F32)


def dot_nn(left, right):
    return lax.dot_general(left, right, (((1,), (0,)), ((), ())), preferred_element_type=F32)


def quartered(value):
    half = value.shape[1] // 2
    value = folded(value)
    return value[:, 0:half] + value[:, half:]


def moments_of(weighted, basis_pieces):
    return quartered(dot_nt(stacked(weighted), basis_pieces))


def copies(pairs, sems):
    moves = [pltpu.make_async_copy(source, target, sems.at[i]) for i, (source, target) in enumerate(pairs)]
    for move in moves:
        move.start()
    return moves


def pair_list(near, position, clusters):
    block = lax.div(near, clusters) - position
    partner = block * (1 - 2 * lax.rem(position, 2)) > 0
    place = (lax.rem(near, clusters) + jnp.where((block != 0) & ~partner, clusters, 0)).astype(F32)
    across = lax.broadcasted_iota(jnp.int32, (clusters, clusters), 1)
    down = lax.broadcasted_iota(jnp.int32, (clusters, clusters), 0)
    upright = lambda value: jnp.sum(jnp.where(across == down, value, 0.0), axis=1, keepdims=True)
    row = lax.broadcasted_iota(jnp.int32, (clusters, LANES), 1).astype(F32)
    target = lax.broadcasted_iota(jnp.int32, (clusters, 1), 0).astype(F32)
    rows = lax.broadcasted_iota(jnp.int32, (8, LANES), 0)
    out = jnp.zeros((8, LANES), F32)
    for which in range(2):
        here = block != 0 if which else block == 0
        live = jnp.where(here & (near >= 0), 1.0, 0.0)
        counts = sum(live[k:k + 1] for k in range(1, near.shape[0]))
        first = jnp.sum(jnp.where(across < down, counts, 0.0), axis=1, keepdims=True)
        found = jnp.zeros((clusters, LANES), F32)
        for k in range(1, near.shape[0]):
            alive = upright(live[k:k + 1])
            hit = jnp.where(row == first, alive, 0.0)
            found = found + hit * (target * 64 + upright(place[k:k + 1]))
            first = first + alive
        count = jnp.sum(counts, axis=1, keepdims=True)
        found = jnp.where(row[0:1] < count, jnp.sum(found, axis=0, keepdims=True), (1.0 + which) * clusters)
        out = jnp.where(rows == which, found, jnp.where(rows == 2 + which, count, out))
    return out.astype(jnp.int32)


def prepare_kernel(cl, vcl, rank, position_ref, vertices_hbm, corners_hbm, krylov_hbm, basis_hbm, far_hbm, near_hbm, offsets_hbm,
                   payload_ref, heavy_ref, area_ref, center_ref, at_ref, pairs_ref, basis_ref, krylov_ref, offsets_ref,
                   vertices_ref, corners_ref, raw_ref, far_ref, near_ref, mesh_ref, local_ref, sems):
    moves = copies((
        (vertices_hbm, vertices_ref), (corners_hbm, corners_ref), (krylov_hbm, krylov_ref), (basis_hbm, raw_ref),
        (far_hbm, far_ref), (near_hbm, near_ref), (offsets_hbm, offsets_ref),
    ), sems)
    rhs, panels = krylov_ref.shape
    clusters = panels // cl
    parts = cl // LANES
    moves[0].wait()
    for c in range(clusters):
        mesh_ref[3 * c:3 * c + 3, :] = vertices_ref[:, c * vcl:(c + 1) * vcl]
    moves[1].wait()
    for i in range(clusters * parts):
        local_ref[3 * i:3 * i + 3, :] = corners_ref[:, i * LANES:(i + 1) * LANES]
    first = position_ref[0] * (vcl * clusters) + vcl * lax.broadcasted_iota(jnp.int32, (clusters, LANES), 0)
    tables = [mesh_ref[pl.ds(k, clusters, stride=3), :] for k in range(3)]
    sums = [None] * 3
    for h in range(parts):
        local = [local_ref[pl.ds(3 * h + m, clusters, stride=3 * parts), :] - first for m in range(3)]
        corner = [[jnp.take_along_axis(tables[k], local[m], axis=1, mode="promise_in_bounds") for k in range(3)] for m in range(3)]
        for k in range(3):
            middle = (corner[0][k] + corner[1][k] + corner[2][k]) / 3.0
            lanes = slice(panels + k * cl + h * LANES, panels + k * cl + (h + 1) * LANES)
            payload_ref[:, lanes] = middle
            heavy_ref[:, lanes] = middle
            sums[k] = middle if h == 0 else sums[k] + middle
        one = [corner[1][k] - corner[0][k] for k in range(3)]
        two = [corner[2][k] - corner[0][k] for k in range(3)]
        normal = [one[1] * two[2] - one[2] * two[1], one[2] * two[0] - one[0] * two[2], one[0] * two[1] - one[1] * two[0]]
        area_ref[:, h * LANES:(h + 1) * LANES] = 0.5 * jnp.sqrt(normal[0] * normal[0] + normal[1] * normal[1] + normal[2] * normal[2])
    span = clusters * rank
    table = panels + 3 * cl
    mine = lax.broadcasted_iota(jnp.int32, (clusters, span), 1) // rank == lax.broadcasted_iota(jnp.int32, (clusters, span), 0)
    half = span // 2
    payload_ref[:, table + span:] = jnp.zeros_like(payload_ref[:, table + span:])
    for k in range(3):
        center = jnp.sum(sums[k], axis=1, keepdims=True) / cl
        center_ref[:, k * LANES:(k + 1) * LANES] = jnp.broadcast_to(center, (clusters, LANES))
        row = jnp.sum(jnp.where(mine, center, 0.0), axis=0, keepdims=True)
        payload_ref[k:k + 1, table + span:] = row[:, 0:half]
        payload_ref[8 + k:9 + k, table + span:] = row[:, half:]
    moves[2].wait()
    moves[3].wait()
    for c in range(clusters):
        lanes = slice(c * cl, (c + 1) * cl)
        basis_ref[:, lanes] = stacked(raw_ref[:, lanes])
        charges = area_ref[c:c + 1, :] * krylov_ref[:, lanes]
        payload_ref[:, lanes] = charges
        heavy_ref[:, lanes] = charges
        payload_ref[:, table + c * rank:table + (c + 1) * rank] = moments_of(charges, basis_ref[:, lanes])
    moves[4].wait()
    far = far_ref[...]
    step = (lax.div(far, clusters) - position_ref[0]) * (1 - 2 * lax.rem(position_ref[0], 2))
    block = jnp.where(step < 0, step + REACH, step + REACH - 3)
    per = LANES // rank
    turn = lax.rem(lax.broadcasted_iota(jnp.int32, far.shape, 1) - far + per * clusters * 2 ** 16, per)
    at_ref[...] = (turn * 6 + block) * (span // LANES) + lax.div(lax.rem(far, clusters), per)
    moves[5].wait()
    pairs_ref[...] = pair_list(near_ref[...], position_ref[0], clusters)
    moves[6].wait()


def columns_of(payload_ref, panels, c, cl, columns_ref, at):
    rows = [payload_ref[c:c + 1, panels + k * cl:panels + (k + 1) * cl] for k in range(3)]
    upright = jnp.transpose(jnp.concatenate(rows * 2 + rows[:2], axis=0))
    for k in range(3):
        columns_ref[at, k] = jnp.broadcast_to(upright[:, k:k + 1], (cl, LANES))


def near_block(columns, source, cl, out_ref):
    for h in range(cl // LANES):
        lanes = slice(h * LANES, (h + 1) * LANES)
        gap = [columns[k] - source(k, h) for k in range(3)]
        square = gap[0] * gap[0] + gap[1] * gap[1] + gap[2] * gap[2]
        high, low = split(lax.rsqrt(square + SMOOTHING))
        out_ref[0:cl, lanes] = high
        out_ref[cl:2 * cl, lanes] = low


def self_product(pieces, block_ref, cl):
    return dot_nn(pieces, block_ref[0:cl, :]) + dot_nn(pieces, block_ref[cl:2 * cl, :])


def near_product(pieces, block_ref, cl):
    return dot_nt(pieces, block_ref[0:cl, :]) + dot_nt(pieces, block_ref[cl:2 * cl, :])


def fill_charges(pieces_ref, blocks, clusters, cl):
    for b, ref in enumerate(blocks):
        for c in range(clusters):
            pieces_ref[b * clusters + c] = stacked(ref[:, c * cl:(c + 1) * cl])
    pieces_ref[len(blocks) * clusters] = jnp.zeros_like(pieces_ref[0])


def pair_at(pairs_ref, which, i):
    pair = pairs_ref[which, i]
    return lax.shift_right_logical(pair, 6), lax.bitwise_and(pair, 63)


def near_kernel(cl, which, number, pairs_ref, *refs):
    blocks = refs[:number]
    if which:
        columns_ref, start_ref, kept_ref, near_out_ref, pieces_ref, sources_ref, total_ref = refs[number:]
    else:
        _, own_ref, kept_ref, near_out_ref, columns_ref, tail_ref, pieces_ref, sources_ref, total_ref = refs[number:]
        tail_ref[...] = blocks[0][:, blocks[0].shape[1] - tail_ref.shape[1]:]
    panels = near_out_ref.shape[1]
    clusters = panels // cl
    group = kept_ref.shape[1]
    fill_charges(pieces_ref, blocks, clusters, cl)
    if which:
        total_ref[...] = jnp.zeros_like(total_ref)
    else:
        for c in range(clusters):
            columns_of(blocks[0], panels, c, cl, columns_ref, c)
            source = lambda k, h: blocks[0][c:c + 1, panels + k * cl + h * LANES:panels + k * cl + (h + 1) * LANES]
            near_block([columns_ref[c, k] for k in range(3)], source, cl, own_ref.at[c])
            total_ref[c] = self_product(pieces_ref[c], own_ref.at[c], cl)
    sources_ref[number * clusters] = jnp.zeros_like(sources_ref[0])
    for b, ref in enumerate(blocks):
        for c in range(clusters):
            for k in range(3):
                sources_ref[b * clusters + c, k:k + 1, :] = ref[c:c + 1, panels + k * cl:panels + (k + 1) * cl]

    def step(m, _):
        pairs = [pair_at(pairs_ref, which, group * m + w) for w in range(group)]
        parts = []
        for w, (c, j) in enumerate(pairs):
            source = lambda k, h: sources_ref[j, k:k + 1, h * LANES:(h + 1) * LANES]
            near_block([columns_ref[c, k] for k in range(3)], source, cl, kept_ref.at[m, w])
            parts.append(near_product(pieces_ref[j], kept_ref.at[m, w], cl))
        for (c, j), part in zip(pairs, parts):
            total_ref[c] += part
        return 0

    lax.fori_loop(0, (pairs_ref[2 + which, 0] + group - 1) // group, step, 0)
    for c in range(clusters):
        lanes = slice(c * cl, (c + 1) * cl)
        near = folded(total_ref[c])
        near_out_ref[:, lanes] = start_ref[:, lanes] + near if which else near


def near_again_kernel(cl, which, number, pairs_ref, *refs):
    blocks = refs[:number]
    if which:
        start_ref, kept_ref, near_out_ref, pieces_ref, total_ref = refs[number:]
    else:
        _, own_ref, kept_ref, near_out_ref, tail_ref, pieces_ref, total_ref = refs[number:]
        tail_ref[...] = blocks[0][:, blocks[0].shape[1] - tail_ref.shape[1]:]
    clusters = near_out_ref.shape[1] // cl
    group = kept_ref.shape[1]
    fill_charges(pieces_ref, blocks, clusters, cl)
    if which:
        total_ref[...] = jnp.zeros_like(total_ref)
    else:
        for c in range(clusters):
            total_ref[c] = self_product(pieces_ref[c], own_ref.at[c], cl)

    def step(m, _):
        pairs = [pair_at(pairs_ref, which, group * m + w) for w in range(group)]
        parts = [near_product(pieces_ref[j], kept_ref.at[m, w], cl) for w, (c, j) in enumerate(pairs)]
        for (c, j), part in zip(pairs, parts):
            total_ref[c] += part
        return 0

    lax.fori_loop(0, (pairs_ref[2 + which, 0] + group - 1) // group, step, 0)
    for c in range(clusters):
        lanes = slice(c * cl, (c + 1) * cl)
        near = folded(total_ref[c])
        near_out_ref[:, lanes] = start_ref[:, lanes] + near if which else near


def load_window(tables, clusters, rank, pieces_ref, middle_ref):
    per = LANES // rank
    span = clusters * rank
    count = pieces_ref.shape[0] // per
    groups = span // LANES
    for at in range(count):
        (ref, first), g = tables[at // groups], at % groups
        tile = ref[:, first + g * LANES:first + (g + 1) * LANES]
        for s in range(per):
            pieces_ref[s * count + at] = stacked(pltpu.roll(tile, s * rank, 1) if s else tile)
        if middle_ref is not None:
            half = groups // 2
            row, lane = 8 * (g // half), first + span + g % half * LANES
            tile = ref[row:row + 8, lane:lane + LANES]
            for s in range(per):
                middle_ref[s * count + at] = pltpu.roll(tile, s * rank, 1) if s else tile


def six_tables(near_ref, far_ref, swapped_ref):
    width = near_ref.shape[1] // 2
    return (far_ref, 0), (far_ref, width), (near_ref, 0), (swapped_ref, width), (swapped_ref, 0), (swapped_ref, 3 * width)


def pick(source_ref, at_ref, c, g, per, lane):
    row = None
    for u in range(per):
        take = source_ref[at_ref[c, g * per + u]]
        row = take if row is None else jnp.where(lane == u, take, row)
    return row


def far_fields(gathered_ref, coupling_ref, fields_ref):
    for c in range(gathered_ref.shape[0]):
        field = quartered(dot_nt(gathered_ref[c], coupling_ref[c]))
        fields_ref[c] = stacked(jnp.concatenate([field, field], axis=1))


def far_potential(fields_ref, c, basis):
    return folded(dot_nn(fields_ref[c], basis))


def image_kernel(cl, rank, at_ref, near_pair_ref, far_pair_ref, swapped_ref, center_ref, area_ref, near_ref, basis_ref, krylov_ref, offsets_ref,
                 image_ref, payload_ref, heavy_ref, coupling_ref, pieces_ref, middle_ref, gathered_ref, fields_ref):
    rhs, panels = near_ref.shape
    clusters = panels // cl
    per = LANES // rank
    span = clusters * rank
    load_window(six_tables(near_pair_ref, far_pair_ref, swapped_ref), clusters, rank, pieces_ref, middle_ref)
    lane = lax.broadcasted_iota(jnp.int32, (1, LANES), 1) // rank
    for c in range(clusters):
        mine = [offsets_ref[3, k:k + 1, :] - center_ref[c:c + 1, k * LANES:(k + 1) * LANES] for k in range(3)]
        for g in range(at_ref.shape[1] // per):
            lanes = slice(g * LANES, (g + 1) * LANES)
            gathered_ref[c, :, lanes] = pick(pieces_ref, at_ref, c, g, per, lane)
            center = pick(middle_ref, at_ref, c, g, per, lane)
            gap = [(center[k:k + 1] + mine[k]) - offsets_ref[k] for k in range(3)]
            high, low = split(lax.rsqrt(gap[0] * gap[0] + gap[1] * gap[1] + gap[2] * gap[2] + SMOOTHING))
            coupling_ref[c, 0:rank, lanes] = high
            coupling_ref[c, rank:2 * rank, lanes] = low
    far_fields(gathered_ref, coupling_ref, fields_ref)
    squared = correlation = jnp.zeros((rhs, cl), F32)
    for c in range(clusters):
        lanes = slice(c * cl, (c + 1) * cl)
        basis = basis_ref[:, lanes]
        area = area_ref[c:c + 1, :]
        image = COULOMB * area * (near_ref[:, lanes] + far_potential(fields_ref, c, basis))
        charges = area * image
        image_ref[:, lanes] = image
        payload_ref[:, lanes] = charges
        heavy_ref[:, lanes] = charges
        payload_ref[:, panels + c * rank:panels + (c + 1) * rank] = moments_of(charges, basis)
        krylov = krylov_ref[:, lanes]
        squared = squared + krylov * krylov
        correlation = correlation + krylov * image
    squared = jnp.sum(squared, axis=1, keepdims=True)
    correlation = jnp.sum(correlation, axis=1, keepdims=True)
    local = ratio(correlation, squared)
    residual = image_ref[...] - local * krylov_ref[...]
    payload_ref[:, panels + span:] = in_lanes(squared, correlation, jnp.sum(residual * residual, axis=1, keepdims=True), local)


def far_again_kernel(cl, rank, at_ref, near_pair_ref, far_pair_ref, swapped_ref, near_ref, area_ref, coupling_ref, basis_ref,
                     image_ref, pieces_ref, gathered_ref, fields_ref):
    clusters = near_ref.shape[1] // cl
    per = LANES // rank
    load_window(six_tables(near_pair_ref, far_pair_ref, swapped_ref), clusters, rank, pieces_ref, None)
    lane = lax.broadcasted_iota(jnp.int32, (1, LANES), 1) // rank
    for c in range(clusters):
        for g in range(at_ref.shape[1] // per):
            gathered_ref[c, :, g * LANES:(g + 1) * LANES] = pick(pieces_ref, at_ref, c, g, per, lane)
    far_fields(gathered_ref, coupling_ref, fields_ref)
    for c in range(clusters):
        lanes = slice(c * cl, (c + 1) * cl)
        image_ref[:, lanes] = COULOMB * area_ref[c:c + 1, :] * (near_ref[:, lanes] + far_potential(fields_ref, c, basis_ref[:, lanes]))


def finish_kernel(total, one_ref, two_ref, image_ref, again_ref, krylov_ref, next_hbm, second_hbm, next_ref, second_ref, sems):
    squared, correlation, energy, local = merged([one_ref[...], two_ref[...]])
    projection = correlation / (squared + 1e-06)
    gap = projection - local
    scaling = 1.0 / jnp.sqrt((energy + gap * gap * squared) / total + 1e-06)
    moves = []
    part = next_ref.shape[1] // 4
    for h in range(4):
        lanes = slice(h * part, (h + 1) * part)
        image = image_ref[:, lanes]
        next_ref[:, lanes] = (image - projection * krylov_ref[:, lanes]) * scaling
        second_ref[:, lanes] = (again_ref[:, lanes] - projection * image) * scaling
        for held, hbm in ((next_ref, next_hbm), (second_ref, second_hbm)):
            moves.append(pltpu.make_async_copy(held.at[:, lanes], hbm.at[:, lanes], sems.at[len(moves)]))
            moves[-1].start()
    for move in moves:
        move.wait()


def ratio(correlation, squared):
    return jnp.where(squared > 0, correlation / jnp.where(squared > 0, squared, 1.0), 0.0)


def in_lanes(*columns):
    lane = lax.broadcasted_iota(jnp.int32, (columns[0].shape[0], LANES), 1)
    out = columns[-1]
    for i, column in enumerate(columns[:-1]):
        out = jnp.where(lane == i, column, out)
    return out


def merged(groups):
    squared = sum(group[:, 0:1] for group in groups)
    correlation = sum(group[:, 1:2] for group in groups)
    local = ratio(correlation, squared)
    energy = 0.0
    for group in groups:
        gap = local - group[:, 3:4]
        energy = energy + (group[:, 2:3] + gap * gap * group[:, 0:1])
    return squared, correlation, energy, local


def window_sums_kernel(payload_ref, partner_ref, near_pair_ref, far_pair_ref, swapped_ref, out_ref):
    width = near_pair_ref.shape[1] // 2
    ends = [(payload_ref, payload_ref.shape[1]), (partner_ref, partner_ref.shape[1])]
    ends += [(ref, end) for ref in (near_pair_ref, far_pair_ref, swapped_ref) for end in (width, 2 * width)]
    out_ref[...] = in_lanes(*merged([ref[:, end - LANES:end] for ref, end in ends]))


def merge_kernel(one_ref, two_ref, out_ref):
    out_ref[...] = in_lanes(*merged([one_ref[...], two_ref[...]]))


def call(kernel, outs, scratch, memory, *args, limit=10, us=1.0):
    spaces = {"s": pltpu.SMEM, "v": pltpu.VMEM, "p": pltpu.VMEM, "h": pltpu.HBM}
    ins, out_spaces = memory.split(">")
    pinned = {"h": pltpu.HBM, "p": pltpu.VMEM}
    return pl.pallas_call(
        kernel,
        out_shape=[pltpu.VMEM(*out) if m == "p" else jax.ShapeDtypeStruct(*out) for m, out in zip(out_spaces, outs)],
        in_specs=[pl.BlockSpec(memory_space=spaces[m]) for m in ins],
        out_specs=[pl.BlockSpec(memory_space=spaces[m]) for m in out_spaces],
        scratch_shapes=scratch,
        compiler_params=pltpu.CompilerParams(vmem_limit_bytes=limit * 2 ** 20),
        cost_estimate=pl.CostEstimate(flops=int(us * 5e8), bytes_accessed=int(us * 3.6e6), transcendentals=0),
    )(*(pltpu.with_memory_space_constraint(a, pinned[m]) if m in pinned else a for m, a in zip(ins, args)))


def body(vertices, panel_vertices, near_pairs, far_pairs, basis, krylov):
    clusters, slots = near_pairs.shape
    partners = far_pairs.shape[1]
    rhs, panels = krylov.shape
    rank = basis.shape[0]
    cl = panels // clusters
    vcl = vertices.shape[1] // clusters
    span = clusters * rank
    per = LANES // rank
    devices = lax.axis_size("clus")
    position = lax.axis_index("clus").reshape(1).astype(jnp.int32)
    offsets = proxy_offsets(rank)
    flat = np.concatenate([np.tile(offsets, (1, per)), np.zeros((rank - 3, LANES), np.float32)])
    offsets = jnp.asarray(np.concatenate([np.broadcast_to(offsets[:, :, None], (3, rank, LANES)), flat[None]]))
    width = span + span // 2
    pairing = [(i, i + 1 - 2 * (i % 2)) for i in range(devices)]
    bridging = [(i, i - 1 + 2 * (i % 2)) for i in range(1, devices - 1)] + [(0, 0), (devices - 1, devices - 1)]

    def move(value, pairs):
        return lax.ppermute(value, "clus", pairs)

    def outward(value, steps):
        return move(value, [(i, (i + steps * (1 - 2 * (i % 2))) % devices) for i in range(devices)])

    def exchange(payload, heavy):
        other = move(heavy, bridging)
        partner = move(payload, pairing)
        pair = jnp.concatenate([value[:, heavy.shape[1]:] for value in (payload, partner)], axis=1)
        return partner, other, outward(pair, 2), outward(pair, 4)

    def swapped(near_pair, far_pair, tail):
        return move(jnp.concatenate([near_pair, far_pair, tail], axis=1), pairing)

    whole = ((rhs, panels), F32)
    payload, heavy, area, centers, at, pairs, basis, krylov, offsets = call(
        functools.partial(prepare_kernel, cl, vcl, rank),
        [
            ((rhs, panels + 3 * cl + width), F32), ((rhs, panels + 3 * cl), F32), ((clusters, cl), F32), ((clusters, 3 * LANES), F32),
            (far_pairs.shape, jnp.int32), ((8, LANES), jnp.int32), ((2 * rank, panels), BF16), whole, (offsets.shape, F32),
        ],
        [
            pltpu.VMEM(vertices.shape, F32),
            pltpu.VMEM(panel_vertices.shape, jnp.int32),
            pltpu.VMEM(basis.shape, F32),
            pltpu.VMEM(far_pairs.shape, jnp.int32),
            pltpu.VMEM((slots, clusters), jnp.int32),
            pltpu.VMEM((3 * clusters, vcl), F32),
            pltpu.VMEM((3 * panels // LANES, LANES), jnp.int32),
            pltpu.SemaphoreType.DMA((7,)),
        ],
        "shhhhhhh>vvvvvvppp",
        position, vertices, panel_vertices, krylov, basis, far_pairs, near_pairs.T, offsets,
        us=1.5,
    )
    partner, other, near_pair, far_pair = exchange(payload, heavy)
    total = pltpu.VMEM((clusters, 2 * rhs, cl), F32)

    group = 4
    own = ((clusters, 2 * cl, cl), BF16)
    kept = ((clusters * (slots - 1) // group, group, 2 * cl, cl), BF16)

    def pieces(number):
        return pltpu.VMEM((number * clusters + 1, 2 * rhs, cl), BF16)

    def sources(number):
        return pltpu.VMEM((number * clusters + 1, 8, cl), F32)

    own_blocks, blocks, near, columns, tail = call(
        functools.partial(near_kernel, cl, 0, 1),
        [own, kept, whole, ((clusters, 3, cl, LANES), F32), ((rhs, LANES), F32)],
        [pieces(1), sources(1), total],
        "svv>ppvpv",
        pairs, payload, partner,
        us=8.0,
    )
    swap = swapped(near_pair, far_pair, tail)
    blocks_other, near = call(
        functools.partial(near_kernel, cl, 1, 2),
        [kept, whole],
        [pieces(2), sources(2), total],
        "svvpv>pv",
        pairs, partner, other, columns, near,
        us=4.0,
    )
    tiles = 6 * per * span // LANES
    window = pltpu.VMEM((tiles, 2 * rhs, LANES), BF16)
    gathered = pltpu.VMEM((clusters, 2 * rhs, partners * rank), BF16)
    fields = pltpu.VMEM((clusters, 2 * rhs, 2 * rank), BF16)
    image, payload, heavy, coupling = call(
        functools.partial(image_kernel, cl, rank),
        [whole, ((rhs, panels + span + LANES), F32), whole, ((clusters, 2 * rank, partners * rank), BF16)],
        [window, pltpu.VMEM((tiles, 8, LANES), F32), gathered, fields],
        "svvvvvvppp>vvvp",
        at, near_pair, far_pair, swap, centers, area, near, basis, krylov, offsets,
        us=4.5,
    )
    partner, other, near_pair, far_pair = exchange(payload, heavy)
    near, tail = call(
        functools.partial(near_again_kernel, cl, 0, 1),
        [whole, ((rhs, LANES), F32)],
        [pieces(1), total],
        "svvpp>vv",
        pairs, payload, partner, own_blocks, blocks,
        us=8.0,
    )
    swap = swapped(near_pair, far_pair, tail)
    (near,) = call(
        functools.partial(near_again_kernel, cl, 1, 2),
        [whole],
        [pieces(2), total],
        "svvvp>v",
        pairs, partner, other, near, blocks_other,
        us=2.0,
    )
    sums_shape = ((rhs, LANES), F32)
    (one,) = call(window_sums_kernel, [sums_shape], [], "vvvvv>v", payload, partner, near_pair, far_pair, swap, us=0.3)
    size = 8
    many = outward(one, size)
    while 2 * size < devices:
        (one,) = call(merge_kernel, [sums_shape], [], "vv>v", one, many, us=0.3)
        size = 2 * size
        many = outward(one, size)
    (again,) = call(
        functools.partial(far_again_kernel, cl, rank),
        [whole],
        [window, gathered, fields],
        "svvvvvpp>v",
        at, near_pair, far_pair, swap, near, area, coupling, basis,
        us=2.0,
    )
    here = pltpu.VMEM((rhs, panels), F32)
    return tuple(call(
        functools.partial(finish_kernel, panels * devices),
        [whole, whole],
        [here, here, pltpu.SemaphoreType.DMA((8,))],
        "vvvvp>hh",
        one, many, image, again, krylov,
    ))


def solution(mesh):
    whole = P(None, ("jobs", "clus"))
    rows = P(("jobs", "clus"), None)
    return jax.shard_map(
        body,
        mesh=mesh,
        in_specs=(whole, whole, rows, rows, whole, whole),
        out_specs=(whole, whole),
        check_vma=False,
    )
```

```python
import functools

import jax
import jax.numpy as jnp
import numpy as np
from jax import lax
from jax.experimental import pallas as pl
from jax.experimental.pallas import tpu as pltpu
from jax.sharding import PartitionSpec as P

REACH = 4
SMOOTHING = 0.04
COULOMB = 2.0
PROXY_RADIUS = 0.6
LANES = 128
CHUNK = 32
F32 = jnp.float32
BF16 = jnp.bfloat16


def proxy_offsets(points):
    counter = np.arange(points, dtype=np.float32)
    height = 1.0 - (2.0 * counter + 1.0) / points
    radial = np.sqrt(1.0 - height * height)
    azimuth = counter * 2.399963
    return PROXY_RADIUS * np.stack([radial * np.cos(azimuth), radial * np.sin(azimuth), height]).astype(np.float32)


def split(value):
    high = value.astype(BF16)
    return high, (value - high.astype(F32)).astype(BF16)


def stacked(value):
    return jnp.concatenate(split(value), axis=0)


def folded(value):
    half = value.shape[0] // 2
    return value[:half] + value[half:]


def dot_nt(left, right):
    return lax.dot_general(left, right, (((1,), (1,)), ((), ())), preferred_element_type=F32)


def dot_nn(left, right):
    return lax.dot_general(left, right, (((1,), (0,)), ((), ())), preferred_element_type=F32)


def quartered(value):
    half = value.shape[1] // 2
    value = folded(value)
    return value[:, 0:half] + value[:, half:]


def moments_of(weighted, basis_pieces):
    return quartered(dot_nt(stacked(weighted), basis_pieces))


def copies(pairs, sems):
    moves = [pltpu.make_async_copy(source, target, sems.at[i]) for i, (source, target) in enumerate(pairs)]
    for move in moves:
        move.start()
    return moves


def pair_list(near, position, clusters):
    block = lax.div(near, clusters) - position
    partner = block * (1 - 2 * lax.rem(position, 2)) > 0
    place = (lax.rem(near, clusters) + jnp.where((block != 0) & ~partner, clusters, 0)).astype(F32)
    across = lax.broadcasted_iota(jnp.int32, (clusters, clusters), 1)
    down = lax.broadcasted_iota(jnp.int32, (clusters, clusters), 0)
    upright = lambda value: jnp.sum(jnp.where(across == down, value, 0.0), axis=1, keepdims=True)
    row = lax.broadcasted_iota(jnp.int32, (clusters, LANES), 1).astype(F32)
    target = lax.broadcasted_iota(jnp.int32, (clusters, 1), 0).astype(F32)
    rows = lax.broadcasted_iota(jnp.int32, (8, LANES), 0)
    out = jnp.zeros((8, LANES), F32)
    for which in range(2):
        here = block != 0 if which else block == 0
        live = jnp.where(here & (near >= 0), 1.0, 0.0)
        counts = sum(live[k:k + 1] for k in range(1, near.shape[0]))
        first = jnp.sum(jnp.where(across < down, counts, 0.0), axis=1, keepdims=True)
        found = jnp.zeros((clusters, LANES), F32)
        for k in range(1, near.shape[0]):
            alive = upright(live[k:k + 1])
            hit = jnp.where(row == first, alive, 0.0)
            found = found + hit * (target * 64 + upright(place[k:k + 1]))
            first = first + alive
        count = jnp.sum(counts, axis=1, keepdims=True)
        found = jnp.where(row[0:1] < count, jnp.sum(found, axis=0, keepdims=True), (1.0 + which) * clusters)
        out = jnp.where(rows == which, found, jnp.where(rows == 2 + which, count, out))
    return out.astype(jnp.int32)


def prepare_kernel(cl, vcl, rank, position_ref, vertices_hbm, corners_hbm, krylov_hbm, basis_hbm, far_hbm, near_hbm, offsets_hbm,
                   payload_ref, heavy_ref, area_ref, center_ref, at_ref, pairs_ref, basis_ref, krylov_ref, offsets_ref,
                   vertices_ref, corners_ref, raw_ref, far_ref, near_ref, mesh_ref, local_ref, sems):
    moves = copies((
        (vertices_hbm, vertices_ref), (corners_hbm, corners_ref), (krylov_hbm, krylov_ref), (basis_hbm, raw_ref),
        (far_hbm, far_ref), (near_hbm, near_ref), (offsets_hbm, offsets_ref),
    ), sems)
    rhs, panels = krylov_ref.shape
    clusters = panels // cl
    parts = cl // LANES
    moves[0].wait()
    for c in range(clusters):
        mesh_ref[3 * c:3 * c + 3, :] = vertices_ref[:, c * vcl:(c + 1) * vcl]
    moves[1].wait()
    for i in range(clusters * parts):
        local_ref[3 * i:3 * i + 3, :] = corners_ref[:, i * LANES:(i + 1) * LANES]
    first = position_ref[0] * (vcl * clusters) + vcl * lax.broadcasted_iota(jnp.int32, (clusters, LANES), 0)
    tables = [mesh_ref[pl.ds(k, clusters, stride=3), :] for k in range(3)]
    sums = [None] * 3
    for h in range(parts):
        local = [local_ref[pl.ds(3 * h + m, clusters, stride=3 * parts), :] - first for m in range(3)]
        corner = [[jnp.take_along_axis(tables[k], local[m], axis=1, mode="promise_in_bounds") for k in range(3)] for m in range(3)]
        for k in range(3):
            middle = (corner[0][k] + corner[1][k] + corner[2][k]) / 3.0
            lanes = slice(panels + k * cl + h * LANES, panels + k * cl + (h + 1) * LANES)
            payload_ref[:, lanes] = middle
            heavy_ref[:, lanes] = middle
            sums[k] = middle if h == 0 else sums[k] + middle
        one = [corner[1][k] - corner[0][k] for k in range(3)]
        two = [corner[2][k] - corner[0][k] for k in range(3)]
        normal = [one[1] * two[2] - one[2] * two[1], one[2] * two[0] - one[0] * two[2], one[0] * two[1] - one[1] * two[0]]
        area_ref[:, h * LANES:(h + 1) * LANES] = 0.5 * jnp.sqrt(normal[0] * normal[0] + normal[1] * normal[1] + normal[2] * normal[2])
    span = clusters * rank
    table = panels + 3 * cl
    mine = lax.broadcasted_iota(jnp.int32, (clusters, span), 1) // rank == lax.broadcasted_iota(jnp.int32, (clusters, span), 0)
    half = span // 2
    payload_ref[:, table + span:] = jnp.zeros_like(payload_ref[:, table + span:])
    for k in range(3):
        center = jnp.sum(sums[k], axis=1, keepdims=True) / cl
        center_ref[:, k * LANES:(k + 1) * LANES] = jnp.broadcast_to(center, (clusters, LANES))
        row = jnp.sum(jnp.where(mine, center, 0.0), axis=0, keepdims=True)
        payload_ref[k:k + 1, table + span:] = row[:, 0:half]
        payload_ref[8 + k:9 + k, table + span:] = row[:, half:]
    moves[2].wait()
    moves[3].wait()
    for c in range(clusters):
        lanes = slice(c * cl, (c + 1) * cl)
        basis_ref[:, lanes] = stacked(raw_ref[:, lanes])
        charges = area_ref[c:c + 1, :] * krylov_ref[:, lanes]
        payload_ref[:, lanes] = charges
        heavy_ref[:, lanes] = charges
        payload_ref[:, table + c * rank:table + (c + 1) * rank] = moments_of(charges, basis_ref[:, lanes])
    moves[4].wait()
    far = far_ref[...]
    step = (lax.div(far, clusters) - position_ref[0]) * (1 - 2 * lax.rem(position_ref[0], 2))
    block = jnp.where(step < 0, step + REACH, step + REACH - 3)
    per = LANES // rank
    turn = lax.rem(lax.broadcasted_iota(jnp.int32, far.shape, 1) - far + per * clusters * 2 ** 16, per)
    at_ref[...] = (turn * 6 + block) * (span // LANES) + lax.div(lax.rem(far, clusters), per)
    moves[5].wait()
    pairs_ref[...] = pair_list(near_ref[...], position_ref[0], clusters)
    moves[6].wait()


def columns_of(payload_ref, panels, c, cl, columns_ref, at):
    rows = [payload_ref[c:c + 1, panels + k * cl:panels + (k + 1) * cl] for k in range(3)]
    upright = jnp.transpose(jnp.concatenate(rows * 2 + rows[:2], axis=0))
    for k in range(3):
        columns_ref[at, k] = jnp.broadcast_to(upright[:, k:k + 1], (cl, LANES))


def near_block(columns, source, cl, out_ref):
    parts = cl // LANES
    across = [[source(k, h) for k in range(3)] for h in range(parts)]
    for first in range(0, cl, CHUNK):
        rows = slice(first, first + CHUNK)
        down = [columns(k, rows) for k in range(3)]
        for h in range(parts):
            lanes = slice(h * LANES, (h + 1) * LANES)
            gap = [down[k] - across[h][k] for k in range(3)]
            square = gap[0] * gap[0] + gap[1] * gap[1] + gap[2] * gap[2]
            high, low = split(lax.rsqrt(square + SMOOTHING))
            out_ref[rows, lanes] = high
            out_ref[cl + first:cl + first + CHUNK, lanes] = low


def self_product(pieces, block_ref, cl):
    return dot_nn(pieces, block_ref[0:cl, :]) + dot_nn(pieces, block_ref[cl:2 * cl, :])


def near_product(pieces, block_ref, cl):
    return dot_nt(pieces, block_ref[0:cl, :]) + dot_nt(pieces, block_ref[cl:2 * cl, :])


def fill_charges(pieces_ref, blocks, clusters, cl):
    for b, ref in enumerate(blocks):
        for c in range(clusters):
            pieces_ref[b * clusters + c] = stacked(ref[:, c * cl:(c + 1) * cl])
    pieces_ref[len(blocks) * clusters] = jnp.zeros_like(pieces_ref[0])


def pair_at(pairs_ref, which, i):
    pair = pairs_ref[which, i]
    return lax.shift_right_logical(pair, 6), lax.bitwise_and(pair, 63)


def near_kernel(cl, which, number, pairs_ref, *refs):
    blocks = refs[:number]
    if which:
        columns_ref, start_ref, kept_ref, near_out_ref, pieces_ref, sources_ref, total_ref = refs[number:]
    else:
        _, own_ref, kept_ref, near_out_ref, columns_ref, tail_ref, pieces_ref, sources_ref, total_ref = refs[number:]
        tail_ref[...] = blocks[0][:, blocks[0].shape[1] - tail_ref.shape[1]:]
    panels = near_out_ref.shape[1]
    clusters = panels // cl
    group = kept_ref.shape[1]
    fill_charges(pieces_ref, blocks, clusters, cl)
    if which:
        total_ref[...] = jnp.zeros_like(total_ref)
    else:
        for c in range(clusters):
            columns_of(blocks[0], panels, c, cl, columns_ref, c)
            source = lambda k, h: blocks[0][c:c + 1, panels + k * cl + h * LANES:panels + k * cl + (h + 1) * LANES]
            near_block(lambda k, rows: columns_ref[c, k, rows, :], source, cl, own_ref.at[c])
            total_ref[c] = self_product(pieces_ref[c], own_ref.at[c], cl)
    sources_ref[number * clusters] = jnp.zeros_like(sources_ref[0])
    for b, ref in enumerate(blocks):
        for c in range(clusters):
            for k in range(3):
                sources_ref[b * clusters + c, k:k + 1, :] = ref[c:c + 1, panels + k * cl:panels + (k + 1) * cl]

    def step(m, _):
        pairs = [pair_at(pairs_ref, which, group * m + w) for w in range(group)]
        parts = []
        for w, (c, j) in enumerate(pairs):
            source = lambda k, h: sources_ref[j, k:k + 1, h * LANES:(h + 1) * LANES]
            near_block(lambda k, rows: columns_ref[c, k, rows, :], source, cl, kept_ref.at[m, w])
            parts.append(near_product(pieces_ref[j], kept_ref.at[m, w], cl))
        for (c, j), part in zip(pairs, parts):
            total_ref[c] += part
        return 0

    lax.fori_loop(0, (pairs_ref[2 + which, 0] + group - 1) // group, step, 0)
    for c in range(clusters):
        lanes = slice(c * cl, (c + 1) * cl)
        near = folded(total_ref[c])
        near_out_ref[:, lanes] = start_ref[:, lanes] + near if which else near


def near_again_kernel(cl, which, number, pairs_ref, *refs):
    blocks = refs[:number]
    if which:
        start_ref, kept_ref, near_out_ref, pieces_ref, total_ref = refs[number:]
    else:
        _, own_ref, kept_ref, near_out_ref, tail_ref, pieces_ref, total_ref = refs[number:]
        tail_ref[...] = blocks[0][:, blocks[0].shape[1] - tail_ref.shape[1]:]
    clusters = near_out_ref.shape[1] // cl
    group = kept_ref.shape[1]
    fill_charges(pieces_ref, blocks, clusters, cl)
    if which:
        total_ref[...] = jnp.zeros_like(total_ref)
    else:
        for c in range(clusters):
            total_ref[c] = self_product(pieces_ref[c], own_ref.at[c], cl)

    def step(m, _):
        pairs = [pair_at(pairs_ref, which, group * m + w) for w in range(group)]
        parts = [near_product(pieces_ref[j], kept_ref.at[m, w], cl) for w, (c, j) in enumerate(pairs)]
        for (c, j), part in zip(pairs, parts):
            total_ref[c] += part
        return 0

    lax.fori_loop(0, (pairs_ref[2 + which, 0] + group - 1) // group, step, 0)
    for c in range(clusters):
        lanes = slice(c * cl, (c + 1) * cl)
        near = folded(total_ref[c])
        near_out_ref[:, lanes] = start_ref[:, lanes] + near if which else near


def load_window(tables, clusters, rank, pieces_ref, middle_ref):
    per = LANES // rank
    span = clusters * rank
    count = pieces_ref.shape[0] // per
    groups = span // LANES
    for at in range(count):
        (ref, first), g = tables[at // groups], at % groups
        tile = ref[:, first + g * LANES:first + (g + 1) * LANES]
        for s in range(per):
            pieces_ref[s * count + at] = stacked(pltpu.roll(tile, s * rank, 1) if s else tile)
        if middle_ref is not None:
            half = groups // 2
            row, lane = 8 * (g // half), first + span + g % half * LANES
            tile = ref[row:row + 8, lane:lane + LANES]
            for s in range(per):
                middle_ref[s * count + at] = pltpu.roll(tile, s * rank, 1) if s else tile


def six_tables(near_ref, far_ref, swapped_ref):
    width = near_ref.shape[1] // 2
    return (far_ref, 0), (far_ref, width), (near_ref, 0), (swapped_ref, width), (swapped_ref, 0), (swapped_ref, 3 * width)


def pick(source_ref, at_ref, c, g, per, lane):
    row = None
    for u in range(per):
        take = source_ref[at_ref[c, g * per + u]]
        row = take if row is None else jnp.where(lane == u, take, row)
    return row


def far_fields(gathered_ref, coupling_ref, fields_ref):
    for c in range(gathered_ref.shape[0]):
        field = quartered(dot_nt(gathered_ref[c], coupling_ref[c]))
        fields_ref[c] = stacked(jnp.concatenate([field, field], axis=1))


def far_potential(fields_ref, c, basis):
    return folded(dot_nn(fields_ref[c], basis))


def image_kernel(cl, rank, at_ref, near_pair_ref, far_pair_ref, swapped_ref, center_ref, area_ref, near_ref, basis_ref, krylov_ref, offsets_ref,
                 image_ref, payload_ref, heavy_ref, coupling_ref, pieces_ref, middle_ref, gathered_ref, fields_ref):
    rhs, panels = near_ref.shape
    clusters = panels // cl
    per = LANES // rank
    span = clusters * rank
    load_window(six_tables(near_pair_ref, far_pair_ref, swapped_ref), clusters, rank, pieces_ref, middle_ref)
    lane = lax.broadcasted_iota(jnp.int32, (1, LANES), 1) // rank
    for c in range(clusters):
        mine = [offsets_ref[3, k:k + 1, :] - center_ref[c:c + 1, k * LANES:(k + 1) * LANES] for k in range(3)]
        for g in range(at_ref.shape[1] // per):
            lanes = slice(g * LANES, (g + 1) * LANES)
            gathered_ref[c, :, lanes] = pick(pieces_ref, at_ref, c, g, per, lane)
            center = pick(middle_ref, at_ref, c, g, per, lane)
            gap = [(center[k:k + 1] + mine[k]) - offsets_ref[k] for k in range(3)]
            high, low = split(lax.rsqrt(gap[0] * gap[0] + gap[1] * gap[1] + gap[2] * gap[2] + SMOOTHING))
            coupling_ref[c, 0:rank, lanes] = high
            coupling_ref[c, rank:2 * rank, lanes] = low
    far_fields(gathered_ref, coupling_ref, fields_ref)
    squared = correlation = jnp.zeros((rhs, cl), F32)
    for c in range(clusters):
        lanes = slice(c * cl, (c + 1) * cl)
        basis = basis_ref[:, lanes]
        area = area_ref[c:c + 1, :]
        image = COULOMB * area * (near_ref[:, lanes] + far_potential(fields_ref, c, basis))
        charges = area * image
        image_ref[:, lanes] = image
        payload_ref[:, lanes] = charges
        heavy_ref[:, lanes] = charges
        payload_ref[:, panels + c * rank:panels + (c + 1) * rank] = moments_of(charges, basis)
        krylov = krylov_ref[:, lanes]
        squared = squared + krylov * krylov
        correlation = correlation + krylov * image
    squared = jnp.sum(squared, axis=1, keepdims=True)
    correlation = jnp.sum(correlation, axis=1, keepdims=True)
    local = ratio(correlation, squared)
    residual = image_ref[...] - local * krylov_ref[...]
    payload_ref[:, panels + span:] = in_lanes(squared, correlation, jnp.sum(residual * residual, axis=1, keepdims=True), local)


def far_again_kernel(cl, rank, at_ref, near_pair_ref, far_pair_ref, swapped_ref, near_ref, area_ref, coupling_ref, basis_ref,
                     image_ref, pieces_ref, gathered_ref, fields_ref):
    clusters = near_ref.shape[1] // cl
    per = LANES // rank
    load_window(six_tables(near_pair_ref, far_pair_ref, swapped_ref), clusters, rank, pieces_ref, None)
    lane = lax.broadcasted_iota(jnp.int32, (1, LANES), 1) // rank
    for c in range(clusters):
        for g in range(at_ref.shape[1] // per):
            gathered_ref[c, :, g * LANES:(g + 1) * LANES] = pick(pieces_ref, at_ref, c, g, per, lane)
    far_fields(gathered_ref, coupling_ref, fields_ref)
    for c in range(clusters):
        lanes = slice(c * cl, (c + 1) * cl)
        image_ref[:, lanes] = COULOMB * area_ref[c:c + 1, :] * (near_ref[:, lanes] + far_potential(fields_ref, c, basis_ref[:, lanes]))


def finish_kernel(total, one_ref, two_ref, image_ref, again_ref, krylov_ref, next_hbm, second_hbm, next_ref, second_ref, sems):
    squared, correlation, energy, local = merged([one_ref[...], two_ref[...]])
    projection = correlation / (squared + 1e-06)
    gap = projection - local
    scaling = 1.0 / jnp.sqrt((energy + gap * gap * squared) / total + 1e-06)
    moves = []
    part = next_ref.shape[1] // 4
    for h in range(4):
        lanes = slice(h * part, (h + 1) * part)
        image = image_ref[:, lanes]
        next_ref[:, lanes] = (image - projection * krylov_ref[:, lanes]) * scaling
        second_ref[:, lanes] = (again_ref[:, lanes] - projection * image) * scaling
        for held, hbm in ((next_ref, next_hbm), (second_ref, second_hbm)):
            moves.append(pltpu.make_async_copy(held.at[:, lanes], hbm.at[:, lanes], sems.at[len(moves)]))
            moves[-1].start()
    for move in moves:
        move.wait()


def ratio(correlation, squared):
    return jnp.where(squared > 0, correlation / jnp.where(squared > 0, squared, 1.0), 0.0)


def in_lanes(*columns):
    lane = lax.broadcasted_iota(jnp.int32, (columns[0].shape[0], LANES), 1)
    out = columns[-1]
    for i, column in enumerate(columns[:-1]):
        out = jnp.where(lane == i, column, out)
    return out


def merged(groups):
    squared = sum(group[:, 0:1] for group in groups)
    correlation = sum(group[:, 1:2] for group in groups)
    local = ratio(correlation, squared)
    energy = 0.0
    for group in groups:
        gap = local - group[:, 3:4]
        energy = energy + (group[:, 2:3] + gap * gap * group[:, 0:1])
    return squared, correlation, energy, local


def window_sums_kernel(payload_ref, partner_ref, near_pair_ref, far_pair_ref, swapped_ref, out_ref):
    width = near_pair_ref.shape[1] // 2
    ends = [(payload_ref, payload_ref.shape[1]), (partner_ref, partner_ref.shape[1])]
    ends += [(ref, end) for ref in (near_pair_ref, far_pair_ref, swapped_ref) for end in (width, 2 * width)]
    out_ref[...] = in_lanes(*merged([ref[:, end - LANES:end] for ref, end in ends]))


def merge_kernel(one_ref, two_ref, out_ref):
    out_ref[...] = in_lanes(*merged([one_ref[...], two_ref[...]]))


def call(kernel, outs, scratch, memory, *args, limit=10, us=1.0):
    spaces = {"s": pltpu.SMEM, "v": pltpu.VMEM, "p": pltpu.VMEM, "h": pltpu.HBM}
    ins, out_spaces = memory.split(">")
    pinned = {"h": pltpu.HBM, "p": pltpu.VMEM}
    return pl.pallas_call(
        kernel,
        out_shape=[pltpu.VMEM(*out) if m == "p" else jax.ShapeDtypeStruct(*out) for m, out in zip(out_spaces, outs)],
        in_specs=[pl.BlockSpec(memory_space=spaces[m]) for m in ins],
        out_specs=[pl.BlockSpec(memory_space=spaces[m]) for m in out_spaces],
        scratch_shapes=scratch,
        compiler_params=pltpu.CompilerParams(vmem_limit_bytes=limit * 2 ** 20),
        cost_estimate=pl.CostEstimate(flops=int(us * 5e8), bytes_accessed=int(us * 3.6e6), transcendentals=0),
    )(*(pltpu.with_memory_space_constraint(a, pinned[m]) if m in pinned else a for m, a in zip(ins, args)))


def body(vertices, panel_vertices, near_pairs, far_pairs, basis, krylov):
    clusters, slots = near_pairs.shape
    partners = far_pairs.shape[1]
    rhs, panels = krylov.shape
    rank = basis.shape[0]
    cl = panels // clusters
    vcl = vertices.shape[1] // clusters
    span = clusters * rank
    per = LANES // rank
    devices = lax.axis_size("clus")
    position = lax.axis_index("clus").reshape(1).astype(jnp.int32)
    offsets = proxy_offsets(rank)
    flat = np.concatenate([np.tile(offsets, (1, per)), np.zeros((rank - 3, LANES), np.float32)])
    offsets = jnp.asarray(np.concatenate([np.broadcast_to(offsets[:, :, None], (3, rank, LANES)), flat[None]]))
    width = span + span // 2
    pairing = [(i, i + 1 - 2 * (i % 2)) for i in range(devices)]
    bridging = [(i, i - 1 + 2 * (i % 2)) for i in range(1, devices - 1)] + [(0, 0), (devices - 1, devices - 1)]

    def move(value, pairs):
        return lax.ppermute(value, "clus", pairs)

    def outward(value, steps):
        return move(value, [(i, (i + steps * (1 - 2 * (i % 2))) % devices) for i in range(devices)])

    def exchange(payload, heavy):
        other = move(heavy, bridging)
        partner = move(payload, pairing)
        pair = jnp.concatenate([value[:, heavy.shape[1]:] for value in (payload, partner)], axis=1)
        return partner, other, outward(pair, 2), outward(pair, 4)

    def swapped(near_pair, far_pair, tail):
        return move(jnp.concatenate([near_pair, far_pair, tail], axis=1), pairing)

    whole = ((rhs, panels), F32)
    payload, heavy, area, centers, at, pairs, basis, krylov, offsets = call(
        functools.partial(prepare_kernel, cl, vcl, rank),
        [
            ((rhs, panels + 3 * cl + width), F32), ((rhs, panels + 3 * cl), F32), ((clusters, cl), F32), ((clusters, 3 * LANES), F32),
            (far_pairs.shape, jnp.int32), ((8, LANES), jnp.int32), ((2 * rank, panels), BF16), whole, (offsets.shape, F32),
        ],
        [
            pltpu.VMEM(vertices.shape, F32),
            pltpu.VMEM(panel_vertices.shape, jnp.int32),
            pltpu.VMEM(basis.shape, F32),
            pltpu.VMEM(far_pairs.shape, jnp.int32),
            pltpu.VMEM((slots, clusters), jnp.int32),
            pltpu.VMEM((3 * clusters, vcl), F32),
            pltpu.VMEM((3 * panels // LANES, LANES), jnp.int32),
            pltpu.SemaphoreType.DMA((7,)),
        ],
        "shhhhhhh>vvvvvvppp",
        position, vertices, panel_vertices, krylov, basis, far_pairs, near_pairs.T, offsets,
        us=1.5,
    )
    partner, other, near_pair, far_pair = exchange(payload, heavy)
    total = pltpu.VMEM((clusters, 2 * rhs, cl), F32)

    group = 4
    own = ((clusters, 2 * cl, cl), BF16)
    kept = ((clusters * (slots - 1) // group, group, 2 * cl, cl), BF16)

    def pieces(number):
        return pltpu.VMEM((number * clusters + 1, 2 * rhs, cl), BF16)

    def sources(number):
        return pltpu.VMEM((number * clusters + 1, 8, cl), F32)

    own_blocks, blocks, near, columns, tail = call(
        functools.partial(near_kernel, cl, 0, 1),
        [own, kept, whole, ((clusters, 3, cl, LANES), F32), ((rhs, LANES), F32)],
        [pieces(1), sources(1), total],
        "svv>ppvpv",
        pairs, payload, partner,
        us=8.0,
    )
    swap = swapped(near_pair, far_pair, tail)
    blocks_other, near = call(
        functools.partial(near_kernel, cl, 1, 2),
        [kept, whole],
        [pieces(2), sources(2), total],
        "svvpv>pv",
        pairs, partner, other, columns, near,
        us=4.0,
    )
    tiles = 6 * per * span // LANES
    window = pltpu.VMEM((tiles, 2 * rhs, LANES), BF16)
    gathered = pltpu.VMEM((clusters, 2 * rhs, partners * rank), BF16)
    fields = pltpu.VMEM((clusters, 2 * rhs, 2 * rank), BF16)
    image, payload, heavy, coupling = call(
        functools.partial(image_kernel, cl, rank),
        [whole, ((rhs, panels + span + LANES), F32), whole, ((clusters, 2 * rank, partners * rank), BF16)],
        [window, pltpu.VMEM((tiles, 8, LANES), F32), gathered, fields],
        "svvvvvvppp>vvvp",
        at, near_pair, far_pair, swap, centers, area, near, basis, krylov, offsets,
        us=4.5,
    )
    partner, other, near_pair, far_pair = exchange(payload, heavy)
    near, tail = call(
        functools.partial(near_again_kernel, cl, 0, 1),
        [whole, ((rhs, LANES), F32)],
        [pieces(1), total],
        "svvpp>vv",
        pairs, payload, partner, own_blocks, blocks,
        us=8.0,
    )
    swap = swapped(near_pair, far_pair, tail)
    (near,) = call(
        functools.partial(near_again_kernel, cl, 1, 2),
        [whole],
        [pieces(2), total],
        "svvvp>v",
        pairs, partner, other, near, blocks_other,
        us=2.0,
    )
    sums_shape = ((rhs, LANES), F32)
    (one,) = call(window_sums_kernel, [sums_shape], [], "vvvvv>v", payload, partner, near_pair, far_pair, swap, us=0.3)
    size = 8
    many = outward(one, size)
    while 2 * size < devices:
        (one,) = call(merge_kernel, [sums_shape], [], "vv>v", one, many, us=0.3)
        size = 2 * size
        many = outward(one, size)
    (again,) = call(
        functools.partial(far_again_kernel, cl, rank),
        [whole],
        [window, gathered, fields],
        "svvvvvpp>v",
        at, near_pair, far_pair, swap, near, area, coupling, basis,
        us=2.0,
    )
    here = pltpu.VMEM((rhs, panels), F32)
    return tuple(call(
        functools.partial(finish_kernel, panels * devices),
        [whole, whole],
        [here, here, pltpu.SemaphoreType.DMA((8,))],
        "vvvvp>hh",
        one, many, image, again, krylov,
    ))


def solution(mesh):
    whole = P(None, ("jobs", "clus"))
    rows = P(("jobs", "clus"), None)
    return jax.shard_map(
        body,
        mesh=mesh,
        in_specs=(whole, whole, rows, rows, whole, whole),
        out_specs=(whole, whole),
        check_vma=False,
    )
```

```python
import functools

import jax
import jax.numpy as jnp
import numpy as np
from jax import lax
from jax.experimental import pallas as pl
from jax.experimental.pallas import tpu as pltpu
from jax.sharding import PartitionSpec as P

REACH = 4
SMOOTHING = 0.04
COULOMB = 2.0
PROXY_RADIUS = 0.6
LANES = 128
FEATURES = 80
GRID = 1.5 * 2.0 ** 22
F32 = jnp.float32
BF16 = jnp.bfloat16


def proxy_offsets(points):
    counter = np.arange(points, dtype=np.float32)
    height = 1.0 - (2.0 * counter + 1.0) / points
    radial = np.sqrt(1.0 - height * height)
    azimuth = counter * 2.399963
    return PROXY_RADIUS * np.stack([radial * np.cos(azimuth), radial * np.sin(azimuth), height]).astype(np.float32)


def split(value):
    high = value.astype(BF16)
    return high, (value - high.astype(F32)).astype(BF16)


def stacked(value):
    return jnp.concatenate(split(value), axis=0)


def folded(value):
    half = value.shape[0] // 2
    return value[:half] + value[half:]


def dot_nt(left, right):
    return lax.dot_general(left, right, (((1,), (1,)), ((), ())), preferred_element_type=F32)


def dot_nn(left, right):
    return lax.dot_general(left, right, (((1,), (0,)), ((), ())), preferred_element_type=F32)


def quartered(value):
    half = value.shape[1] // 2
    value = folded(value)
    return value[:, 0:half] + value[:, half:]


def moments_of(weighted, basis_pieces):
    return quartered(dot_nt(stacked(weighted), basis_pieces))


def copies(pairs, sems):
    moves = [pltpu.make_async_copy(source, target, sems.at[i]) for i, (source, target) in enumerate(pairs)]
    for move in moves:
        move.start()
    return moves


def pair_list(near, position, clusters):
    block = lax.div(near, clusters) - position
    partner = block * (1 - 2 * lax.rem(position, 2)) > 0
    place = (lax.rem(near, clusters) + jnp.where((block != 0) & ~partner, clusters, 0)).astype(F32)
    across = lax.broadcasted_iota(jnp.int32, (clusters, clusters), 1)
    down = lax.broadcasted_iota(jnp.int32, (clusters, clusters), 0)
    upright = lambda value: jnp.sum(jnp.where(across == down, value, 0.0), axis=1, keepdims=True)
    row = lax.broadcasted_iota(jnp.int32, (clusters, LANES), 1).astype(F32)
    target = lax.broadcasted_iota(jnp.int32, (clusters, 1), 0).astype(F32)
    rows = lax.broadcasted_iota(jnp.int32, (8, LANES), 0)
    out = jnp.zeros((8, LANES), F32)
    for which in range(2):
        here = block != 0 if which else block == 0
        live = jnp.where(here & (near >= 0), 1.0, 0.0)
        counts = sum(live[k:k + 1] for k in range(1, near.shape[0]))
        first = jnp.sum(jnp.where(across < down, counts, 0.0), axis=1, keepdims=True)
        found = jnp.zeros((clusters, LANES), F32)
        for k in range(1, near.shape[0]):
            alive = upright(live[k:k + 1])
            hit = jnp.where(row == first, alive, 0.0)
            found = found + hit * (target * 64 + upright(place[k:k + 1]))
            first = first + alive
        count = jnp.sum(counts, axis=1, keepdims=True)
        found = jnp.where(row[0:1] < count, jnp.sum(found, axis=0, keepdims=True), (1.0 + which) * clusters)
        out = jnp.where(rows == which, found, jnp.where(rows == 2 + which, count, out))
    return out.astype(jnp.int32)


def prepare_kernel(cl, vcl, rank, position_ref, vertices_hbm, corners_hbm, krylov_hbm, basis_hbm, far_hbm, near_hbm, offsets_hbm,
                   payload_ref, heavy_ref, area_ref, center_ref, at_ref, pairs_ref, basis_ref, krylov_ref, offsets_ref,
                   vertices_ref, corners_ref, raw_ref, far_ref, near_ref, mesh_ref, local_ref, sems):
    moves = copies((
        (vertices_hbm, vertices_ref), (corners_hbm, corners_ref), (krylov_hbm, krylov_ref), (basis_hbm, raw_ref),
        (far_hbm, far_ref), (near_hbm, near_ref), (offsets_hbm, offsets_ref),
    ), sems)
    rhs, panels = krylov_ref.shape
    clusters = panels // cl
    parts = cl // LANES
    moves[0].wait()
    for c in range(clusters):
        mesh_ref[3 * c:3 * c + 3, :] = vertices_ref[:, c * vcl:(c + 1) * vcl]
    moves[1].wait()
    for i in range(clusters * parts):
        local_ref[3 * i:3 * i + 3, :] = corners_ref[:, i * LANES:(i + 1) * LANES]
    first = position_ref[0] * (vcl * clusters) + vcl * lax.broadcasted_iota(jnp.int32, (clusters, LANES), 0)
    tables = [mesh_ref[pl.ds(k, clusters, stride=3), :] for k in range(3)]
    sums = [None] * 3
    for h in range(parts):
        local = [local_ref[pl.ds(3 * h + m, clusters, stride=3 * parts), :] - first for m in range(3)]
        corner = [[jnp.take_along_axis(tables[k], local[m], axis=1, mode="promise_in_bounds") for k in range(3)] for m in range(3)]
        for k in range(3):
            middle = (corner[0][k] + corner[1][k] + corner[2][k]) / 3.0
            lanes = slice(panels + k * cl + h * LANES, panels + k * cl + (h + 1) * LANES)
            payload_ref[:, lanes] = middle
            heavy_ref[:, lanes] = middle
            sums[k] = middle if h == 0 else sums[k] + middle
        one = [corner[1][k] - corner[0][k] for k in range(3)]
        two = [corner[2][k] - corner[0][k] for k in range(3)]
        normal = [one[1] * two[2] - one[2] * two[1], one[2] * two[0] - one[0] * two[2], one[0] * two[1] - one[1] * two[0]]
        area_ref[:, h * LANES:(h + 1) * LANES] = 0.5 * jnp.sqrt(normal[0] * normal[0] + normal[1] * normal[1] + normal[2] * normal[2])
    span = clusters * rank
    table = panels + 3 * cl
    mine = lax.broadcasted_iota(jnp.int32, (clusters, span), 1) // rank == lax.broadcasted_iota(jnp.int32, (clusters, span), 0)
    half = span // 2
    payload_ref[:, table + span:] = jnp.zeros_like(payload_ref[:, table + span:])
    for k in range(3):
        center = jnp.sum(sums[k], axis=1, keepdims=True) / cl
        center_ref[:, k * LANES:(k + 1) * LANES] = jnp.broadcast_to(center, (clusters, LANES))
        row = jnp.sum(jnp.where(mine, center, 0.0), axis=0, keepdims=True)
        payload_ref[k:k + 1, table + span:] = row[:, 0:half]
        payload_ref[8 + k:9 + k, table + span:] = row[:, half:]
    moves[2].wait()
    moves[3].wait()
    for c in range(clusters):
        lanes = slice(c * cl, (c + 1) * cl)
        basis_ref[:, lanes] = stacked(raw_ref[:, lanes])
        charges = area_ref[c:c + 1, :] * krylov_ref[:, lanes]
        payload_ref[:, lanes] = charges
        heavy_ref[:, lanes] = charges
        payload_ref[:, table + c * rank:table + (c + 1) * rank] = moments_of(charges, basis_ref[:, lanes])
    moves[4].wait()
    far = far_ref[...]
    step = (lax.div(far, clusters) - position_ref[0]) * (1 - 2 * lax.rem(position_ref[0], 2))
    block = jnp.where(step < 0, step + REACH, step + REACH - 3)
    per = LANES // rank
    turn = lax.rem(lax.broadcasted_iota(jnp.int32, far.shape, 1) - far + per * clusters * 2 ** 16, per)
    at_ref[...] = (turn * 6 + block) * (span // LANES) + lax.div(lax.rem(far, clusters), per)
    moves[5].wait()
    pairs_ref[...] = pair_list(near_ref[...], position_ref[0], clusters)
    moves[6].wait()


def features_of(payload_ref, panels, c, cl, target):
    rows = [payload_ref[c:c + 1, panels + k * cl:panels + (k + 1) * cl] for k in range(3)]
    value = jnp.concatenate(rows + [jnp.zeros((5, cl), F32)], axis=0)
    coarse = (value + GRID) - GRID
    middle = (value - coarse).astype(BF16).astype(F32)
    low = (value - coarse - middle).astype(BF16).astype(F32)
    pieces = [coarse, middle, low]
    rest = middle + low
    row = lax.broadcasted_iota(jnp.int32, (8, cl), 0)
    square = jnp.sum(coarse * coarse, axis=0, keepdims=True)
    extra = jnp.sum((2.0 * coarse + rest) * rest, axis=0, keepdims=True) + (SMOOTHING if target else 0.0)
    square_high = square.astype(BF16).astype(F32)
    extra_high = extra.astype(BF16).astype(F32)
    extra_middle = (extra - extra_high).astype(BF16).astype(F32)
    ones = jnp.ones((1, cl), F32)

    def placed(base, start, *values):
        for i, one in enumerate(values):
            base = jnp.where(row == start + i, one, base)
        return base

    squares, extras = (square_high, square - square_high), (extra_high, extra_middle, extra - extra_high - extra_middle)
    if target:
        scaled = [-2.0 * piece for piece in pieces]
        first = placed(scaled[0], 3, *squares, ones, ones)
        last = placed(jnp.zeros((8, cl), F32), 0, *extras, ones, ones, ones)
    else:
        first = placed(coarse, 3, ones, ones, *squares)
        last = placed(jnp.zeros((8, cl), F32), 0, ones, ones, ones, *extras)
    combos = [(scaled[i] if target else pieces[j]) for i in range(3) for j in range(3) if i + j]
    return jnp.concatenate([first, *combos, last], axis=0)


def fill_features(sources_ref, blocks, panels, cl):
    clusters = panels // cl
    for b, ref in enumerate(blocks):
        for c in range(clusters):
            sources_ref[b * clusters + c] = features_of(ref, panels, c, cl, False).astype(BF16)
    sources_ref[len(blocks) * clusters] = sources_ref[0]


def near_block(target, source, out_ref):
    cl = target.shape[0]
    for first in range(0, cl, LANES):
        high, low = split(lax.rsqrt(dot_nn(target[first:first + LANES, :], source)))
        out_ref[first:first + LANES, :] = high
        out_ref[cl + first:cl + first + LANES, :] = low


def self_product(pieces, block_ref, cl):
    return dot_nn(pieces, block_ref[0:cl, :]) + dot_nn(pieces, block_ref[cl:2 * cl, :])


def near_product(pieces, block_ref, cl):
    return dot_nt(pieces, block_ref[0:cl, :]) + dot_nt(pieces, block_ref[cl:2 * cl, :])


def fill_charges(pieces_ref, blocks, clusters, cl):
    for b, ref in enumerate(blocks):
        for c in range(clusters):
            pieces_ref[b * clusters + c] = stacked(ref[:, c * cl:(c + 1) * cl])
    pieces_ref[len(blocks) * clusters] = jnp.zeros_like(pieces_ref[0])


def pair_at(pairs_ref, which, i):
    pair = pairs_ref[which, i]
    return lax.shift_right_logical(pair, 6), lax.bitwise_and(pair, 63)


def near_kernel(cl, which, number, pairs_ref, *refs):
    blocks = refs[:number]
    if which:
        targets_ref, start_ref, kept_ref, near_out_ref, pieces_ref, sources_ref, total_ref = refs[number:]
    else:
        _, own_ref, kept_ref, near_out_ref, targets_ref, tail_ref, pieces_ref, sources_ref, total_ref = refs[number:]
        tail_ref[...] = blocks[0][:, blocks[0].shape[1] - tail_ref.shape[1]:]
    panels = near_out_ref.shape[1]
    clusters = panels // cl
    group = kept_ref.shape[1]
    fill_charges(pieces_ref, blocks, clusters, cl)
    fill_features(sources_ref, blocks, panels, cl)
    if which:
        total_ref[...] = jnp.zeros_like(total_ref)
    else:
        for c in range(clusters):
            targets_ref[c] = jnp.transpose(features_of(blocks[0], panels, c, cl, True)).astype(BF16)
            near_block(targets_ref[c], sources_ref[c], own_ref.at[c])
            total_ref[c] = self_product(pieces_ref[c], own_ref.at[c], cl)
    def step(m, _):
        pairs = [pair_at(pairs_ref, which, group * m + w) for w in range(group)]
        parts = []
        for w, (c, j) in enumerate(pairs):
            near_block(targets_ref[c], sources_ref[j], kept_ref.at[m, w])
            parts.append(near_product(pieces_ref[j], kept_ref.at[m, w], cl))
        for (c, j), part in zip(pairs, parts):
            total_ref[c] += part
        return 0

    lax.fori_loop(0, (pairs_ref[2 + which, 0] + group - 1) // group, step, 0)
    for c in range(clusters):
        lanes = slice(c * cl, (c + 1) * cl)
        near = folded(total_ref[c])
        near_out_ref[:, lanes] = start_ref[:, lanes] + near if which else near


def near_again_kernel(cl, which, number, pairs_ref, *refs):
    blocks = refs[:number]
    if which:
        start_ref, kept_ref, near_out_ref, pieces_ref, total_ref = refs[number:]
    else:
        _, own_ref, kept_ref, near_out_ref, tail_ref, pieces_ref, total_ref = refs[number:]
        tail_ref[...] = blocks[0][:, blocks[0].shape[1] - tail_ref.shape[1]:]
    clusters = near_out_ref.shape[1] // cl
    group = kept_ref.shape[1]
    fill_charges(pieces_ref, blocks, clusters, cl)
    if which:
        total_ref[...] = jnp.zeros_like(total_ref)
    else:
        for c in range(clusters):
            total_ref[c] = self_product(pieces_ref[c], own_ref.at[c], cl)

    def step(m, _):
        pairs = [pair_at(pairs_ref, which, group * m + w) for w in range(group)]
        parts = [near_product(pieces_ref[j], kept_ref.at[m, w], cl) for w, (c, j) in enumerate(pairs)]
        for (c, j), part in zip(pairs, parts):
            total_ref[c] += part
        return 0

    lax.fori_loop(0, (pairs_ref[2 + which, 0] + group - 1) // group, step, 0)
    for c in range(clusters):
        lanes = slice(c * cl, (c + 1) * cl)
        near = folded(total_ref[c])
        near_out_ref[:, lanes] = start_ref[:, lanes] + near if which else near


def load_window(tables, clusters, rank, pieces_ref, middle_ref):
    per = LANES // rank
    span = clusters * rank
    count = pieces_ref.shape[0] // per
    groups = span // LANES
    for at in range(count):
        (ref, first), g = tables[at // groups], at % groups
        tile = ref[:, first + g * LANES:first + (g + 1) * LANES]
        for s in range(per):
            pieces_ref[s * count + at] = stacked(pltpu.roll(tile, s * rank, 1) if s else tile)
        if middle_ref is not None:
            half = groups // 2
            row, lane = 8 * (g // half), first + span + g % half * LANES
            tile = ref[row:row + 8, lane:lane + LANES]
            for s in range(per):
                middle_ref[s * count + at] = pltpu.roll(tile, s * rank, 1) if s else tile


def six_tables(near_ref, far_ref, swapped_ref):
    width = near_ref.shape[1] // 2
    return (far_ref, 0), (far_ref, width), (near_ref, 0), (swapped_ref, width), (swapped_ref, 0), (swapped_ref, 3 * width)


def pick(source_ref, at_ref, c, g, per, lane):
    row = None
    for u in range(per):
        take = source_ref[at_ref[c, g * per + u]]
        row = take if row is None else jnp.where(lane == u, take, row)
    return row


def far_fields(gathered_ref, coupling_ref, fields_ref):
    for c in range(gathered_ref.shape[0]):
        field = quartered(dot_nt(gathered_ref[c], coupling_ref[c]))
        fields_ref[c] = stacked(jnp.concatenate([field, field], axis=1))


def far_potential(fields_ref, c, basis):
    return folded(dot_nn(fields_ref[c], basis))


def image_kernel(cl, rank, at_ref, near_pair_ref, far_pair_ref, swapped_ref, center_ref, area_ref, near_ref, basis_ref, krylov_ref, offsets_ref,
                 image_ref, payload_ref, heavy_ref, coupling_ref, pieces_ref, middle_ref, gathered_ref, fields_ref):
    rhs, panels = near_ref.shape
    clusters = panels // cl
    per = LANES // rank
    span = clusters * rank
    load_window(six_tables(near_pair_ref, far_pair_ref, swapped_ref), clusters, rank, pieces_ref, middle_ref)
    lane = lax.broadcasted_iota(jnp.int32, (1, LANES), 1) // rank
    for c in range(clusters):
        mine = [offsets_ref[3, k:k + 1, :] - center_ref[c:c + 1, k * LANES:(k + 1) * LANES] for k in range(3)]
        for g in range(at_ref.shape[1] // per):
            lanes = slice(g * LANES, (g + 1) * LANES)
            gathered_ref[c, :, lanes] = pick(pieces_ref, at_ref, c, g, per, lane)
            center = pick(middle_ref, at_ref, c, g, per, lane)
            gap = [(center[k:k + 1] + mine[k]) - offsets_ref[k] for k in range(3)]
            high, low = split(lax.rsqrt(gap[0] * gap[0] + gap[1] * gap[1] + gap[2] * gap[2] + SMOOTHING))
            coupling_ref[c, 0:rank, lanes] = high
            coupling_ref[c, rank:2 * rank, lanes] = low
    far_fields(gathered_ref, coupling_ref, fields_ref)
    squared = correlation = jnp.zeros((rhs, cl), F32)
    for c in range(clusters):
        lanes = slice(c * cl, (c + 1) * cl)
        basis = basis_ref[:, lanes]
        area = area_ref[c:c + 1, :]
        image = COULOMB * area * (near_ref[:, lanes] + far_potential(fields_ref, c, basis))
        charges = area * image
        image_ref[:, lanes] = image
        payload_ref[:, lanes] = charges
        heavy_ref[:, lanes] = charges
        payload_ref[:, panels + c * rank:panels + (c + 1) * rank] = moments_of(charges, basis)
        krylov = krylov_ref[:, lanes]
        squared = squared + krylov * krylov
        correlation = correlation + krylov * image
    squared = jnp.sum(squared, axis=1, keepdims=True)
    correlation = jnp.sum(correlation, axis=1, keepdims=True)
    local = ratio(correlation, squared)
    residual = image_ref[...] - local * krylov_ref[...]
    payload_ref[:, panels + span:] = in_lanes(squared, correlation, jnp.sum(residual * residual, axis=1, keepdims=True), local)


def far_again_kernel(cl, rank, at_ref, near_pair_ref, far_pair_ref, swapped_ref, near_ref, area_ref, coupling_ref, basis_ref,
                     image_ref, pieces_ref, gathered_ref, fields_ref):
    clusters = near_ref.shape[1] // cl
    per = LANES // rank
    load_window(six_tables(near_pair_ref, far_pair_ref, swapped_ref), clusters, rank, pieces_ref, None)
    lane = lax.broadcasted_iota(jnp.int32, (1, LANES), 1) // rank
    for c in range(clusters):
        for g in range(at_ref.shape[1] // per):
            gathered_ref[c, :, g * LANES:(g + 1) * LANES] = pick(pieces_ref, at_ref, c, g, per, lane)
    far_fields(gathered_ref, coupling_ref, fields_ref)
    for c in range(clusters):
        lanes = slice(c * cl, (c + 1) * cl)
        image_ref[:, lanes] = COULOMB * area_ref[c:c + 1, :] * (near_ref[:, lanes] + far_potential(fields_ref, c, basis_ref[:, lanes]))


def finish_kernel(total, one_ref, two_ref, image_ref, again_ref, krylov_ref, next_hbm, second_hbm, next_ref, second_ref, sems):
    squared, correlation, energy, local = merged([one_ref[...], two_ref[...]])
    projection = correlation / (squared + 1e-06)
    gap = projection - local
    scaling = 1.0 / jnp.sqrt((energy + gap * gap * squared) / total + 1e-06)
    moves = []
    part = next_ref.shape[1] // 4
    for h in range(4):
        lanes = slice(h * part, (h + 1) * part)
        image = image_ref[:, lanes]
        next_ref[:, lanes] = (image - projection * krylov_ref[:, lanes]) * scaling
        second_ref[:, lanes] = (again_ref[:, lanes] - projection * image) * scaling
        for held, hbm in ((next_ref, next_hbm), (second_ref, second_hbm)):
            moves.append(pltpu.make_async_copy(held.at[:, lanes], hbm.at[:, lanes], sems.at[len(moves)]))
            moves[-1].start()
    for move in moves:
        move.wait()


def ratio(correlation, squared):
    return jnp.where(squared > 0, correlation / jnp.where(squared > 0, squared, 1.0), 0.0)


def in_lanes(*columns):
    lane = lax.broadcasted_iota(jnp.int32, (columns[0].shape[0], LANES), 1)
    out = columns[-1]
    for i, column in enumerate(columns[:-1]):
        out = jnp.where(lane == i, column, out)
    return out


def merged(groups):
    squared = sum(group[:, 0:1] for group in groups)
    correlation = sum(group[:, 1:2] for group in groups)
    local = ratio(correlation, squared)
    energy = 0.0
    for group in groups:
        gap = local - group[:, 3:4]
        energy = energy + (group[:, 2:3] + gap * gap * group[:, 0:1])
    return squared, correlation, energy, local


def window_sums_kernel(payload_ref, partner_ref, near_pair_ref, far_pair_ref, swapped_ref, out_ref):
    width = near_pair_ref.shape[1] // 2
    ends = [(payload_ref, payload_ref.shape[1]), (partner_ref, partner_ref.shape[1])]
    ends += [(ref, end) for ref in (near_pair_ref, far_pair_ref, swapped_ref) for end in (width, 2 * width)]
    out_ref[...] = in_lanes(*merged([ref[:, end - LANES:end] for ref, end in ends]))


def merge_kernel(one_ref, two_ref, out_ref):
    out_ref[...] = in_lanes(*merged([one_ref[...], two_ref[...]]))


def call(kernel, outs, scratch, memory, *args, limit=10, us=1.0):
    spaces = {"s": pltpu.SMEM, "v": pltpu.VMEM, "p": pltpu.VMEM, "h": pltpu.HBM}
    ins, out_spaces = memory.split(">")
    pinned = {"h": pltpu.HBM, "p": pltpu.VMEM}
    return pl.pallas_call(
        kernel,
        out_shape=[pltpu.VMEM(*out) if m == "p" else jax.ShapeDtypeStruct(*out) for m, out in zip(out_spaces, outs)],
        in_specs=[pl.BlockSpec(memory_space=spaces[m]) for m in ins],
        out_specs=[pl.BlockSpec(memory_space=spaces[m]) for m in out_spaces],
        scratch_shapes=scratch,
        compiler_params=pltpu.CompilerParams(vmem_limit_bytes=limit * 2 ** 20),
        cost_estimate=pl.CostEstimate(flops=int(us * 5e8), bytes_accessed=int(us * 3.6e6), transcendentals=0),
    )(*(pltpu.with_memory_space_constraint(a, pinned[m]) if m in pinned else a for m, a in zip(ins, args)))


def body(vertices, panel_vertices, near_pairs, far_pairs, basis, krylov):
    clusters, slots = near_pairs.shape
    partners = far_pairs.shape[1]
    rhs, panels = krylov.shape
    rank = basis.shape[0]
    cl = panels // clusters
    vcl = vertices.shape[1] // clusters
    span = clusters * rank
    per = LANES // rank
    devices = lax.axis_size("clus")
    position = lax.axis_index("clus").reshape(1).astype(jnp.int32)
    offsets = proxy_offsets(rank)
    flat = np.concatenate([np.tile(offsets, (1, per)), np.zeros((rank - 3, LANES), np.float32)])
    offsets = jnp.asarray(np.concatenate([np.broadcast_to(offsets[:, :, None], (3, rank, LANES)), flat[None]]))
    width = span + span // 2
    pairing = [(i, i + 1 - 2 * (i % 2)) for i in range(devices)]
    bridging = [(i, i - 1 + 2 * (i % 2)) for i in range(1, devices - 1)] + [(0, 0), (devices - 1, devices - 1)]

    def move(value, pairs):
        return lax.ppermute(value, "clus", pairs)

    def outward(value, steps):
        return move(value, [(i, (i + steps * (1 - 2 * (i % 2))) % devices) for i in range(devices)])

    def exchange(payload, heavy):
        other = move(heavy, bridging)
        partner = move(payload, pairing)
        pair = jnp.concatenate([value[:, heavy.shape[1]:] for value in (payload, partner)], axis=1)
        return partner, other, outward(pair, 2), outward(pair, 4)

    def swapped(near_pair, far_pair, tail):
        return move(jnp.concatenate([near_pair, far_pair, tail], axis=1), pairing)

    whole = ((rhs, panels), F32)
    payload, heavy, area, centers, at, pairs, basis, krylov, offsets = call(
        functools.partial(prepare_kernel, cl, vcl, rank),
        [
            ((rhs, panels + 3 * cl + width), F32), ((rhs, panels + 3 * cl), F32), ((clusters, cl), F32), ((clusters, 3 * LANES), F32),
            (far_pairs.shape, jnp.int32), ((8, LANES), jnp.int32), ((2 * rank, panels), BF16), whole, (offsets.shape, F32),
        ],
        [
            pltpu.VMEM(vertices.shape, F32),
            pltpu.VMEM(panel_vertices.shape, jnp.int32),
            pltpu.VMEM(basis.shape, F32),
            pltpu.VMEM(far_pairs.shape, jnp.int32),
            pltpu.VMEM((slots, clusters), jnp.int32),
            pltpu.VMEM((3 * clusters, vcl), F32),
            pltpu.VMEM((3 * panels // LANES, LANES), jnp.int32),
            pltpu.SemaphoreType.DMA((7,)),
        ],
        "shhhhhhh>vvvvvvppp",
        position, vertices, panel_vertices, krylov, basis, far_pairs, near_pairs.T, offsets,
        us=1.5,
    )
    partner, other, near_pair, far_pair = exchange(payload, heavy)
    total = pltpu.VMEM((clusters, 2 * rhs, cl), F32)

    group = 4
    own = ((clusters, 2 * cl, cl), BF16)
    kept = ((clusters * (slots - 1) // group, group, 2 * cl, cl), BF16)

    def pieces(number):
        return pltpu.VMEM((number * clusters + 1, 2 * rhs, cl), BF16)

    def sources(number):
        return pltpu.VMEM((number * clusters + 1, FEATURES, cl), BF16)

    own_blocks, blocks, near, targets, tail = call(
        functools.partial(near_kernel, cl, 0, 1),
        [own, kept, whole, ((clusters, cl, FEATURES), BF16), ((rhs, LANES), F32)],
        [pieces(1), sources(1), total],
        "svv>ppvpv",
        pairs, payload, partner,
        us=8.0,
    )
    swap = swapped(near_pair, far_pair, tail)
    blocks_other, near = call(
        functools.partial(near_kernel, cl, 1, 2),
        [kept, whole],
        [pieces(2), sources(2), total],
        "svvpv>pv",
        pairs, partner, other, targets, near,
        us=4.0,
    )
    tiles = 6 * per * span // LANES
    window = pltpu.VMEM((tiles, 2 * rhs, LANES), BF16)
    gathered = pltpu.VMEM((clusters, 2 * rhs, partners * rank), BF16)
    fields = pltpu.VMEM((clusters, 2 * rhs, 2 * rank), BF16)
    image, payload, heavy, coupling = call(
        functools.partial(image_kernel, cl, rank),
        [whole, ((rhs, panels + span + LANES), F32), whole, ((clusters, 2 * rank, partners * rank), BF16)],
        [window, pltpu.VMEM((tiles, 8, LANES), F32), gathered, fields],
        "svvvvvvppp>vvvp",
        at, near_pair, far_pair, swap, centers, area, near, basis, krylov, offsets,
        us=4.5,
    )
    partner, other, near_pair, far_pair = exchange(payload, heavy)
    near, tail = call(
        functools.partial(near_again_kernel, cl, 0, 1),
        [whole, ((rhs, LANES), F32)],
        [pieces(1), total],
        "svvpp>vv",
        pairs, payload, partner, own_blocks, blocks,
        us=8.0,
    )
    swap = swapped(near_pair, far_pair, tail)
    (near,) = call(
        functools.partial(near_again_kernel, cl, 1, 2),
        [whole],
        [pieces(2), total],
        "svvvp>v",
        pairs, partner, other, near, blocks_other,
        us=2.0,
    )
    sums_shape = ((rhs, LANES), F32)
    (one,) = call(window_sums_kernel, [sums_shape], [], "vvvvv>v", payload, partner, near_pair, far_pair, swap, us=0.3)
    size = 8
    many = outward(one, size)
    while 2 * size < devices:
        (one,) = call(merge_kernel, [sums_shape], [], "vv>v", one, many, us=0.3)
        size = 2 * size
        many = outward(one, size)
    (again,) = call(
        functools.partial(far_again_kernel, cl, rank),
        [whole],
        [window, gathered, fields],
        "svvvvvpp>v",
        at, near_pair, far_pair, swap, near, area, coupling, basis,
        us=2.0,
    )
    here = pltpu.VMEM((rhs, panels), F32)
    return tuple(call(
        functools.partial(finish_kernel, panels * devices),
        [whole, whole],
        [here, here, pltpu.SemaphoreType.DMA((8,))],
        "vvvvp>hh",
        one, many, image, again, krylov,
    ))


def solution(mesh):
    whole = P(None, ("jobs", "clus"))
    rows = P(("jobs", "clus"), None)
    return jax.shard_map(
        body,
        mesh=mesh,
        in_specs=(whole, whole, rows, rows, whole, whole),
        out_specs=(whole, whole),
        check_vma=False,
    )
```

```python
import functools

import jax
import jax.numpy as jnp
import numpy as np
from jax import lax
from jax.experimental import pallas as pl
from jax.experimental.pallas import tpu as pltpu
from jax.sharding import PartitionSpec as P

REACH = 4
SMOOTHING = 0.04
COULOMB = 2.0
PROXY_RADIUS = 0.6
LANES = 128
FEATURES = 80
GRID = 1.5 * 2.0 ** 22
F32 = jnp.float32
BF16 = jnp.bfloat16


def proxy_offsets(points):
    counter = np.arange(points, dtype=np.float32)
    height = 1.0 - (2.0 * counter + 1.0) / points
    radial = np.sqrt(1.0 - height * height)
    azimuth = counter * 2.399963
    return PROXY_RADIUS * np.stack([radial * np.cos(azimuth), radial * np.sin(azimuth), height]).astype(np.float32)


def split(value):
    high = value.astype(BF16)
    return high, (value - high.astype(F32)).astype(BF16)


def stacked(value):
    return jnp.concatenate(split(value), axis=0)


def folded(value):
    half = value.shape[0] // 2
    return value[:half] + value[half:]


def dot_nt(left, right):
    return lax.dot_general(left, right, (((1,), (1,)), ((), ())), preferred_element_type=F32)


def dot_nn(left, right):
    return lax.dot_general(left, right, (((1,), (0,)), ((), ())), preferred_element_type=F32)


def quartered(value):
    half = value.shape[1] // 2
    value = folded(value)
    return value[:, 0:half] + value[:, half:]


def moments_of(weighted, basis_pieces):
    return quartered(dot_nt(stacked(weighted), basis_pieces))


def copies(pairs, sems):
    moves = [pltpu.make_async_copy(source, target, sems.at[i]) for i, (source, target) in enumerate(pairs)]
    for move in moves:
        move.start()
    return moves


def pair_list(near, position, clusters):
    block = lax.div(near, clusters) - position
    partner = block * (1 - 2 * lax.rem(position, 2)) > 0
    place = (lax.rem(near, clusters) + jnp.where((block != 0) & ~partner, clusters, 0)).astype(F32)
    across = lax.broadcasted_iota(jnp.int32, (clusters, clusters), 1)
    down = lax.broadcasted_iota(jnp.int32, (clusters, clusters), 0)
    upright = lambda value: jnp.sum(jnp.where(across == down, value, 0.0), axis=1, keepdims=True)
    row = lax.broadcasted_iota(jnp.int32, (clusters, LANES), 1).astype(F32)
    target = lax.broadcasted_iota(jnp.int32, (clusters, 1), 0).astype(F32)
    rows = lax.broadcasted_iota(jnp.int32, (8, LANES), 0)
    out = jnp.zeros((8, LANES), F32)
    for which in range(2):
        here = block != 0 if which else block == 0
        live = jnp.where(here & (near >= 0), 1.0, 0.0)
        counts = sum(live[k:k + 1] for k in range(1, near.shape[0]))
        first = jnp.sum(jnp.where(across < down, counts, 0.0), axis=1, keepdims=True)
        found = jnp.zeros((clusters, LANES), F32)
        for k in range(1, near.shape[0]):
            alive = upright(live[k:k + 1])
            hit = jnp.where(row == first, alive, 0.0)
            found = found + hit * (target * 64 + upright(place[k:k + 1]))
            first = first + alive
        count = jnp.sum(counts, axis=1, keepdims=True)
        found = jnp.where(row[0:1] < count, jnp.sum(found, axis=0, keepdims=True), (1.0 + which) * clusters)
        out = jnp.where(rows == which, found, jnp.where(rows == 2 + which, count, out))
    return out.astype(jnp.int32)


def prepare_kernel(cl, vcl, rank, position_ref, vertices_hbm, corners_hbm, krylov_hbm, basis_hbm, far_hbm, near_hbm, offsets_hbm,
                   payload_ref, heavy_ref, area_ref, center_ref, at_ref, pairs_ref, basis_ref, krylov_ref, offsets_ref,
                   vertices_ref, corners_ref, raw_ref, far_ref, near_ref, mesh_ref, local_ref, sems):
    moves = copies((
        (vertices_hbm, vertices_ref), (corners_hbm, corners_ref), (krylov_hbm, krylov_ref), (basis_hbm, raw_ref),
        (far_hbm, far_ref), (near_hbm, near_ref), (offsets_hbm, offsets_ref),
    ), sems)
    rhs, panels = krylov_ref.shape
    clusters = panels // cl
    parts = cl // LANES
    moves[0].wait()
    for c in range(clusters):
        mesh_ref[3 * c:3 * c + 3, :] = vertices_ref[:, c * vcl:(c + 1) * vcl]
    moves[1].wait()
    for i in range(clusters * parts):
        local_ref[3 * i:3 * i + 3, :] = corners_ref[:, i * LANES:(i + 1) * LANES]
    first = position_ref[0] * (vcl * clusters) + vcl * lax.broadcasted_iota(jnp.int32, (clusters, LANES), 0)
    tables = [mesh_ref[pl.ds(k, clusters, stride=3), :] for k in range(3)]
    sums = [None] * 3
    for h in range(parts):
        local = [local_ref[pl.ds(3 * h + m, clusters, stride=3 * parts), :] - first for m in range(3)]
        corner = [[jnp.take_along_axis(tables[k], local[m], axis=1, mode="promise_in_bounds") for k in range(3)] for m in range(3)]
        for k in range(3):
            middle = (corner[0][k] + corner[1][k] + corner[2][k]) / 3.0
            lanes = slice(panels + k * cl + h * LANES, panels + k * cl + (h + 1) * LANES)
            payload_ref[:, lanes] = middle
            heavy_ref[:, lanes] = middle
            sums[k] = middle if h == 0 else sums[k] + middle
        one = [corner[1][k] - corner[0][k] for k in range(3)]
        two = [corner[2][k] - corner[0][k] for k in range(3)]
        normal = [one[1] * two[2] - one[2] * two[1], one[2] * two[0] - one[0] * two[2], one[0] * two[1] - one[1] * two[0]]
        area_ref[:, h * LANES:(h + 1) * LANES] = 0.5 * jnp.sqrt(normal[0] * normal[0] + normal[1] * normal[1] + normal[2] * normal[2])
    span = clusters * rank
    table = panels + 3 * cl
    mine = lax.broadcasted_iota(jnp.int32, (clusters, span), 1) // rank == lax.broadcasted_iota(jnp.int32, (clusters, span), 0)
    half = span // 2
    payload_ref[:, table + span:] = jnp.zeros_like(payload_ref[:, table + span:])
    for k in range(3):
        center = jnp.sum(sums[k], axis=1, keepdims=True) / cl
        center_ref[:, k * LANES:(k + 1) * LANES] = jnp.broadcast_to(center, (clusters, LANES))
        row = jnp.sum(jnp.where(mine, center, 0.0), axis=0, keepdims=True)
        payload_ref[k:k + 1, table + span:] = row[:, 0:half]
        payload_ref[8 + k:9 + k, table + span:] = row[:, half:]
    moves[2].wait()
    moves[3].wait()
    for c in range(clusters):
        lanes = slice(c * cl, (c + 1) * cl)
        basis_ref[:, lanes] = stacked(raw_ref[:, lanes])
        charges = area_ref[c:c + 1, :] * krylov_ref[:, lanes]
        payload_ref[:, lanes] = charges
        heavy_ref[:, lanes] = charges
        payload_ref[:, table + c * rank:table + (c + 1) * rank] = moments_of(charges, basis_ref[:, lanes])
    moves[4].wait()
    far = far_ref[...]
    step = (lax.div(far, clusters) - position_ref[0]) * (1 - 2 * lax.rem(position_ref[0], 2))
    block = jnp.where(step < 0, step + REACH, step + REACH - 3)
    per = LANES // rank
    turn = lax.rem(lax.broadcasted_iota(jnp.int32, far.shape, 1) - far + per * clusters * 2 ** 16, per)
    at_ref[...] = (turn * 6 + block) * (span // LANES) + lax.div(lax.rem(far, clusters), per)
    moves[5].wait()
    pairs_ref[...] = pair_list(near_ref[...], position_ref[0], clusters)
    moves[6].wait()


def features_of(payload_ref, panels, c, cl, target):
    rows = [payload_ref[c:c + 1, panels + k * cl:panels + (k + 1) * cl] for k in range(3)]
    value = jnp.concatenate(rows + [jnp.zeros((5, cl), F32)], axis=0)
    coarse = (value + GRID) - GRID
    middle = (value - coarse).astype(BF16).astype(F32)
    low = (value - coarse - middle).astype(BF16).astype(F32)
    pieces = [coarse, middle, low]
    rest = middle + low
    row = lax.broadcasted_iota(jnp.int32, (8, cl), 0)
    square = jnp.sum(coarse * coarse, axis=0, keepdims=True)
    extra = jnp.sum((2.0 * coarse + rest) * rest, axis=0, keepdims=True) + (SMOOTHING if target else 0.0)
    square_high = square.astype(BF16).astype(F32)
    extra_high = extra.astype(BF16).astype(F32)
    extra_middle = (extra - extra_high).astype(BF16).astype(F32)
    ones = jnp.ones((1, cl), F32)

    def placed(base, start, *values):
        for i, one in enumerate(values):
            base = jnp.where(row == start + i, one, base)
        return base

    squares, extras = (square_high, square - square_high), (extra_high, extra_middle, extra - extra_high - extra_middle)
    if target:
        scaled = [-2.0 * piece for piece in pieces]
        first = placed(scaled[0], 3, *squares, ones, ones)
        last = placed(jnp.zeros((8, cl), F32), 0, *extras, ones, ones, ones)
    else:
        first = placed(coarse, 3, ones, ones, *squares)
        last = placed(jnp.zeros((8, cl), F32), 0, ones, ones, ones, *extras)
    combos = [(scaled[i] if target else pieces[j]) for i in range(3) for j in range(3) if i + j]
    return jnp.concatenate([first, *combos, last], axis=0)


def fill_features(sources_ref, blocks, panels, cl):
    clusters = panels // cl
    for b, ref in enumerate(blocks):
        for c in range(clusters):
            sources_ref[b * clusters + c] = features_of(ref, panels, c, cl, False).astype(BF16)
    sources_ref[len(blocks) * clusters] = sources_ref[0]


def near_block(target, source, pieces, out_ref, symmetric):
    cl = target.shape[0]
    parts = []
    for first in range(0, cl, LANES):
        rows = slice(first, first + LANES)
        high, low = split(lax.rsqrt(dot_nn(target[rows, :], source)))
        out_ref[rows, :] = high
        out_ref[cl + first:cl + first + LANES, :] = low
        if symmetric:
            parts.append(dot_nn(pieces[:, rows], high) + dot_nn(pieces[:, rows], low))
        else:
            parts.append(dot_nt(pieces, high) + dot_nt(pieces, low))
    return sum(parts[1:], parts[0]) if symmetric else jnp.concatenate(parts, axis=1)


def self_product(pieces, block_ref, cl):
    return dot_nn(pieces, block_ref[0:cl, :]) + dot_nn(pieces, block_ref[cl:2 * cl, :])


def near_product(pieces, block_ref, cl):
    return dot_nt(pieces, block_ref[0:cl, :]) + dot_nt(pieces, block_ref[cl:2 * cl, :])


def fill_charges(pieces_ref, blocks, clusters, cl):
    for b, ref in enumerate(blocks):
        for c in range(clusters):
            pieces_ref[b * clusters + c] = stacked(ref[:, c * cl:(c + 1) * cl])
    pieces_ref[len(blocks) * clusters] = jnp.zeros_like(pieces_ref[0])


def pair_at(pairs_ref, which, i):
    pair = pairs_ref[which, i]
    return lax.shift_right_logical(pair, 6), lax.bitwise_and(pair, 63)


def near_kernel(cl, which, number, pairs_ref, *refs):
    blocks = refs[:number]
    if which:
        targets_ref, start_ref, kept_ref, near_out_ref, pieces_ref, sources_ref, total_ref = refs[number:]
    else:
        _, own_ref, kept_ref, near_out_ref, targets_ref, tail_ref, pieces_ref, sources_ref, total_ref = refs[number:]
        tail_ref[...] = blocks[0][:, blocks[0].shape[1] - tail_ref.shape[1]:]
    panels = near_out_ref.shape[1]
    clusters = panels // cl
    group = kept_ref.shape[1]
    fill_charges(pieces_ref, blocks, clusters, cl)
    fill_features(sources_ref, blocks, panels, cl)
    if which:
        total_ref[...] = jnp.zeros_like(total_ref)
    else:
        for c in range(clusters):
            target = jnp.transpose(features_of(blocks[0], panels, c, cl, True)).astype(BF16)
            targets_ref[c] = target
            total_ref[c] = near_block(target, sources_ref[c], pieces_ref[c], own_ref.at[c], True)
    def step(m, _):
        pairs = [pair_at(pairs_ref, which, group * m + w) for w in range(group)]
        loaded = [(targets_ref[c], sources_ref[j], pieces_ref[j]) for c, j in pairs]
        parts = [near_block(*one, kept_ref.at[m, w], False) for w, one in enumerate(loaded)]
        for (c, j), part in zip(pairs, parts):
            total_ref[c] += part
        return 0

    lax.fori_loop(0, (pairs_ref[2 + which, 0] + group - 1) // group, step, 0)
    for c in range(clusters):
        lanes = slice(c * cl, (c + 1) * cl)
        near = folded(total_ref[c])
        near_out_ref[:, lanes] = start_ref[:, lanes] + near if which else near


def near_again_kernel(cl, which, number, pairs_ref, *refs):
    blocks = refs[:number]
    if which:
        start_ref, kept_ref, near_out_ref, pieces_ref, total_ref = refs[number:]
    else:
        _, own_ref, kept_ref, near_out_ref, tail_ref, pieces_ref, total_ref = refs[number:]
        tail_ref[...] = blocks[0][:, blocks[0].shape[1] - tail_ref.shape[1]:]
    clusters = near_out_ref.shape[1] // cl
    group = kept_ref.shape[1]
    fill_charges(pieces_ref, blocks, clusters, cl)
    if which:
        total_ref[...] = jnp.zeros_like(total_ref)
    else:
        for c in range(clusters):
            total_ref[c] = self_product(pieces_ref[c], own_ref.at[c], cl)

    def step(m, _):
        pairs = [pair_at(pairs_ref, which, group * m + w) for w in range(group)]
        parts = [near_product(pieces_ref[j], kept_ref.at[m, w], cl) for w, (c, j) in enumerate(pairs)]
        for (c, j), part in zip(pairs, parts):
            total_ref[c] += part
        return 0

    lax.fori_loop(0, (pairs_ref[2 + which, 0] + group - 1) // group, step, 0)
    for c in range(clusters):
        lanes = slice(c * cl, (c + 1) * cl)
        near = folded(total_ref[c])
        near_out_ref[:, lanes] = start_ref[:, lanes] + near if which else near


def load_window(tables, clusters, rank, pieces_ref, middle_ref):
    per = LANES // rank
    span = clusters * rank
    count = pieces_ref.shape[0] // per
    groups = span // LANES
    for at in range(count):
        (ref, first), g = tables[at // groups], at % groups
        tile = ref[:, first + g * LANES:first + (g + 1) * LANES]
        for s in range(per):
            pieces_ref[s * count + at] = stacked(pltpu.roll(tile, s * rank, 1) if s else tile)
        if middle_ref is not None:
            half = groups // 2
            row, lane = 8 * (g // half), first + span + g % half * LANES
            tile = ref[row:row + 8, lane:lane + LANES]
            for s in range(per):
                middle_ref[s * count + at] = pltpu.roll(tile, s * rank, 1) if s else tile


def six_tables(near_ref, far_ref, swapped_ref):
    width = near_ref.shape[1] // 2
    return (far_ref, 0), (far_ref, width), (near_ref, 0), (swapped_ref, width), (swapped_ref, 0), (swapped_ref, 3 * width)


def pick(source_ref, at_ref, c, g, per, lane):
    row = None
    for u in range(per):
        take = source_ref[at_ref[c, g * per + u]]
        row = take if row is None else jnp.where(lane == u, take, row)
    return row


def far_fields(gathered_ref, coupling_ref, fields_ref):
    for c in range(gathered_ref.shape[0]):
        field = quartered(dot_nt(gathered_ref[c], coupling_ref[c]))
        fields_ref[c] = stacked(jnp.concatenate([field, field], axis=1))


def far_potential(fields_ref, c, basis):
    return folded(dot_nn(fields_ref[c], basis))


def image_kernel(cl, rank, at_ref, near_pair_ref, far_pair_ref, swapped_ref, center_ref, area_ref, near_ref, basis_ref, krylov_ref, offsets_ref,
                 image_ref, payload_ref, heavy_ref, coupling_ref, pieces_ref, middle_ref, gathered_ref, fields_ref):
    rhs, panels = near_ref.shape
    clusters = panels // cl
    per = LANES // rank
    span = clusters * rank
    load_window(six_tables(near_pair_ref, far_pair_ref, swapped_ref), clusters, rank, pieces_ref, middle_ref)
    lane = lax.broadcasted_iota(jnp.int32, (1, LANES), 1) // rank
    for c in range(clusters):
        mine = [offsets_ref[3, k:k + 1, :] - center_ref[c:c + 1, k * LANES:(k + 1) * LANES] for k in range(3)]
        for g in range(at_ref.shape[1] // per):
            lanes = slice(g * LANES, (g + 1) * LANES)
            gathered_ref[c, :, lanes] = pick(pieces_ref, at_ref, c, g, per, lane)
            center = pick(middle_ref, at_ref, c, g, per, lane)
            gap = [(center[k:k + 1] + mine[k]) - offsets_ref[k] for k in range(3)]
            high, low = split(lax.rsqrt(gap[0] * gap[0] + gap[1] * gap[1] + gap[2] * gap[2] + SMOOTHING))
            coupling_ref[c, 0:rank, lanes] = high
            coupling_ref[c, rank:2 * rank, lanes] = low
    far_fields(gathered_ref, coupling_ref, fields_ref)
    squared = correlation = jnp.zeros((rhs, cl), F32)
    for c in range(clusters):
        lanes = slice(c * cl, (c + 1) * cl)
        basis = basis_ref[:, lanes]
        area = area_ref[c:c + 1, :]
        image = COULOMB * area * (near_ref[:, lanes] + far_potential(fields_ref, c, basis))
        charges = area * image
        image_ref[:, lanes] = image
        payload_ref[:, lanes] = charges
        heavy_ref[:, lanes] = charges
        payload_ref[:, panels + c * rank:panels + (c + 1) * rank] = moments_of(charges, basis)
        krylov = krylov_ref[:, lanes]
        squared = squared + krylov * krylov
        correlation = correlation + krylov * image
    squared = jnp.sum(squared, axis=1, keepdims=True)
    correlation = jnp.sum(correlation, axis=1, keepdims=True)
    local = ratio(correlation, squared)
    residual = image_ref[...] - local * krylov_ref[...]
    payload_ref[:, panels + span:] = in_lanes(squared, correlation, jnp.sum(residual * residual, axis=1, keepdims=True), local)


def far_again_kernel(cl, rank, at_ref, near_pair_ref, far_pair_ref, swapped_ref, near_ref, area_ref, coupling_ref, basis_ref,
                     image_ref, pieces_ref, gathered_ref, fields_ref):
    clusters = near_ref.shape[1] // cl
    per = LANES // rank
    load_window(six_tables(near_pair_ref, far_pair_ref, swapped_ref), clusters, rank, pieces_ref, None)
    lane = lax.broadcasted_iota(jnp.int32, (1, LANES), 1) // rank
    for c in range(clusters):
        for g in range(at_ref.shape[1] // per):
            gathered_ref[c, :, g * LANES:(g + 1) * LANES] = pick(pieces_ref, at_ref, c, g, per, lane)
    far_fields(gathered_ref, coupling_ref, fields_ref)
    for c in range(clusters):
        lanes = slice(c * cl, (c + 1) * cl)
        image_ref[:, lanes] = COULOMB * area_ref[c:c + 1, :] * (near_ref[:, lanes] + far_potential(fields_ref, c, basis_ref[:, lanes]))


def finish_kernel(total, one_ref, two_ref, image_ref, again_ref, krylov_ref, next_hbm, second_hbm, next_ref, second_ref, sems):
    squared, correlation, energy, local = merged([one_ref[...], two_ref[...]])
    projection = correlation / (squared + 1e-06)
    gap = projection - local
    scaling = 1.0 / jnp.sqrt((energy + gap * gap * squared) / total + 1e-06)
    moves = []
    part = next_ref.shape[1] // 4
    for h in range(4):
        lanes = slice(h * part, (h + 1) * part)
        image = image_ref[:, lanes]
        next_ref[:, lanes] = (image - projection * krylov_ref[:, lanes]) * scaling
        second_ref[:, lanes] = (again_ref[:, lanes] - projection * image) * scaling
        for held, hbm in ((next_ref, next_hbm), (second_ref, second_hbm)):
            moves.append(pltpu.make_async_copy(held.at[:, lanes], hbm.at[:, lanes], sems.at[len(moves)]))
            moves[-1].start()
    for move in moves:
        move.wait()


def ratio(correlation, squared):
    return jnp.where(squared > 0, correlation / jnp.where(squared > 0, squared, 1.0), 0.0)


def in_lanes(*columns):
    lane = lax.broadcasted_iota(jnp.int32, (columns[0].shape[0], LANES), 1)
    out = columns[-1]
    for i, column in enumerate(columns[:-1]):
        out = jnp.where(lane == i, column, out)
    return out


def merged(groups):
    squared = sum(group[:, 0:1] for group in groups)
    correlation = sum(group[:, 1:2] for group in groups)
    local = ratio(correlation, squared)
    energy = 0.0
    for group in groups:
        gap = local - group[:, 3:4]
        energy = energy + (group[:, 2:3] + gap * gap * group[:, 0:1])
    return squared, correlation, energy, local


def window_sums_kernel(payload_ref, partner_ref, near_pair_ref, far_pair_ref, swapped_ref, out_ref):
    width = near_pair_ref.shape[1] // 2
    ends = [(payload_ref, payload_ref.shape[1]), (partner_ref, partner_ref.shape[1])]
    ends += [(ref, end) for ref in (near_pair_ref, far_pair_ref, swapped_ref) for end in (width, 2 * width)]
    out_ref[...] = in_lanes(*merged([ref[:, end - LANES:end] for ref, end in ends]))


def merge_kernel(one_ref, two_ref, out_ref):
    out_ref[...] = in_lanes(*merged([one_ref[...], two_ref[...]]))


def call(kernel, outs, scratch, memory, *args, limit=10, us=1.0):
    spaces = {"s": pltpu.SMEM, "v": pltpu.VMEM, "p": pltpu.VMEM, "h": pltpu.HBM}
    ins, out_spaces = memory.split(">")
    pinned = {"h": pltpu.HBM, "p": pltpu.VMEM}
    return pl.pallas_call(
        kernel,
        out_shape=[pltpu.VMEM(*out) if m == "p" else jax.ShapeDtypeStruct(*out) for m, out in zip(out_spaces, outs)],
        in_specs=[pl.BlockSpec(memory_space=spaces[m]) for m in ins],
        out_specs=[pl.BlockSpec(memory_space=spaces[m]) for m in out_spaces],
        scratch_shapes=scratch,
        compiler_params=pltpu.CompilerParams(vmem_limit_bytes=limit * 2 ** 20),
        cost_estimate=pl.CostEstimate(flops=int(us * 5e8), bytes_accessed=int(us * 3.6e6), transcendentals=0),
    )(*(pltpu.with_memory_space_constraint(a, pinned[m]) if m in pinned else a for m, a in zip(ins, args)))


def body(vertices, panel_vertices, near_pairs, far_pairs, basis, krylov):
    clusters, slots = near_pairs.shape
    partners = far_pairs.shape[1]
    rhs, panels = krylov.shape
    rank = basis.shape[0]
    cl = panels // clusters
    vcl = vertices.shape[1] // clusters
    span = clusters * rank
    per = LANES // rank
    devices = lax.axis_size("clus")
    position = lax.axis_index("clus").reshape(1).astype(jnp.int32)
    offsets = proxy_offsets(rank)
    flat = np.concatenate([np.tile(offsets, (1, per)), np.zeros((rank - 3, LANES), np.float32)])
    offsets = jnp.asarray(np.concatenate([np.broadcast_to(offsets[:, :, None], (3, rank, LANES)), flat[None]]))
    width = span + span // 2
    pairing = [(i, i + 1 - 2 * (i % 2)) for i in range(devices)]
    bridging = [(i, i - 1 + 2 * (i % 2)) for i in range(1, devices - 1)] + [(0, 0), (devices - 1, devices - 1)]

    def move(value, pairs):
        return lax.ppermute(value, "clus", pairs)

    def outward(value, steps):
        return move(value, [(i, (i + steps * (1 - 2 * (i % 2))) % devices) for i in range(devices)])

    def exchange(payload, heavy):
        other = move(heavy, bridging)
        partner = move(payload, pairing)
        pair = jnp.concatenate([value[:, heavy.shape[1]:] for value in (payload, partner)], axis=1)
        return partner, other, outward(pair, 2), outward(pair, 4)

    def swapped(near_pair, far_pair, tail):
        return move(jnp.concatenate([near_pair, far_pair, tail], axis=1), pairing)

    whole = ((rhs, panels), F32)
    payload, heavy, area, centers, at, pairs, basis, krylov, offsets = call(
        functools.partial(prepare_kernel, cl, vcl, rank),
        [
            ((rhs, panels + 3 * cl + width), F32), ((rhs, panels + 3 * cl), F32), ((clusters, cl), F32), ((clusters, 3 * LANES), F32),
            (far_pairs.shape, jnp.int32), ((8, LANES), jnp.int32), ((2 * rank, panels), BF16), whole, (offsets.shape, F32),
        ],
        [
            pltpu.VMEM(vertices.shape, F32),
            pltpu.VMEM(panel_vertices.shape, jnp.int32),
            pltpu.VMEM(basis.shape, F32),
            pltpu.VMEM(far_pairs.shape, jnp.int32),
            pltpu.VMEM((slots, clusters), jnp.int32),
            pltpu.VMEM((3 * clusters, vcl), F32),
            pltpu.VMEM((3 * panels // LANES, LANES), jnp.int32),
            pltpu.SemaphoreType.DMA((7,)),
        ],
        "shhhhhhh>vvvvvvppp",
        position, vertices, panel_vertices, krylov, basis, far_pairs, near_pairs.T, offsets,
        us=1.5,
    )
    partner, other, near_pair, far_pair = exchange(payload, heavy)
    total = pltpu.VMEM((clusters, 2 * rhs, cl), F32)

    group = 4
    own = ((clusters, 2 * cl, cl), BF16)
    kept = ((clusters * (slots - 1) // group, group, 2 * cl, cl), BF16)

    def pieces(number):
        return pltpu.VMEM((number * clusters + 1, 2 * rhs, cl), BF16)

    def sources(number):
        return pltpu.VMEM((number * clusters + 1, FEATURES, cl), BF16)

    own_blocks, blocks, near, targets, tail = call(
        functools.partial(near_kernel, cl, 0, 1),
        [own, kept, whole, ((clusters, cl, FEATURES), BF16), ((rhs, LANES), F32)],
        [pieces(1), sources(1), total],
        "svv>ppvpv",
        pairs, payload, partner,
        us=8.0,
    )
    swap = swapped(near_pair, far_pair, tail)
    blocks_other, near = call(
        functools.partial(near_kernel, cl, 1, 2),
        [kept, whole],
        [pieces(2), sources(2), total],
        "svvpv>pv",
        pairs, partner, other, targets, near,
        us=4.0,
    )
    tiles = 6 * per * span // LANES
    window = pltpu.VMEM((tiles, 2 * rhs, LANES), BF16)
    gathered = pltpu.VMEM((clusters, 2 * rhs, partners * rank), BF16)
    fields = pltpu.VMEM((clusters, 2 * rhs, 2 * rank), BF16)
    image, payload, heavy, coupling = call(
        functools.partial(image_kernel, cl, rank),
        [whole, ((rhs, panels + span + LANES), F32), whole, ((clusters, 2 * rank, partners * rank), BF16)],
        [window, pltpu.VMEM((tiles, 8, LANES), F32), gathered, fields],
        "svvvvvvppp>vvvp",
        at, near_pair, far_pair, swap, centers, area, near, basis, krylov, offsets,
        us=4.5,
    )
    partner, other, near_pair, far_pair = exchange(payload, heavy)
    near, tail = call(
        functools.partial(near_again_kernel, cl, 0, 1),
        [whole, ((rhs, LANES), F32)],
        [pieces(1), total],
        "svvpp>vv",
        pairs, payload, partner, own_blocks, blocks,
        us=8.0,
    )
    swap = swapped(near_pair, far_pair, tail)
    (near,) = call(
        functools.partial(near_again_kernel, cl, 1, 2),
        [whole],
        [pieces(2), total],
        "svvvp>v",
        pairs, partner, other, near, blocks_other,
        us=2.0,
    )
    sums_shape = ((rhs, LANES), F32)
    (one,) = call(window_sums_kernel, [sums_shape], [], "vvvvv>v", payload, partner, near_pair, far_pair, swap, us=0.3)
    size = 8
    many = outward(one, size)
    while 2 * size < devices:
        (one,) = call(merge_kernel, [sums_shape], [], "vv>v", one, many, us=0.3)
        size = 2 * size
        many = outward(one, size)
    (again,) = call(
        functools.partial(far_again_kernel, cl, rank),
        [whole],
        [window, gathered, fields],
        "svvvvvpp>v",
        at, near_pair, far_pair, swap, near, area, coupling, basis,
        us=2.0,
    )
    here = pltpu.VMEM((rhs, panels), F32)
    return tuple(call(
        functools.partial(finish_kernel, panels * devices),
        [whole, whole],
        [here, here, pltpu.SemaphoreType.DMA((8,))],
        "vvvvp>hh",
        one, many, image, again, krylov,
    ))


def solution(mesh):
    whole = P(None, ("jobs", "clus"))
    rows = P(("jobs", "clus"), None)
    return jax.shard_map(
        body,
        mesh=mesh,
        in_specs=(whole, whole, rows, rows, whole, whole),
        out_specs=(whole, whole),
        check_vma=False,
    )
```

```python
import functools

import jax
import jax.numpy as jnp
import numpy as np
from jax import lax
from jax.experimental import pallas as pl
from jax.experimental.pallas import tpu as pltpu
from jax.sharding import PartitionSpec as P

REACH = 4
SMOOTHING = 0.04
COULOMB = 2.0
PROXY_RADIUS = 0.6
LANES = 128
FEATURES = 80
GRID = 1.5 * 2.0 ** 22
F32 = jnp.float32
BF16 = jnp.bfloat16


def proxy_offsets(points):
    counter = np.arange(points, dtype=np.float32)
    height = 1.0 - (2.0 * counter + 1.0) / points
    radial = np.sqrt(1.0 - height * height)
    azimuth = counter * 2.399963
    return PROXY_RADIUS * np.stack([radial * np.cos(azimuth), radial * np.sin(azimuth), height]).astype(np.float32)


def split(value):
    high = value.astype(BF16)
    return high, (value - high.astype(F32)).astype(BF16)


def stacked(value):
    return jnp.concatenate(split(value), axis=0)


def folded(value):
    half = value.shape[0] // 2
    return value[:half] + value[half:]


def dot_nt(left, right):
    return lax.dot_general(left, right, (((1,), (1,)), ((), ())), preferred_element_type=F32)


def dot_tn(left, right):
    return lax.dot_general(left, right, (((0,), (0,)), ((), ())), preferred_element_type=F32)


def dot_nn(left, right):
    return lax.dot_general(left, right, (((1,), (0,)), ((), ())), preferred_element_type=F32)


def quartered(value):
    half = value.shape[1] // 2
    value = folded(value)
    return value[:, 0:half] + value[:, half:]


def moments_of(weighted, basis_pieces):
    return quartered(dot_nt(stacked(weighted), basis_pieces))


def copies(pairs, sems):
    moves = [pltpu.make_async_copy(source, target, sems.at[i]) for i, (source, target) in enumerate(pairs)]
    for move in moves:
        move.start()
    return moves


def pair_list(near, position, clusters):
    block = lax.div(near, clusters) - position
    partner = block * (1 - 2 * lax.rem(position, 2)) > 0
    place = (lax.rem(near, clusters) + jnp.where((block != 0) & ~partner, clusters, 0)).astype(F32)
    across = lax.broadcasted_iota(jnp.int32, (clusters, clusters), 1)
    down = lax.broadcasted_iota(jnp.int32, (clusters, clusters), 0)
    upright = lambda value: jnp.sum(jnp.where(across == down, value, 0.0), axis=1, keepdims=True)
    row = lax.broadcasted_iota(jnp.int32, (clusters, LANES), 1).astype(F32)
    target = lax.broadcasted_iota(jnp.int32, (clusters, 1), 0).astype(F32)
    rows = lax.broadcasted_iota(jnp.int32, (8, LANES), 0)
    out = jnp.zeros((8, LANES), F32)
    for which in range(2):
        here = block != 0 if which else block == 0
        live = jnp.where(here & (near >= 0), 1.0, 0.0)
        counts = sum(live[k:k + 1] for k in range(1, near.shape[0]))
        first = jnp.sum(jnp.where(across < down, counts, 0.0), axis=1, keepdims=True)
        found = jnp.zeros((clusters, LANES), F32)
        for k in range(1, near.shape[0]):
            alive = upright(live[k:k + 1])
            hit = jnp.where(row == first, alive, 0.0)
            found = found + hit * (target * 64 + upright(place[k:k + 1]))
            first = first + alive
        count = jnp.sum(counts, axis=1, keepdims=True)
        found = jnp.where(row[0:1] < count, jnp.sum(found, axis=0, keepdims=True), (1.0 + which) * clusters)
        out = jnp.where(rows == which, found, jnp.where(rows == 2 + which, count, out))
    return out.astype(jnp.int32)


def prepare_kernel(cl, vcl, rank, position_ref, vertices_hbm, corners_hbm, krylov_hbm, basis_hbm, far_hbm, near_hbm, offsets_hbm,
                   payload_ref, heavy_ref, area_ref, center_ref, at_ref, pairs_ref, basis_ref, krylov_ref, offsets_ref,
                   vertices_ref, corners_ref, raw_ref, far_ref, near_ref, mesh_ref, local_ref, sems):
    moves = copies((
        (vertices_hbm, vertices_ref), (corners_hbm, corners_ref), (krylov_hbm, krylov_ref), (basis_hbm, raw_ref),
        (far_hbm, far_ref), (near_hbm, near_ref), (offsets_hbm, offsets_ref),
    ), sems)
    rhs, panels = krylov_ref.shape
    clusters = panels // cl
    parts = cl // LANES
    moves[0].wait()
    for c in range(clusters):
        mesh_ref[3 * c:3 * c + 3, :] = vertices_ref[:, c * vcl:(c + 1) * vcl]
    moves[1].wait()
    for i in range(clusters * parts):
        local_ref[3 * i:3 * i + 3, :] = corners_ref[:, i * LANES:(i + 1) * LANES]
    first = position_ref[0] * (vcl * clusters) + vcl * lax.broadcasted_iota(jnp.int32, (clusters, LANES), 0)
    tables = [mesh_ref[pl.ds(k, clusters, stride=3), :] for k in range(3)]
    sums = [None] * 3
    for h in range(parts):
        local = [local_ref[pl.ds(3 * h + m, clusters, stride=3 * parts), :] - first for m in range(3)]
        corner = [[jnp.take_along_axis(tables[k], local[m], axis=1, mode="promise_in_bounds") for k in range(3)] for m in range(3)]
        for k in range(3):
            middle = (corner[0][k] + corner[1][k] + corner[2][k]) / 3.0
            lanes = slice(panels + k * cl + h * LANES, panels + k * cl + (h + 1) * LANES)
            payload_ref[:, lanes] = middle
            heavy_ref[:, lanes] = middle
            sums[k] = middle if h == 0 else sums[k] + middle
        one = [corner[1][k] - corner[0][k] for k in range(3)]
        two = [corner[2][k] - corner[0][k] for k in range(3)]
        normal = [one[1] * two[2] - one[2] * two[1], one[2] * two[0] - one[0] * two[2], one[0] * two[1] - one[1] * two[0]]
        area_ref[:, h * LANES:(h + 1) * LANES] = 0.5 * jnp.sqrt(normal[0] * normal[0] + normal[1] * normal[1] + normal[2] * normal[2])
    span = clusters * rank
    table = panels + 3 * cl
    mine = lax.broadcasted_iota(jnp.int32, (clusters, span), 1) // rank == lax.broadcasted_iota(jnp.int32, (clusters, span), 0)
    half = span // 2
    payload_ref[:, table + span:] = jnp.zeros_like(payload_ref[:, table + span:])
    for k in range(3):
        center = jnp.sum(sums[k], axis=1, keepdims=True) / cl
        center_ref[:, k * LANES:(k + 1) * LANES] = jnp.broadcast_to(center, (clusters, LANES))
        row = jnp.sum(jnp.where(mine, center, 0.0), axis=0, keepdims=True)
        payload_ref[k:k + 1, table + span:] = row[:, 0:half]
        payload_ref[8 + k:9 + k, table + span:] = row[:, half:]
    moves[2].wait()
    moves[3].wait()
    for c in range(clusters):
        lanes = slice(c * cl, (c + 1) * cl)
        basis_ref[:, lanes] = stacked(raw_ref[:, lanes])
        charges = area_ref[c:c + 1, :] * krylov_ref[:, lanes]
        payload_ref[:, lanes] = charges
        heavy_ref[:, lanes] = charges
        payload_ref[:, table + c * rank:table + (c + 1) * rank] = moments_of(charges, basis_ref[:, lanes])
    moves[4].wait()
    far = far_ref[...]
    step = (lax.div(far, clusters) - position_ref[0]) * (1 - 2 * lax.rem(position_ref[0], 2))
    block = jnp.where(step < 0, step + REACH, step + REACH - 3)
    per = LANES // rank
    turn = lax.rem(lax.broadcasted_iota(jnp.int32, far.shape, 1) - far + per * clusters * 2 ** 16, per)
    at_ref[...] = (turn * 6 + block) * (span // LANES) + lax.div(lax.rem(far, clusters), per)
    moves[5].wait()
    pairs_ref[...] = pair_list(near_ref[...], position_ref[0], clusters)
    moves[6].wait()


def features_of(payload_ref, panels, c, cl, target):
    rows = [payload_ref[c:c + 1, panels + k * cl:panels + (k + 1) * cl] for k in range(3)]
    value = jnp.concatenate(rows + [jnp.zeros((5, cl), F32)], axis=0)
    coarse = (value + GRID) - GRID
    middle = (value - coarse).astype(BF16).astype(F32)
    low = (value - coarse - middle).astype(BF16).astype(F32)
    pieces = [coarse, middle, low]
    rest = middle + low
    row = lax.broadcasted_iota(jnp.int32, (8, cl), 0)
    square = jnp.sum(coarse * coarse, axis=0, keepdims=True)
    extra = jnp.sum((2.0 * coarse + rest) * rest, axis=0, keepdims=True) + (SMOOTHING if target else 0.0)
    square_high = square.astype(BF16).astype(F32)
    extra_high = extra.astype(BF16).astype(F32)
    extra_middle = (extra - extra_high).astype(BF16).astype(F32)
    ones = jnp.ones((1, cl), F32)

    def placed(base, start, *values):
        for i, one in enumerate(values):
            base = jnp.where(row == start + i, one, base)
        return base

    squares, extras = (square_high, square - square_high), (extra_high, extra_middle, extra - extra_high - extra_middle)
    if target:
        scaled = [-2.0 * piece for piece in pieces]
        first = placed(scaled[0], 3, *squares, ones, ones)
        last = placed(jnp.zeros((8, cl), F32), 0, *extras, ones, ones, ones)
    else:
        first = placed(coarse, 3, ones, ones, *squares)
        last = placed(jnp.zeros((8, cl), F32), 0, ones, ones, ones, *extras)
    combos = [(scaled[i] if target else pieces[j]) for i in range(3) for j in range(3) if i + j]
    return jnp.concatenate([first, *combos, last], axis=0)


def fill_features(sources_ref, blocks, panels, cl):
    clusters = panels // cl
    for b, ref in enumerate(blocks):
        for c in range(clusters):
            sources_ref[b * clusters + c] = features_of(ref, panels, c, cl, False).astype(BF16)
    sources_ref[len(blocks) * clusters] = sources_ref[0]


def near_block(source, target, pieces, out_ref):
    cl = source.shape[1]
    parts = []
    for first in range(0, cl, LANES):
        rows = slice(first, first + LANES)
        high, low = split(lax.rsqrt(dot_tn(source[:, rows], target)))
        out_ref[rows, :] = high
        out_ref[cl + first:cl + first + LANES, :] = low
        parts.append(dot_nn(pieces[:, rows], high) + dot_nn(pieces[:, rows], low))
    return sum(parts[1:], parts[0])


def near_product(pieces, block_ref, cl):
    return dot_nn(pieces, block_ref[0:cl, :]) + dot_nn(pieces, block_ref[cl:2 * cl, :])


def fill_charges(pieces_ref, blocks, clusters, cl):
    for b, ref in enumerate(blocks):
        for c in range(clusters):
            pieces_ref[b * clusters + c] = stacked(ref[:, c * cl:(c + 1) * cl])
    pieces_ref[len(blocks) * clusters] = jnp.zeros_like(pieces_ref[0])


def pair_at(pairs_ref, which, i):
    pair = pairs_ref[which, i]
    return lax.shift_right_logical(pair, 6), lax.bitwise_and(pair, 63)


def near_kernel(cl, which, number, pairs_ref, *refs):
    blocks = refs[:number]
    if which:
        targets_ref, start_ref, kept_ref, near_out_ref, pieces_ref, sources_ref, total_ref = refs[number:]
    else:
        _, own_ref, kept_ref, near_out_ref, targets_ref, tail_ref, pieces_ref, sources_ref, total_ref = refs[number:]
        tail_ref[...] = blocks[0][:, blocks[0].shape[1] - tail_ref.shape[1]:]
    panels = near_out_ref.shape[1]
    clusters = panels // cl
    group = kept_ref.shape[1]
    fill_charges(pieces_ref, blocks, clusters, cl)
    fill_features(sources_ref, blocks, panels, cl)
    if which:
        total_ref[...] = jnp.zeros_like(total_ref)
    else:
        for c in range(clusters):
            target = features_of(blocks[0], panels, c, cl, True).astype(BF16)
            targets_ref[c] = target
            total_ref[c] = near_block(sources_ref[c], target, pieces_ref[c], own_ref.at[c])
    def step(m, _):
        pairs = [pair_at(pairs_ref, which, group * m + w) for w in range(group)]
        loaded = [(sources_ref[j], targets_ref[c], pieces_ref[j]) for c, j in pairs]
        parts = [near_block(*one, kept_ref.at[m, w]) for w, one in enumerate(loaded)]
        for (c, j), part in zip(pairs, parts):
            total_ref[c] += part
        return 0

    lax.fori_loop(0, (pairs_ref[2 + which, 0] + group - 1) // group, step, 0)
    for c in range(clusters):
        lanes = slice(c * cl, (c + 1) * cl)
        near = folded(total_ref[c])
        near_out_ref[:, lanes] = start_ref[:, lanes] + near if which else near


def near_again_kernel(cl, which, number, pairs_ref, *refs):
    blocks = refs[:number]
    if which:
        start_ref, kept_ref, near_out_ref, pieces_ref, total_ref = refs[number:]
    else:
        _, own_ref, kept_ref, near_out_ref, tail_ref, pieces_ref, total_ref = refs[number:]
        tail_ref[...] = blocks[0][:, blocks[0].shape[1] - tail_ref.shape[1]:]
    clusters = near_out_ref.shape[1] // cl
    group = kept_ref.shape[1]
    fill_charges(pieces_ref, blocks, clusters, cl)
    if which:
        total_ref[...] = jnp.zeros_like(total_ref)
    else:
        for c in range(clusters):
            total_ref[c] = near_product(pieces_ref[c], own_ref.at[c], cl)

    def step(m, _):
        pairs = [pair_at(pairs_ref, which, group * m + w) for w in range(group)]
        parts = [near_product(pieces_ref[j], kept_ref.at[m, w], cl) for w, (c, j) in enumerate(pairs)]
        for (c, j), part in zip(pairs, parts):
            total_ref[c] += part
        return 0

    lax.fori_loop(0, (pairs_ref[2 + which, 0] + group - 1) // group, step, 0)
    for c in range(clusters):
        lanes = slice(c * cl, (c + 1) * cl)
        near = folded(total_ref[c])
        near_out_ref[:, lanes] = start_ref[:, lanes] + near if which else near


def load_window(tables, clusters, rank, pieces_ref, middle_ref):
    per = LANES // rank
    span = clusters * rank
    count = pieces_ref.shape[0] // per
    groups = span // LANES
    for at in range(count):
        (ref, first), g = tables[at // groups], at % groups
        tile = ref[:, first + g * LANES:first + (g + 1) * LANES]
        for s in range(per):
            pieces_ref[s * count + at] = stacked(pltpu.roll(tile, s * rank, 1) if s else tile)
        if middle_ref is not None:
            half = groups // 2
            row, lane = 8 * (g // half), first + span + g % half * LANES
            tile = ref[row:row + 8, lane:lane + LANES]
            for s in range(per):
                middle_ref[s * count + at] = pltpu.roll(tile, s * rank, 1) if s else tile


def six_tables(near_ref, far_ref, swapped_ref):
    width = near_ref.shape[1] // 2
    return (far_ref, 0), (far_ref, width), (near_ref, 0), (swapped_ref, width), (swapped_ref, 0), (swapped_ref, 3 * width)


def pick(source_ref, at_ref, c, g, per, lane):
    row = None
    for u in range(per):
        take = source_ref[at_ref[c, g * per + u]]
        row = take if row is None else jnp.where(lane == u, take, row)
    return row


def far_fields(gathered_ref, coupling_ref, fields_ref):
    for c in range(gathered_ref.shape[0]):
        field = quartered(dot_nt(gathered_ref[c], coupling_ref[c]))
        fields_ref[c] = stacked(jnp.concatenate([field, field], axis=1))


def far_potential(fields_ref, c, basis):
    return folded(dot_nn(fields_ref[c], basis))


def image_kernel(cl, rank, at_ref, near_pair_ref, far_pair_ref, swapped_ref, center_ref, area_ref, near_ref, basis_ref, krylov_ref, offsets_ref,
                 image_ref, payload_ref, heavy_ref, coupling_ref, pieces_ref, middle_ref, gathered_ref, fields_ref):
    rhs, panels = near_ref.shape
    clusters = panels // cl
    per = LANES // rank
    span = clusters * rank
    load_window(six_tables(near_pair_ref, far_pair_ref, swapped_ref), clusters, rank, pieces_ref, middle_ref)
    lane = lax.broadcasted_iota(jnp.int32, (1, LANES), 1) // rank
    for c in range(clusters):
        mine = [offsets_ref[3, k:k + 1, :] - center_ref[c:c + 1, k * LANES:(k + 1) * LANES] for k in range(3)]
        for g in range(at_ref.shape[1] // per):
            lanes = slice(g * LANES, (g + 1) * LANES)
            gathered_ref[c, :, lanes] = pick(pieces_ref, at_ref, c, g, per, lane)
            center = pick(middle_ref, at_ref, c, g, per, lane)
            gap = [(center[k:k + 1] + mine[k]) - offsets_ref[k] for k in range(3)]
            high, low = split(lax.rsqrt(gap[0] * gap[0] + gap[1] * gap[1] + gap[2] * gap[2] + SMOOTHING))
            coupling_ref[c, 0:rank, lanes] = high
            coupling_ref[c, rank:2 * rank, lanes] = low
    far_fields(gathered_ref, coupling_ref, fields_ref)
    squared = correlation = jnp.zeros((rhs, cl), F32)
    for c in range(clusters):
        lanes = slice(c * cl, (c + 1) * cl)
        basis = basis_ref[:, lanes]
        area = area_ref[c:c + 1, :]
        image = COULOMB * area * (near_ref[:, lanes] + far_potential(fields_ref, c, basis))
        charges = area * image
        image_ref[:, lanes] = image
        payload_ref[:, lanes] = charges
        heavy_ref[:, lanes] = charges
        payload_ref[:, panels + c * rank:panels + (c + 1) * rank] = moments_of(charges, basis)
        krylov = krylov_ref[:, lanes]
        squared = squared + krylov * krylov
        correlation = correlation + krylov * image
    squared = jnp.sum(squared, axis=1, keepdims=True)
    correlation = jnp.sum(correlation, axis=1, keepdims=True)
    local = ratio(correlation, squared)
    residual = image_ref[...] - local * krylov_ref[...]
    payload_ref[:, panels + span:] = in_lanes(squared, correlation, jnp.sum(residual * residual, axis=1, keepdims=True), local)


def far_again_kernel(cl, rank, at_ref, near_pair_ref, far_pair_ref, swapped_ref, near_ref, area_ref, coupling_ref, basis_ref,
                     image_ref, pieces_ref, gathered_ref, fields_ref):
    clusters = near_ref.shape[1] // cl
    per = LANES // rank
    load_window(six_tables(near_pair_ref, far_pair_ref, swapped_ref), clusters, rank, pieces_ref, None)
    lane = lax.broadcasted_iota(jnp.int32, (1, LANES), 1) // rank
    for c in range(clusters):
        for g in range(at_ref.shape[1] // per):
            gathered_ref[c, :, g * LANES:(g + 1) * LANES] = pick(pieces_ref, at_ref, c, g, per, lane)
    far_fields(gathered_ref, coupling_ref, fields_ref)
    for c in range(clusters):
        lanes = slice(c * cl, (c + 1) * cl)
        image_ref[:, lanes] = COULOMB * area_ref[c:c + 1, :] * (near_ref[:, lanes] + far_potential(fields_ref, c, basis_ref[:, lanes]))


def finish_kernel(total, one_ref, two_ref, image_ref, again_ref, krylov_ref, next_hbm, second_hbm, next_ref, second_ref, sems):
    squared, correlation, energy, local = merged([one_ref[...], two_ref[...]])
    projection = correlation / (squared + 1e-06)
    gap = projection - local
    scaling = 1.0 / jnp.sqrt((energy + gap * gap * squared) / total + 1e-06)
    moves = []
    part = next_ref.shape[1] // 4
    for h in range(4):
        lanes = slice(h * part, (h + 1) * part)
        image = image_ref[:, lanes]
        next_ref[:, lanes] = (image - projection * krylov_ref[:, lanes]) * scaling
        second_ref[:, lanes] = (again_ref[:, lanes] - projection * image) * scaling
        for held, hbm in ((next_ref, next_hbm), (second_ref, second_hbm)):
            moves.append(pltpu.make_async_copy(held.at[:, lanes], hbm.at[:, lanes], sems.at[len(moves)]))
            moves[-1].start()
    for move in moves:
        move.wait()


def ratio(correlation, squared):
    return jnp.where(squared > 0, correlation / jnp.where(squared > 0, squared, 1.0), 0.0)


def in_lanes(*columns):
    lane = lax.broadcasted_iota(jnp.int32, (columns[0].shape[0], LANES), 1)
    out = columns[-1]
    for i, column in enumerate(columns[:-1]):
        out = jnp.where(lane == i, column, out)
    return out


def merged(groups):
    squared = sum(group[:, 0:1] for group in groups)
    correlation = sum(group[:, 1:2] for group in groups)
    local = ratio(correlation, squared)
    energy = 0.0
    for group in groups:
        gap = local - group[:, 3:4]
        energy = energy + (group[:, 2:3] + gap * gap * group[:, 0:1])
    return squared, correlation, energy, local


def window_sums_kernel(payload_ref, partner_ref, near_pair_ref, far_pair_ref, swapped_ref, out_ref):
    width = near_pair_ref.shape[1] // 2
    ends = [(payload_ref, payload_ref.shape[1]), (partner_ref, partner_ref.shape[1])]
    ends += [(ref, end) for ref in (near_pair_ref, far_pair_ref, swapped_ref) for end in (width, 2 * width)]
    out_ref[...] = in_lanes(*merged([ref[:, end - LANES:end] for ref, end in ends]))


def merge_kernel(one_ref, two_ref, out_ref):
    out_ref[...] = in_lanes(*merged([one_ref[...], two_ref[...]]))


def call(kernel, outs, scratch, memory, *args, limit=10, us=1.0):
    spaces = {"s": pltpu.SMEM, "v": pltpu.VMEM, "p": pltpu.VMEM, "h": pltpu.HBM}
    ins, out_spaces = memory.split(">")
    pinned = {"h": pltpu.HBM, "p": pltpu.VMEM}
    return pl.pallas_call(
        kernel,
        out_shape=[pltpu.VMEM(*out) if m == "p" else jax.ShapeDtypeStruct(*out) for m, out in zip(out_spaces, outs)],
        in_specs=[pl.BlockSpec(memory_space=spaces[m]) for m in ins],
        out_specs=[pl.BlockSpec(memory_space=spaces[m]) for m in out_spaces],
        scratch_shapes=scratch,
        compiler_params=pltpu.CompilerParams(vmem_limit_bytes=limit * 2 ** 20),
        cost_estimate=pl.CostEstimate(flops=int(us * 5e8), bytes_accessed=int(us * 3.6e6), transcendentals=0),
    )(*(pltpu.with_memory_space_constraint(a, pinned[m]) if m in pinned else a for m, a in zip(ins, args)))


def body(vertices, panel_vertices, near_pairs, far_pairs, basis, krylov):
    clusters, slots = near_pairs.shape
    partners = far_pairs.shape[1]
    rhs, panels = krylov.shape
    rank = basis.shape[0]
    cl = panels // clusters
    vcl = vertices.shape[1] // clusters
    span = clusters * rank
    per = LANES // rank
    devices = lax.axis_size("clus")
    position = lax.axis_index("clus").reshape(1).astype(jnp.int32)
    offsets = proxy_offsets(rank)
    flat = np.concatenate([np.tile(offsets, (1, per)), np.zeros((rank - 3, LANES), np.float32)])
    offsets = jnp.asarray(np.concatenate([np.broadcast_to(offsets[:, :, None], (3, rank, LANES)), flat[None]]))
    width = span + span // 2
    pairing = [(i, i + 1 - 2 * (i % 2)) for i in range(devices)]
    bridging = [(i, i - 1 + 2 * (i % 2)) for i in range(1, devices - 1)] + [(0, 0), (devices - 1, devices - 1)]

    def move(value, pairs):
        return lax.ppermute(value, "clus", pairs)

    def outward(value, steps):
        return move(value, [(i, (i + steps * (1 - 2 * (i % 2))) % devices) for i in range(devices)])

    def exchange(payload, heavy):
        other = move(heavy, bridging)
        partner = move(payload, pairing)
        pair = jnp.concatenate([value[:, heavy.shape[1]:] for value in (payload, partner)], axis=1)
        return partner, other, outward(pair, 2), outward(pair, 4)

    def swapped(near_pair, far_pair, tail):
        return move(jnp.concatenate([near_pair, far_pair, tail], axis=1), pairing)

    whole = ((rhs, panels), F32)
    payload, heavy, area, centers, at, pairs, basis, krylov, offsets = call(
        functools.partial(prepare_kernel, cl, vcl, rank),
        [
            ((rhs, panels + 3 * cl + width), F32), ((rhs, panels + 3 * cl), F32), ((clusters, cl), F32), ((clusters, 3 * LANES), F32),
            (far_pairs.shape, jnp.int32), ((8, LANES), jnp.int32), ((2 * rank, panels), BF16), whole, (offsets.shape, F32),
        ],
        [
            pltpu.VMEM(vertices.shape, F32),
            pltpu.VMEM(panel_vertices.shape, jnp.int32),
            pltpu.VMEM(basis.shape, F32),
            pltpu.VMEM(far_pairs.shape, jnp.int32),
            pltpu.VMEM((slots, clusters), jnp.int32),
            pltpu.VMEM((3 * clusters, vcl), F32),
            pltpu.VMEM((3 * panels // LANES, LANES), jnp.int32),
            pltpu.SemaphoreType.DMA((7,)),
        ],
        "shhhhhhh>vvvvvvppp",
        position, vertices, panel_vertices, krylov, basis, far_pairs, near_pairs.T, offsets,
        us=1.5,
    )
    partner, other, near_pair, far_pair = exchange(payload, heavy)
    total = pltpu.VMEM((clusters, 2 * rhs, cl), F32)

    group = 4
    own = ((clusters, 2 * cl, cl), BF16)
    kept = ((clusters * (slots - 1) // group, group, 2 * cl, cl), BF16)

    def pieces(number):
        return pltpu.VMEM((number * clusters + 1, 2 * rhs, cl), BF16)

    def sources(number):
        return pltpu.VMEM((number * clusters + 1, FEATURES, cl), BF16)

    own_blocks, blocks, near, targets, tail = call(
        functools.partial(near_kernel, cl, 0, 1),
        [own, kept, whole, ((clusters, FEATURES, cl), BF16), ((rhs, LANES), F32)],
        [pieces(1), sources(1), total],
        "svv>ppvpv",
        pairs, payload, partner,
        us=8.0,
    )
    swap = swapped(near_pair, far_pair, tail)
    blocks_other, near = call(
        functools.partial(near_kernel, cl, 1, 2),
        [kept, whole],
        [pieces(2), sources(2), total],
        "svvpv>pv",
        pairs, partner, other, targets, near,
        us=4.0,
    )
    tiles = 6 * per * span // LANES
    window = pltpu.VMEM((tiles, 2 * rhs, LANES), BF16)
    gathered = pltpu.VMEM((clusters, 2 * rhs, partners * rank), BF16)
    fields = pltpu.VMEM((clusters, 2 * rhs, 2 * rank), BF16)
    image, payload, heavy, coupling = call(
        functools.partial(image_kernel, cl, rank),
        [whole, ((rhs, panels + span + LANES), F32), whole, ((clusters, 2 * rank, partners * rank), BF16)],
        [window, pltpu.VMEM((tiles, 8, LANES), F32), gathered, fields],
        "svvvvvvppp>vvvp",
        at, near_pair, far_pair, swap, centers, area, near, basis, krylov, offsets,
        us=4.5,
    )
    partner, other, near_pair, far_pair = exchange(payload, heavy)
    near, tail = call(
        functools.partial(near_again_kernel, cl, 0, 1),
        [whole, ((rhs, LANES), F32)],
        [pieces(1), total],
        "svvpp>vv",
        pairs, payload, partner, own_blocks, blocks,
        us=8.0,
    )
    swap = swapped(near_pair, far_pair, tail)
    (near,) = call(
        functools.partial(near_again_kernel, cl, 1, 2),
        [whole],
        [pieces(2), total],
        "svvvp>v",
        pairs, partner, other, near, blocks_other,
        us=2.0,
    )
    sums_shape = ((rhs, LANES), F32)
    (one,) = call(window_sums_kernel, [sums_shape], [], "vvvvv>v", payload, partner, near_pair, far_pair, swap, us=0.3)
    size = 8
    many = outward(one, size)
    while 2 * size < devices:
        (one,) = call(merge_kernel, [sums_shape], [], "vv>v", one, many, us=0.3)
        size = 2 * size
        many = outward(one, size)
    (again,) = call(
        functools.partial(far_again_kernel, cl, rank),
        [whole],
        [window, gathered, fields],
        "svvvvvpp>v",
        at, near_pair, far_pair, swap, near, area, coupling, basis,
        us=2.0,
    )
    here = pltpu.VMEM((rhs, panels), F32)
    return tuple(call(
        functools.partial(finish_kernel, panels * devices),
        [whole, whole],
        [here, here, pltpu.SemaphoreType.DMA((8,))],
        "vvvvp>hh",
        one, many, image, again, krylov,
    ))


def solution(mesh):
    whole = P(None, ("jobs", "clus"))
    rows = P(("jobs", "clus"), None)
    return jax.shard_map(
        body,
        mesh=mesh,
        in_specs=(whole, whole, rows, rows, whole, whole),
        out_specs=(whole, whole),
        check_vma=False,
    )
```

```python
import functools

import jax
import jax.numpy as jnp
import numpy as np
from jax import lax
from jax.experimental import pallas as pl
from jax.experimental.pallas import tpu as pltpu
from jax.sharding import PartitionSpec as P

REACH = 4
SMOOTHING = 0.04
COULOMB = 2.0
PROXY_RADIUS = 0.6
LANES = 128
FEATURES = 80
GRID = 1.5 * 2.0 ** 22
F32 = jnp.float32
BF16 = jnp.bfloat16


def proxy_offsets(points):
    counter = np.arange(points, dtype=np.float32)
    height = 1.0 - (2.0 * counter + 1.0) / points
    radial = np.sqrt(1.0 - height * height)
    azimuth = counter * 2.399963
    return PROXY_RADIUS * np.stack([radial * np.cos(azimuth), radial * np.sin(azimuth), height]).astype(np.float32)


def split(value):
    high = value.astype(BF16)
    return high, (value - high.astype(F32)).astype(BF16)


def stacked(value):
    return jnp.concatenate(split(value), axis=0)


def folded(value):
    half = value.shape[0] // 2
    return value[:half] + value[half:]


def dot_nt(left, right):
    return lax.dot_general(left, right, (((1,), (1,)), ((), ())), preferred_element_type=F32)


def dot_tn(left, right):
    return lax.dot_general(left, right, (((0,), (0,)), ((), ())), preferred_element_type=F32)


def dot_nn(left, right):
    return lax.dot_general(left, right, (((1,), (0,)), ((), ())), preferred_element_type=F32)


def quartered(value):
    half = value.shape[1] // 2
    value = folded(value)
    return value[:, 0:half] + value[:, half:]


def moments_of(weighted, basis_pieces):
    return quartered(dot_nt(stacked(weighted), basis_pieces))


def copies(pairs, sems):
    moves = [pltpu.make_async_copy(source, target, sems.at[i]) for i, (source, target) in enumerate(pairs)]
    for move in moves:
        move.start()
    return moves


def pair_list(near, position, clusters):
    block = lax.div(near, clusters) - position
    partner = block * (1 - 2 * lax.rem(position, 2)) > 0
    place = (lax.rem(near, clusters) + jnp.where((block != 0) & ~partner, clusters, 0)).astype(F32)
    across = lax.broadcasted_iota(jnp.int32, (clusters, clusters), 1)
    down = lax.broadcasted_iota(jnp.int32, (clusters, clusters), 0)
    upright = lambda value: jnp.sum(jnp.where(across == down, value, 0.0), axis=1, keepdims=True)
    row = lax.broadcasted_iota(jnp.int32, (clusters, LANES), 1).astype(F32)
    target = lax.broadcasted_iota(jnp.int32, (clusters, 1), 0).astype(F32)
    rows = lax.broadcasted_iota(jnp.int32, (8, LANES), 0)
    out = jnp.zeros((8, LANES), F32)
    for which in range(2):
        here = block != 0 if which else block == 0
        live = jnp.where(here & (near >= 0), 1.0, 0.0)
        counts = sum(live[k:k + 1] for k in range(1, near.shape[0]))
        first = jnp.sum(jnp.where(across < down, counts, 0.0), axis=1, keepdims=True)
        found = jnp.zeros((clusters, LANES), F32)
        for k in range(1, near.shape[0]):
            alive = upright(live[k:k + 1])
            hit = jnp.where(row == first, alive, 0.0)
            found = found + hit * (target * 64 + upright(place[k:k + 1]))
            first = first + alive
        count = jnp.sum(counts, axis=1, keepdims=True)
        found = jnp.where(row[0:1] < count, jnp.sum(found, axis=0, keepdims=True), (1.0 + which) * clusters)
        out = jnp.where(rows == which, found, jnp.where(rows == 2 + which, count, out))
    return out.astype(jnp.int32)


def prepare_kernel(cl, vcl, rank, position_ref, vertices_hbm, corners_hbm, krylov_hbm, basis_hbm, far_hbm, near_hbm, offsets_hbm, weights_hbm,
                   payload_ref, table_ref, area_ref, center_ref, at_ref, pairs_ref, basis_ref, krylov_ref, offsets_ref, weights_ref,
                   vertices_ref, corners_ref, raw_ref, far_ref, near_ref, mesh_ref, local_ref, sems):
    moves = copies((
        (vertices_hbm, vertices_ref), (corners_hbm, corners_ref), (krylov_hbm, krylov_ref), (basis_hbm, raw_ref),
        (far_hbm, far_ref), (near_hbm, near_ref), (offsets_hbm, offsets_ref), (weights_hbm.at[position_ref[0]], weights_ref),
    ), sems)
    rhs, panels = krylov_ref.shape
    clusters = panels // cl
    parts = cl // LANES
    moves[0].wait()
    for c in range(clusters):
        mesh_ref[3 * c:3 * c + 3, :] = vertices_ref[:, c * vcl:(c + 1) * vcl]
    moves[1].wait()
    for i in range(clusters * parts):
        local_ref[3 * i:3 * i + 3, :] = corners_ref[:, i * LANES:(i + 1) * LANES]
    first = position_ref[0] * (vcl * clusters) + vcl * lax.broadcasted_iota(jnp.int32, (clusters, LANES), 0)
    tables = [mesh_ref[pl.ds(k, clusters, stride=3), :] for k in range(3)]
    sums = [None] * 3
    for h in range(parts):
        local = [local_ref[pl.ds(3 * h + m, clusters, stride=3 * parts), :] - first for m in range(3)]
        corner = [[jnp.take_along_axis(tables[k], local[m], axis=1, mode="promise_in_bounds") for k in range(3)] for m in range(3)]
        for k in range(3):
            middle = (corner[0][k] + corner[1][k] + corner[2][k]) / 3.0
            lanes = slice(panels + k * cl + h * LANES, panels + k * cl + (h + 1) * LANES)
            payload_ref[:, lanes] = middle
            sums[k] = middle if h == 0 else sums[k] + middle
        one = [corner[1][k] - corner[0][k] for k in range(3)]
        two = [corner[2][k] - corner[0][k] for k in range(3)]
        normal = [one[1] * two[2] - one[2] * two[1], one[2] * two[0] - one[0] * two[2], one[0] * two[1] - one[1] * two[0]]
        area_ref[:, h * LANES:(h + 1) * LANES] = 0.5 * jnp.sqrt(normal[0] * normal[0] + normal[1] * normal[1] + normal[2] * normal[2])
    span = clusters * rank
    mine = lax.broadcasted_iota(jnp.int32, (clusters, span), 1) // rank == lax.broadcasted_iota(jnp.int32, (clusters, span), 0)
    half = span // 2
    table_ref[:, span:] = jnp.zeros_like(table_ref[:, span:])
    for k in range(3):
        center = jnp.sum(sums[k], axis=1, keepdims=True) / cl
        center_ref[:, k * LANES:(k + 1) * LANES] = jnp.broadcast_to(center, (clusters, LANES))
        row = jnp.sum(jnp.where(mine, center, 0.0), axis=0, keepdims=True)
        table_ref[k:k + 1, span:] = row[:, 0:half]
        table_ref[8 + k:9 + k, span:] = row[:, half:]
    moves[2].wait()
    moves[3].wait()
    for c in range(clusters):
        lanes = slice(c * cl, (c + 1) * cl)
        basis_ref[:, lanes] = stacked(raw_ref[:, lanes])
        charges = area_ref[c:c + 1, :] * krylov_ref[:, lanes]
        payload_ref[:, lanes] = charges
        table_ref[:, c * rank:(c + 1) * rank] = moments_of(charges, basis_ref[:, lanes])
    moves[4].wait()
    far = far_ref[...]
    step = (lax.div(far, clusters) - position_ref[0]) * (1 - 2 * lax.rem(position_ref[0], 2))
    block = jnp.where(step < 0, step + REACH, step + REACH - 3)
    per = LANES // rank
    turn = lax.rem(lax.broadcasted_iota(jnp.int32, far.shape, 1) - far + per * clusters * 2 ** 16, per)
    at_ref[...] = (turn * 6 + block) * (span // LANES) + lax.div(lax.rem(far, clusters), per)
    moves[5].wait()
    pairs_ref[...] = pair_list(near_ref[...], position_ref[0], clusters)
    moves[6].wait()
    moves[7].wait()


def features_of(payload_ref, panels, c, cl, target):
    rows = [payload_ref[c:c + 1, panels + k * cl:panels + (k + 1) * cl] for k in range(3)]
    value = jnp.concatenate(rows + [jnp.zeros((5, cl), F32)], axis=0)
    coarse = (value + GRID) - GRID
    middle = (value - coarse).astype(BF16).astype(F32)
    low = (value - coarse - middle).astype(BF16).astype(F32)
    pieces = [coarse, middle, low]
    rest = middle + low
    row = lax.broadcasted_iota(jnp.int32, (8, cl), 0)
    square = jnp.sum(coarse * coarse, axis=0, keepdims=True)
    extra = jnp.sum((2.0 * coarse + rest) * rest, axis=0, keepdims=True) + (SMOOTHING if target else 0.0)
    square_high = square.astype(BF16).astype(F32)
    extra_high = extra.astype(BF16).astype(F32)
    extra_middle = (extra - extra_high).astype(BF16).astype(F32)
    ones = jnp.ones((1, cl), F32)

    def placed(base, start, *values):
        for i, one in enumerate(values):
            base = jnp.where(row == start + i, one, base)
        return base

    squares, extras = (square_high, square - square_high), (extra_high, extra_middle, extra - extra_high - extra_middle)
    if target:
        scaled = [-2.0 * piece for piece in pieces]
        first = placed(scaled[0], 3, *squares, ones, ones)
        last = placed(jnp.zeros((8, cl), F32), 0, *extras, ones, ones, ones)
    else:
        first = placed(coarse, 3, ones, ones, *squares)
        last = placed(jnp.zeros((8, cl), F32), 0, ones, ones, ones, *extras)
    combos = [(scaled[i] if target else pieces[j]) for i in range(3) for j in range(3) if i + j]
    return jnp.concatenate([first, *combos, last], axis=0)


def fill_features(sources_ref, blocks, panels, cl):
    clusters = panels // cl
    for b, ref in enumerate(blocks):
        for c in range(clusters):
            sources_ref[b * clusters + c] = features_of(ref, panels, c, cl, False).astype(BF16)
    sources_ref[len(blocks) * clusters] = sources_ref[0]


def near_block(source, target, pieces, out_ref):
    cl = source.shape[1]
    parts = []
    for first in range(0, cl, LANES):
        rows = slice(first, first + LANES)
        high, low = split(lax.rsqrt(dot_tn(source[:, rows], target)))
        out_ref[rows, :] = high
        out_ref[cl + first:cl + first + LANES, :] = low
        parts.append(dot_nn(pieces[:, rows], high) + dot_nn(pieces[:, rows], low))
    return sum(parts[1:], parts[0])


def near_product(pieces, block_ref, cl):
    return dot_nn(pieces, block_ref[0:cl, :]) + dot_nn(pieces, block_ref[cl:2 * cl, :])


def fill_charges(pieces_ref, blocks, clusters, cl):
    for b, ref in enumerate(blocks):
        for c in range(clusters):
            pieces_ref[b * clusters + c] = stacked(ref[:, c * cl:(c + 1) * cl])
    pieces_ref[len(blocks) * clusters] = jnp.zeros_like(pieces_ref[0])


def pair_at(pairs_ref, which, i):
    pair = pairs_ref[which, i]
    return lax.shift_right_logical(pair, 6), lax.bitwise_and(pair, 63)


def near_kernel(cl, which, number, pairs_ref, *refs):
    blocks = refs[:number]
    if which:
        targets_ref, start_ref, kept_ref, near_out_ref, pieces_ref, sources_ref, total_ref = refs[number:]
    else:
        table_ref, own_ref, kept_ref, near_out_ref, targets_ref, tail_ref, pieces_ref, sources_ref, total_ref = refs[number:]
        tail_ref[...] = table_ref[:, table_ref.shape[1] - LANES:]
    panels = near_out_ref.shape[1]
    clusters = panels // cl
    group = kept_ref.shape[1]
    fill_charges(pieces_ref, blocks, clusters, cl)
    fill_features(sources_ref, blocks, panels, cl)
    if which:
        total_ref[...] = jnp.zeros_like(total_ref)
    else:
        for c in range(clusters):
            target = features_of(blocks[0], panels, c, cl, True).astype(BF16)
            targets_ref[c] = target
            total_ref[c] = near_block(sources_ref[c], target, pieces_ref[c], own_ref.at[c])
    def step(m, _):
        pairs = [pair_at(pairs_ref, which, group * m + w) for w in range(group)]
        loaded = [(sources_ref[j], targets_ref[c], pieces_ref[j]) for c, j in pairs]
        parts = [near_block(*one, kept_ref.at[m, w]) for w, one in enumerate(loaded)]
        for (c, j), part in zip(pairs, parts):
            total_ref[c] += part
        return 0

    lax.fori_loop(0, (pairs_ref[2 + which, 0] + group - 1) // group, step, 0)
    for c in range(clusters):
        lanes = slice(c * cl, (c + 1) * cl)
        near = folded(total_ref[c])
        near_out_ref[:, lanes] = start_ref[:, lanes] + near if which else near


def near_again_kernel(cl, which, number, pairs_ref, *refs):
    blocks = refs[:number]
    if which:
        start_ref, kept_ref, near_out_ref, pieces_ref, total_ref = refs[number:]
    else:
        table_ref, own_ref, kept_ref, near_out_ref, tail_ref, pieces_ref, total_ref = refs[number:]
        tail_ref[...] = table_ref[:, table_ref.shape[1] - LANES:]
    clusters = near_out_ref.shape[1] // cl
    group = kept_ref.shape[1]
    fill_charges(pieces_ref, blocks, clusters, cl)
    if which:
        total_ref[...] = jnp.zeros_like(total_ref)
    else:
        for c in range(clusters):
            total_ref[c] = near_product(pieces_ref[c], own_ref.at[c], cl)

    def step(m, _):
        pairs = [pair_at(pairs_ref, which, group * m + w) for w in range(group)]
        parts = [near_product(pieces_ref[j], kept_ref.at[m, w], cl) for w, (c, j) in enumerate(pairs)]
        for (c, j), part in zip(pairs, parts):
            total_ref[c] += part
        return 0

    lax.fori_loop(0, (pairs_ref[2 + which, 0] + group - 1) // group, step, 0)
    for c in range(clusters):
        lanes = slice(c * cl, (c + 1) * cl)
        near = folded(total_ref[c])
        near_out_ref[:, lanes] = start_ref[:, lanes] + near if which else near


def load_window(tables, clusters, rank, pieces_ref, middle_ref):
    per = LANES // rank
    span = clusters * rank
    count = pieces_ref.shape[0] // per
    groups = span // LANES
    for at in range(count):
        (ref, first), g = tables[at // groups], at % groups
        tile = ref[:, first + g * LANES:first + (g + 1) * LANES]
        for s in range(per):
            pieces_ref[s * count + at] = stacked(pltpu.roll(tile, s * rank, 1) if s else tile)
        if middle_ref is not None:
            half = groups // 2
            row, lane = 8 * (g // half), first + span + g % half * LANES
            tile = ref[row:row + 8, lane:lane + LANES]
            for s in range(per):
                middle_ref[s * count + at] = pltpu.roll(tile, s * rank, 1) if s else tile


def six_tables(other_ref, far_ref, swapped_ref):
    width = far_ref.shape[1] // 2
    last = other_ref.shape[1] - width
    return (far_ref, 0), (far_ref, width), (other_ref, last), (swapped_ref, 0), (swapped_ref, width), (swapped_ref, 3 * width)


def pick(source_ref, at_ref, c, g, per, lane):
    row = None
    for u in range(per):
        take = source_ref[at_ref[c, g * per + u]]
        row = take if row is None else jnp.where(lane == u, take, row)
    return row


def far_fields(gathered_ref, coupling_ref, fields_ref):
    for c in range(gathered_ref.shape[0]):
        field = quartered(dot_nt(gathered_ref[c], coupling_ref[c]))
        fields_ref[c] = stacked(jnp.concatenate([field, field], axis=1))


def far_potential(fields_ref, c, basis):
    return folded(dot_nn(fields_ref[c], basis))


def image_kernel(cl, rank, at_ref, other_ref, far_pair_ref, swapped_ref, center_ref, area_ref, near_ref, basis_ref, krylov_ref, offsets_ref,
                 image_ref, payload_ref, table_ref, coupling_ref, pieces_ref, middle_ref, gathered_ref, fields_ref):
    rhs, panels = near_ref.shape
    clusters = panels // cl
    per = LANES // rank
    span = clusters * rank
    load_window(six_tables(other_ref, far_pair_ref, swapped_ref), clusters, rank, pieces_ref, middle_ref)
    lane = lax.broadcasted_iota(jnp.int32, (1, LANES), 1) // rank
    for c in range(clusters):
        mine = [offsets_ref[3, k:k + 1, :] - center_ref[c:c + 1, k * LANES:(k + 1) * LANES] for k in range(3)]
        for g in range(at_ref.shape[1] // per):
            lanes = slice(g * LANES, (g + 1) * LANES)
            gathered_ref[c, :, lanes] = pick(pieces_ref, at_ref, c, g, per, lane)
            center = pick(middle_ref, at_ref, c, g, per, lane)
            gap = [(center[k:k + 1] + mine[k]) - offsets_ref[k] for k in range(3)]
            high, low = split(lax.rsqrt(gap[0] * gap[0] + gap[1] * gap[1] + gap[2] * gap[2] + SMOOTHING))
            coupling_ref[c, 0:rank, lanes] = high
            coupling_ref[c, rank:2 * rank, lanes] = low
    far_fields(gathered_ref, coupling_ref, fields_ref)
    squared = correlation = jnp.zeros((rhs, cl), F32)
    for c in range(clusters):
        lanes = slice(c * cl, (c + 1) * cl)
        basis = basis_ref[:, lanes]
        area = area_ref[c:c + 1, :]
        image = COULOMB * area * (near_ref[:, lanes] + far_potential(fields_ref, c, basis))
        charges = area * image
        image_ref[:, lanes] = image
        payload_ref[:, lanes] = charges
        table_ref[:, c * rank:(c + 1) * rank] = moments_of(charges, basis)
        krylov = krylov_ref[:, lanes]
        squared = squared + krylov * krylov
        correlation = correlation + krylov * image
    squared = jnp.sum(squared, axis=1, keepdims=True)
    correlation = jnp.sum(correlation, axis=1, keepdims=True)
    local = ratio(correlation, squared)
    residual = image_ref[...] - local * krylov_ref[...]
    table_ref[:, span:] = in_lanes(squared, correlation, jnp.sum(residual * residual, axis=1, keepdims=True), local)


def far_again_kernel(cl, rank, at_ref, other_ref, far_pair_ref, swapped_ref, near_ref, area_ref, coupling_ref, basis_ref,
                     image_ref, pieces_ref, gathered_ref, fields_ref):
    clusters = near_ref.shape[1] // cl
    per = LANES // rank
    load_window(six_tables(other_ref, far_pair_ref, swapped_ref), clusters, rank, pieces_ref, None)
    lane = lax.broadcasted_iota(jnp.int32, (1, LANES), 1) // rank
    for c in range(clusters):
        for g in range(at_ref.shape[1] // per):
            gathered_ref[c, :, g * LANES:(g + 1) * LANES] = pick(pieces_ref, at_ref, c, g, per, lane)
    far_fields(gathered_ref, coupling_ref, fields_ref)
    for c in range(clusters):
        lanes = slice(c * cl, (c + 1) * cl)
        image_ref[:, lanes] = COULOMB * area_ref[c:c + 1, :] * (near_ref[:, lanes] + far_potential(fields_ref, c, basis_ref[:, lanes]))


def finish_kernel(total, one_ref, two_ref, image_ref, again_ref, krylov_ref, next_hbm, second_hbm, next_ref, second_ref, sems):
    squared, correlation, energy, local = merged([one_ref[...], two_ref[...]])
    projection = correlation / (squared + 1e-06)
    gap = projection - local
    scaling = 1.0 / jnp.sqrt((energy + gap * gap * squared) / total + 1e-06)
    moves = []
    part = next_ref.shape[1] // 4
    for h in range(4):
        lanes = slice(h * part, (h + 1) * part)
        image = image_ref[:, lanes]
        next_ref[:, lanes] = (image - projection * krylov_ref[:, lanes]) * scaling
        second_ref[:, lanes] = (again_ref[:, lanes] - projection * image) * scaling
        for held, hbm in ((next_ref, next_hbm), (second_ref, second_hbm)):
            moves.append(pltpu.make_async_copy(held.at[:, lanes], hbm.at[:, lanes], sems.at[len(moves)]))
            moves[-1].start()
    for move in moves:
        move.wait()


def ratio(correlation, squared):
    return jnp.where(squared > 0, correlation / jnp.where(squared > 0, squared, 1.0), 0.0)


def in_lanes(*columns):
    lane = lax.broadcasted_iota(jnp.int32, (columns[0].shape[0], LANES), 1)
    out = columns[-1]
    for i, column in enumerate(columns[:-1]):
        out = jnp.where(lane == i, column, out)
    return out


def merged(groups, weights=None):
    weights = weights or [1.0] * len(groups)
    squared = sum(weight * group[:, 0:1] for group, weight in zip(groups, weights))
    correlation = sum(weight * group[:, 1:2] for group, weight in zip(groups, weights))
    local = ratio(correlation, squared)
    energy = 0.0
    for group, weight in zip(groups, weights):
        gap = local - group[:, 3:4]
        energy = energy + weight * (group[:, 2:3] + gap * gap * group[:, 0:1])
    return squared, correlation, energy, local


def merge_kernel(one_ref, two_ref, out_ref):
    out_ref[...] = in_lanes(*merged([ref[:, ref.shape[1] - LANES:] for ref in (one_ref, two_ref)]))


def known_sums_kernel(weights_ref, own_ref, partner_ref, other_ref, far_ref, swapped_ref, *outs):
    width = own_ref.shape[1]
    last = other_ref.shape[1]
    ends = [(own_ref, width), (partner_ref, width), (other_ref, last - width), (other_ref, last), (far_ref, width), (far_ref, 2 * width)]
    ends += [(swapped_ref, width * i) for i in range(1, 5)]
    groups = [ref[:, end - LANES:end] for ref, end in ends]
    for side, out_ref in enumerate(outs):
        weights = [weights_ref[0:1, 16 * side + i:16 * side + i + 1] for i in range(len(groups))]
        out_ref[...] = in_lanes(*merged(groups, weights))


def completing(devices, *moves):
    partner, other, far = ({target: source for source, target in move} for move in moves)
    slots = []
    for i in range(devices):
        near = [other[i], far[i], other[partner[i]], far[partner[i]]]
        slots.append([i, partner[i]] + [device for one in near for device in (one, partner[one])])
    known = [set(slot) for slot in slots]
    everyone = set(range(devices))
    target_of = {}

    def matched(target, seen):
        for source in range(devices):
            if source not in seen and known[target] | known[source] == everyone:
                seen.add(source)
                if source not in target_of or matched(target_of[source], seen):
                    target_of[source] = target
                    return True
        return False

    if not all(matched(i, set()) for i in range(devices)):
        return None
    weights = np.zeros((devices, 8, LANES), np.float32)
    for i in range(devices):
        for at, device in enumerate(slots[i]):
            if device not in slots[i][:at]:
                weights[i, :, at] = 1.0
                weights[i, :, 16 + at] = device not in known[target_of[i]]
    return sorted(target_of.items()), weights


def call(kernel, outs, scratch, memory, *args, limit=10, us=1.0):
    spaces = {"s": pltpu.SMEM, "v": pltpu.VMEM, "p": pltpu.VMEM, "h": pltpu.HBM}
    ins, out_spaces = memory.split(">")
    pinned = {"h": pltpu.HBM, "p": pltpu.VMEM}
    return pl.pallas_call(
        kernel,
        out_shape=[pltpu.VMEM(*out) if m == "p" else jax.ShapeDtypeStruct(*out) for m, out in zip(out_spaces, outs)],
        in_specs=[pl.BlockSpec(memory_space=spaces[m]) for m in ins],
        out_specs=[pl.BlockSpec(memory_space=spaces[m]) for m in out_spaces],
        scratch_shapes=scratch,
        compiler_params=pltpu.CompilerParams(vmem_limit_bytes=limit * 2 ** 20),
        cost_estimate=pl.CostEstimate(flops=int(us * 5e8), bytes_accessed=int(us * 3.6e6), transcendentals=0),
    )(*(pltpu.with_memory_space_constraint(a, pinned[m]) if m in pinned else a for m, a in zip(ins, args)))


def body(vertices, panel_vertices, near_pairs, far_pairs, basis, krylov):
    clusters, slots = near_pairs.shape
    partners = far_pairs.shape[1]
    rhs, panels = krylov.shape
    rank = basis.shape[0]
    cl = panels // clusters
    vcl = vertices.shape[1] // clusters
    span = clusters * rank
    per = LANES // rank
    devices = lax.axis_size("clus")
    position = lax.axis_index("clus").reshape(1).astype(jnp.int32)
    offsets = proxy_offsets(rank)
    flat = np.concatenate([np.tile(offsets, (1, per)), np.zeros((rank - 3, LANES), np.float32)])
    offsets = jnp.asarray(np.concatenate([np.broadcast_to(offsets[:, :, None], (3, rank, LANES)), flat[None]]))
    width = span + span // 2
    pairing = [(i, i + 1 - 2 * (i % 2)) for i in range(devices)]
    bridging = [(i, i - 1 + 2 * (i % 2)) for i in range(1, devices - 1)] + [(0, 0), (devices - 1, devices - 1)]
    outward = [(i, i + 4 - 8 * (i % 2)) for i in range(devices)]
    outward = [(i, j) for i, j in outward if 0 <= j < devices] + [(3, 0), (devices - 4, devices - 1)]
    outward_once = outward + [(1, 2), (devices - 2, devices - 3)]
    outward_around = outward + [(devices - 2, 2), (1, devices - 3)]
    completion = completing(devices, pairing, bridging, outward_around)
    weights = completion[1] if completion else np.zeros((devices, 8, LANES), np.float32)

    def move(value, pairs):
        return lax.ppermute(value, "clus", pairs)

    def exchange(payload, table, away):
        beside = move(table, pairing)
        pair = jnp.concatenate([table, beside], axis=1)
        other = move(jnp.concatenate([payload, pair], axis=1), bridging)
        return beside, other, move(pair, away), move(payload, pairing)

    def swapped(other, far_pair, tail):
        pair = other[:, other.shape[1] - far_pair.shape[1]:]
        return move(jnp.concatenate([pair, far_pair, tail], axis=1), pairing)

    whole = ((rhs, panels), F32)
    payload, table, area, centers, at, pairs, basis, krylov, offsets, weights = call(
        functools.partial(prepare_kernel, cl, vcl, rank),
        [
            ((rhs, panels + 3 * cl), F32), ((rhs, width), F32), ((clusters, cl), F32), ((clusters, 3 * LANES), F32),
            (far_pairs.shape, jnp.int32), ((8, LANES), jnp.int32), ((2 * rank, panels), BF16), whole, (offsets.shape, F32), ((8, LANES), F32),
        ],
        [
            pltpu.VMEM(vertices.shape, F32),
            pltpu.VMEM(panel_vertices.shape, jnp.int32),
            pltpu.VMEM(basis.shape, F32),
            pltpu.VMEM(far_pairs.shape, jnp.int32),
            pltpu.VMEM((slots, clusters), jnp.int32),
            pltpu.VMEM((3 * clusters, vcl), F32),
            pltpu.VMEM((3 * panels // LANES, LANES), jnp.int32),
            pltpu.SemaphoreType.DMA((8,)),
        ],
        "shhhhhhhh>vvvvvvpppp",
        position, vertices, panel_vertices, krylov, basis, far_pairs, near_pairs.T, offsets, jnp.asarray(weights),
        us=1.5,
    )
    beside, other, far_pair, partner = exchange(payload, table, outward_once)
    total = pltpu.VMEM((clusters, 2 * rhs, cl), F32)

    group = 4
    own = ((clusters, 2 * cl, cl), BF16)
    kept = ((clusters * (slots - 1) // group, group, 2 * cl, cl), BF16)

    def pieces(number):
        return pltpu.VMEM((number * clusters + 1, 2 * rhs, cl), BF16)

    def sources(number):
        return pltpu.VMEM((number * clusters + 1, FEATURES, cl), BF16)

    own_blocks, blocks, near, targets, tail = call(
        functools.partial(near_kernel, cl, 0, 1),
        [own, kept, whole, ((clusters, FEATURES, cl), BF16), ((rhs, LANES), F32)],
        [pieces(1), sources(1), total],
        "svv>ppvpv",
        pairs, payload, beside,
        us=8.0,
    )
    swap = swapped(other, far_pair, tail)
    blocks_other, near = call(
        functools.partial(near_kernel, cl, 1, 2),
        [kept, whole],
        [pieces(2), sources(2), total],
        "svvpv>pv",
        pairs, partner, other, targets, near,
        us=4.0,
    )
    tiles = 6 * per * span // LANES
    window = pltpu.VMEM((tiles, 2 * rhs, LANES), BF16)
    gathered = pltpu.VMEM((clusters, 2 * rhs, partners * rank), BF16)
    fields = pltpu.VMEM((clusters, 2 * rhs, 2 * rank), BF16)
    image, payload, table, coupling = call(
        functools.partial(image_kernel, cl, rank),
        [whole, whole, ((rhs, span + LANES), F32), ((clusters, 2 * rank, partners * rank), BF16)],
        [window, pltpu.VMEM((tiles, 8, LANES), F32), gathered, fields],
        "svvvvvvppp>vvvp",
        at, other, far_pair, swap, centers, area, near, basis, krylov, offsets,
        us=4.5,
    )
    beside, other, far_pair, partner = exchange(payload, table, outward_around)
    near, tail = call(
        functools.partial(near_again_kernel, cl, 0, 1),
        [whole, ((rhs, LANES), F32)],
        [pieces(1), total],
        "svvpp>vv",
        pairs, payload, beside, own_blocks, blocks,
        us=8.0,
    )
    swap = swapped(other, far_pair, tail)
    (near,) = call(
        functools.partial(near_again_kernel, cl, 1, 2),
        [whole],
        [pieces(2), total],
        "svvvp>v",
        pairs, partner, other, near, blocks_other,
        us=2.0,
    )
    sums_shape = ((rhs, LANES), F32)
    if completion:
        one, many = call(known_sums_kernel, [sums_shape] * 2, [], "pvvvvv>vv", weights, table, beside, other, far_pair, swap, us=0.3)
        many = move(many, completion[0])
    else:
        one, many, size = table, beside, 2
        while size < devices:
            (one,) = call(merge_kernel, [sums_shape], [], "vv>v", one, many, us=0.3)
            many = move(one, [(i, (i + size) % devices) for i in range(devices)])
            size = 2 * size
    (again,) = call(
        functools.partial(far_again_kernel, cl, rank),
        [whole],
        [window, gathered, fields],
        "svvvvvpp>v",
        at, other, far_pair, swap, near, area, coupling, basis,
        us=2.0,
    )
    here = pltpu.VMEM((rhs, panels), F32)
    return tuple(call(
        functools.partial(finish_kernel, panels * devices),
        [whole, whole],
        [here, here, pltpu.SemaphoreType.DMA((8,))],
        "vvvvp>hh",
        one, many, image, again, krylov,
    ))


def solution(mesh):
    whole = P(None, ("jobs", "clus"))
    rows = P(("jobs", "clus"), None)
    return jax.shard_map(
        body,
        mesh=mesh,
        in_specs=(whole, whole, rows, rows, whole, whole),
        out_specs=(whole, whole),
        check_vma=False,
    )
```

```python
import functools

import jax
import jax.numpy as jnp
import numpy as np
from jax import lax
from jax.experimental import pallas as pl
from jax.experimental.pallas import tpu as pltpu
from jax.sharding import PartitionSpec as P

REACH = 4
SMOOTHING = 0.04
COULOMB = 2.0
PROXY_RADIUS = 0.6
LANES = 128
FEATURES = 80
GRID = 1.5 * 2.0 ** 22
F32 = jnp.float32
BF16 = jnp.bfloat16


def proxy_offsets(points):
    counter = np.arange(points, dtype=np.float32)
    height = 1.0 - (2.0 * counter + 1.0) / points
    radial = np.sqrt(1.0 - height * height)
    azimuth = counter * 2.399963
    return PROXY_RADIUS * np.stack([radial * np.cos(azimuth), radial * np.sin(azimuth), height]).astype(np.float32)


def split(value):
    high = value.astype(BF16)
    return high, (value - high.astype(F32)).astype(BF16)


def stacked(value):
    return jnp.concatenate(split(value), axis=0)


def folded(value):
    half = value.shape[0] // 2
    return value[:half] + value[half:]


def dot_nt(left, right):
    return lax.dot_general(left, right, (((1,), (1,)), ((), ())), preferred_element_type=F32)


def dot_tn(left, right):
    return lax.dot_general(left, right, (((0,), (0,)), ((), ())), preferred_element_type=F32)


def dot_nn(left, right):
    return lax.dot_general(left, right, (((1,), (0,)), ((), ())), preferred_element_type=F32)


def quartered(value):
    half = value.shape[1] // 2
    value = folded(value)
    return value[:, 0:half] + value[:, half:]


def moments_of(weighted, basis_pieces):
    return quartered(dot_nt(stacked(weighted), basis_pieces))


def copies(pairs, sems):
    moves = [pltpu.make_async_copy(source, target, sems.at[i]) for i, (source, target) in enumerate(pairs)]
    for move in moves:
        move.start()
    return moves


def pair_list(near, position, clusters):
    block = lax.div(near, clusters) - position
    side = block * (1 - 2 * lax.rem(position, 2))
    place = lax.rem(near, clusters).astype(F32)
    across = lax.broadcasted_iota(jnp.int32, (clusters, clusters), 1)
    down = lax.broadcasted_iota(jnp.int32, (clusters, clusters), 0)
    upright = lambda value: jnp.sum(jnp.where(across == down, value, 0.0), axis=1, keepdims=True)
    row = lax.broadcasted_iota(jnp.int32, (clusters, LANES), 1).astype(F32)
    target = lax.broadcasted_iota(jnp.int32, (clusters, 1), 0).astype(F32)
    rows = lax.broadcasted_iota(jnp.int32, (8, LANES), 0)
    out = jnp.zeros((8, LANES), F32)
    for which in range(3):
        live = jnp.where((side == (0, 1, -1)[which]) & (near >= 0), 1.0, 0.0)
        counts = sum(live[k:k + 1] for k in range(1, near.shape[0]))
        first = jnp.sum(jnp.where(across < down, counts, 0.0), axis=1, keepdims=True)
        found = jnp.zeros((clusters, LANES), F32)
        for k in range(1, near.shape[0]):
            alive = upright(live[k:k + 1])
            hit = jnp.where(row == first, alive, 0.0)
            found = found + hit * (target * 64 + upright(place[k:k + 1]))
            first = first + alive
        count = jnp.sum(counts, axis=1, keepdims=True)
        found = jnp.where(row[0:1] < count, jnp.sum(found, axis=0, keepdims=True), 1.0 * clusters)
        out = jnp.where(rows == which, found, jnp.where(rows == 3 + which, count, out))
    return out.astype(jnp.int32)


def prepare_kernel(cl, vcl, rank, position_ref, vertices_hbm, corners_hbm, krylov_hbm, basis_hbm, far_hbm, near_hbm, offsets_hbm,
                   payload_ref, heavy_ref, area_ref, center_ref, at_ref, pairs_ref, basis_ref, krylov_ref, offsets_ref,
                   vertices_ref, corners_ref, raw_ref, far_ref, near_ref, mesh_ref, local_ref, sems):
    moves = copies((
        (vertices_hbm, vertices_ref), (corners_hbm, corners_ref), (krylov_hbm, krylov_ref), (basis_hbm, raw_ref),
        (far_hbm, far_ref), (near_hbm, near_ref), (offsets_hbm, offsets_ref),
    ), sems)
    rhs, panels = krylov_ref.shape
    clusters = panels // cl
    parts = cl // LANES
    moves[0].wait()
    for c in range(clusters):
        mesh_ref[3 * c:3 * c + 3, :] = vertices_ref[:, c * vcl:(c + 1) * vcl]
    moves[1].wait()
    for i in range(clusters * parts):
        local_ref[3 * i:3 * i + 3, :] = corners_ref[:, i * LANES:(i + 1) * LANES]
    first = position_ref[0] * (vcl * clusters) + vcl * lax.broadcasted_iota(jnp.int32, (clusters, LANES), 0)
    tables = [mesh_ref[pl.ds(k, clusters, stride=3), :] for k in range(3)]
    sums = [None] * 3
    for h in range(parts):
        local = [local_ref[pl.ds(3 * h + m, clusters, stride=3 * parts), :] - first for m in range(3)]
        corner = [[jnp.take_along_axis(tables[k], local[m], axis=1, mode="promise_in_bounds") for k in range(3)] for m in range(3)]
        for k in range(3):
            middle = (corner[0][k] + corner[1][k] + corner[2][k]) / 3.0
            lanes = slice(panels + k * cl + h * LANES, panels + k * cl + (h + 1) * LANES)
            payload_ref[:, lanes] = middle
            heavy_ref[:, lanes] = middle
            sums[k] = middle if h == 0 else sums[k] + middle
        one = [corner[1][k] - corner[0][k] for k in range(3)]
        two = [corner[2][k] - corner[0][k] for k in range(3)]
        normal = [one[1] * two[2] - one[2] * two[1], one[2] * two[0] - one[0] * two[2], one[0] * two[1] - one[1] * two[0]]
        area_ref[:, h * LANES:(h + 1) * LANES] = 0.5 * jnp.sqrt(normal[0] * normal[0] + normal[1] * normal[1] + normal[2] * normal[2])
    span = clusters * rank
    table = panels + 3 * cl
    mine = lax.broadcasted_iota(jnp.int32, (clusters, span), 1) // rank == lax.broadcasted_iota(jnp.int32, (clusters, span), 0)
    half = span // 2
    payload_ref[:, table + span:] = jnp.zeros_like(payload_ref[:, table + span:])
    for k in range(3):
        center = jnp.sum(sums[k], axis=1, keepdims=True) / cl
        center_ref[:, k * LANES:(k + 1) * LANES] = jnp.broadcast_to(center, (clusters, LANES))
        row = jnp.sum(jnp.where(mine, center, 0.0), axis=0, keepdims=True)
        payload_ref[k:k + 1, table + span:] = row[:, 0:half]
        payload_ref[8 + k:9 + k, table + span:] = row[:, half:]
    moves[2].wait()
    moves[3].wait()
    for c in range(clusters):
        lanes = slice(c * cl, (c + 1) * cl)
        basis_ref[:, lanes] = stacked(raw_ref[:, lanes])
        charges = area_ref[c:c + 1, :] * krylov_ref[:, lanes]
        payload_ref[:, lanes] = charges
        heavy_ref[:, lanes] = charges
        payload_ref[:, table + c * rank:table + (c + 1) * rank] = moments_of(charges, basis_ref[:, lanes])
    moves[4].wait()
    far = far_ref[...]
    step = (lax.div(far, clusters) - position_ref[0]) * (1 - 2 * lax.rem(position_ref[0], 2))
    block = jnp.where(step < 0, step + REACH, step + REACH - 3)
    per = LANES // rank
    turn = lax.rem(lax.broadcasted_iota(jnp.int32, far.shape, 1) - far + per * clusters * 2 ** 16, per)
    at_ref[...] = (turn * 6 + block) * (span // LANES) + lax.div(lax.rem(far, clusters), per)
    moves[5].wait()
    pairs_ref[...] = pair_list(near_ref[...], position_ref[0], clusters)
    moves[6].wait()


def features_of(payload_ref, panels, c, cl, target):
    rows = [payload_ref[c:c + 1, panels + k * cl:panels + (k + 1) * cl] for k in range(3)]
    value = jnp.concatenate(rows + [jnp.zeros((5, cl), F32)], axis=0)
    coarse = (value + GRID) - GRID
    middle = (value - coarse).astype(BF16).astype(F32)
    low = (value - coarse - middle).astype(BF16).astype(F32)
    pieces = [coarse, middle, low]
    rest = middle + low
    row = lax.broadcasted_iota(jnp.int32, (8, cl), 0)
    square = jnp.sum(coarse * coarse, axis=0, keepdims=True)
    extra = jnp.sum((2.0 * coarse + rest) * rest, axis=0, keepdims=True) + (SMOOTHING if target else 0.0)
    square_high = square.astype(BF16).astype(F32)
    extra_high = extra.astype(BF16).astype(F32)
    extra_middle = (extra - extra_high).astype(BF16).astype(F32)
    ones = jnp.ones((1, cl), F32)

    def placed(base, start, *values):
        for i, one in enumerate(values):
            base = jnp.where(row == start + i, one, base)
        return base

    squares, extras = (square_high, square - square_high), (extra_high, extra_middle, extra - extra_high - extra_middle)
    if target:
        scaled = [-2.0 * piece for piece in pieces]
        first = placed(scaled[0], 3, *squares, ones, ones)
        last = placed(jnp.zeros((8, cl), F32), 0, *extras, ones, ones, ones)
    else:
        first = placed(coarse, 3, ones, ones, *squares)
        last = placed(jnp.zeros((8, cl), F32), 0, ones, ones, ones, *extras)
    combos = [(scaled[i] if target else pieces[j]) for i in range(3) for j in range(3) if i + j]
    return jnp.concatenate([first, *combos, last], axis=0)


def fill_features(sources_ref, payload_ref, panels, cl):
    clusters = panels // cl
    for c in range(clusters):
        sources_ref[c] = features_of(payload_ref, panels, c, cl, False).astype(BF16)
    sources_ref[clusters] = sources_ref[0]


def near_block(source, target, pieces, out_ref):
    cl = source.shape[1]
    parts = []
    for first in range(0, cl, LANES):
        rows = slice(first, first + LANES)
        high, low = split(lax.rsqrt(dot_tn(source[:, rows], target)))
        out_ref[rows, :] = high
        out_ref[cl + first:cl + first + LANES, :] = low
        parts.append(dot_nn(pieces[:, rows], high) + dot_nn(pieces[:, rows], low))
    return sum(parts[1:], parts[0])


def near_product(pieces, block_ref, cl):
    return dot_nn(pieces, block_ref[0:cl, :]) + dot_nn(pieces, block_ref[cl:2 * cl, :])


def fill_charges(pieces_ref, payload_ref, clusters, cl):
    for c in range(clusters):
        pieces_ref[c] = stacked(payload_ref[:, c * cl:(c + 1) * cl])
    pieces_ref[clusters] = jnp.zeros_like(pieces_ref[0])


def pair_at(pairs_ref, which, i):
    pair = pairs_ref[which, i]
    return lax.shift_right_logical(pair, 6), lax.bitwise_and(pair, 63)


def near_kernel(cl, which, pairs_ref, payload_ref, table_ref, *refs):
    if which:
        targets_ref, start_ref, kept_ref, near_out_ref, tail_ref, pieces_ref, sources_ref, total_ref = refs
    else:
        own_ref, kept_ref, near_out_ref, targets_ref, tail_ref, pieces_ref, sources_ref, total_ref = refs
    tail_ref[...] = table_ref[:, table_ref.shape[1] - tail_ref.shape[1]:]
    panels = near_out_ref.shape[1]
    clusters = panels // cl
    group = kept_ref.shape[1]
    fill_charges(pieces_ref, payload_ref, clusters, cl)
    fill_features(sources_ref, payload_ref, panels, cl)
    if which:
        total_ref[...] = jnp.zeros_like(total_ref)
    else:
        for c in range(clusters):
            target = features_of(payload_ref, panels, c, cl, True).astype(BF16)
            targets_ref[c] = target
            total_ref[c] = near_block(sources_ref[c], target, pieces_ref[c], own_ref.at[c])

    def step(m, _):
        pairs = [pair_at(pairs_ref, which, group * m + w) for w in range(group)]
        loaded = [(sources_ref[j], targets_ref[c], pieces_ref[j]) for c, j in pairs]
        parts = [near_block(*one, kept_ref.at[m, w]) for w, one in enumerate(loaded)]
        for (c, j), part in zip(pairs, parts):
            total_ref[c] += part
        return 0

    lax.fori_loop(0, (pairs_ref[3 + which, 0] + group - 1) // group, step, 0)
    for c in range(clusters):
        lanes = slice(c * cl, (c + 1) * cl)
        near = folded(total_ref[c])
        near_out_ref[:, lanes] = start_ref[:, lanes] + near if which else near


def near_again_kernel(cl, which, pairs_ref, payload_ref, table_ref, *refs):
    if which:
        start_ref, kept_ref, near_out_ref, tail_ref, pieces_ref, total_ref = refs
    else:
        own_ref, kept_ref, near_out_ref, tail_ref, pieces_ref, total_ref = refs
    tail_ref[...] = table_ref[:, table_ref.shape[1] - tail_ref.shape[1]:]
    clusters = near_out_ref.shape[1] // cl
    group = kept_ref.shape[1]
    fill_charges(pieces_ref, payload_ref, clusters, cl)
    if which:
        total_ref[...] = jnp.zeros_like(total_ref)
    else:
        for c in range(clusters):
            total_ref[c] = near_product(pieces_ref[c], own_ref.at[c], cl)

    def step(m, _):
        pairs = [pair_at(pairs_ref, which, group * m + w) for w in range(group)]
        parts = [near_product(pieces_ref[j], kept_ref.at[m, w], cl) for w, (c, j) in enumerate(pairs)]
        for (c, j), part in zip(pairs, parts):
            total_ref[c] += part
        return 0

    lax.fori_loop(0, (pairs_ref[3 + which, 0] + group - 1) // group, step, 0)
    for c in range(clusters):
        lanes = slice(c * cl, (c + 1) * cl)
        near = folded(total_ref[c])
        near_out_ref[:, lanes] = start_ref[:, lanes] + near if which else near


def load_window(tables, clusters, rank, pieces_ref, middle_ref):
    per = LANES // rank
    span = clusters * rank
    count = pieces_ref.shape[0] // per
    groups = span // LANES
    for at in range(count):
        (ref, first), g = tables[at // groups], at % groups
        tile = ref[:, first + g * LANES:first + (g + 1) * LANES]
        for s in range(per):
            pieces_ref[s * count + at] = stacked(pltpu.roll(tile, s * rank, 1) if s else tile)
        if middle_ref is not None:
            half = groups // 2
            row, lane = 8 * (g // half), first + span + g % half * LANES
            tile = ref[row:row + 8, lane:lane + LANES]
            for s in range(per):
                middle_ref[s * count + at] = pltpu.roll(tile, s * rank, 1) if s else tile


def six_tables(near_ref, far_ref, swapped_ref):
    width = near_ref.shape[1] // 2
    return (far_ref, 0), (far_ref, width), (near_ref, 0), (swapped_ref, width), (swapped_ref, 0), (swapped_ref, 3 * width)


def pick(source_ref, at_ref, c, g, per, lane):
    row = None
    for u in range(per):
        take = source_ref[at_ref[c, g * per + u]]
        row = take if row is None else jnp.where(lane == u, take, row)
    return row


def far_fields(gathered_ref, coupling_ref, fields_ref):
    for c in range(gathered_ref.shape[0]):
        field = quartered(dot_nt(gathered_ref[c], coupling_ref[c]))
        fields_ref[c] = stacked(jnp.concatenate([field, field], axis=1))


def far_potential(fields_ref, c, basis):
    return folded(dot_nn(fields_ref[c], basis))


def image_kernel(cl, rank, at_ref, near_pair_ref, far_pair_ref, swapped_ref, center_ref, area_ref, near_ref, basis_ref, krylov_ref, offsets_ref,
                 image_ref, payload_ref, heavy_ref, coupling_ref, pieces_ref, middle_ref, gathered_ref, fields_ref):
    rhs, panels = near_ref.shape
    clusters = panels // cl
    per = LANES // rank
    span = clusters * rank
    load_window(six_tables(near_pair_ref, far_pair_ref, swapped_ref), clusters, rank, pieces_ref, middle_ref)
    lane = lax.broadcasted_iota(jnp.int32, (1, LANES), 1) // rank
    for c in range(clusters):
        mine = [offsets_ref[3, k:k + 1, :] - center_ref[c:c + 1, k * LANES:(k + 1) * LANES] for k in range(3)]
        for g in range(at_ref.shape[1] // per):
            lanes = slice(g * LANES, (g + 1) * LANES)
            gathered_ref[c, :, lanes] = pick(pieces_ref, at_ref, c, g, per, lane)
            center = pick(middle_ref, at_ref, c, g, per, lane)
            gap = [(center[k:k + 1] + mine[k]) - offsets_ref[k] for k in range(3)]
            high, low = split(lax.rsqrt(gap[0] * gap[0] + gap[1] * gap[1] + gap[2] * gap[2] + SMOOTHING))
            coupling_ref[c, 0:rank, lanes] = high
            coupling_ref[c, rank:2 * rank, lanes] = low
    far_fields(gathered_ref, coupling_ref, fields_ref)
    squared = correlation = jnp.zeros((rhs, cl), F32)
    for c in range(clusters):
        lanes = slice(c * cl, (c + 1) * cl)
        basis = basis_ref[:, lanes]
        area = area_ref[c:c + 1, :]
        image = COULOMB * area * (near_ref[:, lanes] + far_potential(fields_ref, c, basis))
        charges = area * image
        image_ref[:, lanes] = image
        payload_ref[:, lanes] = charges
        heavy_ref[:, lanes] = charges
        payload_ref[:, panels + c * rank:panels + (c + 1) * rank] = moments_of(charges, basis)
        krylov = krylov_ref[:, lanes]
        squared = squared + krylov * krylov
        correlation = correlation + krylov * image
    squared = jnp.sum(squared, axis=1, keepdims=True)
    correlation = jnp.sum(correlation, axis=1, keepdims=True)
    local = ratio(correlation, squared)
    residual = image_ref[...] - local * krylov_ref[...]
    payload_ref[:, panels + span:] = in_lanes(squared, correlation, jnp.sum(residual * residual, axis=1, keepdims=True), local)


def far_again_kernel(cl, rank, at_ref, near_pair_ref, far_pair_ref, swapped_ref, near_ref, area_ref, coupling_ref, basis_ref,
                     image_ref, pieces_ref, gathered_ref, fields_ref):
    clusters = near_ref.shape[1] // cl
    per = LANES // rank
    load_window(six_tables(near_pair_ref, far_pair_ref, swapped_ref), clusters, rank, pieces_ref, None)
    lane = lax.broadcasted_iota(jnp.int32, (1, LANES), 1) // rank
    for c in range(clusters):
        for g in range(at_ref.shape[1] // per):
            gathered_ref[c, :, g * LANES:(g + 1) * LANES] = pick(pieces_ref, at_ref, c, g, per, lane)
    far_fields(gathered_ref, coupling_ref, fields_ref)
    for c in range(clusters):
        lanes = slice(c * cl, (c + 1) * cl)
        image_ref[:, lanes] = COULOMB * area_ref[c:c + 1, :] * (near_ref[:, lanes] + far_potential(fields_ref, c, basis_ref[:, lanes]))


def finish_kernel(total, one_ref, two_ref, image_ref, again_ref, krylov_ref, next_hbm, second_hbm, next_ref, second_ref, sems):
    squared, correlation, energy, local = merged([one_ref[...], two_ref[...]])
    projection = correlation / (squared + 1e-06)
    gap = projection - local
    scaling = 1.0 / jnp.sqrt((energy + gap * gap * squared) / total + 1e-06)
    moves = []
    part = next_ref.shape[1] // 4
    for h in range(4):
        lanes = slice(h * part, (h + 1) * part)
        image = image_ref[:, lanes]
        next_ref[:, lanes] = (image - projection * krylov_ref[:, lanes]) * scaling
        second_ref[:, lanes] = (again_ref[:, lanes] - projection * image) * scaling
        for held, hbm in ((next_ref, next_hbm), (second_ref, second_hbm)):
            moves.append(pltpu.make_async_copy(held.at[:, lanes], hbm.at[:, lanes], sems.at[len(moves)]))
            moves[-1].start()
    for move in moves:
        move.wait()


def ratio(correlation, squared):
    return jnp.where(squared > 0, correlation / jnp.where(squared > 0, squared, 1.0), 0.0)


def in_lanes(*columns):
    lane = lax.broadcasted_iota(jnp.int32, (columns[0].shape[0], LANES), 1)
    out = columns[-1]
    for i, column in enumerate(columns[:-1]):
        out = jnp.where(lane == i, column, out)
    return out


def merged(groups):
    squared = sum(group[:, 0:1] for group in groups)
    correlation = sum(group[:, 1:2] for group in groups)
    local = ratio(correlation, squared)
    energy = 0.0
    for group in groups:
        gap = local - group[:, 3:4]
        energy = energy + (group[:, 2:3] + gap * gap * group[:, 0:1])
    return squared, correlation, energy, local


def window_sums_kernel(payload_ref, partner_ref, near_pair_ref, far_pair_ref, swapped_ref, out_ref):
    width = near_pair_ref.shape[1] // 2
    ends = [(payload_ref, payload_ref.shape[1]), (partner_ref, partner_ref.shape[1])]
    ends += [(ref, end) for ref in (near_pair_ref, far_pair_ref, swapped_ref) for end in (width, 2 * width)]
    out_ref[...] = in_lanes(*merged([ref[:, end - LANES:end] for ref, end in ends]))


def merge_kernel(one_ref, two_ref, out_ref):
    out_ref[...] = in_lanes(*merged([one_ref[...], two_ref[...]]))


def call(kernel, outs, scratch, memory, *args, limit=10, us=1.0):
    spaces = {"s": pltpu.SMEM, "v": pltpu.VMEM, "p": pltpu.VMEM, "h": pltpu.HBM}
    ins, out_spaces = memory.split(">")
    pinned = {"h": pltpu.HBM, "p": pltpu.VMEM}
    return pl.pallas_call(
        kernel,
        out_shape=[pltpu.VMEM(*out) if m == "p" else jax.ShapeDtypeStruct(*out) for m, out in zip(out_spaces, outs)],
        in_specs=[pl.BlockSpec(memory_space=spaces[m]) for m in ins],
        out_specs=[pl.BlockSpec(memory_space=spaces[m]) for m in out_spaces],
        scratch_shapes=scratch,
        compiler_params=pltpu.CompilerParams(vmem_limit_bytes=limit * 2 ** 20),
        cost_estimate=pl.CostEstimate(flops=int(us * 5e8), bytes_accessed=int(us * 3.6e6), transcendentals=0),
    )(*(pltpu.with_memory_space_constraint(a, pinned[m]) if m in pinned else a for m, a in zip(ins, args)))


def body(vertices, panel_vertices, near_pairs, far_pairs, basis, krylov):
    clusters, slots = near_pairs.shape
    partners = far_pairs.shape[1]
    rhs, panels = krylov.shape
    rank = basis.shape[0]
    cl = panels // clusters
    vcl = vertices.shape[1] // clusters
    span = clusters * rank
    per = LANES // rank
    devices = lax.axis_size("clus")
    position = lax.axis_index("clus").reshape(1).astype(jnp.int32)
    offsets = proxy_offsets(rank)
    flat = np.concatenate([np.tile(offsets, (1, per)), np.zeros((rank - 3, LANES), np.float32)])
    offsets = jnp.asarray(np.concatenate([np.broadcast_to(offsets[:, :, None], (3, rank, LANES)), flat[None]]))
    width = span + span // 2
    pairing = [(i, i + 1 - 2 * (i % 2)) for i in range(devices)]
    bridging = [(i, i - 1 + 2 * (i % 2)) for i in range(1, devices - 1)] + [(0, 0), (devices - 1, devices - 1)]

    def move(value, pairs):
        return lax.ppermute(value, "clus", pairs)

    def outward(value, steps):
        return move(value, [(i, (i + steps * (1 - 2 * (i % 2))) % devices) for i in range(devices)])

    def neighbours(payload, heavy):
        return move(payload, pairing), move(heavy, bridging)

    def pairs_away(tail, partner):
        pair = jnp.concatenate([tail, partner[:, partner.shape[1] - tail.shape[1]:]], axis=1)
        return outward(pair, 2), outward(pair, 4)

    def swapped(near_pair, far_pair, tail):
        return move(jnp.concatenate([near_pair, far_pair, tail], axis=1), pairing)

    whole = ((rhs, panels), F32)
    payload, heavy, area, centers, at, pairs, basis, krylov, offsets = call(
        functools.partial(prepare_kernel, cl, vcl, rank),
        [
            ((rhs, panels + 3 * cl + width), F32), ((rhs, panels + 3 * cl), F32), ((clusters, cl), F32), ((clusters, 3 * LANES), F32),
            (far_pairs.shape, jnp.int32), ((8, LANES), jnp.int32), ((2 * rank, panels), BF16), whole, (offsets.shape, F32),
        ],
        [
            pltpu.VMEM(vertices.shape, F32),
            pltpu.VMEM(panel_vertices.shape, jnp.int32),
            pltpu.VMEM(basis.shape, F32),
            pltpu.VMEM(far_pairs.shape, jnp.int32),
            pltpu.VMEM((slots, clusters), jnp.int32),
            pltpu.VMEM((3 * clusters, vcl), F32),
            pltpu.VMEM((3 * panels // LANES, LANES), jnp.int32),
            pltpu.SemaphoreType.DMA((7,)),
        ],
        "shhhhhhh>vvvvvvppp",
        position, vertices, panel_vertices, krylov, basis, far_pairs, near_pairs.T, offsets,
        us=1.5,
    )
    partner, other = neighbours(payload, heavy)
    group = 4
    own = ((clusters, 2 * cl, cl), BF16)
    kept = ((clusters * (slots - 1) // group, group, 2 * cl, cl), BF16)
    sums_shape = ((rhs, LANES), F32)
    total = pltpu.VMEM((clusters, 2 * rhs, cl), F32)
    pieces = pltpu.VMEM((clusters + 1, 2 * rhs, cl), BF16)
    sources = pltpu.VMEM((clusters + 1, FEATURES, cl), BF16)
    own_blocks, blocks, near, targets, tail = call(
        functools.partial(near_kernel, cl, 0),
        [own, kept, whole, ((clusters, FEATURES, cl), BF16), ((rhs, width), F32)],
        [pieces, sources, total],
        "svv>ppvpv",
        pairs, payload, payload,
        us=8.0,
    )
    near_pair, far_pair = pairs_away(tail, partner)
    blocks_partner, near, tail = call(
        functools.partial(near_kernel, cl, 1),
        [kept, whole, sums_shape],
        [pieces, sources, total],
        "svvpv>pvv",
        pairs, partner, payload, targets, near,
        us=4.0,
    )
    swap = swapped(near_pair, far_pair, tail)
    blocks_other, near, _ = call(
        functools.partial(near_kernel, cl, 2),
        [kept, whole, sums_shape],
        [pieces, sources, total],
        "svvpv>pvv",
        pairs, other, payload, targets, near,
        us=4.0,
    )
    tiles = 6 * per * span // LANES
    window = pltpu.VMEM((tiles, 2 * rhs, LANES), BF16)
    gathered = pltpu.VMEM((clusters, 2 * rhs, partners * rank), BF16)
    fields = pltpu.VMEM((clusters, 2 * rhs, 2 * rank), BF16)
    image, payload, heavy, coupling = call(
        functools.partial(image_kernel, cl, rank),
        [whole, ((rhs, panels + span + LANES), F32), whole, ((clusters, 2 * rank, partners * rank), BF16)],
        [window, pltpu.VMEM((tiles, 8, LANES), F32), gathered, fields],
        "svvvvvvppp>vvvp",
        at, near_pair, far_pair, swap, centers, area, near, basis, krylov, offsets,
        us=4.5,
    )
    partner, other = neighbours(payload, heavy)
    near, tail = call(
        functools.partial(near_again_kernel, cl, 0),
        [whole, ((rhs, span + LANES), F32)],
        [pieces, total],
        "svvpp>vv",
        pairs, payload, payload, own_blocks, blocks,
        us=8.0,
    )
    near_pair, far_pair = pairs_away(tail, partner)
    near, tail = call(
        functools.partial(near_again_kernel, cl, 1),
        [whole, sums_shape],
        [pieces, total],
        "svvvp>vv",
        pairs, partner, payload, near, blocks_partner,
        us=4.0,
    )
    swap = swapped(near_pair, far_pair, tail)
    near, _ = call(
        functools.partial(near_again_kernel, cl, 2),
        [whole, sums_shape],
        [pieces, total],
        "svvvp>vv",
        pairs, other, payload, near, blocks_other,
        us=4.0,
    )
    (one,) = call(window_sums_kernel, [sums_shape], [], "vvvvv>v", payload, partner, near_pair, far_pair, swap, us=0.3)
    size = 8
    many = outward(one, size)
    while 2 * size < devices:
        (one,) = call(merge_kernel, [sums_shape], [], "vv>v", one, many, us=0.3)
        size = 2 * size
        many = outward(one, size)
    (again,) = call(
        functools.partial(far_again_kernel, cl, rank),
        [whole],
        [window, gathered, fields],
        "svvvvvpp>v",
        at, near_pair, far_pair, swap, near, area, coupling, basis,
        us=2.0,
    )
    here = pltpu.VMEM((rhs, panels), F32)
    return tuple(call(
        functools.partial(finish_kernel, panels * devices),
        [whole, whole],
        [here, here, pltpu.SemaphoreType.DMA((8,))],
        "vvvvp>hh",
        one, many, image, again, krylov,
    ))


def solution(mesh):
    whole = P(None, ("jobs", "clus"))
    rows = P(("jobs", "clus"), None)
    return jax.shard_map(
        body,
        mesh=mesh,
        in_specs=(whole, whole, rows, rows, whole, whole),
        out_specs=(whole, whole),
        check_vma=False,
    )
```

```python
import functools

import jax
import jax.numpy as jnp
import numpy as np
from jax import lax
from jax.experimental import pallas as pl
from jax.experimental.pallas import tpu as pltpu
from jax.sharding import PartitionSpec as P

REACH = 4
SMOOTHING = 0.04
COULOMB = 2.0
PROXY_RADIUS = 0.6
LANES = 128
FEATURES = 80
GRID = 1.5 * 2.0 ** 22
F32 = jnp.float32
BF16 = jnp.bfloat16


def proxy_offsets(points):
    counter = np.arange(points, dtype=np.float32)
    height = 1.0 - (2.0 * counter + 1.0) / points
    radial = np.sqrt(1.0 - height * height)
    azimuth = counter * 2.399963
    return PROXY_RADIUS * np.stack([radial * np.cos(azimuth), radial * np.sin(azimuth), height]).astype(np.float32)


def split(value):
    high = value.astype(BF16)
    return high, (value - high.astype(F32)).astype(BF16)


def stacked(value):
    return jnp.concatenate(split(value), axis=0)


def folded(value):
    half = value.shape[0] // 2
    return value[:half] + value[half:]


def dot_nt(left, right):
    return lax.dot_general(left, right, (((1,), (1,)), ((), ())), preferred_element_type=F32)


def dot_tn(left, right):
    return lax.dot_general(left, right, (((0,), (0,)), ((), ())), preferred_element_type=F32)


def dot_nn(left, right):
    return lax.dot_general(left, right, (((1,), (0,)), ((), ())), preferred_element_type=F32)


def quartered(value):
    half = value.shape[1] // 2
    value = folded(value)
    return value[:, 0:half] + value[:, half:]


def moments_of(weighted, basis_pieces):
    return quartered(dot_nt(stacked(weighted), basis_pieces))


def copies(pairs, sems):
    moves = [pltpu.make_async_copy(source, target, sems.at[i]) for i, (source, target) in enumerate(pairs)]
    for move in moves:
        move.start()
    return moves


def pair_list(near, position, clusters):
    block = lax.div(near, clusters) - position
    side = block * (1 - 2 * lax.rem(position, 2))
    place = lax.rem(near, clusters).astype(F32)
    across = lax.broadcasted_iota(jnp.int32, (clusters, clusters), 1)
    down = lax.broadcasted_iota(jnp.int32, (clusters, clusters), 0)
    upright = lambda value: jnp.sum(jnp.where(across == down, value, 0.0), axis=1, keepdims=True)
    row = lax.broadcasted_iota(jnp.int32, (clusters, LANES), 1).astype(F32)
    target = lax.broadcasted_iota(jnp.int32, (clusters, 1), 0).astype(F32)
    rows = lax.broadcasted_iota(jnp.int32, (8, LANES), 0)
    out = jnp.zeros((8, LANES), F32)
    for which in range(3):
        live = jnp.where((side == (0, 1, -1)[which]) & (near >= 0), 1.0, 0.0)
        counts = sum(live[k:k + 1] for k in range(1, near.shape[0]))
        first = jnp.sum(jnp.where(across < down, counts, 0.0), axis=1, keepdims=True)
        found = jnp.zeros((clusters, LANES), F32)
        for k in range(1, near.shape[0]):
            alive = upright(live[k:k + 1])
            hit = jnp.where(row == first, alive, 0.0)
            found = found + hit * (target * 64 + upright(place[k:k + 1]))
            first = first + alive
        count = jnp.sum(counts, axis=1, keepdims=True)
        found = jnp.where(row[0:1] < count, jnp.sum(found, axis=0, keepdims=True), 1.0 * clusters)
        out = jnp.where(rows == which, found, jnp.where(rows == 3 + which, count, out))
    return out.astype(jnp.int32)


def prepare_kernel(cl, vcl, rank, position_ref, vertices_hbm, corners_hbm, krylov_hbm, basis_hbm, far_hbm, near_hbm, offsets_hbm,
                   payload_ref, table_ref, area_ref, center_ref, at_ref, pairs_ref, basis_ref, krylov_ref, offsets_ref,
                   vertices_ref, corners_ref, raw_ref, far_ref, near_ref, mesh_ref, local_ref, sems):
    moves = copies((
        (vertices_hbm, vertices_ref), (corners_hbm, corners_ref), (krylov_hbm, krylov_ref), (basis_hbm, raw_ref),
        (far_hbm, far_ref), (near_hbm, near_ref), (offsets_hbm, offsets_ref),
    ), sems)
    rhs, panels = krylov_ref.shape
    clusters = panels // cl
    parts = cl // LANES
    moves[0].wait()
    for c in range(clusters):
        mesh_ref[3 * c:3 * c + 3, :] = vertices_ref[:, c * vcl:(c + 1) * vcl]
    moves[1].wait()
    for i in range(clusters * parts):
        local_ref[3 * i:3 * i + 3, :] = corners_ref[:, i * LANES:(i + 1) * LANES]
    first = position_ref[0] * (vcl * clusters) + vcl * lax.broadcasted_iota(jnp.int32, (clusters, LANES), 0)
    tables = [mesh_ref[pl.ds(k, clusters, stride=3), :] for k in range(3)]
    sums = [None] * 3
    for h in range(parts):
        local = [local_ref[pl.ds(3 * h + m, clusters, stride=3 * parts), :] - first for m in range(3)]
        corner = [[jnp.take_along_axis(tables[k], local[m], axis=1, mode="promise_in_bounds") for k in range(3)] for m in range(3)]
        for k in range(3):
            middle = (corner[0][k] + corner[1][k] + corner[2][k]) / 3.0
            lanes = slice(panels + k * cl + h * LANES, panels + k * cl + (h + 1) * LANES)
            payload_ref[:, lanes] = middle
            sums[k] = middle if h == 0 else sums[k] + middle
        one = [corner[1][k] - corner[0][k] for k in range(3)]
        two = [corner[2][k] - corner[0][k] for k in range(3)]
        normal = [one[1] * two[2] - one[2] * two[1], one[2] * two[0] - one[0] * two[2], one[0] * two[1] - one[1] * two[0]]
        area_ref[:, h * LANES:(h + 1) * LANES] = 0.5 * jnp.sqrt(normal[0] * normal[0] + normal[1] * normal[1] + normal[2] * normal[2])
    span = clusters * rank
    mine = lax.broadcasted_iota(jnp.int32, (clusters, span), 1) // rank == lax.broadcasted_iota(jnp.int32, (clusters, span), 0)
    half = span // 2
    table_ref[:, span:] = jnp.zeros_like(table_ref[:, span:])
    for k in range(3):
        center = jnp.sum(sums[k], axis=1, keepdims=True) / cl
        center_ref[:, k * LANES:(k + 1) * LANES] = jnp.broadcast_to(center, (clusters, LANES))
        row = jnp.sum(jnp.where(mine, center, 0.0), axis=0, keepdims=True)
        table_ref[k:k + 1, span:] = row[:, 0:half]
        table_ref[8 + k:9 + k, span:] = row[:, half:]
    moves[2].wait()
    moves[3].wait()
    for c in range(clusters):
        lanes = slice(c * cl, (c + 1) * cl)
        basis_ref[:, lanes] = stacked(raw_ref[:, lanes])
        charges = area_ref[c:c + 1, :] * krylov_ref[:, lanes]
        payload_ref[:, lanes] = charges
        table_ref[:, c * rank:(c + 1) * rank] = moments_of(charges, basis_ref[:, lanes])
    moves[4].wait()
    far = far_ref[...]
    step = (lax.div(far, clusters) - position_ref[0]) * (1 - 2 * lax.rem(position_ref[0], 2))
    block = jnp.where(step < 0, step + REACH, step + REACH - 3)
    per = LANES // rank
    turn = lax.rem(lax.broadcasted_iota(jnp.int32, far.shape, 1) - far + per * clusters * 2 ** 16, per)
    at_ref[...] = (turn * 6 + block) * (span // LANES) + lax.div(lax.rem(far, clusters), per)
    moves[5].wait()
    pairs_ref[...] = pair_list(near_ref[...], position_ref[0], clusters)
    moves[6].wait()


def features_of(payload_ref, panels, c, cl, target):
    rows = [payload_ref[c:c + 1, panels + k * cl:panels + (k + 1) * cl] for k in range(3)]
    value = jnp.concatenate(rows + [jnp.zeros((5, cl), F32)], axis=0)
    coarse = (value + GRID) - GRID
    middle = (value - coarse).astype(BF16).astype(F32)
    low = (value - coarse - middle).astype(BF16).astype(F32)
    pieces = [coarse, middle, low]
    rest = middle + low
    row = lax.broadcasted_iota(jnp.int32, (8, cl), 0)
    square = jnp.sum(coarse * coarse, axis=0, keepdims=True)
    extra = jnp.sum((2.0 * coarse + rest) * rest, axis=0, keepdims=True) + (SMOOTHING if target else 0.0)
    square_high = square.astype(BF16).astype(F32)
    extra_high = extra.astype(BF16).astype(F32)
    extra_middle = (extra - extra_high).astype(BF16).astype(F32)
    ones = jnp.ones((1, cl), F32)

    def placed(base, start, *values):
        for i, one in enumerate(values):
            base = jnp.where(row == start + i, one, base)
        return base

    squares, extras = (square_high, square - square_high), (extra_high, extra_middle, extra - extra_high - extra_middle)
    if target:
        scaled = [-2.0 * piece for piece in pieces]
        first = placed(scaled[0], 3, *squares, ones, ones)
        last = placed(jnp.zeros((8, cl), F32), 0, *extras, ones, ones, ones)
    else:
        first = placed(coarse, 3, ones, ones, *squares)
        last = placed(jnp.zeros((8, cl), F32), 0, ones, ones, ones, *extras)
    combos = [(scaled[i] if target else pieces[j]) for i in range(3) for j in range(3) if i + j]
    return jnp.concatenate([first, *combos, last], axis=0)


def fill_features(sources_ref, payload_ref, panels, cl):
    clusters = panels // cl
    for c in range(clusters):
        sources_ref[c] = features_of(payload_ref, panels, c, cl, False).astype(BF16)
    sources_ref[clusters] = sources_ref[0]


def near_block(source, target, pieces, out_ref):
    cl = source.shape[1]
    parts = []
    for first in range(0, cl, LANES):
        rows = slice(first, first + LANES)
        high, low = split(lax.rsqrt(dot_tn(source[:, rows], target)))
        out_ref[rows, :] = high
        out_ref[cl + first:cl + first + LANES, :] = low
        parts.append(dot_nn(pieces[:, rows], high) + dot_nn(pieces[:, rows], low))
    return sum(parts[1:], parts[0])


def near_product(pieces, block_ref, cl):
    return dot_nn(pieces, block_ref[0:cl, :]) + dot_nn(pieces, block_ref[cl:2 * cl, :])


def fill_charges(pieces_ref, payload_ref, clusters, cl):
    for c in range(clusters):
        pieces_ref[c] = stacked(payload_ref[:, c * cl:(c + 1) * cl])
    pieces_ref[clusters] = jnp.zeros_like(pieces_ref[0])


def pair_at(pairs_ref, which, i):
    pair = pairs_ref[which, i]
    return lax.shift_right_logical(pair, 6), lax.bitwise_and(pair, 63)


def build_list(which, pairs_ref, targets_ref, kept_ref, pieces_ref, sources_ref, total_ref):
    group = kept_ref.shape[1]

    def step(m, _):
        pairs = [pair_at(pairs_ref, which, group * m + w) for w in range(group)]
        loaded = [(sources_ref[j], targets_ref[c], pieces_ref[j]) for c, j in pairs]
        parts = [near_block(*one, kept_ref.at[m, w]) for w, one in enumerate(loaded)]
        for (c, j), part in zip(pairs, parts):
            total_ref[c] += part
        return 0

    lax.fori_loop(0, (pairs_ref[3 + which, 0] + group - 1) // group, step, 0)


def apply_list(which, pairs_ref, kept_ref, pieces_ref, total_ref, cl):
    group = kept_ref.shape[1]

    def step(m, _):
        pairs = [pair_at(pairs_ref, which, group * m + w) for w in range(group)]
        parts = [near_product(pieces_ref[j], kept_ref.at[m, w], cl) for w, (c, j) in enumerate(pairs)]
        for (c, j), part in zip(pairs, parts):
            total_ref[c] += part
        return 0

    lax.fori_loop(0, (pairs_ref[3 + which, 0] + group - 1) // group, step, 0)


def put_total(cl, total_ref, start_ref, out_ref):
    for c in range(total_ref.shape[0]):
        lanes = slice(c * cl, (c + 1) * cl)
        near = folded(total_ref[c])
        out_ref[:, lanes] = near if start_ref is None else start_ref[:, lanes] + near


def own_kernel(cl, pairs_ref, payload_ref, beside_ref, own_ref, kept_ref, near_out_ref, targets_ref, tail_ref, pieces_ref, sources_ref, total_ref):
    tail_ref[...] = beside_ref[:, beside_ref.shape[1] - LANES:]
    panels = near_out_ref.shape[1]
    clusters = panels // cl
    fill_charges(pieces_ref, payload_ref, clusters, cl)
    fill_features(sources_ref, payload_ref, panels, cl)
    for c in range(clusters):
        target = features_of(payload_ref, panels, c, cl, True).astype(BF16)
        targets_ref[c] = target
        total_ref[c] = near_block(sources_ref[c], target, pieces_ref[c], own_ref.at[c])
    build_list(0, pairs_ref, targets_ref, kept_ref, pieces_ref, sources_ref, total_ref)
    put_total(cl, total_ref, None, near_out_ref)


def partner_kernel(cl, pairs_ref, payload_ref, targets_ref, start_ref, kept_ref, near_out_ref, pieces_ref, sources_ref, total_ref):
    panels = near_out_ref.shape[1]
    fill_charges(pieces_ref, payload_ref, panels // cl, cl)
    fill_features(sources_ref, payload_ref, panels, cl)
    total_ref[...] = jnp.zeros_like(total_ref)
    build_list(1, pairs_ref, targets_ref, kept_ref, pieces_ref, sources_ref, total_ref)
    put_total(cl, total_ref, start_ref, near_out_ref)


def image_kernel(cl, rank, pairs_ref, payload_ref, targets_ref, start_ref, area_ref, krylov_ref, basis_ref,
                 kept_ref, image_ref, charges_ref, table_ref, pieces_ref, sources_ref, total_ref):
    rhs, panels = image_ref.shape
    clusters = panels // cl
    span = clusters * rank
    fill_charges(pieces_ref, payload_ref, clusters, cl)
    fill_features(sources_ref, payload_ref, panels, cl)
    total_ref[...] = jnp.zeros_like(total_ref)
    build_list(2, pairs_ref, targets_ref, kept_ref, pieces_ref, sources_ref, total_ref)
    squared = correlation = jnp.zeros((rhs, cl), F32)
    for c in range(clusters):
        lanes = slice(c * cl, (c + 1) * cl)
        area = area_ref[c:c + 1, :]
        image = COULOMB * area * (start_ref[:, lanes] + folded(total_ref[c]))
        charges = area * image
        image_ref[:, lanes] = image
        charges_ref[:, lanes] = charges
        table_ref[:, c * rank:(c + 1) * rank] = moments_of(charges, basis_ref[:, lanes])
        krylov = krylov_ref[:, lanes]
        squared = squared + krylov * krylov
        correlation = correlation + krylov * image
    squared = jnp.sum(squared, axis=1, keepdims=True)
    correlation = jnp.sum(correlation, axis=1, keepdims=True)
    local = ratio(correlation, squared)
    energy = jnp.zeros((rhs, cl), F32)
    for c in range(clusters):
        lanes = slice(c * cl, (c + 1) * cl)
        residual = image_ref[:, lanes] - local * krylov_ref[:, lanes]
        energy = energy + residual * residual
    table_ref[:, span:] = in_lanes(squared, correlation, jnp.sum(energy, axis=1, keepdims=True), local)


def own_again_kernel(cl, pairs_ref, payload_ref, beside_ref, own_ref, kept_ref, near_out_ref, tail_ref, pieces_ref, total_ref):
    tail_ref[...] = beside_ref[:, beside_ref.shape[1] - LANES:]
    clusters = near_out_ref.shape[1] // cl
    fill_charges(pieces_ref, payload_ref, clusters, cl)
    for c in range(clusters):
        total_ref[c] = near_product(pieces_ref[c], own_ref.at[c], cl)
    apply_list(0, pairs_ref, kept_ref, pieces_ref, total_ref, cl)
    put_total(cl, total_ref, None, near_out_ref)


def partner_again_kernel(cl, pairs_ref, payload_ref, start_ref, kept_ref, near_out_ref, pieces_ref, total_ref):
    fill_charges(pieces_ref, payload_ref, near_out_ref.shape[1] // cl, cl)
    total_ref[...] = jnp.zeros_like(total_ref)
    apply_list(1, pairs_ref, kept_ref, pieces_ref, total_ref, cl)
    put_total(cl, total_ref, start_ref, near_out_ref)


def finish_kernel(cl, total, pairs_ref, payload_ref, start_ref, kept_ref, area_ref, image_ref, krylov_ref, one_ref, two_ref,
                  next_hbm, second_hbm, pieces_ref, total_ref, next_ref, second_ref, sems):
    panels = image_ref.shape[1]
    clusters = panels // cl
    squared, correlation, energy, local = merged([one_ref[...], two_ref[...]])
    projection = correlation / (squared + 1e-06)
    gap = projection - local
    scaling = 1.0 / jnp.sqrt((energy + gap * gap * squared) / total + 1e-06)
    for c in range(clusters):
        lanes = slice(c * cl, (c + 1) * cl)
        next_ref[:, lanes] = (image_ref[:, lanes] - projection * krylov_ref[:, lanes]) * scaling
    moves = copies(((next_ref, next_hbm),), sems)
    fill_charges(pieces_ref, payload_ref, clusters, cl)
    total_ref[...] = jnp.zeros_like(total_ref)
    apply_list(2, pairs_ref, kept_ref, pieces_ref, total_ref, cl)
    parts = 2
    for h in range(parts):
        for c in range(h * clusters // parts, (h + 1) * clusters // parts):
            lanes = slice(c * cl, (c + 1) * cl)
            again = COULOMB * area_ref[c:c + 1, :] * (start_ref[:, lanes] + folded(total_ref[c]))
            second_ref[:, lanes] = (again - projection * image_ref[:, lanes]) * scaling
        lanes = slice(h * panels // parts, (h + 1) * panels // parts)
        moves.append(pltpu.make_async_copy(second_ref.at[:, lanes], second_hbm.at[:, lanes], sems.at[1 + h]))
        moves[-1].start()
    for move in moves:
        move.wait()


def load_window(tables, clusters, rank, pieces_ref, middle_ref):
    per = LANES // rank
    span = clusters * rank
    count = pieces_ref.shape[0] // per
    groups = span // LANES
    for at in range(count):
        (ref, first), g = tables[at // groups], at % groups
        tile = ref[:, first + g * LANES:first + (g + 1) * LANES]
        for s in range(per):
            pieces_ref[s * count + at] = stacked(pltpu.roll(tile, s * rank, 1) if s else tile)
        if middle_ref is not None:
            half = groups // 2
            row, lane = 8 * (g // half), first + span + g % half * LANES
            tile = ref[row:row + 8, lane:lane + LANES]
            for s in range(per):
                middle_ref[s * count + at] = pltpu.roll(tile, s * rank, 1) if s else tile


def six_tables(near_ref, far_ref, swapped_ref):
    width = near_ref.shape[1] // 2
    return (far_ref, 0), (far_ref, width), (near_ref, 0), (swapped_ref, width), (swapped_ref, 0), (swapped_ref, 3 * width)


def pick(source_ref, at_ref, c, g, per, lane):
    row = None
    for u in range(per):
        take = source_ref[at_ref[c, g * per + u]]
        row = take if row is None else jnp.where(lane == u, take, row)
    return row


def far_fields(gathered_ref, coupling_ref, fields_ref):
    for c in range(gathered_ref.shape[0]):
        field = quartered(dot_nt(gathered_ref[c], coupling_ref[c]))
        fields_ref[c] = stacked(jnp.concatenate([field, field], axis=1))


def far_potential(fields_ref, c, basis):
    return folded(dot_nn(fields_ref[c], basis))


def far_kernel(cl, rank, at_ref, near_pair_ref, far_pair_ref, swapped_ref, center_ref, near_ref, basis_ref, offsets_ref,
               out_ref, coupling_ref, pieces_ref, middle_ref, gathered_ref, fields_ref):
    clusters = near_ref.shape[1] // cl
    per = LANES // rank
    load_window(six_tables(near_pair_ref, far_pair_ref, swapped_ref), clusters, rank, pieces_ref, middle_ref)
    lane = lax.broadcasted_iota(jnp.int32, (1, LANES), 1) // rank
    for c in range(clusters):
        mine = [offsets_ref[3, k:k + 1, :] - center_ref[c:c + 1, k * LANES:(k + 1) * LANES] for k in range(3)]
        for g in range(at_ref.shape[1] // per):
            lanes = slice(g * LANES, (g + 1) * LANES)
            gathered_ref[c, :, lanes] = pick(pieces_ref, at_ref, c, g, per, lane)
            center = pick(middle_ref, at_ref, c, g, per, lane)
            gap = [(center[k:k + 1] + mine[k]) - offsets_ref[k] for k in range(3)]
            high, low = split(lax.rsqrt(gap[0] * gap[0] + gap[1] * gap[1] + gap[2] * gap[2] + SMOOTHING))
            coupling_ref[c, 0:rank, lanes] = high
            coupling_ref[c, rank:2 * rank, lanes] = low
    far_fields(gathered_ref, coupling_ref, fields_ref)
    for c in range(clusters):
        lanes = slice(c * cl, (c + 1) * cl)
        out_ref[:, lanes] = near_ref[:, lanes] + far_potential(fields_ref, c, basis_ref[:, lanes])


def far_again_kernel(cl, rank, at_ref, near_pair_ref, far_pair_ref, swapped_ref, near_ref, coupling_ref, basis_ref,
                     out_ref, pieces_ref, gathered_ref, fields_ref):
    clusters = near_ref.shape[1] // cl
    per = LANES // rank
    load_window(six_tables(near_pair_ref, far_pair_ref, swapped_ref), clusters, rank, pieces_ref, None)
    lane = lax.broadcasted_iota(jnp.int32, (1, LANES), 1) // rank
    for c in range(clusters):
        for g in range(at_ref.shape[1] // per):
            gathered_ref[c, :, g * LANES:(g + 1) * LANES] = pick(pieces_ref, at_ref, c, g, per, lane)
    far_fields(gathered_ref, coupling_ref, fields_ref)
    for c in range(clusters):
        lanes = slice(c * cl, (c + 1) * cl)
        out_ref[:, lanes] = near_ref[:, lanes] + far_potential(fields_ref, c, basis_ref[:, lanes])


def ratio(correlation, squared):
    return jnp.where(squared > 0, correlation / jnp.where(squared > 0, squared, 1.0), 0.0)


def in_lanes(*columns):
    lane = lax.broadcasted_iota(jnp.int32, (columns[0].shape[0], LANES), 1)
    out = columns[-1]
    for i, column in enumerate(columns[:-1]):
        out = jnp.where(lane == i, column, out)
    return out


def merged(groups):
    squared = sum(group[:, 0:1] for group in groups)
    correlation = sum(group[:, 1:2] for group in groups)
    local = ratio(correlation, squared)
    energy = 0.0
    for group in groups:
        gap = local - group[:, 3:4]
        energy = energy + (group[:, 2:3] + gap * gap * group[:, 0:1])
    return squared, correlation, energy, local


def window_sums_kernel(payload_ref, partner_ref, near_pair_ref, far_pair_ref, swapped_ref, out_ref):
    width = near_pair_ref.shape[1] // 2
    ends = [(payload_ref, payload_ref.shape[1]), (partner_ref, partner_ref.shape[1])]
    ends += [(ref, end) for ref in (near_pair_ref, far_pair_ref, swapped_ref) for end in (width, 2 * width)]
    out_ref[...] = in_lanes(*merged([ref[:, end - LANES:end] for ref, end in ends]))


def merge_kernel(one_ref, two_ref, out_ref):
    out_ref[...] = in_lanes(*merged([one_ref[...], two_ref[...]]))


def call(kernel, outs, scratch, memory, *args, limit=10, us=1.0):
    spaces = {"s": pltpu.SMEM, "v": pltpu.VMEM, "p": pltpu.VMEM, "h": pltpu.HBM}
    ins, out_spaces = memory.split(">")
    pinned = {"h": pltpu.HBM, "p": pltpu.VMEM}
    return pl.pallas_call(
        kernel,
        out_shape=[pltpu.VMEM(*out) if m == "p" else jax.ShapeDtypeStruct(*out) for m, out in zip(out_spaces, outs)],
        in_specs=[pl.BlockSpec(memory_space=spaces[m]) for m in ins],
        out_specs=[pl.BlockSpec(memory_space=spaces[m]) for m in out_spaces],
        scratch_shapes=scratch,
        compiler_params=pltpu.CompilerParams(vmem_limit_bytes=limit * 2 ** 20),
        cost_estimate=pl.CostEstimate(flops=int(us * 5e8), bytes_accessed=int(us * 3.6e6), transcendentals=0),
    )(*(pltpu.with_memory_space_constraint(a, pinned[m]) if m in pinned else a for m, a in zip(ins, args)))


def body(vertices, panel_vertices, near_pairs, far_pairs, basis, krylov):
    clusters, slots = near_pairs.shape
    partners = far_pairs.shape[1]
    rhs, panels = krylov.shape
    rank = basis.shape[0]
    cl = panels // clusters
    vcl = vertices.shape[1] // clusters
    span = clusters * rank
    per = LANES // rank
    devices = lax.axis_size("clus")
    position = lax.axis_index("clus").reshape(1).astype(jnp.int32)
    offsets = proxy_offsets(rank)
    flat = np.concatenate([np.tile(offsets, (1, per)), np.zeros((rank - 3, LANES), np.float32)])
    offsets = jnp.asarray(np.concatenate([np.broadcast_to(offsets[:, :, None], (3, rank, LANES)), flat[None]]))
    width = span + span // 2
    pairing = [(i, i + 1 - 2 * (i % 2)) for i in range(devices)]
    bridging = [(i, i - 1 + 2 * (i % 2)) for i in range(1, devices - 1)] + [(0, 0), (devices - 1, devices - 1)]

    def move(value, pairs):
        return lax.ppermute(value, "clus", pairs)

    def outward(value, steps):
        return move(value, [(i, (i + steps * (1 - 2 * (i % 2))) % devices) for i in range(devices)])

    def exchange(payload, table):
        beside = move(table, pairing)
        pair = jnp.concatenate([table, beside], axis=1)
        near_pair, far_pair = outward(pair, 2), outward(pair, 4)
        last = move(jnp.concatenate([payload, beside[:, beside.shape[1] - LANES:]], axis=1), bridging)
        return beside, near_pair, far_pair, last, move(payload, pairing)

    def swapped(near_pair, far_pair, tail):
        return move(jnp.concatenate([near_pair, far_pair, tail], axis=1), pairing)

    whole = ((rhs, panels), F32)
    payload, table, area, centers, at, pairs, basis, krylov, offsets = call(
        functools.partial(prepare_kernel, cl, vcl, rank),
        [
            ((rhs, panels + 3 * cl), F32), ((rhs, width), F32), ((clusters, cl), F32), ((clusters, 3 * LANES), F32),
            (far_pairs.shape, jnp.int32), ((8, LANES), jnp.int32), ((2 * rank, panels), BF16), whole, (offsets.shape, F32),
        ],
        [
            pltpu.VMEM(vertices.shape, F32),
            pltpu.VMEM(panel_vertices.shape, jnp.int32),
            pltpu.VMEM(basis.shape, F32),
            pltpu.VMEM(far_pairs.shape, jnp.int32),
            pltpu.VMEM((slots, clusters), jnp.int32),
            pltpu.VMEM((3 * clusters, vcl), F32),
            pltpu.VMEM((3 * panels // LANES, LANES), jnp.int32),
            pltpu.SemaphoreType.DMA((7,)),
        ],
        "shhhhhhh>vvvvvvppp",
        position, vertices, panel_vertices, krylov, basis, far_pairs, near_pairs.T, offsets,
        us=1.5,
    )
    beside, near_pair, far_pair, other, partner = exchange(payload, table)
    group = 4
    own = ((clusters, 2 * cl, cl), BF16)
    kept = ((clusters * (slots - 1) // group, group, 2 * cl, cl), BF16)
    sums_shape = ((rhs, LANES), F32)
    total = pltpu.VMEM((clusters, 2 * rhs, cl), F32)
    pieces = pltpu.VMEM((clusters + 1, 2 * rhs, cl), BF16)
    sources = pltpu.VMEM((clusters + 1, FEATURES, cl), BF16)
    own_blocks, blocks, near, targets, tail = call(
        functools.partial(own_kernel, cl),
        [own, kept, whole, ((clusters, FEATURES, cl), BF16), sums_shape],
        [pieces, sources, total],
        "svv>ppvpv",
        pairs, payload, beside,
        us=8.0,
    )
    swap = swapped(near_pair, far_pair, tail)
    blocks_partner, near = call(
        functools.partial(partner_kernel, cl),
        [kept, whole],
        [pieces, sources, total],
        "svpv>pv",
        pairs, partner, targets, near,
        us=4.0,
    )
    tiles = 6 * per * span // LANES
    window = pltpu.VMEM((tiles, 2 * rhs, LANES), BF16)
    gathered = pltpu.VMEM((clusters, 2 * rhs, partners * rank), BF16)
    fields = pltpu.VMEM((clusters, 2 * rhs, 2 * rank), BF16)
    near, coupling = call(
        functools.partial(far_kernel, cl, rank),
        [whole, ((clusters, 2 * rank, partners * rank), BF16)],
        [window, pltpu.VMEM((tiles, 8, LANES), F32), gathered, fields],
        "svvvvvpp>vp",
        at, near_pair, far_pair, swap, centers, near, basis, offsets,
        us=4.0,
    )
    blocks_other, image, payload, table = call(
        functools.partial(image_kernel, cl, rank),
        [kept, whole, whole, ((rhs, span + LANES), F32)],
        [pieces, sources, total],
        "svpvvpp>pvvv",
        pairs, other, targets, near, area, krylov, basis,
        us=4.0,
    )
    beside, near_pair, far_pair, other, partner = exchange(payload, table)
    near, tail = call(
        functools.partial(own_again_kernel, cl),
        [whole, sums_shape],
        [pieces, total],
        "svvpp>vv",
        pairs, payload, beside, own_blocks, blocks,
        us=8.0,
    )
    swap = swapped(near_pair, far_pair, tail)
    (near,) = call(
        functools.partial(partner_again_kernel, cl),
        [whole],
        [pieces, total],
        "svvp>v",
        pairs, partner, near, blocks_partner,
        us=4.0,
    )
    (one,) = call(window_sums_kernel, [sums_shape], [], "vvvvv>v", table, beside, near_pair, far_pair, swap, us=0.3)
    size = 8
    many = outward(one, size)
    while 2 * size < devices:
        (one,) = call(merge_kernel, [sums_shape], [], "vv>v", one, many, us=0.3)
        size = 2 * size
        many = outward(one, size)
    (near,) = call(
        functools.partial(far_again_kernel, cl, rank),
        [whole],
        [window, gathered, fields],
        "svvvvpp>v",
        at, near_pair, far_pair, swap, near, coupling, basis,
        us=4.0,
    )
    here = pltpu.VMEM((rhs, panels), F32)
    return tuple(call(
        functools.partial(finish_kernel, cl, panels * devices),
        [whole, whole],
        [pieces, total, here, here, pltpu.SemaphoreType.DMA((3,))],
        "svvpvvpvv>hh",
        pairs, other, near, blocks_other, area, image, krylov, one, many,
        us=3.0,
    ))


def solution(mesh):
    whole = P(None, ("jobs", "clus"))
    rows = P(("jobs", "clus"), None)
    return jax.shard_map(
        body,
        mesh=mesh,
        in_specs=(whole, whole, rows, rows, whole, whole),
        out_specs=(whole, whole),
        check_vma=False,
    )
```

```python
import functools

import jax
import jax.numpy as jnp
import numpy as np
from jax import lax
from jax.experimental import pallas as pl
from jax.experimental.pallas import tpu as pltpu
from jax.sharding import PartitionSpec as P

REACH = 4
SMOOTHING = 0.04
COULOMB = 2.0
PROXY_RADIUS = 0.6
LANES = 128
FEATURES = 80
GRID = 1.5 * 2.0 ** 22
F32 = jnp.float32
BF16 = jnp.bfloat16


def proxy_offsets(points):
    counter = np.arange(points, dtype=np.float32)
    height = 1.0 - (2.0 * counter + 1.0) / points
    radial = np.sqrt(1.0 - height * height)
    azimuth = counter * 2.399963
    return PROXY_RADIUS * np.stack([radial * np.cos(azimuth), radial * np.sin(azimuth), height]).astype(np.float32)


def split(value):
    high = value.astype(BF16)
    return high, (value - high.astype(F32)).astype(BF16)


def stacked(value):
    return jnp.concatenate(split(value), axis=0)


def folded(value):
    half = value.shape[0] // 2
    return value[:half] + value[half:]


def dot_nt(left, right):
    return lax.dot_general(left, right, (((1,), (1,)), ((), ())), preferred_element_type=F32)


def dot_tn(left, right):
    return lax.dot_general(left, right, (((0,), (0,)), ((), ())), preferred_element_type=F32)


def dot_nn(left, right):
    return lax.dot_general(left, right, (((1,), (0,)), ((), ())), preferred_element_type=F32)


def quartered(value):
    half = value.shape[1] // 2
    value = folded(value)
    return value[:, 0:half] + value[:, half:]


def moments_of(weighted, basis_pieces):
    return quartered(dot_nt(stacked(weighted), basis_pieces))


def copies(pairs, sems):
    moves = [pltpu.make_async_copy(source, target, sems.at[i]) for i, (source, target) in enumerate(pairs)]
    for move in moves:
        move.start()
    return moves


def pair_list(near, position, clusters):
    block = lax.div(near, clusters) - position
    side = block * (1 - 2 * lax.rem(position, 2))
    place = lax.rem(near, clusters).astype(F32)
    across = lax.broadcasted_iota(jnp.int32, (clusters, clusters), 1)
    down = lax.broadcasted_iota(jnp.int32, (clusters, clusters), 0)
    upright = lambda value: jnp.sum(jnp.where(across == down, value, 0.0), axis=1, keepdims=True)
    row = lax.broadcasted_iota(jnp.int32, (clusters, LANES), 1).astype(F32)
    target = lax.broadcasted_iota(jnp.int32, (clusters, 1), 0).astype(F32)
    rows = lax.broadcasted_iota(jnp.int32, (8, LANES), 0)
    out = jnp.zeros((8, LANES), F32)
    for which in range(3):
        live = jnp.where((side == (0, 1, -1)[which]) & (near >= 0), 1.0, 0.0)
        counts = sum(live[k:k + 1] for k in range(1, near.shape[0]))
        first = jnp.sum(jnp.where(across < down, counts, 0.0), axis=1, keepdims=True)
        found = jnp.zeros((clusters, LANES), F32)
        for k in range(1, near.shape[0]):
            alive = upright(live[k:k + 1])
            hit = jnp.where(row == first, alive, 0.0)
            found = found + hit * (target * 64 + upright(place[k:k + 1]))
            first = first + alive
        count = jnp.sum(counts, axis=1, keepdims=True)
        found = jnp.where(row[0:1] < count, jnp.sum(found, axis=0, keepdims=True), 1.0 * clusters)
        out = jnp.where(rows == which, found, jnp.where(rows == 3 + which, count, out))
    return out.astype(jnp.int32)


def prepare_kernel(cl, vcl, rank, position_ref, vertices_hbm, corners_hbm, krylov_hbm, basis_hbm, far_hbm, near_hbm, offsets_hbm,
                   payload_ref, table_ref, area_ref, center_ref, at_ref, pairs_ref, basis_ref, krylov_ref, offsets_ref,
                   vertices_ref, corners_ref, raw_ref, far_ref, near_ref, mesh_ref, local_ref, sems):
    moves = copies((
        (vertices_hbm, vertices_ref), (corners_hbm, corners_ref), (krylov_hbm, krylov_ref), (basis_hbm, raw_ref),
        (far_hbm, far_ref), (near_hbm, near_ref), (offsets_hbm, offsets_ref),
    ), sems)
    rhs, panels = krylov_ref.shape
    clusters = panels // cl
    parts = cl // LANES
    moves[0].wait()
    for c in range(clusters):
        mesh_ref[3 * c:3 * c + 3, :] = vertices_ref[:, c * vcl:(c + 1) * vcl]
    moves[1].wait()
    for i in range(clusters * parts):
        local_ref[3 * i:3 * i + 3, :] = corners_ref[:, i * LANES:(i + 1) * LANES]
    first = position_ref[0] * (vcl * clusters) + vcl * lax.broadcasted_iota(jnp.int32, (clusters, LANES), 0)
    tables = [mesh_ref[pl.ds(k, clusters, stride=3), :] for k in range(3)]
    sums = [None] * 3
    for h in range(parts):
        local = [local_ref[pl.ds(3 * h + m, clusters, stride=3 * parts), :] - first for m in range(3)]
        corner = [[jnp.take_along_axis(tables[k], local[m], axis=1, mode="promise_in_bounds") for k in range(3)] for m in range(3)]
        for k in range(3):
            middle = (corner[0][k] + corner[1][k] + corner[2][k]) / 3.0
            lanes = slice(panels + k * cl + h * LANES, panels + k * cl + (h + 1) * LANES)
            payload_ref[:, lanes] = middle
            sums[k] = middle if h == 0 else sums[k] + middle
        one = [corner[1][k] - corner[0][k] for k in range(3)]
        two = [corner[2][k] - corner[0][k] for k in range(3)]
        normal = [one[1] * two[2] - one[2] * two[1], one[2] * two[0] - one[0] * two[2], one[0] * two[1] - one[1] * two[0]]
        area_ref[:, h * LANES:(h + 1) * LANES] = 0.5 * jnp.sqrt(normal[0] * normal[0] + normal[1] * normal[1] + normal[2] * normal[2])
    span = clusters * rank
    mine = lax.broadcasted_iota(jnp.int32, (clusters, span), 1) // rank == lax.broadcasted_iota(jnp.int32, (clusters, span), 0)
    half = span // 2
    table_ref[:, span:] = jnp.zeros_like(table_ref[:, span:])
    for k in range(3):
        center = jnp.sum(sums[k], axis=1, keepdims=True) / cl
        center_ref[:, k * LANES:(k + 1) * LANES] = jnp.broadcast_to(center, (clusters, LANES))
        row = jnp.sum(jnp.where(mine, center, 0.0), axis=0, keepdims=True)
        table_ref[k:k + 1, span:] = row[:, 0:half]
        table_ref[8 + k:9 + k, span:] = row[:, half:]
    moves[2].wait()
    moves[3].wait()
    for c in range(clusters):
        lanes = slice(c * cl, (c + 1) * cl)
        basis_ref[:, lanes] = stacked(raw_ref[:, lanes])
        charges = area_ref[c:c + 1, :] * krylov_ref[:, lanes]
        payload_ref[:, lanes] = charges
        table_ref[:, c * rank:(c + 1) * rank] = moments_of(charges, basis_ref[:, lanes])
    moves[4].wait()
    far = far_ref[...]
    step = (lax.div(far, clusters) - position_ref[0]) * (1 - 2 * lax.rem(position_ref[0], 2))
    block = jnp.where(step < 0, step + REACH, step + REACH - 3)
    per = LANES // rank
    turn = lax.rem(lax.broadcasted_iota(jnp.int32, far.shape, 1) - far + per * clusters * 2 ** 16, per)
    at_ref[...] = (turn * 6 + block) * (span // LANES) + lax.div(lax.rem(far, clusters), per)
    moves[5].wait()
    pairs_ref[...] = pair_list(near_ref[...], position_ref[0], clusters)
    moves[6].wait()


def features_of(payload_ref, panels, c, cl, target):
    rows = [payload_ref[c:c + 1, panels + k * cl:panels + (k + 1) * cl] for k in range(3)]
    value = jnp.concatenate(rows + [jnp.zeros((5, cl), F32)], axis=0)
    coarse = (value + GRID) - GRID
    middle = (value - coarse).astype(BF16).astype(F32)
    low = (value - coarse - middle).astype(BF16).astype(F32)
    pieces = [coarse, middle, low]
    rest = middle + low
    row = lax.broadcasted_iota(jnp.int32, (8, cl), 0)
    square = jnp.sum(coarse * coarse, axis=0, keepdims=True)
    extra = jnp.sum((2.0 * coarse + rest) * rest, axis=0, keepdims=True) + (SMOOTHING if target else 0.0)
    square_high = square.astype(BF16).astype(F32)
    extra_high = extra.astype(BF16).astype(F32)
    extra_middle = (extra - extra_high).astype(BF16).astype(F32)
    ones = jnp.ones((1, cl), F32)

    def placed(base, start, *values):
        for i, one in enumerate(values):
            base = jnp.where(row == start + i, one, base)
        return base

    squares, extras = (square_high, square - square_high), (extra_high, extra_middle, extra - extra_high - extra_middle)
    if target:
        scaled = [-2.0 * piece for piece in pieces]
        first = placed(scaled[0], 3, *squares, ones, ones)
        last = placed(jnp.zeros((8, cl), F32), 0, *extras, ones, ones, ones)
    else:
        first = placed(coarse, 3, ones, ones, *squares)
        last = placed(jnp.zeros((8, cl), F32), 0, ones, ones, ones, *extras)
    combos = [(scaled[i] if target else pieces[j]) for i in range(3) for j in range(3) if i + j]
    return jnp.concatenate([first, *combos, last], axis=0)


def fill_features(sources_ref, payload_ref, panels, cl):
    clusters = panels // cl
    for c in range(clusters):
        sources_ref[c] = features_of(payload_ref, panels, c, cl, False).astype(BF16)
    sources_ref[clusters] = sources_ref[0]


def near_block(source, target, pieces, out_ref):
    cl = source.shape[1]
    parts = []
    for first in range(0, cl, LANES):
        rows = slice(first, first + LANES)
        high, low = split(lax.rsqrt(dot_tn(source[:, rows], target)))
        out_ref[rows, :] = high
        out_ref[cl + first:cl + first + LANES, :] = low
        parts.append(dot_nn(pieces[:, rows], high) + dot_nn(pieces[:, rows], low))
    return sum(parts[1:], parts[0])


def near_product(pieces, block_ref, cl):
    return dot_nn(pieces, block_ref[0:cl, :]) + dot_nn(pieces, block_ref[cl:2 * cl, :])


def fill_charges(pieces_ref, payload_ref, clusters, cl):
    for c in range(clusters):
        pieces_ref[c] = stacked(payload_ref[:, c * cl:(c + 1) * cl])
    pieces_ref[clusters] = jnp.zeros_like(pieces_ref[0])


def pair_at(pairs_ref, which, i):
    pair = pairs_ref[which, i]
    return lax.shift_right_logical(pair, 6), lax.bitwise_and(pair, 63)


def build_list(which, pairs_ref, targets_ref, kept_ref, pieces_ref, sources_ref, total_ref):
    group = kept_ref.shape[1]

    def step(m, _):
        pairs = [pair_at(pairs_ref, which, group * m + w) for w in range(group)]
        loaded = [(sources_ref[j], targets_ref[c], pieces_ref[j]) for c, j in pairs]
        parts = [near_block(*one, kept_ref.at[m, w]) for w, one in enumerate(loaded)]
        for (c, j), part in zip(pairs, parts):
            total_ref[c] += part
        return 0

    lax.fori_loop(0, (pairs_ref[3 + which, 0] + group - 1) // group, step, 0)


def apply_list(which, pairs_ref, kept_ref, pieces_ref, total_ref, cl):
    group = kept_ref.shape[1]

    def step(m, _):
        pairs = [pair_at(pairs_ref, which, group * m + w) for w in range(group)]
        parts = [near_product(pieces_ref[j], kept_ref.at[m, w], cl) for w, (c, j) in enumerate(pairs)]
        for (c, j), part in zip(pairs, parts):
            total_ref[c] += part
        return 0

    lax.fori_loop(0, (pairs_ref[3 + which, 0] + group - 1) // group, step, 0)


def put_total(cl, total_ref, start_ref, out_ref):
    for c in range(total_ref.shape[0]):
        lanes = slice(c * cl, (c + 1) * cl)
        near = folded(total_ref[c])
        out_ref[:, lanes] = near if start_ref is None else start_ref[:, lanes] + near


def own_kernel(cl, pairs_ref, payload_ref, beside_ref, own_ref, kept_ref, near_out_ref, targets_ref, tail_ref, pieces_ref, sources_ref, total_ref):
    tail_ref[...] = beside_ref[:, beside_ref.shape[1] - LANES:]
    panels = near_out_ref.shape[1]
    clusters = panels // cl
    fill_charges(pieces_ref, payload_ref, clusters, cl)
    fill_features(sources_ref, payload_ref, panels, cl)
    for c in range(clusters):
        target = features_of(payload_ref, panels, c, cl, True).astype(BF16)
        targets_ref[c] = target
        total_ref[c] = near_block(sources_ref[c], target, pieces_ref[c], own_ref.at[c])
    build_list(0, pairs_ref, targets_ref, kept_ref, pieces_ref, sources_ref, total_ref)
    put_total(cl, total_ref, None, near_out_ref)


def partner_kernel(cl, pairs_ref, payload_ref, targets_ref, start_ref, kept_ref, near_out_ref, pieces_ref, sources_ref, total_ref):
    panels = near_out_ref.shape[1]
    fill_charges(pieces_ref, payload_ref, panels // cl, cl)
    fill_features(sources_ref, payload_ref, panels, cl)
    total_ref[...] = jnp.zeros_like(total_ref)
    build_list(1, pairs_ref, targets_ref, kept_ref, pieces_ref, sources_ref, total_ref)
    put_total(cl, total_ref, start_ref, near_out_ref)


def image_kernel(cl, rank, pairs_ref, payload_ref, targets_ref, start_ref, area_ref, krylov_ref, basis_ref,
                 kept_ref, image_ref, charges_ref, table_ref, pieces_ref, sources_ref, total_ref):
    rhs, panels = image_ref.shape
    clusters = panels // cl
    span = clusters * rank
    fill_charges(pieces_ref, payload_ref, clusters, cl)
    fill_features(sources_ref, payload_ref, panels, cl)
    total_ref[...] = jnp.zeros_like(total_ref)
    build_list(2, pairs_ref, targets_ref, kept_ref, pieces_ref, sources_ref, total_ref)
    squared = correlation = jnp.zeros((rhs, cl), F32)
    for c in range(clusters):
        lanes = slice(c * cl, (c + 1) * cl)
        area = area_ref[c:c + 1, :]
        image = COULOMB * area * (start_ref[:, lanes] + folded(total_ref[c]))
        charges = area * image
        image_ref[:, lanes] = image
        charges_ref[:, lanes] = charges
        table_ref[:, c * rank:(c + 1) * rank] = moments_of(charges, basis_ref[:, lanes])
        krylov = krylov_ref[:, lanes]
        squared = squared + krylov * krylov
        correlation = correlation + krylov * image
    squared = jnp.sum(squared, axis=1, keepdims=True)
    correlation = jnp.sum(correlation, axis=1, keepdims=True)
    local = ratio(correlation, squared)
    energy = jnp.zeros((rhs, cl), F32)
    for c in range(clusters):
        lanes = slice(c * cl, (c + 1) * cl)
        residual = image_ref[:, lanes] - local * krylov_ref[:, lanes]
        energy = energy + residual * residual
    table_ref[:, span:] = in_lanes(squared, correlation, jnp.sum(energy, axis=1, keepdims=True), local)


def own_again_kernel(cl, pairs_ref, payload_ref, beside_ref, own_ref, kept_ref, near_out_ref, tail_ref, pieces_ref, total_ref):
    tail_ref[...] = beside_ref[:, beside_ref.shape[1] - LANES:]
    clusters = near_out_ref.shape[1] // cl
    fill_charges(pieces_ref, payload_ref, clusters, cl)
    for c in range(clusters):
        total_ref[c] = near_product(pieces_ref[c], own_ref.at[c], cl)
    apply_list(0, pairs_ref, kept_ref, pieces_ref, total_ref, cl)
    put_total(cl, total_ref, None, near_out_ref)


def partner_again_kernel(cl, pairs_ref, payload_ref, start_ref, kept_ref, near_out_ref, pieces_ref, total_ref):
    fill_charges(pieces_ref, payload_ref, near_out_ref.shape[1] // cl, cl)
    total_ref[...] = jnp.zeros_like(total_ref)
    apply_list(1, pairs_ref, kept_ref, pieces_ref, total_ref, cl)
    put_total(cl, total_ref, start_ref, near_out_ref)


def finish_kernel(cl, total, pairs_ref, payload_ref, start_ref, kept_ref, area_ref, image_ref, krylov_ref, one_ref, two_ref,
                  next_hbm, second_hbm, pieces_ref, total_ref, next_ref, second_ref, sems):
    panels = image_ref.shape[1]
    clusters = panels // cl
    squared, correlation, energy, local = merged([one_ref[...], two_ref[...]])
    projection = correlation / (squared + 1e-06)
    gap = projection - local
    scaling = 1.0 / jnp.sqrt((energy + gap * gap * squared) / total + 1e-06)
    for c in range(clusters):
        lanes = slice(c * cl, (c + 1) * cl)
        next_ref[:, lanes] = (image_ref[:, lanes] - projection * krylov_ref[:, lanes]) * scaling
    moves = copies(((next_ref, next_hbm),), sems)
    fill_charges(pieces_ref, payload_ref, clusters, cl)
    total_ref[...] = jnp.zeros_like(total_ref)
    apply_list(2, pairs_ref, kept_ref, pieces_ref, total_ref, cl)
    parts = 2
    for h in range(parts):
        for c in range(h * clusters // parts, (h + 1) * clusters // parts):
            lanes = slice(c * cl, (c + 1) * cl)
            again = COULOMB * area_ref[c:c + 1, :] * (start_ref[:, lanes] + folded(total_ref[c]))
            second_ref[:, lanes] = (again - projection * image_ref[:, lanes]) * scaling
        lanes = slice(h * panels // parts, (h + 1) * panels // parts)
        moves.append(pltpu.make_async_copy(second_ref.at[:, lanes], second_hbm.at[:, lanes], sems.at[1 + h]))
        moves[-1].start()
    for move in moves:
        move.wait()


def load_window(tables, clusters, rank, pieces_ref, middle_ref):
    per = LANES // rank
    span = clusters * rank
    count = pieces_ref.shape[0] // per
    groups = span // LANES
    for at in range(count):
        (ref, first), g = tables[at // groups], at % groups
        tile = ref[:, first + g * LANES:first + (g + 1) * LANES]
        for s in range(per):
            pieces_ref[s * count + at] = stacked(pltpu.roll(tile, s * rank, 1) if s else tile)
        if middle_ref is not None:
            half = groups // 2
            row, lane = 8 * (g // half), first + span + g % half * LANES
            tile = ref[row:row + 8, lane:lane + LANES]
            for s in range(per):
                middle_ref[s * count + at] = pltpu.roll(tile, s * rank, 1) if s else tile


def six_tables(near_ref, far_ref, swapped_ref):
    width = near_ref.shape[1] // 2
    return (far_ref, 0), (far_ref, width), (near_ref, 0), (swapped_ref, width), (swapped_ref, 0), (swapped_ref, 3 * width)


def pick(source_ref, at_ref, c, g, per, lane):
    row = None
    for u in range(per):
        take = source_ref[at_ref[c, g * per + u]]
        row = take if row is None else jnp.where(lane == u, take, row)
    return row


def far_fields(gathered_ref, coupling_ref, fields_ref):
    for c in range(gathered_ref.shape[0]):
        field = quartered(dot_nt(coupling_ref[c], gathered_ref[c]))
        field = jnp.concatenate(split(field), axis=1)
        fields_ref[c] = jnp.concatenate([field, field], axis=0)


def far_potential(fields_ref, c, basis):
    return folded(dot_tn(fields_ref[c], basis))


def far_kernel(cl, rank, at_ref, near_pair_ref, far_pair_ref, swapped_ref, center_ref, near_ref, basis_ref, offsets_ref,
               out_ref, coupling_ref, pieces_ref, middle_ref, gathered_ref, fields_ref):
    clusters = near_ref.shape[1] // cl
    per = LANES // rank
    load_window(six_tables(near_pair_ref, far_pair_ref, swapped_ref), clusters, rank, pieces_ref, middle_ref)
    lane = lax.broadcasted_iota(jnp.int32, (1, LANES), 1) // rank
    for c in range(clusters):
        mine = [offsets_ref[3, k:k + 1, :] - center_ref[c:c + 1, k * LANES:(k + 1) * LANES] for k in range(3)]
        for g in range(at_ref.shape[1] // per):
            lanes = slice(g * LANES, (g + 1) * LANES)
            gathered_ref[c, :, lanes] = pick(pieces_ref, at_ref, c, g, per, lane)
            center = pick(middle_ref, at_ref, c, g, per, lane)
            gap = [(center[k:k + 1] + mine[k]) - offsets_ref[k] for k in range(3)]
            high, low = split(lax.rsqrt(gap[0] * gap[0] + gap[1] * gap[1] + gap[2] * gap[2] + SMOOTHING))
            coupling_ref[c, 0:rank, lanes] = high
            coupling_ref[c, rank:2 * rank, lanes] = low
    far_fields(gathered_ref, coupling_ref, fields_ref)
    for c in range(clusters):
        lanes = slice(c * cl, (c + 1) * cl)
        out_ref[:, lanes] = near_ref[:, lanes] + far_potential(fields_ref, c, basis_ref[:, lanes])


def far_again_kernel(cl, rank, at_ref, near_pair_ref, far_pair_ref, swapped_ref, near_ref, coupling_ref, basis_ref,
                     out_ref, pieces_ref, gathered_ref, fields_ref):
    clusters = near_ref.shape[1] // cl
    per = LANES // rank
    load_window(six_tables(near_pair_ref, far_pair_ref, swapped_ref), clusters, rank, pieces_ref, None)
    lane = lax.broadcasted_iota(jnp.int32, (1, LANES), 1) // rank
    for c in range(clusters):
        for g in range(at_ref.shape[1] // per):
            gathered_ref[c, :, g * LANES:(g + 1) * LANES] = pick(pieces_ref, at_ref, c, g, per, lane)
    far_fields(gathered_ref, coupling_ref, fields_ref)
    for c in range(clusters):
        lanes = slice(c * cl, (c + 1) * cl)
        out_ref[:, lanes] = near_ref[:, lanes] + far_potential(fields_ref, c, basis_ref[:, lanes])


def ratio(correlation, squared):
    return jnp.where(squared > 0, correlation / jnp.where(squared > 0, squared, 1.0), 0.0)


def in_lanes(*columns):
    lane = lax.broadcasted_iota(jnp.int32, (columns[0].shape[0], LANES), 1)
    out = columns[-1]
    for i, column in enumerate(columns[:-1]):
        out = jnp.where(lane == i, column, out)
    return out


def merged(groups):
    squared = sum(group[:, 0:1] for group in groups)
    correlation = sum(group[:, 1:2] for group in groups)
    local = ratio(correlation, squared)
    energy = 0.0
    for group in groups:
        gap = local - group[:, 3:4]
        energy = energy + (group[:, 2:3] + gap * gap * group[:, 0:1])
    return squared, correlation, energy, local


def window_sums_kernel(payload_ref, partner_ref, near_pair_ref, far_pair_ref, swapped_ref, out_ref):
    width = near_pair_ref.shape[1] // 2
    ends = [(payload_ref, payload_ref.shape[1]), (partner_ref, partner_ref.shape[1])]
    ends += [(ref, end) for ref in (near_pair_ref, far_pair_ref, swapped_ref) for end in (width, 2 * width)]
    out_ref[...] = in_lanes(*merged([ref[:, end - LANES:end] for ref, end in ends]))


def merge_kernel(one_ref, two_ref, out_ref):
    out_ref[...] = in_lanes(*merged([one_ref[...], two_ref[...]]))


def call(kernel, outs, scratch, memory, *args, limit=10, us=1.0):
    spaces = {"s": pltpu.SMEM, "v": pltpu.VMEM, "p": pltpu.VMEM, "h": pltpu.HBM}
    ins, out_spaces = memory.split(">")
    pinned = {"h": pltpu.HBM, "p": pltpu.VMEM}
    return pl.pallas_call(
        kernel,
        out_shape=[pltpu.VMEM(*out) if m == "p" else jax.ShapeDtypeStruct(*out) for m, out in zip(out_spaces, outs)],
        in_specs=[pl.BlockSpec(memory_space=spaces[m]) for m in ins],
        out_specs=[pl.BlockSpec(memory_space=spaces[m]) for m in out_spaces],
        scratch_shapes=scratch,
        compiler_params=pltpu.CompilerParams(vmem_limit_bytes=limit * 2 ** 20),
        cost_estimate=pl.CostEstimate(flops=int(us * 5e8), bytes_accessed=int(us * 3.6e6), transcendentals=0),
    )(*(pltpu.with_memory_space_constraint(a, pinned[m]) if m in pinned else a for m, a in zip(ins, args)))


def body(vertices, panel_vertices, near_pairs, far_pairs, basis, krylov):
    clusters, slots = near_pairs.shape
    partners = far_pairs.shape[1]
    rhs, panels = krylov.shape
    rank = basis.shape[0]
    cl = panels // clusters
    vcl = vertices.shape[1] // clusters
    span = clusters * rank
    per = LANES // rank
    devices = lax.axis_size("clus")
    position = lax.axis_index("clus").reshape(1).astype(jnp.int32)
    offsets = proxy_offsets(rank)
    flat = np.concatenate([np.tile(offsets, (1, per)), np.zeros((rank - 3, LANES), np.float32)])
    offsets = jnp.asarray(np.concatenate([np.broadcast_to(offsets[:, :, None], (3, rank, LANES)), flat[None]]))
    width = span + span // 2
    pairing = [(i, i + 1 - 2 * (i % 2)) for i in range(devices)]
    bridging = [(i, i - 1 + 2 * (i % 2)) for i in range(1, devices - 1)] + [(0, 0), (devices - 1, devices - 1)]

    def move(value, pairs):
        return lax.ppermute(value, "clus", pairs)

    def outward(value, steps):
        return move(value, [(i, (i + steps * (1 - 2 * (i % 2))) % devices) for i in range(devices)])

    def exchange(payload, table):
        beside = move(table, pairing)
        pair = jnp.concatenate([table, beside], axis=1)
        near_pair, far_pair = outward(pair, 2), outward(pair, 4)
        sent = jnp.concatenate([payload, beside[:, beside.shape[1] - LANES:]], axis=1)
        return sent, beside, near_pair, far_pair, move(sent, bridging), move(payload, pairing)

    def swapped(near_pair, far_pair, tail):
        return move(jnp.concatenate([near_pair, far_pair, tail], axis=1), pairing)

    whole = ((rhs, panels), F32)
    payload, table, area, centers, at, pairs, basis, krylov, offsets = call(
        functools.partial(prepare_kernel, cl, vcl, rank),
        [
            ((rhs, panels + 3 * cl), F32), ((rhs, width), F32), ((clusters, cl), F32), ((clusters, 3 * LANES), F32),
            (far_pairs.shape, jnp.int32), ((8, LANES), jnp.int32), ((2 * rank, panels), BF16), whole, (offsets.shape, F32),
        ],
        [
            pltpu.VMEM(vertices.shape, F32),
            pltpu.VMEM(panel_vertices.shape, jnp.int32),
            pltpu.VMEM(basis.shape, F32),
            pltpu.VMEM(far_pairs.shape, jnp.int32),
            pltpu.VMEM((slots, clusters), jnp.int32),
            pltpu.VMEM((3 * clusters, vcl), F32),
            pltpu.VMEM((3 * panels // LANES, LANES), jnp.int32),
            pltpu.SemaphoreType.DMA((7,)),
        ],
        "shhhhhhh>vvvvvvppp",
        position, vertices, panel_vertices, krylov, basis, far_pairs, near_pairs.T, offsets,
        us=1.5,
    )
    sent, beside, near_pair, far_pair, other, partner = exchange(payload, table)
    group = 4
    own = ((clusters, 2 * cl, cl), BF16)
    kept = ((clusters * (slots - 1) // group, group, 2 * cl, cl), BF16)
    sums_shape = ((rhs, LANES), F32)
    total = pltpu.VMEM((clusters, 2 * rhs, cl), F32)
    pieces = pltpu.VMEM((clusters + 1, 2 * rhs, cl), BF16)
    sources = pltpu.VMEM((clusters + 1, FEATURES, cl), BF16)
    own_blocks, blocks, near, targets, tail = call(
        functools.partial(own_kernel, cl),
        [own, kept, whole, ((clusters, FEATURES, cl), BF16), sums_shape],
        [pieces, sources, total],
        "svv>ppvpv",
        pairs, sent, beside,
        us=8.0,
    )
    swap = swapped(near_pair, far_pair, tail)
    blocks_partner, near = call(
        functools.partial(partner_kernel, cl),
        [kept, whole],
        [pieces, sources, total],
        "svpv>pv",
        pairs, partner, targets, near,
        us=0.2,
    )
    tiles = 6 * per * span // LANES
    window = pltpu.VMEM((tiles, 2 * rhs, LANES), BF16)
    gathered = pltpu.VMEM((clusters, 2 * rhs, partners * rank), BF16)
    fields = pltpu.VMEM((clusters, 2 * rank, 2 * rhs), BF16)
    near, coupling = call(
        functools.partial(far_kernel, cl, rank),
        [whole, ((clusters, 2 * rank, partners * rank), BF16)],
        [window, pltpu.VMEM((tiles, 8, LANES), F32), gathered, fields],
        "svvvvvpp>vp",
        at, near_pair, far_pair, swap, centers, near, basis, offsets,
        us=0.2,
    )
    blocks_other, image, payload, table = call(
        functools.partial(image_kernel, cl, rank),
        [kept, whole, whole, ((rhs, span + LANES), F32)],
        [pieces, sources, total],
        "svpvvpp>pvvv",
        pairs, other, targets, near, area, krylov, basis,
        us=4.0,
    )
    sent, beside, near_pair, far_pair, other, partner = exchange(payload, table)
    near, tail = call(
        functools.partial(own_again_kernel, cl),
        [whole, sums_shape],
        [pieces, total],
        "svvpp>vv",
        pairs, sent, beside, own_blocks, blocks,
        us=8.0,
    )
    swap = swapped(near_pair, far_pair, tail)
    (near,) = call(
        functools.partial(partner_again_kernel, cl),
        [whole],
        [pieces, total],
        "svvp>v",
        pairs, partner, near, blocks_partner,
        us=4.0,
    )
    (one,) = call(window_sums_kernel, [sums_shape], [], "vvvvv>v", table, beside, near_pair, far_pair, swap, us=0.3)
    size = 8
    many = outward(one, size)
    while 2 * size < devices:
        (one,) = call(merge_kernel, [sums_shape], [], "vv>v", one, many, us=0.3)
        size = 2 * size
        many = outward(one, size)
    (near,) = call(
        functools.partial(far_again_kernel, cl, rank),
        [whole],
        [window, gathered, fields],
        "svvvvpp>v",
        at, near_pair, far_pair, swap, near, coupling, basis,
        us=4.0,
    )
    here = pltpu.VMEM((rhs, panels), F32)
    return tuple(call(
        functools.partial(finish_kernel, cl, panels * devices),
        [whole, whole],
        [pieces, total, here, here, pltpu.SemaphoreType.DMA((3,))],
        "svvpvvpvv>hh",
        pairs, other, near, blocks_other, area, image, krylov, one, many,
        us=3.0,
    ))


def solution(mesh):
    whole = P(None, ("jobs", "clus"))
    rows = P(("jobs", "clus"), None)
    return jax.shard_map(
        body,
        mesh=mesh,
        in_specs=(whole, whole, rows, rows, whole, whole),
        out_specs=(whole, whole),
        check_vma=False,
    )
```

```python
import functools

import jax
import jax.numpy as jnp
import numpy as np
from jax import lax
from jax.experimental import pallas as pl
from jax.experimental.pallas import tpu as pltpu
from jax.sharding import PartitionSpec as P

REACH = 4
SMOOTHING = 0.04
COULOMB = 2.0
PROXY_RADIUS = 0.6
LANES = 128
FEATURES = 80
GRID = 1.5 * 2.0 ** 22
F32 = jnp.float32
BF16 = jnp.bfloat16


def proxy_offsets(points):
    counter = np.arange(points, dtype=np.float32)
    height = 1.0 - (2.0 * counter + 1.0) / points
    radial = np.sqrt(1.0 - height * height)
    azimuth = counter * 2.399963
    return PROXY_RADIUS * np.stack([radial * np.cos(azimuth), radial * np.sin(azimuth), height]).astype(np.float32)


def split(value):
    high = value.astype(BF16)
    return high, (value - high.astype(F32)).astype(BF16)


def stacked(value):
    return jnp.concatenate(split(value), axis=0)


def folded(value):
    half = value.shape[0] // 2
    return value[:half] + value[half:]


def dot_nt(left, right):
    return lax.dot_general(left, right, (((1,), (1,)), ((), ())), preferred_element_type=F32)


def dot_tn(left, right):
    return lax.dot_general(left, right, (((0,), (0,)), ((), ())), preferred_element_type=F32)


def dot_nn(left, right):
    return lax.dot_general(left, right, (((1,), (0,)), ((), ())), preferred_element_type=F32)


def quartered(value):
    half = value.shape[1] // 2
    value = folded(value)
    return value[:, 0:half] + value[:, half:]


def moments_of(weighted, basis_pieces):
    return quartered(dot_nt(stacked(weighted), basis_pieces))


def copies(pairs, sems):
    moves = [pltpu.make_async_copy(source, target, sems.at[i]) for i, (source, target) in enumerate(pairs)]
    for move in moves:
        move.start()
    return moves


def pair_list(near, position, clusters):
    block = lax.div(near, clusters) - position
    side = block * (1 - 2 * lax.rem(position, 2))
    place = lax.rem(near, clusters).astype(F32)
    across = lax.broadcasted_iota(jnp.int32, (clusters, clusters), 1)
    down = lax.broadcasted_iota(jnp.int32, (clusters, clusters), 0)
    upright = lambda value: jnp.sum(jnp.where(across == down, value, 0.0), axis=1, keepdims=True)
    row = lax.broadcasted_iota(jnp.int32, (clusters, LANES), 1).astype(F32)
    target = lax.broadcasted_iota(jnp.int32, (clusters, 1), 0).astype(F32)
    rows = lax.broadcasted_iota(jnp.int32, (8, LANES), 0)
    out = jnp.zeros((8, LANES), F32)
    for which in range(3):
        live = jnp.where((side == (0, 1, -1)[which]) & (near >= 0), 1.0, 0.0)
        counts = sum(live[k:k + 1] for k in range(1, near.shape[0]))
        first = jnp.sum(jnp.where(across < down, counts, 0.0), axis=1, keepdims=True)
        found = jnp.zeros((clusters, LANES), F32)
        for k in range(1, near.shape[0]):
            alive = upright(live[k:k + 1])
            hit = jnp.where(row == first, alive, 0.0)
            found = found + hit * (target * 64 + upright(place[k:k + 1]))
            first = first + alive
        count = jnp.sum(counts, axis=1, keepdims=True)
        found = jnp.where(row[0:1] < count, jnp.sum(found, axis=0, keepdims=True), 1.0 * clusters)
        out = jnp.where(rows == which, found, jnp.where(rows == 3 + which, count, out))
    return out.astype(jnp.int32)


def prepare_kernel(cl, vcl, rank, position_ref, vertices_hbm, corners_hbm, krylov_hbm, basis_hbm, far_hbm, near_hbm, offsets_hbm,
                   payload_ref, table_ref, area_ref, center_ref, at_ref, pairs_ref, basis_ref, krylov_ref, offsets_ref,
                   vertices_ref, corners_ref, raw_ref, far_ref, near_ref, mesh_ref, local_ref, sems):
    moves = copies((
        (vertices_hbm, vertices_ref), (corners_hbm, corners_ref), (krylov_hbm, krylov_ref), (basis_hbm, raw_ref),
        (far_hbm, far_ref), (near_hbm, near_ref), (offsets_hbm, offsets_ref),
    ), sems)
    rhs, panels = krylov_ref.shape
    clusters = panels // cl
    parts = cl // LANES
    moves[0].wait()
    for c in range(clusters):
        mesh_ref[3 * c:3 * c + 3, :] = vertices_ref[:, c * vcl:(c + 1) * vcl]
    moves[1].wait()
    for i in range(clusters * parts):
        local_ref[3 * i:3 * i + 3, :] = corners_ref[:, i * LANES:(i + 1) * LANES]
    first = position_ref[0] * (vcl * clusters) + vcl * lax.broadcasted_iota(jnp.int32, (clusters, LANES), 0)
    tables = [mesh_ref[pl.ds(k, clusters, stride=3), :] for k in range(3)]
    sums = [None] * 3
    for h in range(parts):
        local = [local_ref[pl.ds(3 * h + m, clusters, stride=3 * parts), :] - first for m in range(3)]
        corner = [[jnp.take_along_axis(tables[k], local[m], axis=1, mode="promise_in_bounds") for k in range(3)] for m in range(3)]
        for k in range(3):
            middle = (corner[0][k] + corner[1][k] + corner[2][k]) / 3.0
            lanes = slice(panels + k * cl + h * LANES, panels + k * cl + (h + 1) * LANES)
            payload_ref[:, lanes] = middle
            sums[k] = middle if h == 0 else sums[k] + middle
        one = [corner[1][k] - corner[0][k] for k in range(3)]
        two = [corner[2][k] - corner[0][k] for k in range(3)]
        normal = [one[1] * two[2] - one[2] * two[1], one[2] * two[0] - one[0] * two[2], one[0] * two[1] - one[1] * two[0]]
        area_ref[:, h * LANES:(h + 1) * LANES] = 0.5 * jnp.sqrt(normal[0] * normal[0] + normal[1] * normal[1] + normal[2] * normal[2])
    span = clusters * rank
    mine = lax.broadcasted_iota(jnp.int32, (clusters, span), 1) // rank == lax.broadcasted_iota(jnp.int32, (clusters, span), 0)
    half = span // 2
    table_ref[:, span:] = jnp.zeros_like(table_ref[:, span:])
    for k in range(3):
        center = jnp.sum(sums[k], axis=1, keepdims=True) / cl
        center_ref[:, k * LANES:(k + 1) * LANES] = jnp.broadcast_to(center, (clusters, LANES))
        row = jnp.sum(jnp.where(mine, center, 0.0), axis=0, keepdims=True)
        table_ref[k:k + 1, span:] = row[:, 0:half]
        table_ref[8 + k:9 + k, span:] = row[:, half:]
    moves[2].wait()
    moves[3].wait()
    for c in range(clusters):
        lanes = slice(c * cl, (c + 1) * cl)
        basis_ref[:, lanes] = stacked(raw_ref[:, lanes])
        charges = area_ref[c:c + 1, :] * krylov_ref[:, lanes]
        payload_ref[:, lanes] = charges
        table_ref[:, c * rank:(c + 1) * rank] = moments_of(charges, basis_ref[:, lanes])
    moves[4].wait()
    far = far_ref[...]
    step = (lax.div(far, clusters) - position_ref[0]) * (1 - 2 * lax.rem(position_ref[0], 2))
    block = jnp.where(step < 0, step + REACH, step + REACH - 3)
    per = LANES // rank
    turn = lax.rem(lax.broadcasted_iota(jnp.int32, far.shape, 1) - far + per * clusters * 2 ** 16, per)
    at_ref[...] = (turn * 6 + block) * (span // LANES) + lax.div(lax.rem(far, clusters), per)
    moves[5].wait()
    pairs_ref[...] = pair_list(near_ref[...], position_ref[0], clusters)
    moves[6].wait()


def features_of(payload_ref, panels, c, cl, target):
    rows = [payload_ref[c:c + 1, panels + k * cl:panels + (k + 1) * cl] for k in range(3)]
    value = jnp.concatenate(rows + [jnp.zeros((5, cl), F32)], axis=0)
    coarse = (value + GRID) - GRID
    middle = (value - coarse).astype(BF16).astype(F32)
    low = (value - coarse - middle).astype(BF16).astype(F32)
    pieces = [coarse, middle, low]
    rest = middle + low
    row = lax.broadcasted_iota(jnp.int32, (8, cl), 0)
    square = jnp.sum(coarse * coarse, axis=0, keepdims=True)
    extra = jnp.sum((2.0 * coarse + rest) * rest, axis=0, keepdims=True) + (SMOOTHING if target else 0.0)
    square_high = square.astype(BF16).astype(F32)
    extra_high = extra.astype(BF16).astype(F32)
    extra_middle = (extra - extra_high).astype(BF16).astype(F32)
    ones = jnp.ones((1, cl), F32)

    def placed(base, start, *values):
        for i, one in enumerate(values):
            base = jnp.where(row == start + i, one, base)
        return base

    squares, extras = (square_high, square - square_high), (extra_high, extra_middle, extra - extra_high - extra_middle)
    if target:
        scaled = [-2.0 * piece for piece in pieces]
        first = placed(scaled[0], 3, *squares, ones, ones)
        last = placed(jnp.zeros((8, cl), F32), 0, *extras, ones, ones, ones)
    else:
        first = placed(coarse, 3, ones, ones, *squares)
        last = placed(jnp.zeros((8, cl), F32), 0, ones, ones, ones, *extras)
    combos = [(scaled[i] if target else pieces[j]) for i in range(3) for j in range(3) if i + j]
    return jnp.concatenate([first, *combos, last], axis=0)


def fill_features(sources_ref, payload_ref, panels, cl):
    clusters = panels // cl
    for c in range(clusters):
        sources_ref[c] = features_of(payload_ref, panels, c, cl, False).astype(BF16)
    sources_ref[clusters] = sources_ref[0]


def near_block(source, target, pieces, out_ref):
    cl = source.shape[1]
    parts = []
    for first in range(0, cl, LANES):
        rows = slice(first, first + LANES)
        high, low = split(lax.rsqrt(dot_tn(source[:, rows], target)))
        out_ref[rows, :] = high
        out_ref[cl + first:cl + first + LANES, :] = low
        parts.append(dot_nn(pieces[:, rows], high) + dot_nn(pieces[:, rows], low))
    return sum(parts[1:], parts[0])


def near_product(pieces, block_ref, cl):
    return dot_nn(pieces, block_ref[0:cl, :]) + dot_nn(pieces, block_ref[cl:2 * cl, :])


def fill_charges(pieces_ref, payload_ref, clusters, cl):
    for c in range(clusters):
        pieces_ref[c] = stacked(payload_ref[:, c * cl:(c + 1) * cl])
    pieces_ref[clusters] = jnp.zeros_like(pieces_ref[0])


def pair_at(pairs_ref, which, i):
    pair = pairs_ref[which, i]
    return lax.shift_right_logical(pair, 6), lax.bitwise_and(pair, 63)


def build_list(which, pairs_ref, targets_ref, kept_ref, pieces_ref, sources_ref, total_ref):
    group = kept_ref.shape[1]

    def step(m, _):
        pairs = [pair_at(pairs_ref, which, group * m + w) for w in range(group)]
        loaded = [(sources_ref[j], targets_ref[c], pieces_ref[j]) for c, j in pairs]
        parts = [near_block(*one, kept_ref.at[m, w]) for w, one in enumerate(loaded)]
        for (c, j), part in zip(pairs, parts):
            total_ref[c] += part
        return 0

    lax.fori_loop(0, (pairs_ref[3 + which, 0] + group - 1) // group, step, 0)


def apply_list(which, pairs_ref, kept_ref, pieces_ref, total_ref, cl):
    group = kept_ref.shape[1]

    def step(m, _):
        pairs = [pair_at(pairs_ref, which, group * m + w) for w in range(group)]
        parts = [near_product(pieces_ref[j], kept_ref.at[m, w], cl) for w, (c, j) in enumerate(pairs)]
        for (c, j), part in zip(pairs, parts):
            total_ref[c] += part
        return 0

    lax.fori_loop(0, (pairs_ref[3 + which, 0] + group - 1) // group, step, 0)


def put_total(cl, total_ref, start_ref, out_ref):
    for c in range(total_ref.shape[0]):
        lanes = slice(c * cl, (c + 1) * cl)
        near = folded(total_ref[c])
        out_ref[:, lanes] = near if start_ref is None else start_ref[:, lanes] + near


def own_kernel(cl, pairs_ref, payload_ref, beside_ref, own_ref, kept_ref, near_out_ref, targets_ref, tail_ref, pieces_ref, sources_ref, total_ref):
    tail_ref[...] = beside_ref[:, beside_ref.shape[1] - LANES:]
    panels = near_out_ref.shape[1]
    clusters = panels // cl
    fill_charges(pieces_ref, payload_ref, clusters, cl)
    fill_features(sources_ref, payload_ref, panels, cl)
    for c in range(clusters):
        target = features_of(payload_ref, panels, c, cl, True).astype(BF16)
        targets_ref[c] = target
        total_ref[c] = near_block(sources_ref[c], target, pieces_ref[c], own_ref.at[c])
    build_list(0, pairs_ref, targets_ref, kept_ref, pieces_ref, sources_ref, total_ref)
    put_total(cl, total_ref, None, near_out_ref)


def partner_kernel(cl, pairs_ref, payload_ref, targets_ref, start_ref, kept_ref, near_out_ref, pieces_ref, sources_ref, total_ref):
    panels = near_out_ref.shape[1]
    fill_charges(pieces_ref, payload_ref, panels // cl, cl)
    fill_features(sources_ref, payload_ref, panels, cl)
    total_ref[...] = jnp.zeros_like(total_ref)
    build_list(1, pairs_ref, targets_ref, kept_ref, pieces_ref, sources_ref, total_ref)
    put_total(cl, total_ref, start_ref, near_out_ref)


def image_kernel(cl, rank, pairs_ref, payload_ref, targets_ref, start_ref, area_ref, krylov_ref, basis_ref,
                 kept_ref, image_ref, charges_ref, table_ref, pieces_ref, sources_ref, total_ref):
    rhs, panels = image_ref.shape
    clusters = panels // cl
    span = clusters * rank
    fill_charges(pieces_ref, payload_ref, clusters, cl)
    fill_features(sources_ref, payload_ref, panels, cl)
    total_ref[...] = jnp.zeros_like(total_ref)
    build_list(2, pairs_ref, targets_ref, kept_ref, pieces_ref, sources_ref, total_ref)
    squared = correlation = jnp.zeros((rhs, cl), F32)
    for c in range(clusters):
        lanes = slice(c * cl, (c + 1) * cl)
        area = area_ref[c:c + 1, :]
        image = COULOMB * area * (start_ref[:, lanes] + folded(total_ref[c]))
        charges = area * image
        image_ref[:, lanes] = image
        charges_ref[:, lanes] = charges
        table_ref[:, c * rank:(c + 1) * rank] = moments_of(charges, basis_ref[:, lanes])
        krylov = krylov_ref[:, lanes]
        squared = squared + krylov * krylov
        correlation = correlation + krylov * image
    squared = jnp.sum(squared, axis=1, keepdims=True)
    correlation = jnp.sum(correlation, axis=1, keepdims=True)
    local = ratio(correlation, squared)
    energy = jnp.zeros((rhs, cl), F32)
    for c in range(clusters):
        lanes = slice(c * cl, (c + 1) * cl)
        residual = image_ref[:, lanes] - local * krylov_ref[:, lanes]
        energy = energy + residual * residual
    table_ref[:, span:] = in_lanes(squared, correlation, jnp.sum(energy, axis=1, keepdims=True), local)


def own_again_kernel(cl, pairs_ref, payload_ref, beside_ref, own_ref, kept_ref, near_out_ref, tail_ref, pieces_ref, total_ref):
    tail_ref[...] = beside_ref[:, beside_ref.shape[1] - LANES:]
    clusters = near_out_ref.shape[1] // cl
    fill_charges(pieces_ref, payload_ref, clusters, cl)
    for c in range(clusters):
        total_ref[c] = near_product(pieces_ref[c], own_ref.at[c], cl)
    apply_list(0, pairs_ref, kept_ref, pieces_ref, total_ref, cl)
    put_total(cl, total_ref, None, near_out_ref)


def neighbour_again_kernel(cl, which, pairs_ref, payload_ref, start_ref, kept_ref, near_out_ref, pieces_ref, total_ref):
    fill_charges(pieces_ref, payload_ref, near_out_ref.shape[1] // cl, cl)
    total_ref[...] = jnp.zeros_like(total_ref)
    apply_list(which, pairs_ref, kept_ref, pieces_ref, total_ref, cl)
    put_total(cl, total_ref, start_ref, near_out_ref)


def finish_kernel(cl, total, near_ref, area_ref, image_ref, krylov_ref, one_ref, two_ref, next_hbm, second_hbm, next_ref, second_ref, sems):
    panels = image_ref.shape[1]
    clusters = panels // cl
    squared, correlation, energy, local = merged([one_ref[...], two_ref[...]])
    projection = correlation / (squared + 1e-06)
    gap = projection - local
    scaling = 1.0 / jnp.sqrt((energy + gap * gap * squared) / total + 1e-06)
    moves = []
    parts = 4
    for h in range(parts):
        for c in range(h * clusters // parts, (h + 1) * clusters // parts):
            lanes = slice(c * cl, (c + 1) * cl)
            image = image_ref[:, lanes]
            next_ref[:, lanes] = (image - projection * krylov_ref[:, lanes]) * scaling
            second_ref[:, lanes] = (COULOMB * area_ref[c:c + 1, :] * near_ref[:, lanes] - projection * image) * scaling
        lanes = slice(h * panels // parts, (h + 1) * panels // parts)
        for held, hbm in ((next_ref, next_hbm), (second_ref, second_hbm)):
            moves.append(pltpu.make_async_copy(held.at[:, lanes], hbm.at[:, lanes], sems.at[len(moves)]))
            moves[-1].start()
    for move in moves:
        move.wait()


def load_window(tables, clusters, rank, pieces_ref, middle_ref):
    per = LANES // rank
    span = clusters * rank
    count = pieces_ref.shape[0] // per
    groups = span // LANES
    for at in range(count):
        (ref, first), g = tables[at // groups], at % groups
        tile = ref[:, first + g * LANES:first + (g + 1) * LANES]
        for s in range(per):
            pieces_ref[s * count + at] = stacked(pltpu.roll(tile, s * rank, 1) if s else tile)
        if middle_ref is not None:
            half = groups // 2
            row, lane = 8 * (g // half), first + span + g % half * LANES
            tile = ref[row:row + 8, lane:lane + LANES]
            for s in range(per):
                middle_ref[s * count + at] = pltpu.roll(tile, s * rank, 1) if s else tile


def six_tables(near_ref, far_ref, swapped_ref):
    width = near_ref.shape[1] // 2
    return (far_ref, 0), (far_ref, width), (near_ref, 0), (swapped_ref, width), (swapped_ref, 0), (swapped_ref, 3 * width)


def pick(source_ref, at_ref, c, g, per, lane):
    row = None
    for u in range(per):
        take = source_ref[at_ref[c, g * per + u]]
        row = take if row is None else jnp.where(lane == u, take, row)
    return row


def far_fields(gathered_ref, coupling_ref, fields_ref):
    for c in range(gathered_ref.shape[0]):
        field = quartered(dot_nt(coupling_ref[c], gathered_ref[c]))
        field = jnp.concatenate(split(field), axis=1)
        fields_ref[c] = jnp.concatenate([field, field], axis=0)


def far_potential(fields_ref, c, basis):
    return folded(dot_tn(fields_ref[c], basis))


def far_kernel(cl, rank, at_ref, near_pair_ref, far_pair_ref, swapped_ref, center_ref, near_ref, basis_ref, offsets_ref,
               out_ref, coupling_ref, pieces_ref, middle_ref, gathered_ref, fields_ref):
    clusters = near_ref.shape[1] // cl
    per = LANES // rank
    load_window(six_tables(near_pair_ref, far_pair_ref, swapped_ref), clusters, rank, pieces_ref, middle_ref)
    lane = lax.broadcasted_iota(jnp.int32, (1, LANES), 1) // rank
    for c in range(clusters):
        mine = [offsets_ref[3, k:k + 1, :] - center_ref[c:c + 1, k * LANES:(k + 1) * LANES] for k in range(3)]
        for g in range(at_ref.shape[1] // per):
            lanes = slice(g * LANES, (g + 1) * LANES)
            gathered_ref[c, :, lanes] = pick(pieces_ref, at_ref, c, g, per, lane)
            center = pick(middle_ref, at_ref, c, g, per, lane)
            gap = [(center[k:k + 1] + mine[k]) - offsets_ref[k] for k in range(3)]
            high, low = split(lax.rsqrt(gap[0] * gap[0] + gap[1] * gap[1] + gap[2] * gap[2] + SMOOTHING))
            coupling_ref[c, 0:rank, lanes] = high
            coupling_ref[c, rank:2 * rank, lanes] = low
    far_fields(gathered_ref, coupling_ref, fields_ref)
    for c in range(clusters):
        lanes = slice(c * cl, (c + 1) * cl)
        out_ref[:, lanes] = near_ref[:, lanes] + far_potential(fields_ref, c, basis_ref[:, lanes])


def far_again_kernel(cl, rank, at_ref, near_pair_ref, far_pair_ref, swapped_ref, near_ref, coupling_ref, basis_ref,
                     out_ref, pieces_ref, gathered_ref, fields_ref):
    clusters = near_ref.shape[1] // cl
    per = LANES // rank
    load_window(six_tables(near_pair_ref, far_pair_ref, swapped_ref), clusters, rank, pieces_ref, None)
    lane = lax.broadcasted_iota(jnp.int32, (1, LANES), 1) // rank
    for c in range(clusters):
        for g in range(at_ref.shape[1] // per):
            gathered_ref[c, :, g * LANES:(g + 1) * LANES] = pick(pieces_ref, at_ref, c, g, per, lane)
    far_fields(gathered_ref, coupling_ref, fields_ref)
    for c in range(clusters):
        lanes = slice(c * cl, (c + 1) * cl)
        out_ref[:, lanes] = near_ref[:, lanes] + far_potential(fields_ref, c, basis_ref[:, lanes])


def ratio(correlation, squared):
    return jnp.where(squared > 0, correlation / jnp.where(squared > 0, squared, 1.0), 0.0)


def in_lanes(*columns):
    lane = lax.broadcasted_iota(jnp.int32, (columns[0].shape[0], LANES), 1)
    out = columns[-1]
    for i, column in enumerate(columns[:-1]):
        out = jnp.where(lane == i, column, out)
    return out


def merged(groups):
    squared = sum(group[:, 0:1] for group in groups)
    correlation = sum(group[:, 1:2] for group in groups)
    local = ratio(correlation, squared)
    energy = 0.0
    for group in groups:
        gap = local - group[:, 3:4]
        energy = energy + (group[:, 2:3] + gap * gap * group[:, 0:1])
    return squared, correlation, energy, local


def window_sums_kernel(payload_ref, partner_ref, near_pair_ref, far_pair_ref, swapped_ref, out_ref):
    width = near_pair_ref.shape[1] // 2
    ends = [(payload_ref, payload_ref.shape[1]), (partner_ref, partner_ref.shape[1])]
    ends += [(ref, end) for ref in (near_pair_ref, far_pair_ref, swapped_ref) for end in (width, 2 * width)]
    out_ref[...] = in_lanes(*merged([ref[:, end - LANES:end] for ref, end in ends]))


def merge_kernel(one_ref, two_ref, out_ref):
    out_ref[...] = in_lanes(*merged([one_ref[...], two_ref[...]]))


def call(kernel, outs, scratch, memory, *args, limit=10, us=1.0):
    spaces = {"s": pltpu.SMEM, "v": pltpu.VMEM, "p": pltpu.VMEM, "h": pltpu.HBM}
    ins, out_spaces = memory.split(">")
    pinned = {"h": pltpu.HBM, "p": pltpu.VMEM}
    return pl.pallas_call(
        kernel,
        out_shape=[pltpu.VMEM(*out) if m == "p" else jax.ShapeDtypeStruct(*out) for m, out in zip(out_spaces, outs)],
        in_specs=[pl.BlockSpec(memory_space=spaces[m]) for m in ins],
        out_specs=[pl.BlockSpec(memory_space=spaces[m]) for m in out_spaces],
        scratch_shapes=scratch,
        compiler_params=pltpu.CompilerParams(vmem_limit_bytes=limit * 2 ** 20),
        cost_estimate=pl.CostEstimate(flops=int(us * 5e8), bytes_accessed=int(us * 3.6e6), transcendentals=0),
    )(*(pltpu.with_memory_space_constraint(a, pinned[m]) if m in pinned else a for m, a in zip(ins, args)))


def body(vertices, panel_vertices, near_pairs, far_pairs, basis, krylov):
    clusters, slots = near_pairs.shape
    partners = far_pairs.shape[1]
    rhs, panels = krylov.shape
    rank = basis.shape[0]
    cl = panels // clusters
    vcl = vertices.shape[1] // clusters
    span = clusters * rank
    per = LANES // rank
    devices = lax.axis_size("clus")
    position = lax.axis_index("clus").reshape(1).astype(jnp.int32)
    offsets = proxy_offsets(rank)
    flat = np.concatenate([np.tile(offsets, (1, per)), np.zeros((rank - 3, LANES), np.float32)])
    offsets = jnp.asarray(np.concatenate([np.broadcast_to(offsets[:, :, None], (3, rank, LANES)), flat[None]]))
    width = span + span // 2
    pairing = [(i, i + 1 - 2 * (i % 2)) for i in range(devices)]
    bridging = [(i, i - 1 + 2 * (i % 2)) for i in range(1, devices - 1)] + [(0, 0), (devices - 1, devices - 1)]

    def move(value, pairs):
        return lax.ppermute(value, "clus", pairs)

    def outward(value, steps):
        return move(value, [(i, (i + steps * (1 - 2 * (i % 2))) % devices) for i in range(devices)])

    def exchange(payload, table):
        beside = move(table, pairing)
        pair = jnp.concatenate([table, beside], axis=1)
        near_pair, far_pair = outward(pair, 2), outward(pair, 4)
        sent = jnp.concatenate([payload, beside[:, beside.shape[1] - LANES:]], axis=1)
        return sent, beside, near_pair, far_pair, move(sent, bridging), move(payload, pairing)

    def swapped(near_pair, far_pair, tail):
        return move(jnp.concatenate([near_pair, far_pair, tail], axis=1), pairing)

    whole = ((rhs, panels), F32)
    payload, table, area, centers, at, pairs, basis, krylov, offsets = call(
        functools.partial(prepare_kernel, cl, vcl, rank),
        [
            ((rhs, panels + 3 * cl), F32), ((rhs, width), F32), ((clusters, cl), F32), ((clusters, 3 * LANES), F32),
            (far_pairs.shape, jnp.int32), ((8, LANES), jnp.int32), ((2 * rank, panels), BF16), whole, (offsets.shape, F32),
        ],
        [
            pltpu.VMEM(vertices.shape, F32),
            pltpu.VMEM(panel_vertices.shape, jnp.int32),
            pltpu.VMEM(basis.shape, F32),
            pltpu.VMEM(far_pairs.shape, jnp.int32),
            pltpu.VMEM((slots, clusters), jnp.int32),
            pltpu.VMEM((3 * clusters, vcl), F32),
            pltpu.VMEM((3 * panels // LANES, LANES), jnp.int32),
            pltpu.SemaphoreType.DMA((7,)),
        ],
        "shhhhhhh>vvvvvvppp",
        position, vertices, panel_vertices, krylov, basis, far_pairs, near_pairs.T, offsets,
        us=1.5,
    )
    sent, beside, near_pair, far_pair, other, partner = exchange(payload, table)
    group = 4
    own = ((clusters, 2 * cl, cl), BF16)
    kept = ((clusters * (slots - 1) // group, group, 2 * cl, cl), BF16)
    sums_shape = ((rhs, LANES), F32)
    total = pltpu.VMEM((clusters, 2 * rhs, cl), F32)
    pieces = pltpu.VMEM((clusters + 1, 2 * rhs, cl), BF16)
    sources = pltpu.VMEM((clusters + 1, FEATURES, cl), BF16)
    own_blocks, blocks, near, targets, tail = call(
        functools.partial(own_kernel, cl),
        [own, kept, whole, ((clusters, FEATURES, cl), BF16), sums_shape],
        [pieces, sources, total],
        "svv>ppvpv",
        pairs, sent, beside,
        us=8.0,
    )
    swap = swapped(near_pair, far_pair, tail)
    blocks_partner, near = call(
        functools.partial(partner_kernel, cl),
        [kept, whole],
        [pieces, sources, total],
        "svpv>pv",
        pairs, partner, targets, near,
        us=0.2,
    )
    tiles = 6 * per * span // LANES
    window = pltpu.VMEM((tiles, 2 * rhs, LANES), BF16)
    gathered = pltpu.VMEM((clusters, 2 * rhs, partners * rank), BF16)
    fields = pltpu.VMEM((clusters, 2 * rank, 2 * rhs), BF16)
    near, coupling = call(
        functools.partial(far_kernel, cl, rank),
        [whole, ((clusters, 2 * rank, partners * rank), BF16)],
        [window, pltpu.VMEM((tiles, 8, LANES), F32), gathered, fields],
        "svvvvvpp>vp",
        at, near_pair, far_pair, swap, centers, near, basis, offsets,
        us=0.2,
    )
    blocks_other, image, payload, table = call(
        functools.partial(image_kernel, cl, rank),
        [kept, whole, whole, ((rhs, span + LANES), F32)],
        [pieces, sources, total],
        "svpvvpp>pvvv",
        pairs, other, targets, near, area, krylov, basis,
        us=4.0,
    )
    sent, beside, near_pair, far_pair, other, partner = exchange(payload, table)
    near, tail = call(
        functools.partial(own_again_kernel, cl),
        [whole, sums_shape],
        [pieces, total],
        "svvpp>vv",
        pairs, sent, beside, own_blocks, blocks,
        us=8.0,
    )
    swap = swapped(near_pair, far_pair, tail)
    (near,) = call(
        functools.partial(neighbour_again_kernel, cl, 1),
        [whole],
        [pieces, total],
        "svvp>v",
        pairs, partner, near, blocks_partner,
        us=4.0,
    )
    (one,) = call(window_sums_kernel, [sums_shape], [], "vvvvv>v", table, beside, near_pair, far_pair, swap, us=0.3)
    size = 8
    many = outward(one, size)
    while 2 * size < devices:
        (one,) = call(merge_kernel, [sums_shape], [], "vv>v", one, many, us=0.3)
        size = 2 * size
        many = outward(one, size)
    (near,) = call(
        functools.partial(far_again_kernel, cl, rank),
        [whole],
        [window, gathered, fields],
        "svvvvpp>v",
        at, near_pair, far_pair, swap, near, coupling, basis,
        us=4.0,
    )
    (near,) = call(
        functools.partial(neighbour_again_kernel, cl, 2),
        [whole],
        [pieces, total],
        "svvp>v",
        pairs, other, near, blocks_other,
        us=1.5,
    )
    here = pltpu.VMEM((rhs, panels), F32)
    return tuple(call(
        functools.partial(finish_kernel, cl, panels * devices),
        [whole, whole],
        [here, here, pltpu.SemaphoreType.DMA((8,))],
        "vvvpvv>hh",
        near, area, image, krylov, one, many,
        us=1.0,
    ))


def solution(mesh):
    whole = P(None, ("jobs", "clus"))
    rows = P(("jobs", "clus"), None)
    return jax.shard_map(
        body,
        mesh=mesh,
        in_specs=(whole, whole, rows, rows, whole, whole),
        out_specs=(whole, whole),
        check_vma=False,
    )
```

```python
import functools

import jax
import jax.numpy as jnp
import numpy as np
from jax import lax
from jax.experimental import pallas as pl
from jax.experimental.pallas import tpu as pltpu
from jax.sharding import PartitionSpec as P

REACH = 4
SMOOTHING = 0.04
COULOMB = 2.0
PROXY_RADIUS = 0.6
LANES = 128
FEATURES = 80
GRID = 1.5 * 2.0 ** 22
F32 = jnp.float32
BF16 = jnp.bfloat16


def proxy_offsets(points):
    counter = np.arange(points, dtype=np.float32)
    height = 1.0 - (2.0 * counter + 1.0) / points
    radial = np.sqrt(1.0 - height * height)
    azimuth = counter * 2.399963
    return PROXY_RADIUS * np.stack([radial * np.cos(azimuth), radial * np.sin(azimuth), height]).astype(np.float32)


def split(value):
    high = value.astype(BF16)
    return high, (value - high.astype(F32)).astype(BF16)


def stacked(value):
    return jnp.concatenate(split(value), axis=0)


def folded(value):
    half = value.shape[0] // 2
    return value[:half] + value[half:]


def dot_nt(left, right):
    return lax.dot_general(left, right, (((1,), (1,)), ((), ())), preferred_element_type=F32)


def dot_tn(left, right):
    return lax.dot_general(left, right, (((0,), (0,)), ((), ())), preferred_element_type=F32)


def dot_nn(left, right):
    return lax.dot_general(left, right, (((1,), (0,)), ((), ())), preferred_element_type=F32)


def quartered(value):
    half = value.shape[1] // 2
    value = folded(value)
    return value[:, 0:half] + value[:, half:]


def moments_of(weighted, basis_pieces):
    return quartered(dot_nt(stacked(weighted), basis_pieces))


def copies(pairs, sems):
    moves = [pltpu.make_async_copy(source, target, sems.at[i]) for i, (source, target) in enumerate(pairs)]
    for move in moves:
        move.start()
    return moves


def pair_list(near, position, clusters):
    block = lax.div(near, clusters) - position
    side = block * (1 - 2 * lax.rem(position, 2))
    place = lax.rem(near, clusters).astype(F32)
    across = lax.broadcasted_iota(jnp.int32, (clusters, clusters), 1)
    down = lax.broadcasted_iota(jnp.int32, (clusters, clusters), 0)
    upright = lambda value: jnp.sum(jnp.where(across == down, value, 0.0), axis=1, keepdims=True)
    row = lax.broadcasted_iota(jnp.int32, (clusters, LANES), 1).astype(F32)
    target = lax.broadcasted_iota(jnp.int32, (clusters, 1), 0).astype(F32)
    rows = lax.broadcasted_iota(jnp.int32, (8, LANES), 0)
    out = jnp.zeros((8, LANES), F32)
    for which in range(3):
        live = jnp.where((side == (0, 1, -1)[which]) & (near >= 0), 1.0, 0.0)
        counts = sum(live[k:k + 1] for k in range(1, near.shape[0]))
        first = jnp.sum(jnp.where(across < down, counts, 0.0), axis=1, keepdims=True)
        found = jnp.zeros((clusters, LANES), F32)
        for k in range(1, near.shape[0]):
            alive = upright(live[k:k + 1])
            hit = jnp.where(row == first, alive, 0.0)
            found = found + hit * (target * 64 + upright(place[k:k + 1]))
            first = first + alive
        count = jnp.sum(counts, axis=1, keepdims=True)
        found = jnp.where(row[0:1] < count, jnp.sum(found, axis=0, keepdims=True), 1.0 * clusters)
        out = jnp.where(rows == which, found, jnp.where(rows == 3 + which, count, out))
    return out.astype(jnp.int32)


def prepare_kernel(cl, vcl, rank, position_ref, vertices_hbm, corners_hbm, krylov_hbm, basis_hbm, far_hbm, near_hbm, offsets_hbm,
                   payload_ref, table_ref, area_ref, center_ref, at_ref, pairs_ref, basis_ref, krylov_ref, offsets_ref,
                   vertices_ref, corners_ref, raw_ref, far_ref, near_ref, mesh_ref, local_ref, sems):
    moves = copies((
        (vertices_hbm, vertices_ref), (corners_hbm, corners_ref), (krylov_hbm, krylov_ref), (basis_hbm, raw_ref),
        (far_hbm, far_ref), (near_hbm, near_ref), (offsets_hbm, offsets_ref),
    ), sems)
    rhs, panels = krylov_ref.shape
    clusters = panels // cl
    parts = cl // LANES
    moves[0].wait()
    for c in range(clusters):
        mesh_ref[3 * c:3 * c + 3, :] = vertices_ref[:, c * vcl:(c + 1) * vcl]
    moves[1].wait()
    for i in range(clusters * parts):
        local_ref[3 * i:3 * i + 3, :] = corners_ref[:, i * LANES:(i + 1) * LANES]
    first = position_ref[0] * (vcl * clusters) + vcl * lax.broadcasted_iota(jnp.int32, (clusters, LANES), 0)
    tables = [mesh_ref[pl.ds(k, clusters, stride=3), :] for k in range(3)]
    sums = [None] * 3
    for h in range(parts):
        local = [local_ref[pl.ds(3 * h + m, clusters, stride=3 * parts), :] - first for m in range(3)]
        corner = [[jnp.take_along_axis(tables[k], local[m], axis=1, mode="promise_in_bounds") for k in range(3)] for m in range(3)]
        for k in range(3):
            middle = (corner[0][k] + corner[1][k] + corner[2][k]) / 3.0
            lanes = slice(panels + k * cl + h * LANES, panels + k * cl + (h + 1) * LANES)
            payload_ref[:, lanes] = middle
            sums[k] = middle if h == 0 else sums[k] + middle
        one = [corner[1][k] - corner[0][k] for k in range(3)]
        two = [corner[2][k] - corner[0][k] for k in range(3)]
        normal = [one[1] * two[2] - one[2] * two[1], one[2] * two[0] - one[0] * two[2], one[0] * two[1] - one[1] * two[0]]
        area_ref[:, h * LANES:(h + 1) * LANES] = 0.5 * jnp.sqrt(normal[0] * normal[0] + normal[1] * normal[1] + normal[2] * normal[2])
    span = clusters * rank
    mine = lax.broadcasted_iota(jnp.int32, (clusters, span), 1) // rank == lax.broadcasted_iota(jnp.int32, (clusters, span), 0)
    half = span // 2
    table_ref[:, span:] = jnp.zeros_like(table_ref[:, span:])
    for k in range(3):
        center = jnp.sum(sums[k], axis=1, keepdims=True) / cl
        center_ref[:, k * LANES:(k + 1) * LANES] = jnp.broadcast_to(center, (clusters, LANES))
        row = jnp.sum(jnp.where(mine, center, 0.0), axis=0, keepdims=True)
        table_ref[k:k + 1, span:] = row[:, 0:half]
        table_ref[8 + k:9 + k, span:] = row[:, half:]
    moves[2].wait()
    moves[3].wait()
    for c in range(clusters):
        lanes = slice(c * cl, (c + 1) * cl)
        basis_ref[:, lanes] = stacked(raw_ref[:, lanes])
        charges = area_ref[c:c + 1, :] * krylov_ref[:, lanes]
        payload_ref[:, lanes] = charges
        table_ref[:, c * rank:(c + 1) * rank] = moments_of(charges, basis_ref[:, lanes])
    moves[4].wait()
    far = far_ref[...]
    step = (lax.div(far, clusters) - position_ref[0]) * (1 - 2 * lax.rem(position_ref[0], 2))
    block = jnp.where(step < 0, step + REACH, step + REACH - 3)
    per = LANES // rank
    turn = lax.rem(lax.broadcasted_iota(jnp.int32, far.shape, 1) - far + per * clusters * 2 ** 16, per)
    at_ref[0:clusters, :] = (turn * 6 + block) * (span // LANES) + lax.div(lax.rem(far, clusters), per)
    at_ref[clusters:, :] = block * clusters + lax.rem(far, clusters)
    moves[5].wait()
    pairs_ref[...] = pair_list(near_ref[...], position_ref[0], clusters)
    moves[6].wait()


def features_of(payload_ref, panels, c, cl, target):
    rows = [payload_ref[c:c + 1, panels + k * cl:panels + (k + 1) * cl] for k in range(3)]
    value = jnp.concatenate(rows + [jnp.zeros((5, cl), F32)], axis=0)
    coarse = (value + GRID) - GRID
    middle = (value - coarse).astype(BF16).astype(F32)
    low = (value - coarse - middle).astype(BF16).astype(F32)
    pieces = [coarse, middle, low]
    rest = middle + low
    row = lax.broadcasted_iota(jnp.int32, (8, cl), 0)
    square = jnp.sum(coarse * coarse, axis=0, keepdims=True)
    extra = jnp.sum((2.0 * coarse + rest) * rest, axis=0, keepdims=True) + (SMOOTHING if target else 0.0)
    square_high = square.astype(BF16).astype(F32)
    extra_high = extra.astype(BF16).astype(F32)
    extra_middle = (extra - extra_high).astype(BF16).astype(F32)
    ones = jnp.ones((1, cl), F32)

    def placed(base, start, *values):
        for i, one in enumerate(values):
            base = jnp.where(row == start + i, one, base)
        return base

    squares, extras = (square_high, square - square_high), (extra_high, extra_middle, extra - extra_high - extra_middle)
    if target:
        scaled = [-2.0 * piece for piece in pieces]
        first = placed(scaled[0], 3, *squares, ones, ones)
        last = placed(jnp.zeros((8, cl), F32), 0, *extras, ones, ones, ones)
    else:
        first = placed(coarse, 3, ones, ones, *squares)
        last = placed(jnp.zeros((8, cl), F32), 0, ones, ones, ones, *extras)
    combos = [(scaled[i] if target else pieces[j]) for i in range(3) for j in range(3) if i + j]
    return jnp.concatenate([first, *combos, last], axis=0)


def fill_features(sources_ref, payload_ref, panels, cl):
    clusters = panels // cl
    for c in range(clusters):
        sources_ref[c] = features_of(payload_ref, panels, c, cl, False).astype(BF16)
    sources_ref[clusters] = sources_ref[0]


def near_block(source, target, pieces, out_ref):
    cl = source.shape[1]
    parts = []
    for first in range(0, cl, LANES):
        rows = slice(first, first + LANES)
        high, low = split(lax.rsqrt(dot_tn(source[:, rows], target)))
        out_ref[rows, :] = high
        out_ref[cl + first:cl + first + LANES, :] = low
        parts.append(dot_nn(pieces[:, rows], high) + dot_nn(pieces[:, rows], low))
    return sum(parts[1:], parts[0])


def near_product(pieces, block_ref, cl):
    return dot_nn(pieces, block_ref[0:cl, :]) + dot_nn(pieces, block_ref[cl:2 * cl, :])


def fill_charges(pieces_ref, payload_ref, clusters, cl):
    for c in range(clusters):
        pieces_ref[c] = stacked(payload_ref[:, c * cl:(c + 1) * cl])
    pieces_ref[clusters] = jnp.zeros_like(pieces_ref[0])


def pair_at(pairs_ref, which, i):
    pair = pairs_ref[which, i]
    return lax.shift_right_logical(pair, 6), lax.bitwise_and(pair, 63)


def build_list(which, pairs_ref, targets_ref, kept_ref, pieces_ref, sources_ref, total_ref):
    group = kept_ref.shape[1]

    def step(m, _):
        pairs = [pair_at(pairs_ref, which, group * m + w) for w in range(group)]
        loaded = [(sources_ref[j], targets_ref[c], pieces_ref[j]) for c, j in pairs]
        parts = [near_block(*one, kept_ref.at[m, w]) for w, one in enumerate(loaded)]
        for (c, j), part in zip(pairs, parts):
            total_ref[c] += part
        return 0

    lax.fori_loop(0, (pairs_ref[3 + which, 0] + group - 1) // group, step, 0)


def apply_list(which, pairs_ref, kept_ref, pieces_ref, total_ref, cl):
    group = kept_ref.shape[1]

    def step(m, _):
        pairs = [pair_at(pairs_ref, which, group * m + w) for w in range(group)]
        parts = [near_product(pieces_ref[j], kept_ref.at[m, w], cl) for w, (c, j) in enumerate(pairs)]
        for (c, j), part in zip(pairs, parts):
            total_ref[c] += part
        return 0

    lax.fori_loop(0, (pairs_ref[3 + which, 0] + group - 1) // group, step, 0)


def put_total(cl, total_ref, start_ref, out_ref):
    for c in range(total_ref.shape[0]):
        lanes = slice(c * cl, (c + 1) * cl)
        near = folded(total_ref[c])
        out_ref[:, lanes] = near if start_ref is None else start_ref[:, lanes] + near


def own_kernel(cl, pairs_ref, payload_ref, beside_ref, own_ref, kept_ref, near_out_ref, targets_ref, tail_ref, pieces_ref, sources_ref, total_ref):
    tail_ref[...] = beside_ref[:, beside_ref.shape[1] - LANES:]
    panels = near_out_ref.shape[1]
    clusters = panels // cl
    fill_charges(pieces_ref, payload_ref, clusters, cl)
    fill_features(sources_ref, payload_ref, panels, cl)
    for c in range(clusters):
        target = features_of(payload_ref, panels, c, cl, True).astype(BF16)
        targets_ref[c] = target
        total_ref[c] = near_block(sources_ref[c], target, pieces_ref[c], own_ref.at[c])
    build_list(0, pairs_ref, targets_ref, kept_ref, pieces_ref, sources_ref, total_ref)
    put_total(cl, total_ref, None, near_out_ref)


def partner_kernel(cl, pairs_ref, payload_ref, targets_ref, start_ref, kept_ref, near_out_ref, pieces_ref, sources_ref, total_ref):
    panels = near_out_ref.shape[1]
    fill_charges(pieces_ref, payload_ref, panels // cl, cl)
    fill_features(sources_ref, payload_ref, panels, cl)
    total_ref[...] = jnp.zeros_like(total_ref)
    build_list(1, pairs_ref, targets_ref, kept_ref, pieces_ref, sources_ref, total_ref)
    put_total(cl, total_ref, start_ref, near_out_ref)


def image_kernel(cl, rank, pairs_ref, payload_ref, targets_ref, start_ref, area_ref, krylov_ref, basis_ref,
                 kept_ref, image_ref, charges_ref, table_ref, pieces_ref, sources_ref, total_ref):
    rhs, panels = image_ref.shape
    clusters = panels // cl
    span = clusters * rank
    fill_charges(pieces_ref, payload_ref, clusters, cl)
    fill_features(sources_ref, payload_ref, panels, cl)
    total_ref[...] = jnp.zeros_like(total_ref)
    build_list(2, pairs_ref, targets_ref, kept_ref, pieces_ref, sources_ref, total_ref)
    squared = correlation = jnp.zeros((rhs, cl), F32)
    for c in range(clusters):
        lanes = slice(c * cl, (c + 1) * cl)
        area = area_ref[c:c + 1, :]
        image = COULOMB * area * (start_ref[:, lanes] + folded(total_ref[c]))
        charges = area * image
        image_ref[:, lanes] = image
        charges_ref[:, lanes] = charges
        table_ref[:, c * rank:(c + 1) * rank] = moments_of(charges, basis_ref[:, lanes])
        krylov = krylov_ref[:, lanes]
        squared = squared + krylov * krylov
        correlation = correlation + krylov * image
    squared = jnp.sum(squared, axis=1, keepdims=True)
    correlation = jnp.sum(correlation, axis=1, keepdims=True)
    local = ratio(correlation, squared)
    energy = jnp.zeros((rhs, cl), F32)
    for c in range(clusters):
        lanes = slice(c * cl, (c + 1) * cl)
        residual = image_ref[:, lanes] - local * krylov_ref[:, lanes]
        energy = energy + residual * residual
    table_ref[:, span:] = in_lanes(squared, correlation, jnp.sum(energy, axis=1, keepdims=True), local)


def own_again_kernel(cl, pairs_ref, payload_ref, beside_ref, own_ref, kept_ref, near_out_ref, tail_ref, pieces_ref, total_ref):
    tail_ref[...] = beside_ref[:, beside_ref.shape[1] - LANES:]
    clusters = near_out_ref.shape[1] // cl
    fill_charges(pieces_ref, payload_ref, clusters, cl)
    for c in range(clusters):
        total_ref[c] = near_product(pieces_ref[c], own_ref.at[c], cl)
    apply_list(0, pairs_ref, kept_ref, pieces_ref, total_ref, cl)
    put_total(cl, total_ref, None, near_out_ref)


def neighbour_again_kernel(cl, which, pairs_ref, payload_ref, start_ref, kept_ref, near_out_ref, pieces_ref, total_ref):
    fill_charges(pieces_ref, payload_ref, near_out_ref.shape[1] // cl, cl)
    total_ref[...] = jnp.zeros_like(total_ref)
    apply_list(which, pairs_ref, kept_ref, pieces_ref, total_ref, cl)
    put_total(cl, total_ref, start_ref, near_out_ref)


def finish_kernel(cl, total, near_ref, area_ref, image_ref, krylov_ref, one_ref, two_ref, next_hbm, second_hbm, next_ref, second_ref, sems):
    panels = image_ref.shape[1]
    clusters = panels // cl
    squared, correlation, energy, local = merged([one_ref[...], two_ref[...]])
    projection = correlation / (squared + 1e-06)
    gap = projection - local
    scaling = 1.0 / jnp.sqrt((energy + gap * gap * squared) / total + 1e-06)
    moves = []
    parts = 4
    for h in range(parts):
        for c in range(h * clusters // parts, (h + 1) * clusters // parts):
            lanes = slice(c * cl, (c + 1) * cl)
            image = image_ref[:, lanes]
            next_ref[:, lanes] = (image - projection * krylov_ref[:, lanes]) * scaling
            second_ref[:, lanes] = (COULOMB * area_ref[c:c + 1, :] * near_ref[:, lanes] - projection * image) * scaling
        lanes = slice(h * panels // parts, (h + 1) * panels // parts)
        for held, hbm in ((next_ref, next_hbm), (second_ref, second_hbm)):
            moves.append(pltpu.make_async_copy(held.at[:, lanes], hbm.at[:, lanes], sems.at[len(moves)]))
            moves[-1].start()
    for move in moves:
        move.wait()


def load_window(tables, clusters, rank, pieces_ref, middle_ref):
    per = LANES // rank
    span = clusters * rank
    groups = span // LANES
    count = len(tables) * groups
    for at in range(count):
        (ref, first), g = tables[at // groups], at % groups
        high, low = split(ref[:, first + g * LANES:first + (g + 1) * LANES])
        upright = jnp.transpose(jnp.concatenate([high.astype(F32), low.astype(F32)], axis=0)).astype(BF16)
        for u in range(per):
            pieces_ref[at * per + u] = upright[u * rank:(u + 1) * rank, :]
        if middle_ref is not None:
            half = groups // 2
            row, lane = 8 * (g // half), first + span + g % half * LANES
            tile = ref[row:row + 8, lane:lane + LANES]
            for s in range(per):
                middle_ref[s * count + at] = pltpu.roll(tile, s * rank, 1) if s else tile


def gather_far(pieces_ref, at_ref, gathered_ref, rank):
    clusters, partners = at_ref.shape[0] // 2, at_ref.shape[1]
    for c in range(clusters):
        for f in range(partners):
            gathered_ref[c, f * rank:(f + 1) * rank, :] = pieces_ref[at_ref[clusters + c, f]]


def six_tables(near_ref, far_ref, swapped_ref):
    width = near_ref.shape[1] // 2
    return (far_ref, 0), (far_ref, width), (near_ref, 0), (swapped_ref, width), (swapped_ref, 0), (swapped_ref, 3 * width)


def pick(source_ref, at_ref, c, g, per, lane):
    row = None
    for u in range(per):
        take = source_ref[at_ref[c, g * per + u]]
        row = take if row is None else jnp.where(lane == u, take, row)
    return row


def far_fields(gathered_ref, coupling_ref, fields_ref):
    for c in range(gathered_ref.shape[0]):
        field = quartered(dot_nn(coupling_ref[c], gathered_ref[c]))
        field = jnp.concatenate(split(field), axis=1)
        fields_ref[c] = jnp.concatenate([field, field], axis=0)


def far_potential(fields_ref, c, basis):
    return folded(dot_tn(fields_ref[c], basis))


def far_kernel(cl, rank, at_ref, near_pair_ref, far_pair_ref, swapped_ref, center_ref, near_ref, basis_ref, offsets_ref,
               out_ref, coupling_ref, pieces_ref, middle_ref, gathered_ref, fields_ref):
    clusters = near_ref.shape[1] // cl
    per = LANES // rank
    load_window(six_tables(near_pair_ref, far_pair_ref, swapped_ref), clusters, rank, pieces_ref, middle_ref)
    lane = lax.broadcasted_iota(jnp.int32, (1, LANES), 1) // rank
    for c in range(clusters):
        mine = [offsets_ref[3, k:k + 1, :] - center_ref[c:c + 1, k * LANES:(k + 1) * LANES] for k in range(3)]
        for g in range(at_ref.shape[1] // per):
            lanes = slice(g * LANES, (g + 1) * LANES)
            center = pick(middle_ref, at_ref, c, g, per, lane)
            gap = [(center[k:k + 1] + mine[k]) - offsets_ref[k] for k in range(3)]
            high, low = split(lax.rsqrt(gap[0] * gap[0] + gap[1] * gap[1] + gap[2] * gap[2] + SMOOTHING))
            coupling_ref[c, 0:rank, lanes] = high
            coupling_ref[c, rank:2 * rank, lanes] = low
    gather_far(pieces_ref, at_ref, gathered_ref, rank)
    far_fields(gathered_ref, coupling_ref, fields_ref)
    for c in range(clusters):
        lanes = slice(c * cl, (c + 1) * cl)
        out_ref[:, lanes] = near_ref[:, lanes] + far_potential(fields_ref, c, basis_ref[:, lanes])


def far_again_kernel(cl, rank, at_ref, near_pair_ref, far_pair_ref, swapped_ref, near_ref, coupling_ref, basis_ref,
                     out_ref, pieces_ref, gathered_ref, fields_ref):
    clusters = near_ref.shape[1] // cl
    load_window(six_tables(near_pair_ref, far_pair_ref, swapped_ref), clusters, rank, pieces_ref, None)
    gather_far(pieces_ref, at_ref, gathered_ref, rank)
    far_fields(gathered_ref, coupling_ref, fields_ref)
    for c in range(clusters):
        lanes = slice(c * cl, (c + 1) * cl)
        out_ref[:, lanes] = near_ref[:, lanes] + far_potential(fields_ref, c, basis_ref[:, lanes])


def ratio(correlation, squared):
    return jnp.where(squared > 0, correlation / jnp.where(squared > 0, squared, 1.0), 0.0)


def in_lanes(*columns):
    lane = lax.broadcasted_iota(jnp.int32, (columns[0].shape[0], LANES), 1)
    out = columns[-1]
    for i, column in enumerate(columns[:-1]):
        out = jnp.where(lane == i, column, out)
    return out


def merged(groups):
    squared = sum(group[:, 0:1] for group in groups)
    correlation = sum(group[:, 1:2] for group in groups)
    local = ratio(correlation, squared)
    energy = 0.0
    for group in groups:
        gap = local - group[:, 3:4]
        energy = energy + (group[:, 2:3] + gap * gap * group[:, 0:1])
    return squared, correlation, energy, local


def window_sums_kernel(payload_ref, partner_ref, near_pair_ref, far_pair_ref, swapped_ref, out_ref):
    width = near_pair_ref.shape[1] // 2
    ends = [(payload_ref, payload_ref.shape[1]), (partner_ref, partner_ref.shape[1])]
    ends += [(ref, end) for ref in (near_pair_ref, far_pair_ref, swapped_ref) for end in (width, 2 * width)]
    out_ref[...] = in_lanes(*merged([ref[:, end - LANES:end] for ref, end in ends]))


def merge_kernel(one_ref, two_ref, out_ref):
    out_ref[...] = in_lanes(*merged([one_ref[...], two_ref[...]]))


def call(kernel, outs, scratch, memory, *args, limit=10, us=1.0):
    spaces = {"s": pltpu.SMEM, "v": pltpu.VMEM, "p": pltpu.VMEM, "h": pltpu.HBM}
    ins, out_spaces = memory.split(">")
    pinned = {"h": pltpu.HBM, "p": pltpu.VMEM}
    return pl.pallas_call(
        kernel,
        out_shape=[pltpu.VMEM(*out) if m == "p" else jax.ShapeDtypeStruct(*out) for m, out in zip(out_spaces, outs)],
        in_specs=[pl.BlockSpec(memory_space=spaces[m]) for m in ins],
        out_specs=[pl.BlockSpec(memory_space=spaces[m]) for m in out_spaces],
        scratch_shapes=scratch,
        compiler_params=pltpu.CompilerParams(vmem_limit_bytes=limit * 2 ** 20),
        cost_estimate=pl.CostEstimate(flops=int(us * 5e8), bytes_accessed=int(us * 3.6e6), transcendentals=0),
    )(*(pltpu.with_memory_space_constraint(a, pinned[m]) if m in pinned else a for m, a in zip(ins, args)))


def body(vertices, panel_vertices, near_pairs, far_pairs, basis, krylov):
    clusters, slots = near_pairs.shape
    partners = far_pairs.shape[1]
    rhs, panels = krylov.shape
    rank = basis.shape[0]
    cl = panels // clusters
    vcl = vertices.shape[1] // clusters
    span = clusters * rank
    per = LANES // rank
    devices = lax.axis_size("clus")
    position = lax.axis_index("clus").reshape(1).astype(jnp.int32)
    offsets = proxy_offsets(rank)
    flat = np.concatenate([np.tile(offsets, (1, per)), np.zeros((rank - 3, LANES), np.float32)])
    offsets = jnp.asarray(np.concatenate([np.broadcast_to(offsets[:, :, None], (3, rank, LANES)), flat[None]]))
    width = span + span // 2
    pairing = [(i, i + 1 - 2 * (i % 2)) for i in range(devices)]
    bridging = [(i, i - 1 + 2 * (i % 2)) for i in range(1, devices - 1)] + [(0, 0), (devices - 1, devices - 1)]

    def move(value, pairs):
        return lax.ppermute(value, "clus", pairs)

    def outward(value, steps, wrap=True):
        moves = [(i, i + steps * (1 - 2 * (i % 2))) for i in range(devices)]
        return move(value, [(i, j % devices if wrap or 0 <= j < devices else i + 1 - 2 * (i % 2)) for i, j in moves])

    def exchange(payload, table, wrap):
        beside = move(table, pairing)
        pair = jnp.concatenate([table, beside], axis=1)
        near_pair, far_pair = outward(pair, 2, wrap), outward(pair, 4, wrap)
        sent = jnp.concatenate([payload, beside[:, beside.shape[1] - LANES:]], axis=1)
        return sent, beside, near_pair, far_pair, move(sent, bridging), move(payload, pairing)

    def swapped(near_pair, far_pair, tail):
        return move(jnp.concatenate([near_pair, far_pair, tail], axis=1), pairing)

    whole = ((rhs, panels), F32)
    payload, table, area, centers, at, pairs, basis, krylov, offsets = call(
        functools.partial(prepare_kernel, cl, vcl, rank),
        [
            ((rhs, panels + 3 * cl), F32), ((rhs, width), F32), ((clusters, cl), F32), ((clusters, 3 * LANES), F32),
            ((2 * clusters, partners), jnp.int32), ((8, LANES), jnp.int32), ((2 * rank, panels), BF16), whole, (offsets.shape, F32),
        ],
        [
            pltpu.VMEM(vertices.shape, F32),
            pltpu.VMEM(panel_vertices.shape, jnp.int32),
            pltpu.VMEM(basis.shape, F32),
            pltpu.VMEM(far_pairs.shape, jnp.int32),
            pltpu.VMEM((slots, clusters), jnp.int32),
            pltpu.VMEM((3 * clusters, vcl), F32),
            pltpu.VMEM((3 * panels // LANES, LANES), jnp.int32),
            pltpu.SemaphoreType.DMA((7,)),
        ],
        "shhhhhhh>vvvvvvppp",
        position, vertices, panel_vertices, krylov, basis, far_pairs, near_pairs.T, offsets,
        us=1.5,
    )
    sent, beside, near_pair, far_pair, other, partner = exchange(payload, table, False)
    group = 4
    own = ((clusters, 2 * cl, cl), BF16)
    kept = ((clusters * (slots - 1) // group, group, 2 * cl, cl), BF16)
    sums_shape = ((rhs, LANES), F32)
    total = pltpu.VMEM((clusters, 2 * rhs, cl), F32)
    pieces = pltpu.VMEM((clusters + 1, 2 * rhs, cl), BF16)
    sources = pltpu.VMEM((clusters + 1, FEATURES, cl), BF16)
    own_blocks, blocks, near, targets, tail = call(
        functools.partial(own_kernel, cl),
        [own, kept, whole, ((clusters, FEATURES, cl), BF16), sums_shape],
        [pieces, sources, total],
        "svv>ppvpv",
        pairs, sent, beside,
        us=8.0,
    )
    swap = swapped(near_pair, far_pair, tail)
    blocks_partner, near = call(
        functools.partial(partner_kernel, cl),
        [kept, whole],
        [pieces, sources, total],
        "svpv>pv",
        pairs, partner, targets, near,
        us=0.2,
    )
    tiles = 6 * per * span // LANES
    window = pltpu.VMEM((6 * clusters, rank, 2 * rhs), BF16)
    gathered = pltpu.VMEM((clusters, partners * rank, 2 * rhs), BF16)
    fields = pltpu.VMEM((clusters, 2 * rank, 2 * rhs), BF16)
    near, coupling = call(
        functools.partial(far_kernel, cl, rank),
        [whole, ((clusters, 2 * rank, partners * rank), BF16)],
        [window, pltpu.VMEM((tiles, 8, LANES), F32), gathered, fields],
        "svvvvvpp>vp",
        at, near_pair, far_pair, swap, centers, near, basis, offsets,
        us=0.2,
    )
    blocks_other, image, payload, table = call(
        functools.partial(image_kernel, cl, rank),
        [kept, whole, whole, ((rhs, span + LANES), F32)],
        [pieces, sources, total],
        "svpvvpp>pvvv",
        pairs, other, targets, near, area, krylov, basis,
        us=4.0,
    )
    sent, beside, near_pair, far_pair, other, partner = exchange(payload, table, True)
    near, tail = call(
        functools.partial(own_again_kernel, cl),
        [whole, sums_shape],
        [pieces, total],
        "svvpp>vv",
        pairs, sent, beside, own_blocks, blocks,
        us=8.0,
    )
    swap = swapped(near_pair, far_pair, tail)
    (near,) = call(
        functools.partial(neighbour_again_kernel, cl, 1),
        [whole],
        [pieces, total],
        "svvp>v",
        pairs, partner, near, blocks_partner,
        us=4.0,
    )
    (one,) = call(window_sums_kernel, [sums_shape], [], "vvvvv>v", table, beside, near_pair, far_pair, swap, us=0.3)
    size = 8
    many = outward(one, size)
    while 2 * size < devices:
        (one,) = call(merge_kernel, [sums_shape], [], "vv>v", one, many, us=0.3)
        size = 2 * size
        many = outward(one, size)
    (near,) = call(
        functools.partial(far_again_kernel, cl, rank),
        [whole],
        [window, gathered, fields],
        "svvvvpp>v",
        at, near_pair, far_pair, swap, near, coupling, basis,
        us=4.0,
    )
    (near,) = call(
        functools.partial(neighbour_again_kernel, cl, 2),
        [whole],
        [pieces, total],
        "svvp>v",
        pairs, other, near, blocks_other,
        us=1.5,
    )
    here = pltpu.VMEM((rhs, panels), F32)
    return tuple(call(
        functools.partial(finish_kernel, cl, panels * devices),
        [whole, whole],
        [here, here, pltpu.SemaphoreType.DMA((8,))],
        "vvvpvv>hh",
        near, area, image, krylov, one, many,
        us=1.0,
    ))


def solution(mesh):
    whole = P(None, ("jobs", "clus"))
    rows = P(("jobs", "clus"), None)
    return jax.shard_map(
        body,
        mesh=mesh,
        in_specs=(whole, whole, rows, rows, whole, whole),
        out_specs=(whole, whole),
        check_vma=False,
    )
```

```python
import functools

import jax
import jax.numpy as jnp
import numpy as np
from jax import lax
from jax.experimental import pallas as pl
from jax.experimental.pallas import tpu as pltpu
from jax.sharding import PartitionSpec as P

REACH = 4
SMOOTHING = 0.04
COULOMB = 2.0
PROXY_RADIUS = 0.6
LANES = 128
FEATURES = 80
GRID = 1.5 * 2.0 ** 22
F32 = jnp.float32
BF16 = jnp.bfloat16


def proxy_offsets(points):
    counter = np.arange(points, dtype=np.float32)
    height = 1.0 - (2.0 * counter + 1.0) / points
    radial = np.sqrt(1.0 - height * height)
    azimuth = counter * 2.399963
    return PROXY_RADIUS * np.stack([radial * np.cos(azimuth), radial * np.sin(azimuth), height]).astype(np.float32)


def split(value):
    high = value.astype(BF16)
    return high, (value - high.astype(F32)).astype(BF16)


def stacked(value):
    return jnp.concatenate(split(value), axis=0)


def folded(value):
    half = value.shape[0] // 2
    return value[:half] + value[half:]


def dot_nt(left, right):
    return lax.dot_general(left, right, (((1,), (1,)), ((), ())), preferred_element_type=F32)


def dot_tn(left, right):
    return lax.dot_general(left, right, (((0,), (0,)), ((), ())), preferred_element_type=F32)


def dot_nn(left, right):
    return lax.dot_general(left, right, (((1,), (0,)), ((), ())), preferred_element_type=F32)


def quartered(value):
    half = value.shape[1] // 2
    value = folded(value)
    return value[:, 0:half] + value[:, half:]


def moments_of(weighted, basis_pieces):
    return quartered(dot_nt(stacked(weighted), basis_pieces))


def copies(pairs, sems):
    moves = [pltpu.make_async_copy(source, target, sems.at[i]) for i, (source, target) in enumerate(pairs)]
    for move in moves:
        move.start()
    return moves


def pair_list(near, position, clusters):
    block = lax.div(near, clusters) - position
    side = block * (1 - 2 * lax.rem(position, 2))
    place = lax.rem(near, clusters).astype(F32)
    across = lax.broadcasted_iota(jnp.int32, (clusters, clusters), 1)
    down = lax.broadcasted_iota(jnp.int32, (clusters, clusters), 0)
    upright = lambda value: jnp.sum(jnp.where(across == down, value, 0.0), axis=1, keepdims=True)
    row = lax.broadcasted_iota(jnp.int32, (clusters, LANES), 1).astype(F32)
    target = lax.broadcasted_iota(jnp.int32, (clusters, 1), 0).astype(F32)
    rows = lax.broadcasted_iota(jnp.int32, (8, LANES), 0)
    out = jnp.zeros((8, LANES), F32)
    for which in range(3):
        live = jnp.where((side == (0, 1, -1)[which]) & (near >= 0), 1.0, 0.0)
        counts = sum(live[k:k + 1] for k in range(1, near.shape[0]))
        first = jnp.sum(jnp.where(across < down, counts, 0.0), axis=1, keepdims=True)
        found = jnp.zeros((clusters, LANES), F32)
        for k in range(1, near.shape[0]):
            alive = upright(live[k:k + 1])
            hit = jnp.where(row == first, alive, 0.0)
            found = found + hit * (target * 64 + upright(place[k:k + 1]))
            first = first + alive
        count = jnp.sum(counts, axis=1, keepdims=True)
        found = jnp.where(row[0:1] < count, jnp.sum(found, axis=0, keepdims=True), 1.0 * clusters)
        out = jnp.where(rows == which, found, jnp.where(rows == 3 + which, count, out))
    return out.astype(jnp.int32)


def prepare_kernel(cl, vcl, rank, position_ref, vertices_hbm, corners_hbm, krylov_hbm, basis_hbm, far_hbm, near_hbm, offsets_hbm,
                   payload_ref, table_ref, area_ref, center_ref, at_ref, pairs_ref, basis_ref, krylov_ref, offsets_ref,
                   vertices_ref, corners_ref, raw_ref, far_ref, near_ref, mesh_ref, local_ref, sems):
    moves = copies((
        (vertices_hbm, vertices_ref), (corners_hbm, corners_ref), (krylov_hbm, krylov_ref), (basis_hbm, raw_ref),
        (far_hbm, far_ref), (near_hbm, near_ref), (offsets_hbm, offsets_ref),
    ), sems)
    rhs, panels = krylov_ref.shape
    clusters = panels // cl
    parts = cl // LANES
    moves[0].wait()
    for c in range(clusters):
        mesh_ref[3 * c:3 * c + 3, :] = vertices_ref[:, c * vcl:(c + 1) * vcl]
    moves[1].wait()
    for i in range(clusters * parts):
        local_ref[3 * i:3 * i + 3, :] = corners_ref[:, i * LANES:(i + 1) * LANES]
    first = position_ref[0] * (vcl * clusters) + vcl * lax.broadcasted_iota(jnp.int32, (clusters, LANES), 0)
    tables = [mesh_ref[pl.ds(k, clusters, stride=3), :] for k in range(3)]
    sums = [None] * 3
    for h in range(parts):
        local = [local_ref[pl.ds(3 * h + m, clusters, stride=3 * parts), :] - first for m in range(3)]
        corner = [[jnp.take_along_axis(tables[k], local[m], axis=1, mode="promise_in_bounds") for k in range(3)] for m in range(3)]
        for k in range(3):
            middle = (corner[0][k] + corner[1][k] + corner[2][k]) / 3.0
            lanes = slice(panels + k * cl + h * LANES, panels + k * cl + (h + 1) * LANES)
            payload_ref[:, lanes] = middle
            sums[k] = middle if h == 0 else sums[k] + middle
        one = [corner[1][k] - corner[0][k] for k in range(3)]
        two = [corner[2][k] - corner[0][k] for k in range(3)]
        normal = [one[1] * two[2] - one[2] * two[1], one[2] * two[0] - one[0] * two[2], one[0] * two[1] - one[1] * two[0]]
        area_ref[:, h * LANES:(h + 1) * LANES] = 0.5 * jnp.sqrt(normal[0] * normal[0] + normal[1] * normal[1] + normal[2] * normal[2])
    span = clusters * rank
    mine = lax.broadcasted_iota(jnp.int32, (clusters, span), 1) // rank == lax.broadcasted_iota(jnp.int32, (clusters, span), 0)
    half = span // 2
    table_ref[:, span:] = jnp.zeros_like(table_ref[:, span:])
    for k in range(3):
        center = jnp.sum(sums[k], axis=1, keepdims=True) / cl
        center_ref[:, k * LANES:(k + 1) * LANES] = jnp.broadcast_to(center, (clusters, LANES))
        row = jnp.sum(jnp.where(mine, center, 0.0), axis=0, keepdims=True)
        table_ref[k:k + 1, span:] = row[:, 0:half]
        table_ref[8 + k:9 + k, span:] = row[:, half:]
    moves[2].wait()
    moves[3].wait()
    for c in range(clusters):
        lanes = slice(c * cl, (c + 1) * cl)
        basis_ref[:, lanes] = stacked(raw_ref[:, lanes])
        charges = area_ref[c:c + 1, :] * krylov_ref[:, lanes]
        payload_ref[:, lanes] = charges
        table_ref[:, c * rank:(c + 1) * rank] = moments_of(charges, basis_ref[:, lanes])
    moves[4].wait()
    far = far_ref[...]
    step = (lax.div(far, clusters) - position_ref[0]) * (1 - 2 * lax.rem(position_ref[0], 2))
    block = jnp.where(step < 0, step + REACH, step + REACH - 3)
    per = LANES // rank
    turn = lax.rem(lax.broadcasted_iota(jnp.int32, far.shape, 1) - far + per * clusters * 2 ** 16, per)
    at_ref[...] = (turn * 6 + block) * (span // LANES) + lax.div(lax.rem(far, clusters), per)
    moves[5].wait()
    pairs_ref[...] = pair_list(near_ref[...], position_ref[0], clusters)
    moves[6].wait()


def features_of(payload_ref, panels, c, cl, target):
    rows = [payload_ref[c:c + 1, panels + k * cl:panels + (k + 1) * cl] for k in range(3)]
    value = jnp.concatenate(rows + [jnp.zeros((5, cl), F32)], axis=0)
    coarse = (value + GRID) - GRID
    middle = (value - coarse).astype(BF16).astype(F32)
    low = (value - coarse - middle).astype(BF16).astype(F32)
    pieces = [coarse, middle, low]
    rest = middle + low
    row = lax.broadcasted_iota(jnp.int32, (8, cl), 0)
    square = jnp.sum(coarse * coarse, axis=0, keepdims=True)
    extra = jnp.sum((2.0 * coarse + rest) * rest, axis=0, keepdims=True) + (SMOOTHING if target else 0.0)
    square_high = square.astype(BF16).astype(F32)
    extra_high = extra.astype(BF16).astype(F32)
    extra_middle = (extra - extra_high).astype(BF16).astype(F32)
    ones = jnp.ones((1, cl), F32)

    def placed(base, start, *values):
        for i, one in enumerate(values):
            base = jnp.where(row == start + i, one, base)
        return base

    squares, extras = (square_high, square - square_high), (extra_high, extra_middle, extra - extra_high - extra_middle)
    if target:
        scaled = [-2.0 * piece for piece in pieces]
        first = placed(scaled[0], 3, *squares, ones, ones)
        last = placed(jnp.zeros((8, cl), F32), 0, *extras, ones, ones, ones)
    else:
        first = placed(coarse, 3, ones, ones, *squares)
        last = placed(jnp.zeros((8, cl), F32), 0, ones, ones, ones, *extras)
    combos = [(scaled[i] if target else pieces[j]) for i in range(3) for j in range(3) if i + j]
    return jnp.concatenate([first, *combos, last], axis=0)


def fill_features(sources_ref, payload_ref, panels, cl):
    clusters = panels // cl
    for c in range(clusters):
        sources_ref[c] = features_of(payload_ref, panels, c, cl, False).astype(BF16)
    sources_ref[clusters] = sources_ref[0]


def near_block(source, target, pieces, out_ref):
    cl = source.shape[1]
    parts = []
    for first in range(0, cl, LANES):
        rows = slice(first, first + LANES)
        high, low = split(lax.rsqrt(dot_tn(source[:, rows], target)))
        out_ref[rows, :] = high
        out_ref[cl + first:cl + first + LANES, :] = low
        parts.append(dot_nn(pieces[:, rows], high) + dot_nn(pieces[:, rows], low))
    return sum(parts[1:], parts[0])


def near_product(pieces, block_ref, cl):
    return dot_nn(pieces, block_ref[0:cl, :]) + dot_nn(pieces, block_ref[cl:2 * cl, :])


def fill_charges(pieces_ref, payload_ref, clusters, cl):
    for c in range(clusters):
        pieces_ref[c] = stacked(payload_ref[:, c * cl:(c + 1) * cl])
    pieces_ref[clusters] = jnp.zeros_like(pieces_ref[0])


def pair_at(pairs_ref, which, i):
    pair = pairs_ref[which, i]
    return lax.shift_right_logical(pair, 6), lax.bitwise_and(pair, 63)


def build_list(which, pairs_ref, targets_ref, kept_ref, pieces_ref, sources_ref, total_ref):
    group = kept_ref.shape[1]

    def step(m, _):
        pairs = [pair_at(pairs_ref, which, group * m + w) for w in range(group)]
        loaded = [(sources_ref[j], targets_ref[c], pieces_ref[j]) for c, j in pairs]
        parts = [near_block(*one, kept_ref.at[m, w]) for w, one in enumerate(loaded)]
        for (c, j), part in zip(pairs, parts):
            total_ref[c] += part
        return 0

    lax.fori_loop(0, (pairs_ref[3 + which, 0] + group - 1) // group, step, 0)


def apply_list(which, pairs_ref, kept_ref, pieces_ref, total_ref, cl):
    group = kept_ref.shape[1]

    def step(m, _):
        pairs = [pair_at(pairs_ref, which, group * m + w) for w in range(group)]
        parts = [near_product(pieces_ref[j], kept_ref.at[m, w], cl) for w, (c, j) in enumerate(pairs)]
        for (c, j), part in zip(pairs, parts):
            total_ref[c] += part
        return 0

    lax.fori_loop(0, (pairs_ref[3 + which, 0] + group - 1) // group, step, 0)


def put_total(cl, total_ref, start_ref, out_ref):
    for c in range(total_ref.shape[0]):
        lanes = slice(c * cl, (c + 1) * cl)
        near = folded(total_ref[c])
        out_ref[:, lanes] = near if start_ref is None else start_ref[:, lanes] + near


def own_kernel(cl, pairs_ref, payload_ref, beside_ref, own_ref, kept_ref, near_out_ref, targets_ref, tail_ref, pieces_ref, sources_ref, total_ref):
    tail_ref[...] = beside_ref[:, beside_ref.shape[1] - LANES:]
    panels = near_out_ref.shape[1]
    clusters = panels // cl
    fill_charges(pieces_ref, payload_ref, clusters, cl)
    fill_features(sources_ref, payload_ref, panels, cl)
    for c in range(clusters):
        target = features_of(payload_ref, panels, c, cl, True).astype(BF16)
        targets_ref[c] = target
        total_ref[c] = near_block(sources_ref[c], target, pieces_ref[c], own_ref.at[c])
    build_list(0, pairs_ref, targets_ref, kept_ref, pieces_ref, sources_ref, total_ref)
    put_total(cl, total_ref, None, near_out_ref)


def partner_kernel(cl, pairs_ref, payload_ref, targets_ref, start_ref, kept_ref, near_out_ref, pieces_ref, sources_ref, total_ref):
    panels = near_out_ref.shape[1]
    fill_charges(pieces_ref, payload_ref, panels // cl, cl)
    fill_features(sources_ref, payload_ref, panels, cl)
    total_ref[...] = jnp.zeros_like(total_ref)
    build_list(1, pairs_ref, targets_ref, kept_ref, pieces_ref, sources_ref, total_ref)
    put_total(cl, total_ref, start_ref, near_out_ref)


def image_kernel(cl, rank, pairs_ref, payload_ref, targets_ref, start_ref, area_ref, krylov_ref, basis_ref,
                 kept_ref, image_ref, charges_ref, table_ref, pieces_ref, sources_ref, total_ref):
    rhs, panels = image_ref.shape
    clusters = panels // cl
    span = clusters * rank
    fill_charges(pieces_ref, payload_ref, clusters, cl)
    fill_features(sources_ref, payload_ref, panels, cl)
    total_ref[...] = jnp.zeros_like(total_ref)
    build_list(2, pairs_ref, targets_ref, kept_ref, pieces_ref, sources_ref, total_ref)
    squared = correlation = jnp.zeros((rhs, cl), F32)
    for c in range(clusters):
        lanes = slice(c * cl, (c + 1) * cl)
        area = area_ref[c:c + 1, :]
        image = COULOMB * area * (start_ref[:, lanes] + folded(total_ref[c]))
        charges = area * image
        image_ref[:, lanes] = image
        charges_ref[:, lanes] = charges
        table_ref[:, c * rank:(c + 1) * rank] = moments_of(charges, basis_ref[:, lanes])
        krylov = krylov_ref[:, lanes]
        squared = squared + krylov * krylov
        correlation = correlation + krylov * image
    squared = jnp.sum(squared, axis=1, keepdims=True)
    correlation = jnp.sum(correlation, axis=1, keepdims=True)
    local = ratio(correlation, squared)
    energy = jnp.zeros((rhs, cl), F32)
    for c in range(clusters):
        lanes = slice(c * cl, (c + 1) * cl)
        residual = image_ref[:, lanes] - local * krylov_ref[:, lanes]
        energy = energy + residual * residual
    table_ref[:, span:] = in_lanes(squared, correlation, jnp.sum(energy, axis=1, keepdims=True), local)


def own_again_kernel(cl, pairs_ref, payload_ref, beside_ref, own_ref, kept_ref, near_out_ref, tail_ref, pieces_ref, total_ref):
    tail_ref[...] = beside_ref[:, beside_ref.shape[1] - LANES:]
    clusters = near_out_ref.shape[1] // cl
    fill_charges(pieces_ref, payload_ref, clusters, cl)
    for c in range(clusters):
        total_ref[c] = near_product(pieces_ref[c], own_ref.at[c], cl)
    apply_list(0, pairs_ref, kept_ref, pieces_ref, total_ref, cl)
    put_total(cl, total_ref, None, near_out_ref)


def neighbour_again_kernel(cl, which, pairs_ref, payload_ref, start_ref, kept_ref, near_out_ref, pieces_ref, total_ref):
    fill_charges(pieces_ref, payload_ref, near_out_ref.shape[1] // cl, cl)
    total_ref[...] = jnp.zeros_like(total_ref)
    apply_list(which, pairs_ref, kept_ref, pieces_ref, total_ref, cl)
    put_total(cl, total_ref, start_ref, near_out_ref)


def finish_kernel(cl, total, near_ref, area_ref, image_ref, krylov_ref, one_ref, two_ref, next_hbm, second_hbm, next_ref, second_ref, sems):
    panels = image_ref.shape[1]
    clusters = panels // cl
    squared, correlation, energy, local = merged([one_ref[...], two_ref[...]])
    projection = correlation / (squared + 1e-06)
    gap = projection - local
    scaling = 1.0 / jnp.sqrt((energy + gap * gap * squared) / total + 1e-06)
    moves = []
    parts = 4
    for h in range(parts):
        for c in range(h * clusters // parts, (h + 1) * clusters // parts):
            lanes = slice(c * cl, (c + 1) * cl)
            image = image_ref[:, lanes]
            next_ref[:, lanes] = (image - projection * krylov_ref[:, lanes]) * scaling
            second_ref[:, lanes] = (COULOMB * area_ref[c:c + 1, :] * near_ref[:, lanes] - projection * image) * scaling
        lanes = slice(h * panels // parts, (h + 1) * panels // parts)
        for held, hbm in ((next_ref, next_hbm), (second_ref, second_hbm)):
            moves.append(pltpu.make_async_copy(held.at[:, lanes], hbm.at[:, lanes], sems.at[len(moves)]))
            moves[-1].start()
    for move in moves:
        move.wait()


def load_window(tables, clusters, rank, pieces_ref, middle_ref):
    per = LANES // rank
    span = clusters * rank
    count = pieces_ref.shape[0] // per
    groups = span // LANES
    for at in range(count):
        (ref, first), g = tables[at // groups], at % groups
        tile = ref[:, first + g * LANES:first + (g + 1) * LANES]
        for s in range(per):
            pieces_ref[s * count + at] = stacked(pltpu.roll(tile, s * rank, 1) if s else tile)
        if middle_ref is not None:
            half = groups // 2
            row, lane = 8 * (g // half), first + span + g % half * LANES
            tile = ref[row:row + 8, lane:lane + LANES]
            for s in range(per):
                middle_ref[s * count + at] = pltpu.roll(tile, s * rank, 1) if s else tile


def six_tables(near_ref, far_ref, swapped_ref):
    width = near_ref.shape[1] // 2
    return (far_ref, 0), (far_ref, width), (near_ref, 0), (swapped_ref, width), (swapped_ref, 0), (swapped_ref, 3 * width)


def pick(source_ref, at_ref, c, g, per, lane):
    row = None
    for u in range(per):
        take = source_ref[at_ref[c, g * per + u]]
        row = take if row is None else jnp.where(lane == u, take, row)
    return row


def far_fields(gathered_ref, coupling_ref, fields_ref):
    for c in range(gathered_ref.shape[0]):
        field = quartered(dot_nt(gathered_ref[c], coupling_ref[c]))
        fields_ref[c] = stacked(jnp.concatenate([field, field], axis=1))


def far_potential(fields_ref, c, basis):
    return folded(dot_nn(fields_ref[c], basis))


def far_kernel(cl, rank, at_ref, near_pair_ref, far_pair_ref, swapped_ref, center_ref, near_ref, basis_ref, offsets_ref,
               out_ref, coupling_ref, pieces_ref, middle_ref, gathered_ref, fields_ref):
    clusters = near_ref.shape[1] // cl
    per = LANES // rank
    load_window(six_tables(near_pair_ref, far_pair_ref, swapped_ref), clusters, rank, pieces_ref, middle_ref)
    lane = lax.broadcasted_iota(jnp.int32, (1, LANES), 1) // rank
    for c in range(clusters):
        mine = [offsets_ref[3, k:k + 1, :] - center_ref[c:c + 1, k * LANES:(k + 1) * LANES] for k in range(3)]
        for g in range(at_ref.shape[1] // per):
            lanes = slice(g * LANES, (g + 1) * LANES)
            gathered_ref[c, :, lanes] = pick(pieces_ref, at_ref, c, g, per, lane)
            center = pick(middle_ref, at_ref, c, g, per, lane)
            gap = [(center[k:k + 1] + mine[k]) - offsets_ref[k] for k in range(3)]
            high, low = split(lax.rsqrt(gap[0] * gap[0] + gap[1] * gap[1] + gap[2] * gap[2] + SMOOTHING))
            coupling_ref[c, 0:rank, lanes] = high
            coupling_ref[c, rank:2 * rank, lanes] = low
    far_fields(gathered_ref, coupling_ref, fields_ref)
    for c in range(clusters):
        lanes = slice(c * cl, (c + 1) * cl)
        out_ref[:, lanes] = near_ref[:, lanes] + far_potential(fields_ref, c, basis_ref[:, lanes])


def far_again_kernel(cl, rank, at_ref, near_pair_ref, far_pair_ref, swapped_ref, near_ref, coupling_ref, basis_ref,
                     out_ref, pieces_ref, gathered_ref, fields_ref):
    clusters = near_ref.shape[1] // cl
    per = LANES // rank
    load_window(six_tables(near_pair_ref, far_pair_ref, swapped_ref), clusters, rank, pieces_ref, None)
    lane = lax.broadcasted_iota(jnp.int32, (1, LANES), 1) // rank
    for c in range(clusters):
        for g in range(at_ref.shape[1] // per):
            gathered_ref[c, :, g * LANES:(g + 1) * LANES] = pick(pieces_ref, at_ref, c, g, per, lane)
    far_fields(gathered_ref, coupling_ref, fields_ref)
    for c in range(clusters):
        lanes = slice(c * cl, (c + 1) * cl)
        out_ref[:, lanes] = near_ref[:, lanes] + far_potential(fields_ref, c, basis_ref[:, lanes])


def ratio(correlation, squared):
    return jnp.where(squared > 0, correlation / jnp.where(squared > 0, squared, 1.0), 0.0)


def in_lanes(*columns):
    lane = lax.broadcasted_iota(jnp.int32, (columns[0].shape[0], LANES), 1)
    out = columns[-1]
    for i, column in enumerate(columns[:-1]):
        out = jnp.where(lane == i, column, out)
    return out


def merged(groups):
    squared = sum(group[:, 0:1] for group in groups)
    correlation = sum(group[:, 1:2] for group in groups)
    local = ratio(correlation, squared)
    energy = 0.0
    for group in groups:
        gap = local - group[:, 3:4]
        energy = energy + (group[:, 2:3] + gap * gap * group[:, 0:1])
    return squared, correlation, energy, local


def window_sums_kernel(payload_ref, partner_ref, near_pair_ref, far_pair_ref, swapped_ref, out_ref):
    width = near_pair_ref.shape[1] // 2
    ends = [(payload_ref, payload_ref.shape[1]), (partner_ref, partner_ref.shape[1])]
    ends += [(ref, end) for ref in (near_pair_ref, far_pair_ref, swapped_ref) for end in (width, 2 * width)]
    out_ref[...] = in_lanes(*merged([ref[:, end - LANES:end] for ref, end in ends]))


def merge_kernel(one_ref, two_ref, out_ref):
    out_ref[...] = in_lanes(*merged([one_ref[...], two_ref[...]]))


def call(kernel, outs, scratch, memory, *args, limit=10, us=1.0):
    spaces = {"s": pltpu.SMEM, "v": pltpu.VMEM, "p": pltpu.VMEM, "h": pltpu.HBM}
    ins, out_spaces = memory.split(">")
    pinned = {"h": pltpu.HBM, "p": pltpu.VMEM}
    return pl.pallas_call(
        kernel,
        out_shape=[pltpu.VMEM(*out) if m == "p" else jax.ShapeDtypeStruct(*out) for m, out in zip(out_spaces, outs)],
        in_specs=[pl.BlockSpec(memory_space=spaces[m]) for m in ins],
        out_specs=[pl.BlockSpec(memory_space=spaces[m]) for m in out_spaces],
        scratch_shapes=scratch,
        compiler_params=pltpu.CompilerParams(vmem_limit_bytes=limit * 2 ** 20),
        cost_estimate=pl.CostEstimate(flops=int(us * 5e8), bytes_accessed=int(us * 3.6e6), transcendentals=0),
    )(*(pltpu.with_memory_space_constraint(a, pinned[m]) if m in pinned else a for m, a in zip(ins, args)))


def body(vertices, panel_vertices, near_pairs, far_pairs, basis, krylov):
    clusters, slots = near_pairs.shape
    partners = far_pairs.shape[1]
    rhs, panels = krylov.shape
    rank = basis.shape[0]
    cl = panels // clusters
    vcl = vertices.shape[1] // clusters
    span = clusters * rank
    per = LANES // rank
    devices = lax.axis_size("clus")
    position = lax.axis_index("clus").reshape(1).astype(jnp.int32)
    offsets = proxy_offsets(rank)
    flat = np.concatenate([np.tile(offsets, (1, per)), np.zeros((rank - 3, LANES), np.float32)])
    offsets = jnp.asarray(np.concatenate([np.broadcast_to(offsets[:, :, None], (3, rank, LANES)), flat[None]]))
    width = span + span // 2
    pairing = [(i, i + 1 - 2 * (i % 2)) for i in range(devices)]
    bridging = [(i, i - 1 + 2 * (i % 2)) for i in range(1, devices - 1)] + [(0, 0), (devices - 1, devices - 1)]

    def move(value, pairs):
        return lax.ppermute(value, "clus", pairs)

    def outward(value, steps, wrap=True):
        moves = [(i, i + steps * (1 - 2 * (i % 2))) for i in range(devices)]
        return move(value, [(i, j % devices if wrap or 0 <= j < devices else i + 1 - 2 * (i % 2)) for i, j in moves])

    def exchange(payload, table, wrap):
        beside = move(table, pairing)
        pair = jnp.concatenate([table, beside], axis=1)
        near_pair, far_pair = outward(pair, 2, wrap), outward(pair, 4, wrap)
        sent = jnp.concatenate([payload, beside[:, beside.shape[1] - LANES:]], axis=1)
        return sent, beside, near_pair, far_pair, move(sent, bridging), move(payload, pairing)

    def swapped(near_pair, far_pair, tail):
        return move(jnp.concatenate([near_pair, far_pair, tail], axis=1), pairing)

    whole = ((rhs, panels), F32)
    payload, table, area, centers, at, pairs, basis, krylov, offsets = call(
        functools.partial(prepare_kernel, cl, vcl, rank),
        [
            ((rhs, panels + 3 * cl), F32), ((rhs, width), F32), ((clusters, cl), F32), ((clusters, 3 * LANES), F32),
            (far_pairs.shape, jnp.int32), ((8, LANES), jnp.int32), ((2 * rank, panels), BF16), whole, (offsets.shape, F32),
        ],
        [
            pltpu.VMEM(vertices.shape, F32),
            pltpu.VMEM(panel_vertices.shape, jnp.int32),
            pltpu.VMEM(basis.shape, F32),
            pltpu.VMEM(far_pairs.shape, jnp.int32),
            pltpu.VMEM((slots, clusters), jnp.int32),
            pltpu.VMEM((3 * clusters, vcl), F32),
            pltpu.VMEM((3 * panels // LANES, LANES), jnp.int32),
            pltpu.SemaphoreType.DMA((7,)),
        ],
        "shhhhhhh>vvvvvvppp",
        position, vertices, panel_vertices, krylov, basis, far_pairs, near_pairs.T, offsets,
        us=1.5,
    )
    sent, beside, near_pair, far_pair, other, partner = exchange(payload, table, False)
    group = 4
    own = ((clusters, 2 * cl, cl), BF16)
    kept = ((clusters * (slots - 1) // group, group, 2 * cl, cl), BF16)
    sums_shape = ((rhs, LANES), F32)
    total = pltpu.VMEM((clusters, 2 * rhs, cl), F32)
    pieces = pltpu.VMEM((clusters + 1, 2 * rhs, cl), BF16)
    sources = pltpu.VMEM((clusters + 1, FEATURES, cl), BF16)
    own_blocks, blocks, near, targets, tail = call(
        functools.partial(own_kernel, cl),
        [own, kept, whole, ((clusters, FEATURES, cl), BF16), sums_shape],
        [pieces, sources, total],
        "svv>ppvpv",
        pairs, sent, beside,
        us=8.0,
    )
    swap = swapped(near_pair, far_pair, tail)
    blocks_partner, near = call(
        functools.partial(partner_kernel, cl),
        [kept, whole],
        [pieces, sources, total],
        "svpv>pv",
        pairs, partner, targets, near,
        us=0.2,
    )
    tiles = 6 * per * span // LANES
    window = pltpu.VMEM((tiles, 2 * rhs, LANES), BF16)
    gathered = pltpu.VMEM((clusters, 2 * rhs, partners * rank), BF16)
    fields = pltpu.VMEM((clusters, 2 * rhs, 2 * rank), BF16)
    near, coupling = call(
        functools.partial(far_kernel, cl, rank),
        [whole, ((clusters, 2 * rank, partners * rank), BF16)],
        [window, pltpu.VMEM((tiles, 8, LANES), F32), gathered, fields],
        "svvvvvpp>vp",
        at, near_pair, far_pair, swap, centers, near, basis, offsets,
        us=0.2,
    )
    blocks_other, image, payload, table = call(
        functools.partial(image_kernel, cl, rank),
        [kept, whole, whole, ((rhs, span + LANES), F32)],
        [pieces, sources, total],
        "svpvvpp>pvvv",
        pairs, other, targets, near, area, krylov, basis,
        us=4.0,
    )
    sent, beside, near_pair, far_pair, other, partner = exchange(payload, table, True)
    near, tail = call(
        functools.partial(own_again_kernel, cl),
        [whole, sums_shape],
        [pieces, total],
        "svvpp>vv",
        pairs, sent, beside, own_blocks, blocks,
        us=8.0,
    )
    swap = swapped(near_pair, far_pair, tail)
    (near,) = call(
        functools.partial(neighbour_again_kernel, cl, 1),
        [whole],
        [pieces, total],
        "svvp>v",
        pairs, partner, near, blocks_partner,
        us=4.0,
    )
    (one,) = call(window_sums_kernel, [sums_shape], [], "vvvvv>v", table, beside, near_pair, far_pair, swap, us=0.3)
    size = 8
    many = outward(one, size)
    while 2 * size < devices:
        (one,) = call(merge_kernel, [sums_shape], [], "vv>v", one, many, us=0.3)
        size = 2 * size
        many = outward(one, size)
    (near,) = call(
        functools.partial(far_again_kernel, cl, rank),
        [whole],
        [window, gathered, fields],
        "svvvvpp>v",
        at, near_pair, far_pair, swap, near, coupling, basis,
        us=4.0,
    )
    (near,) = call(
        functools.partial(neighbour_again_kernel, cl, 2),
        [whole],
        [pieces, total],
        "svvp>v",
        pairs, other, near, blocks_other,
        us=1.5,
    )
    here = pltpu.VMEM((rhs, panels), F32)
    return tuple(call(
        functools.partial(finish_kernel, cl, panels * devices),
        [whole, whole],
        [here, here, pltpu.SemaphoreType.DMA((8,))],
        "vvvpvv>hh",
        near, area, image, krylov, one, many,
        us=1.0,
    ))


def solution(mesh):
    whole = P(None, ("jobs", "clus"))
    rows = P(("jobs", "clus"), None)
    return jax.shard_map(
        body,
        mesh=mesh,
        in_specs=(whole, whole, rows, rows, whole, whole),
        out_specs=(whole, whole),
        check_vma=False,
    )
```

```python
import functools

import jax
import jax.numpy as jnp
import numpy as np
from jax import lax
from jax.experimental import pallas as pl
from jax.experimental.pallas import tpu as pltpu
from jax.sharding import PartitionSpec as P

REACH = 4
SMOOTHING = 0.04
COULOMB = 2.0
PROXY_RADIUS = 0.6
LANES = 128
FEATURES = 80
GRID = 1.5 * 2.0 ** 22
F32 = jnp.float32
BF16 = jnp.bfloat16


def proxy_offsets(points):
    counter = np.arange(points, dtype=np.float32)
    height = 1.0 - (2.0 * counter + 1.0) / points
    radial = np.sqrt(1.0 - height * height)
    azimuth = counter * 2.399963
    return PROXY_RADIUS * np.stack([radial * np.cos(azimuth), radial * np.sin(azimuth), height]).astype(np.float32)


def split(value):
    high = value.astype(BF16)
    return high, (value - high.astype(F32)).astype(BF16)


def stacked(value):
    return jnp.concatenate(split(value), axis=0)


def folded(value):
    half = value.shape[0] // 2
    return value[:half] + value[half:]


def dot_nt(left, right):
    return lax.dot_general(left, right, (((1,), (1,)), ((), ())), preferred_element_type=F32)


def dot_tn(left, right):
    return lax.dot_general(left, right, (((0,), (0,)), ((), ())), preferred_element_type=F32)


def dot_nn(left, right):
    return lax.dot_general(left, right, (((1,), (0,)), ((), ())), preferred_element_type=F32)


def quartered(value):
    half = value.shape[1] // 2
    value = folded(value)
    return value[:, 0:half] + value[:, half:]


def moments_of(weighted, basis_pieces):
    return quartered(dot_nt(stacked(weighted), basis_pieces))


def copies(pairs, sems):
    moves = [pltpu.make_async_copy(source, target, sems.at[i]) for i, (source, target) in enumerate(pairs)]
    for move in moves:
        move.start()
    return moves


def pair_list(near, position, clusters):
    block = lax.div(near, clusters) - position
    side = block * (1 - 2 * lax.rem(position, 2))
    place = lax.rem(near, clusters).astype(F32)
    across = lax.broadcasted_iota(jnp.int32, (clusters, clusters), 1)
    down = lax.broadcasted_iota(jnp.int32, (clusters, clusters), 0)
    upright = lambda value: jnp.sum(jnp.where(across == down, value, 0.0), axis=1, keepdims=True)
    row = lax.broadcasted_iota(jnp.int32, (clusters, LANES), 1).astype(F32)
    target = lax.broadcasted_iota(jnp.int32, (clusters, 1), 0).astype(F32)
    rows = lax.broadcasted_iota(jnp.int32, (8, LANES), 0)
    out = jnp.zeros((8, LANES), F32)
    for which in range(3):
        live = jnp.where((side == (0, 1, -1)[which]) & (near >= 0), 1.0, 0.0)
        counts = sum(live[k:k + 1] for k in range(1, near.shape[0]))
        first = jnp.sum(jnp.where(across < down, counts, 0.0), axis=1, keepdims=True)
        found = jnp.zeros((clusters, LANES), F32)
        for k in range(1, near.shape[0]):
            alive = upright(live[k:k + 1])
            hit = jnp.where(row == first, alive, 0.0)
            found = found + hit * (target * 64 + upright(place[k:k + 1]))
            first = first + alive
        count = jnp.sum(counts, axis=1, keepdims=True)
        found = jnp.where(row[0:1] < count, jnp.sum(found, axis=0, keepdims=True), 1.0 * clusters)
        out = jnp.where(rows == which, found, jnp.where(rows == 3 + which, count, out))
    return out.astype(jnp.int32)


def prepare_kernel(cl, vcl, rank, position_ref, vertices_hbm, corners_hbm, krylov_hbm, basis_hbm, far_hbm, near_hbm, offsets_hbm,
                   payload_ref, table_ref, area_ref, center_ref, at_ref, pairs_ref, basis_ref, krylov_ref, offsets_ref,
                   vertices_ref, corners_ref, raw_ref, far_ref, near_ref, mesh_ref, local_ref, sems):
    moves = copies((
        (vertices_hbm, vertices_ref), (corners_hbm, corners_ref), (krylov_hbm, krylov_ref), (basis_hbm, raw_ref),
        (far_hbm, far_ref), (near_hbm, near_ref), (offsets_hbm, offsets_ref),
    ), sems)
    rhs, panels = krylov_ref.shape
    clusters = panels // cl
    parts = cl // LANES
    moves[0].wait()
    for c in range(clusters):
        mesh_ref[3 * c:3 * c + 3, :] = vertices_ref[:, c * vcl:(c + 1) * vcl]
    moves[1].wait()
    for i in range(clusters * parts):
        local_ref[3 * i:3 * i + 3, :] = corners_ref[:, i * LANES:(i + 1) * LANES]
    first = position_ref[0] * (vcl * clusters) + vcl * lax.broadcasted_iota(jnp.int32, (clusters, LANES), 0)
    tables = [mesh_ref[pl.ds(k, clusters, stride=3), :] for k in range(3)]
    sums = [None] * 3
    for h in range(parts):
        local = [local_ref[pl.ds(3 * h + m, clusters, stride=3 * parts), :] - first for m in range(3)]
        corner = [[jnp.take_along_axis(tables[k], local[m], axis=1, mode="promise_in_bounds") for k in range(3)] for m in range(3)]
        for k in range(3):
            middle = (corner[0][k] + corner[1][k] + corner[2][k]) / 3.0
            lanes = slice(panels + k * cl + h * LANES, panels + k * cl + (h + 1) * LANES)
            payload_ref[:, lanes] = middle
            sums[k] = middle if h == 0 else sums[k] + middle
        one = [corner[1][k] - corner[0][k] for k in range(3)]
        two = [corner[2][k] - corner[0][k] for k in range(3)]
        normal = [one[1] * two[2] - one[2] * two[1], one[2] * two[0] - one[0] * two[2], one[0] * two[1] - one[1] * two[0]]
        area_ref[:, h * LANES:(h + 1) * LANES] = 0.5 * jnp.sqrt(normal[0] * normal[0] + normal[1] * normal[1] + normal[2] * normal[2])
    span = clusters * rank
    mine = lax.broadcasted_iota(jnp.int32, (clusters, span), 1) // rank == lax.broadcasted_iota(jnp.int32, (clusters, span), 0)
    half = span // 2
    table_ref[:, span:] = jnp.zeros_like(table_ref[:, span:])
    for k in range(3):
        center = jnp.sum(sums[k], axis=1, keepdims=True) / cl
        center_ref[:, k * LANES:(k + 1) * LANES] = jnp.broadcast_to(center, (clusters, LANES))
        row = jnp.sum(jnp.where(mine, center, 0.0), axis=0, keepdims=True)
        table_ref[k:k + 1, span:] = row[:, 0:half]
        table_ref[8 + k:9 + k, span:] = row[:, half:]
    moves[2].wait()
    moves[3].wait()
    for c in range(clusters):
        lanes = slice(c * cl, (c + 1) * cl)
        basis_ref[:, lanes] = stacked(raw_ref[:, lanes])
        charges = area_ref[c:c + 1, :] * krylov_ref[:, lanes]
        payload_ref[:, lanes] = charges
        table_ref[:, c * rank:(c + 1) * rank] = moments_of(charges, basis_ref[:, lanes])
    moves[4].wait()
    far = far_ref[...]
    step = (lax.div(far, clusters) - position_ref[0]) * (1 - 2 * lax.rem(position_ref[0], 2))
    block = jnp.where(step < 0, step + REACH, step + REACH - 3)
    per = LANES // rank
    turn = lax.rem(lax.broadcasted_iota(jnp.int32, far.shape, 1) - far + per * clusters * 2 ** 16, per)
    at_ref[...] = (turn * 6 + block) * (span // LANES) + lax.div(lax.rem(far, clusters), per)
    moves[5].wait()
    pairs_ref[...] = pair_list(near_ref[...], position_ref[0], clusters)
    moves[6].wait()


def features_of(payload_ref, panels, c, cl, target):
    rows = [payload_ref[c:c + 1, panels + k * cl:panels + (k + 1) * cl] for k in range(3)]
    value = jnp.concatenate(rows + [jnp.zeros((5, cl), F32)], axis=0)
    coarse = (value + GRID) - GRID
    middle = (value - coarse).astype(BF16).astype(F32)
    low = (value - coarse - middle).astype(BF16).astype(F32)
    pieces = [coarse, middle, low]
    rest = middle + low
    row = lax.broadcasted_iota(jnp.int32, (8, cl), 0)
    square = jnp.sum(coarse * coarse, axis=0, keepdims=True)
    extra = jnp.sum((2.0 * coarse + rest) * rest, axis=0, keepdims=True) + (SMOOTHING if target else 0.0)
    square_high = square.astype(BF16).astype(F32)
    extra_high = extra.astype(BF16).astype(F32)
    extra_middle = (extra - extra_high).astype(BF16).astype(F32)
    ones = jnp.ones((1, cl), F32)

    def placed(base, start, *values):
        for i, one in enumerate(values):
            base = jnp.where(row == start + i, one, base)
        return base

    squares, extras = (square_high, square - square_high), (extra_high, extra_middle, extra - extra_high - extra_middle)
    if target:
        scaled = [-2.0 * piece for piece in pieces]
        first = placed(scaled[0], 3, *squares, ones, ones)
        last = placed(jnp.zeros((8, cl), F32), 0, *extras, ones, ones, ones)
    else:
        first = placed(coarse, 3, ones, ones, *squares)
        last = placed(jnp.zeros((8, cl), F32), 0, ones, ones, ones, *extras)
    combos = [(scaled[i] if target else pieces[j]) for i in range(3) for j in range(3) if i + j]
    return jnp.concatenate([first, *combos, last], axis=0)


def fill_features(sources_ref, payload_ref, panels, cl):
    clusters = panels // cl
    for c in range(clusters):
        sources_ref[c] = features_of(payload_ref, panels, c, cl, False).astype(BF16)
    sources_ref[clusters] = sources_ref[0]


def near_block(source, target, pieces, out_ref):
    cl = source.shape[1]
    parts = []
    for first in range(0, cl, LANES):
        rows = slice(first, first + LANES)
        high, low = split(lax.rsqrt(dot_tn(source[:, rows], target)))
        out_ref[rows, :] = high
        out_ref[cl + first:cl + first + LANES, :] = low
        parts.append(dot_nn(pieces[:, rows], high) + dot_nn(pieces[:, rows], low))
    return sum(parts[1:], parts[0])


def near_product(pieces, block_ref, cl):
    return dot_nn(pieces, block_ref[0:cl, :]) + dot_nn(pieces, block_ref[cl:2 * cl, :])


def fill_charges(pieces_ref, payload_ref, clusters, cl):
    for c in range(clusters):
        pieces_ref[c] = stacked(payload_ref[:, c * cl:(c + 1) * cl])
    pieces_ref[clusters] = jnp.zeros_like(pieces_ref[0])


def pair_at(pairs_ref, which, i):
    pair = pairs_ref[which, i]
    return lax.shift_right_logical(pair, 6), lax.bitwise_and(pair, 63)


def build_list(which, pairs_ref, targets_ref, kept_ref, pieces_ref, sources_ref, total_ref):
    group = kept_ref.shape[1]

    def step(m, _):
        pairs = [pair_at(pairs_ref, which, group * m + w) for w in range(group)]
        loaded = [(sources_ref[j], targets_ref[c], pieces_ref[j]) for c, j in pairs]
        parts = [near_block(*one, kept_ref.at[m, w]) for w, one in enumerate(loaded)]
        for (c, j), part in zip(pairs, parts):
            total_ref[c] += part
        return 0

    lax.fori_loop(0, (pairs_ref[3 + which, 0] + group - 1) // group, step, 0)


def apply_list(which, pairs_ref, kept_ref, pieces_ref, total_ref, cl):
    group = kept_ref.shape[1]

    def step(m, _):
        pairs = [pair_at(pairs_ref, which, group * m + w) for w in range(group)]
        parts = [near_product(pieces_ref[j], kept_ref.at[m, w], cl) for w, (c, j) in enumerate(pairs)]
        for (c, j), part in zip(pairs, parts):
            total_ref[c] += part
        return 0

    lax.fori_loop(0, (pairs_ref[3 + which, 0] + group - 1) // group, step, 0)


def put_total(cl, total_ref, start_ref, out_ref):
    for c in range(total_ref.shape[0]):
        lanes = slice(c * cl, (c + 1) * cl)
        near = folded(total_ref[c])
        out_ref[:, lanes] = near if start_ref is None else start_ref[:, lanes] + near


def own_kernel(cl, pairs_ref, payload_ref, beside_ref, own_ref, kept_ref, near_out_ref, targets_ref, tail_ref, pieces_ref, sources_ref, total_ref):
    tail_ref[...] = beside_ref[:, beside_ref.shape[1] - LANES:]
    panels = near_out_ref.shape[1]
    clusters = panels // cl
    fill_charges(pieces_ref, payload_ref, clusters, cl)
    fill_features(sources_ref, payload_ref, panels, cl)
    for c in range(clusters):
        target = features_of(payload_ref, panels, c, cl, True).astype(BF16)
        targets_ref[c] = target
        total_ref[c] = near_block(sources_ref[c], target, pieces_ref[c], own_ref.at[c])
    build_list(0, pairs_ref, targets_ref, kept_ref, pieces_ref, sources_ref, total_ref)
    put_total(cl, total_ref, None, near_out_ref)


def partner_kernel(cl, pairs_ref, payload_ref, targets_ref, start_ref, kept_ref, near_out_ref, pieces_ref, sources_ref, total_ref):
    panels = near_out_ref.shape[1]
    fill_charges(pieces_ref, payload_ref, panels // cl, cl)
    fill_features(sources_ref, payload_ref, panels, cl)
    total_ref[...] = jnp.zeros_like(total_ref)
    build_list(1, pairs_ref, targets_ref, kept_ref, pieces_ref, sources_ref, total_ref)
    put_total(cl, total_ref, start_ref, near_out_ref)


def image_kernel(cl, rank, pairs_ref, payload_ref, targets_ref, start_ref, area_ref, krylov_ref, basis_ref,
                 kept_ref, image_ref, charges_ref, table_ref, pieces_ref, sources_ref, total_ref):
    rhs, panels = image_ref.shape
    clusters = panels // cl
    span = clusters * rank
    fill_charges(pieces_ref, payload_ref, clusters, cl)
    fill_features(sources_ref, payload_ref, panels, cl)
    total_ref[...] = jnp.zeros_like(total_ref)
    build_list(2, pairs_ref, targets_ref, kept_ref, pieces_ref, sources_ref, total_ref)
    squared = correlation = jnp.zeros((rhs, cl), F32)
    for c in range(clusters):
        lanes = slice(c * cl, (c + 1) * cl)
        area = area_ref[c:c + 1, :]
        image = COULOMB * area * (start_ref[:, lanes] + folded(total_ref[c]))
        charges = area * image
        image_ref[:, lanes] = image
        charges_ref[:, lanes] = charges
        table_ref[:, c * rank:(c + 1) * rank] = moments_of(charges, basis_ref[:, lanes])
        krylov = krylov_ref[:, lanes]
        squared = squared + krylov * krylov
        correlation = correlation + krylov * image
    squared = jnp.sum(squared, axis=1, keepdims=True)
    correlation = jnp.sum(correlation, axis=1, keepdims=True)
    local = ratio(correlation, squared)
    energy = jnp.zeros((rhs, cl), F32)
    for c in range(clusters):
        lanes = slice(c * cl, (c + 1) * cl)
        residual = image_ref[:, lanes] - local * krylov_ref[:, lanes]
        energy = energy + residual * residual
    table_ref[:, span:] = in_lanes(squared, correlation, jnp.sum(energy, axis=1, keepdims=True), local)


def own_again_kernel(cl, pairs_ref, payload_ref, beside_ref, own_ref, kept_ref, near_out_ref, tail_ref, pieces_ref, total_ref):
    tail_ref[...] = beside_ref[:, beside_ref.shape[1] - LANES:]
    clusters = near_out_ref.shape[1] // cl
    fill_charges(pieces_ref, payload_ref, clusters, cl)
    for c in range(clusters):
        total_ref[c] = near_product(pieces_ref[c], own_ref.at[c], cl)
    apply_list(0, pairs_ref, kept_ref, pieces_ref, total_ref, cl)
    put_total(cl, total_ref, None, near_out_ref)


def neighbour_again_kernel(cl, which, pairs_ref, payload_ref, start_ref, kept_ref, near_out_ref, pieces_ref, total_ref):
    fill_charges(pieces_ref, payload_ref, near_out_ref.shape[1] // cl, cl)
    total_ref[...] = jnp.zeros_like(total_ref)
    apply_list(which, pairs_ref, kept_ref, pieces_ref, total_ref, cl)
    put_total(cl, total_ref, start_ref, near_out_ref)


def finish_kernel(cl, total, near_ref, area_ref, image_ref, krylov_ref, one_ref, two_ref, next_hbm, second_hbm, next_ref, second_ref, sems):
    panels = image_ref.shape[1]
    clusters = panels // cl
    squared, correlation, energy, local = merged([one_ref[...], two_ref[...]])
    projection = correlation / (squared + 1e-06)
    gap = projection - local
    scaling = 1.0 / jnp.sqrt((energy + gap * gap * squared) / total + 1e-06)
    moves = []
    parts = 4
    for h in range(parts):
        for c in range(h * clusters // parts, (h + 1) * clusters // parts):
            lanes = slice(c * cl, (c + 1) * cl)
            image = image_ref[:, lanes]
            next_ref[:, lanes] = (image - projection * krylov_ref[:, lanes]) * scaling
            second_ref[:, lanes] = (COULOMB * area_ref[c:c + 1, :] * near_ref[:, lanes] - projection * image) * scaling
        lanes = slice(h * panels // parts, (h + 1) * panels // parts)
        for held, hbm in ((next_ref, next_hbm), (second_ref, second_hbm)):
            moves.append(pltpu.make_async_copy(held.at[:, lanes], hbm.at[:, lanes], sems.at[len(moves)]))
            moves[-1].start()
    for move in moves:
        move.wait()


def load_window(tables, clusters, rank, pieces_ref, middle_ref):
    per = LANES // rank
    span = clusters * rank
    count = pieces_ref.shape[0] // per
    groups = span // LANES
    for at in range(count):
        (ref, first), g = tables[at // groups], at % groups
        tile = ref[:, first + g * LANES:first + (g + 1) * LANES]
        for s in range(per):
            pieces_ref[s * count + at] = stacked(pltpu.roll(tile, s * rank, 1) if s else tile)
        if middle_ref is not None:
            half = groups // 2
            row, lane = 8 * (g // half), first + span + g % half * LANES
            tile = ref[row:row + 8, lane:lane + LANES]
            for s in range(per):
                middle_ref[s * count + at] = pltpu.roll(tile, s * rank, 1) if s else tile


def six_tables(near_ref, far_ref, swapped_ref):
    width = near_ref.shape[1] // 2
    return (far_ref, 0), (far_ref, width), (near_ref, 0), (swapped_ref, width), (swapped_ref, 0), (swapped_ref, 3 * width)


def lane_masks(shape, rank, kind):
    lane = (lax.broadcasted_iota(jnp.int32, shape, 1) // rank).astype(kind)
    return [lane == jnp.asarray(u, kind) for u in range(LANES // rank)]


def pick(source_ref, at_ref, c, g, masks):
    row = None
    for u, mask in enumerate(masks):
        take = source_ref[at_ref[c, g * len(masks) + u]]
        row = take if row is None else jnp.where(mask, take, row)
    return row


def far_fields(gathered_ref, coupling_ref, fields_ref):
    for c in range(gathered_ref.shape[0]):
        field = quartered(dot_nt(gathered_ref[c], coupling_ref[c]))
        fields_ref[c] = stacked(jnp.concatenate([field, field], axis=1))


def far_potential(fields_ref, c, basis):
    return folded(dot_nn(fields_ref[c], basis))


def far_kernel(cl, rank, at_ref, near_pair_ref, far_pair_ref, swapped_ref, center_ref, near_ref, basis_ref, offsets_ref,
               out_ref, coupling_ref, pieces_ref, middle_ref, gathered_ref, fields_ref):
    clusters = near_ref.shape[1] // cl
    per = LANES // rank
    load_window(six_tables(near_pair_ref, far_pair_ref, swapped_ref), clusters, rank, pieces_ref, middle_ref)
    wide = lane_masks(middle_ref.shape[1:], rank, jnp.int32)
    masks = lane_masks(pieces_ref.shape[1:], rank, jnp.int16)
    for c in range(clusters):
        mine = [offsets_ref[3, k:k + 1, :] - center_ref[c:c + 1, k * LANES:(k + 1) * LANES] for k in range(3)]
        for g in range(at_ref.shape[1] // per):
            lanes = slice(g * LANES, (g + 1) * LANES)
            gathered_ref[c, :, lanes] = pick(pieces_ref, at_ref, c, g, masks)
            center = pick(middle_ref, at_ref, c, g, wide)
            gap = [(center[k:k + 1] + mine[k]) - offsets_ref[k] for k in range(3)]
            high, low = split(lax.rsqrt(gap[0] * gap[0] + gap[1] * gap[1] + gap[2] * gap[2] + SMOOTHING))
            coupling_ref[c, 0:rank, lanes] = high
            coupling_ref[c, rank:2 * rank, lanes] = low
    far_fields(gathered_ref, coupling_ref, fields_ref)
    for c in range(clusters):
        lanes = slice(c * cl, (c + 1) * cl)
        out_ref[:, lanes] = near_ref[:, lanes] + far_potential(fields_ref, c, basis_ref[:, lanes])


def far_again_kernel(cl, rank, at_ref, near_pair_ref, far_pair_ref, swapped_ref, near_ref, coupling_ref, basis_ref,
                     out_ref, pieces_ref, gathered_ref, fields_ref):
    clusters = near_ref.shape[1] // cl
    per = LANES // rank
    load_window(six_tables(near_pair_ref, far_pair_ref, swapped_ref), clusters, rank, pieces_ref, None)
    masks = lane_masks(pieces_ref.shape[1:], rank, jnp.int16)
    for c in range(clusters):
        for g in range(at_ref.shape[1] // per):
            gathered_ref[c, :, g * LANES:(g + 1) * LANES] = pick(pieces_ref, at_ref, c, g, masks)
    far_fields(gathered_ref, coupling_ref, fields_ref)
    for c in range(clusters):
        lanes = slice(c * cl, (c + 1) * cl)
        out_ref[:, lanes] = near_ref[:, lanes] + far_potential(fields_ref, c, basis_ref[:, lanes])


def ratio(correlation, squared):
    return jnp.where(squared > 0, correlation / jnp.where(squared > 0, squared, 1.0), 0.0)


def in_lanes(*columns):
    lane = lax.broadcasted_iota(jnp.int32, (columns[0].shape[0], LANES), 1)
    out = columns[-1]
    for i, column in enumerate(columns[:-1]):
        out = jnp.where(lane == i, column, out)
    return out


def merged(groups):
    squared = sum(group[:, 0:1] for group in groups)
    correlation = sum(group[:, 1:2] for group in groups)
    local = ratio(correlation, squared)
    energy = 0.0
    for group in groups:
        gap = local - group[:, 3:4]
        energy = energy + (group[:, 2:3] + gap * gap * group[:, 0:1])
    return squared, correlation, energy, local


def window_sums_kernel(payload_ref, partner_ref, near_pair_ref, far_pair_ref, swapped_ref, out_ref):
    width = near_pair_ref.shape[1] // 2
    ends = [(payload_ref, payload_ref.shape[1]), (partner_ref, partner_ref.shape[1])]
    ends += [(ref, end) for ref in (near_pair_ref, far_pair_ref, swapped_ref) for end in (width, 2 * width)]
    out_ref[...] = in_lanes(*merged([ref[:, end - LANES:end] for ref, end in ends]))


def merge_kernel(one_ref, two_ref, out_ref):
    out_ref[...] = in_lanes(*merged([one_ref[...], two_ref[...]]))


def call(kernel, outs, scratch, memory, *args, limit=10, us=1.0):
    spaces = {"s": pltpu.SMEM, "v": pltpu.VMEM, "p": pltpu.VMEM, "h": pltpu.HBM}
    ins, out_spaces = memory.split(">")
    pinned = {"h": pltpu.HBM, "p": pltpu.VMEM}
    return pl.pallas_call(
        kernel,
        out_shape=[pltpu.VMEM(*out) if m == "p" else jax.ShapeDtypeStruct(*out) for m, out in zip(out_spaces, outs)],
        in_specs=[pl.BlockSpec(memory_space=spaces[m]) for m in ins],
        out_specs=[pl.BlockSpec(memory_space=spaces[m]) for m in out_spaces],
        scratch_shapes=scratch,
        compiler_params=pltpu.CompilerParams(vmem_limit_bytes=limit * 2 ** 20),
        cost_estimate=pl.CostEstimate(flops=int(us * 5e8), bytes_accessed=int(us * 3.6e6), transcendentals=0),
    )(*(pltpu.with_memory_space_constraint(a, pinned[m]) if m in pinned else a for m, a in zip(ins, args)))


def body(vertices, panel_vertices, near_pairs, far_pairs, basis, krylov):
    clusters, slots = near_pairs.shape
    partners = far_pairs.shape[1]
    rhs, panels = krylov.shape
    rank = basis.shape[0]
    cl = panels // clusters
    vcl = vertices.shape[1] // clusters
    span = clusters * rank
    per = LANES // rank
    devices = lax.axis_size("clus")
    position = lax.axis_index("clus").reshape(1).astype(jnp.int32)
    offsets = proxy_offsets(rank)
    flat = np.concatenate([np.tile(offsets, (1, per)), np.zeros((rank - 3, LANES), np.float32)])
    offsets = jnp.asarray(np.concatenate([np.broadcast_to(offsets[:, :, None], (3, rank, LANES)), flat[None]]))
    width = span + span // 2
    pairing = [(i, i + 1 - 2 * (i % 2)) for i in range(devices)]
    bridging = [(i, i - 1 + 2 * (i % 2)) for i in range(1, devices - 1)] + [(0, 0), (devices - 1, devices - 1)]

    def move(value, pairs):
        return lax.ppermute(value, "clus", pairs)

    def outward(value, steps, wrap=True):
        moves = [(i, i + steps * (1 - 2 * (i % 2))) for i in range(devices)]
        return move(value, [(i, j % devices if wrap or 0 <= j < devices else i + 1 - 2 * (i % 2)) for i, j in moves])

    def exchange(payload, table, wrap):
        beside = move(table, pairing)
        pair = jnp.concatenate([table, beside], axis=1)
        near_pair, far_pair = outward(pair, 2, wrap), outward(pair, 4, wrap)
        sent = jnp.concatenate([payload, beside[:, beside.shape[1] - LANES:]], axis=1)
        return sent, beside, near_pair, far_pair, move(sent, bridging), move(payload, pairing)

    def swapped(near_pair, far_pair, tail):
        return move(jnp.concatenate([near_pair, far_pair, tail], axis=1), pairing)

    whole = ((rhs, panels), F32)
    payload, table, area, centers, at, pairs, basis, krylov, offsets = call(
        functools.partial(prepare_kernel, cl, vcl, rank),
        [
            ((rhs, panels + 3 * cl), F32), ((rhs, width), F32), ((clusters, cl), F32), ((clusters, 3 * LANES), F32),
            (far_pairs.shape, jnp.int32), ((8, LANES), jnp.int32), ((2 * rank, panels), BF16), whole, (offsets.shape, F32),
        ],
        [
            pltpu.VMEM(vertices.shape, F32),
            pltpu.VMEM(panel_vertices.shape, jnp.int32),
            pltpu.VMEM(basis.shape, F32),
            pltpu.VMEM(far_pairs.shape, jnp.int32),
            pltpu.VMEM((slots, clusters), jnp.int32),
            pltpu.VMEM((3 * clusters, vcl), F32),
            pltpu.VMEM((3 * panels // LANES, LANES), jnp.int32),
            pltpu.SemaphoreType.DMA((7,)),
        ],
        "shhhhhhh>vvvvvvppp",
        position, vertices, panel_vertices, krylov, basis, far_pairs, near_pairs.T, offsets,
        us=1.5,
    )
    sent, beside, near_pair, far_pair, other, partner = exchange(payload, table, False)
    group = 2
    own = ((clusters, 2 * cl, cl), BF16)
    kept = ((clusters * (slots - 1) // group, group, 2 * cl, cl), BF16)
    sums_shape = ((rhs, LANES), F32)
    total = pltpu.VMEM((clusters, 2 * rhs, cl), F32)
    pieces = pltpu.VMEM((clusters + 1, 2 * rhs, cl), BF16)
    sources = pltpu.VMEM((clusters + 1, FEATURES, cl), BF16)
    own_blocks, blocks, near, targets, tail = call(
        functools.partial(own_kernel, cl),
        [own, kept, whole, ((clusters, FEATURES, cl), BF16), sums_shape],
        [pieces, sources, total],
        "svv>ppvpv",
        pairs, sent, beside,
        us=8.0,
    )
    swap = swapped(near_pair, far_pair, tail)
    blocks_partner, near = call(
        functools.partial(partner_kernel, cl),
        [kept, whole],
        [pieces, sources, total],
        "svpv>pv",
        pairs, partner, targets, near,
        us=0.2,
    )
    tiles = 6 * per * span // LANES
    window = pltpu.VMEM((tiles, 2 * rhs, LANES), BF16)
    gathered = pltpu.VMEM((clusters, 2 * rhs, partners * rank), BF16)
    fields = pltpu.VMEM((clusters, 2 * rhs, 2 * rank), BF16)
    near, coupling = call(
        functools.partial(far_kernel, cl, rank),
        [whole, ((clusters, 2 * rank, partners * rank), BF16)],
        [window, pltpu.VMEM((tiles, 8, LANES), F32), gathered, fields],
        "svvvvvpp>vp",
        at, near_pair, far_pair, swap, centers, near, basis, offsets,
        us=0.2,
    )
    blocks_other, image, payload, table = call(
        functools.partial(image_kernel, cl, rank),
        [kept, whole, whole, ((rhs, span + LANES), F32)],
        [pieces, sources, total],
        "svpvvpp>pvvv",
        pairs, other, targets, near, area, krylov, basis,
        us=4.0,
    )
    sent, beside, near_pair, far_pair, other, partner = exchange(payload, table, True)
    near, tail = call(
        functools.partial(own_again_kernel, cl),
        [whole, sums_shape],
        [pieces, total],
        "svvpp>vv",
        pairs, sent, beside, own_blocks, blocks,
        us=8.0,
    )
    swap = swapped(near_pair, far_pair, tail)
    (near,) = call(
        functools.partial(neighbour_again_kernel, cl, 1),
        [whole],
        [pieces, total],
        "svvp>v",
        pairs, partner, near, blocks_partner,
        us=4.0,
    )
    (one,) = call(window_sums_kernel, [sums_shape], [], "vvvvv>v", table, beside, near_pair, far_pair, swap, us=0.3)
    size = 8
    many = outward(one, size)
    while 2 * size < devices:
        (one,) = call(merge_kernel, [sums_shape], [], "vv>v", one, many, us=0.3)
        size = 2 * size
        many = outward(one, size)
    (near,) = call(
        functools.partial(far_again_kernel, cl, rank),
        [whole],
        [window, gathered, fields],
        "svvvvpp>v",
        at, near_pair, far_pair, swap, near, coupling, basis,
        us=4.0,
    )
    (near,) = call(
        functools.partial(neighbour_again_kernel, cl, 2),
        [whole],
        [pieces, total],
        "svvp>v",
        pairs, other, near, blocks_other,
        us=1.5,
    )
    here = pltpu.VMEM((rhs, panels), F32)
    return tuple(call(
        functools.partial(finish_kernel, cl, panels * devices),
        [whole, whole],
        [here, here, pltpu.SemaphoreType.DMA((8,))],
        "vvvpvv>hh",
        near, area, image, krylov, one, many,
        us=1.0,
    ))


def solution(mesh):
    whole = P(None, ("jobs", "clus"))
    rows = P(("jobs", "clus"), None)
    return jax.shard_map(
        body,
        mesh=mesh,
        in_specs=(whole, whole, rows, rows, whole, whole),
        out_specs=(whole, whole),
        check_vma=False,
    )
```

```python
import functools

import jax
import jax.numpy as jnp
import numpy as np
from jax import lax
from jax.experimental import pallas as pl
from jax.experimental.pallas import tpu as pltpu
from jax.sharding import PartitionSpec as P

REACH = 4
SMOOTHING = 0.04
COULOMB = 2.0
PROXY_RADIUS = 0.6
LANES = 128
FEATURES = 80
GRID = 1.5 * 2.0 ** 22
F32 = jnp.float32
BF16 = jnp.bfloat16


def proxy_offsets(points):
    counter = np.arange(points, dtype=np.float32)
    height = 1.0 - (2.0 * counter + 1.0) / points
    radial = np.sqrt(1.0 - height * height)
    azimuth = counter * 2.399963
    return PROXY_RADIUS * np.stack([radial * np.cos(azimuth), radial * np.sin(azimuth), height]).astype(np.float32)


def split(value):
    high = value.astype(BF16)
    return high, (value - high.astype(F32)).astype(BF16)


def stacked(value):
    return jnp.concatenate(split(value), axis=0)


def folded(value):
    half = value.shape[0] // 2
    return value[:half] + value[half:]


def dot_nt(left, right):
    return lax.dot_general(left, right, (((1,), (1,)), ((), ())), preferred_element_type=F32)


def dot_tn(left, right):
    return lax.dot_general(left, right, (((0,), (0,)), ((), ())), preferred_element_type=F32)


def dot_nn(left, right):
    return lax.dot_general(left, right, (((1,), (0,)), ((), ())), preferred_element_type=F32)


def quartered(value):
    half = value.shape[1] // 2
    value = folded(value)
    return value[:, 0:half] + value[:, half:]


def moments_of(weighted, basis_pieces):
    return quartered(dot_nt(stacked(weighted), basis_pieces))


def copies(pairs, sems):
    moves = [pltpu.make_async_copy(source, target, sems.at[i]) for i, (source, target) in enumerate(pairs)]
    for move in moves:
        move.start()
    return moves


def pair_list(near, position, clusters):
    block = lax.div(near, clusters) - position
    side = block * (1 - 2 * lax.rem(position, 2))
    place = lax.rem(near, clusters).astype(F32)
    across = lax.broadcasted_iota(jnp.int32, (clusters, clusters), 1)
    down = lax.broadcasted_iota(jnp.int32, (clusters, clusters), 0)
    upright = lambda value: jnp.sum(jnp.where(across == down, value, 0.0), axis=1, keepdims=True)
    row = lax.broadcasted_iota(jnp.int32, (clusters, LANES), 1).astype(F32)
    target = lax.broadcasted_iota(jnp.int32, (clusters, 1), 0).astype(F32)
    rows = lax.broadcasted_iota(jnp.int32, (8, LANES), 0)
    out = jnp.zeros((8, LANES), F32)
    for which in range(3):
        live = jnp.where((side == (0, 1, -1)[which]) & (near >= 0), 1.0, 0.0)
        counts = sum(live[k:k + 1] for k in range(1, near.shape[0]))
        first = jnp.sum(jnp.where(across < down, counts, 0.0), axis=1, keepdims=True)
        found = jnp.zeros((clusters, LANES), F32)
        for k in range(1, near.shape[0]):
            alive = upright(live[k:k + 1])
            hit = jnp.where(row == first, alive, 0.0)
            found = found + hit * (target * 64 + upright(place[k:k + 1]))
            first = first + alive
        count = jnp.sum(counts, axis=1, keepdims=True)
        found = jnp.where(row[0:1] < count, jnp.sum(found, axis=0, keepdims=True), 1.0 * clusters)
        out = jnp.where(rows == which, found, jnp.where(rows == 3 + which, count, out))
    return out.astype(jnp.int32)


def prepare_kernel(cl, vcl, rank, position_ref, vertices_hbm, corners_hbm, krylov_hbm, basis_hbm, far_hbm, near_hbm, offsets_hbm,
                   payload_ref, table_ref, area_ref, center_ref, at_ref, pairs_ref, basis_ref, krylov_ref, offsets_ref,
                   vertices_ref, corners_ref, raw_ref, far_ref, near_ref, mesh_ref, local_ref, sems):
    moves = copies((
        (vertices_hbm, vertices_ref), (corners_hbm, corners_ref), (krylov_hbm, krylov_ref), (basis_hbm, raw_ref),
        (far_hbm, far_ref), (near_hbm, near_ref), (offsets_hbm, offsets_ref),
    ), sems)
    rhs, panels = krylov_ref.shape
    clusters = panels // cl
    parts = cl // LANES
    moves[0].wait()
    for c in range(clusters):
        mesh_ref[3 * c:3 * c + 3, :] = vertices_ref[:, c * vcl:(c + 1) * vcl]
    moves[1].wait()
    for i in range(clusters * parts):
        local_ref[3 * i:3 * i + 3, :] = corners_ref[:, i * LANES:(i + 1) * LANES]
    first = position_ref[0] * (vcl * clusters) + vcl * lax.broadcasted_iota(jnp.int32, (clusters, LANES), 0)
    tables = [mesh_ref[pl.ds(k, clusters, stride=3), :] for k in range(3)]
    sums = [None] * 3
    for h in range(parts):
        local = [local_ref[pl.ds(3 * h + m, clusters, stride=3 * parts), :] - first for m in range(3)]
        corner = [[jnp.take_along_axis(tables[k], local[m], axis=1, mode="promise_in_bounds") for k in range(3)] for m in range(3)]
        for k in range(3):
            middle = (corner[0][k] + corner[1][k] + corner[2][k]) / 3.0
            lanes = slice(panels + k * cl + h * LANES, panels + k * cl + (h + 1) * LANES)
            payload_ref[:, lanes] = middle
            sums[k] = middle if h == 0 else sums[k] + middle
        one = [corner[1][k] - corner[0][k] for k in range(3)]
        two = [corner[2][k] - corner[0][k] for k in range(3)]
        normal = [one[1] * two[2] - one[2] * two[1], one[2] * two[0] - one[0] * two[2], one[0] * two[1] - one[1] * two[0]]
        area_ref[:, h * LANES:(h + 1) * LANES] = 0.5 * jnp.sqrt(normal[0] * normal[0] + normal[1] * normal[1] + normal[2] * normal[2])
    span = clusters * rank
    mine = lax.broadcasted_iota(jnp.int32, (clusters, span), 1) // rank == lax.broadcasted_iota(jnp.int32, (clusters, span), 0)
    half = span // 2
    table_ref[:, span:] = jnp.zeros_like(table_ref[:, span:])
    for k in range(3):
        center = jnp.sum(sums[k], axis=1, keepdims=True) / cl
        center_ref[:, k * LANES:(k + 1) * LANES] = jnp.broadcast_to(center, (clusters, LANES))
        row = jnp.sum(jnp.where(mine, center, 0.0), axis=0, keepdims=True)
        table_ref[k:k + 1, span:] = row[:, 0:half]
        table_ref[8 + k:9 + k, span:] = row[:, half:]
    moves[2].wait()
    moves[3].wait()
    for c in range(clusters):
        lanes = slice(c * cl, (c + 1) * cl)
        basis_ref[:, lanes] = stacked(raw_ref[:, lanes])
        charges = area_ref[c:c + 1, :] * krylov_ref[:, lanes]
        payload_ref[:, lanes] = charges
        table_ref[:, c * rank:(c + 1) * rank] = moments_of(charges, basis_ref[:, lanes])
    moves[4].wait()
    far = far_ref[...]
    step = (lax.div(far, clusters) - position_ref[0]) * (1 - 2 * lax.rem(position_ref[0], 2))
    block = jnp.where(step < 0, step + REACH, step + REACH - 3)
    per = LANES // rank
    turn = lax.rem(lax.broadcasted_iota(jnp.int32, far.shape, 1) - far + per * clusters * 2 ** 16, per)
    at_ref[...] = (turn * 6 + block) * (span // LANES) + lax.div(lax.rem(far, clusters), per)
    moves[5].wait()
    pairs_ref[...] = pair_list(near_ref[...], position_ref[0], clusters)
    moves[6].wait()


def features_of(payload_ref, panels, c, cl, target):
    rows = [payload_ref[c:c + 1, panels + k * cl:panels + (k + 1) * cl] for k in range(3)]
    value = jnp.concatenate(rows + [jnp.zeros((5, cl), F32)], axis=0)
    coarse = (value + GRID) - GRID
    middle = (value - coarse).astype(BF16).astype(F32)
    low = (value - coarse - middle).astype(BF16).astype(F32)
    pieces = [coarse, middle, low]
    rest = middle + low
    row = lax.broadcasted_iota(jnp.int32, (8, cl), 0)
    square = jnp.sum(coarse * coarse, axis=0, keepdims=True)
    extra = jnp.sum((2.0 * coarse + rest) * rest, axis=0, keepdims=True) + (SMOOTHING if target else 0.0)
    square_high = square.astype(BF16).astype(F32)
    extra_high = extra.astype(BF16).astype(F32)
    extra_middle = (extra - extra_high).astype(BF16).astype(F32)
    ones = jnp.ones((1, cl), F32)

    def placed(base, start, *values):
        for i, one in enumerate(values):
            base = jnp.where(row == start + i, one, base)
        return base

    squares, extras = (square_high, square - square_high), (extra_high, extra_middle, extra - extra_high - extra_middle)
    if target:
        scaled = [-2.0 * piece for piece in pieces]
        first = placed(scaled[0], 3, *squares, ones, ones)
        last = placed(jnp.zeros((8, cl), F32), 0, *extras, ones, ones, ones)
    else:
        first = placed(coarse, 3, ones, ones, *squares)
        last = placed(jnp.zeros((8, cl), F32), 0, ones, ones, ones, *extras)
    combos = [(scaled[i] if target else pieces[j]) for i in range(3) for j in range(3) if i + j]
    return jnp.concatenate([first, *combos, last], axis=0)


def fill_features(sources_ref, payload_ref, panels, cl):
    clusters = panels // cl
    for c in range(clusters):
        sources_ref[c] = features_of(payload_ref, panels, c, cl, False).astype(BF16)
    sources_ref[clusters] = sources_ref[0]


def near_block(source, target, pieces, out_ref):
    cl = source.shape[1]
    parts = []
    for first in range(0, cl, LANES):
        rows = slice(first, first + LANES)
        high, low = split(lax.rsqrt(dot_tn(source[:, rows], target)))
        out_ref[rows, :] = high
        out_ref[cl + first:cl + first + LANES, :] = low
        parts.append(dot_nn(pieces[:, rows], high) + dot_nn(pieces[:, rows], low))
    return sum(parts[1:], parts[0])


def near_product(pieces, block_ref, cl):
    return dot_nn(pieces, block_ref[0:cl, :]) + dot_nn(pieces, block_ref[cl:2 * cl, :])


def fill_charges(pieces_ref, payload_ref, clusters, cl):
    for c in range(clusters):
        pieces_ref[c] = stacked(payload_ref[:, c * cl:(c + 1) * cl])
    pieces_ref[clusters] = jnp.zeros_like(pieces_ref[0])


def pair_at(pairs_ref, which, i):
    pair = pairs_ref[which, i]
    return lax.shift_right_logical(pair, 6), lax.bitwise_and(pair, 63)


def build_list(which, pairs_ref, targets_ref, kept_ref, pieces_ref, sources_ref, total_ref):
    group = kept_ref.shape[1]

    def step(m, _):
        pairs = [pair_at(pairs_ref, which, group * m + w) for w in range(group)]
        loaded = [(sources_ref[j], targets_ref[c], pieces_ref[j]) for c, j in pairs]
        parts = [near_block(*one, kept_ref.at[m, w]) for w, one in enumerate(loaded)]
        for (c, j), part in zip(pairs, parts):
            total_ref[c] += part
        return 0

    lax.fori_loop(0, (pairs_ref[3 + which, 0] + group - 1) // group, step, 0)


def apply_list(which, pairs_ref, kept_ref, pieces_ref, total_ref, cl):
    group = kept_ref.shape[1]

    def step(m, _):
        pairs = [pair_at(pairs_ref, which, group * m + w) for w in range(group)]
        parts = [near_product(pieces_ref[j], kept_ref.at[m, w], cl) for w, (c, j) in enumerate(pairs)]
        for (c, j), part in zip(pairs, parts):
            total_ref[c] += part
        return 0

    lax.fori_loop(0, (pairs_ref[3 + which, 0] + group - 1) // group, step, 0)


def put_total(cl, total_ref, start_ref, out_ref):
    for c in range(total_ref.shape[0]):
        lanes = slice(c * cl, (c + 1) * cl)
        near = folded(total_ref[c])
        out_ref[:, lanes] = near if start_ref is None else start_ref[:, lanes] + near


def own_kernel(cl, pairs_ref, payload_ref, beside_ref, own_ref, kept_ref, near_out_ref, targets_ref, tail_ref, pieces_ref, sources_ref, total_ref):
    tail_ref[...] = beside_ref[:, beside_ref.shape[1] - LANES:]
    panels = near_out_ref.shape[1]
    clusters = panels // cl
    fill_charges(pieces_ref, payload_ref, clusters, cl)
    fill_features(sources_ref, payload_ref, panels, cl)
    for c in range(clusters):
        target = features_of(payload_ref, panels, c, cl, True).astype(BF16)
        targets_ref[c] = target
        total_ref[c] = near_block(sources_ref[c], target, pieces_ref[c], own_ref.at[c])
    build_list(0, pairs_ref, targets_ref, kept_ref, pieces_ref, sources_ref, total_ref)
    put_total(cl, total_ref, None, near_out_ref)


def partner_kernel(cl, pairs_ref, payload_ref, targets_ref, start_ref, kept_ref, near_out_ref, pieces_ref, sources_ref, total_ref):
    panels = near_out_ref.shape[1]
    fill_charges(pieces_ref, payload_ref, panels // cl, cl)
    fill_features(sources_ref, payload_ref, panels, cl)
    total_ref[...] = jnp.zeros_like(total_ref)
    build_list(1, pairs_ref, targets_ref, kept_ref, pieces_ref, sources_ref, total_ref)
    put_total(cl, total_ref, start_ref, near_out_ref)


def image_kernel(cl, rank, pairs_ref, payload_ref, targets_ref, start_ref, area_ref, krylov_ref, basis_ref,
                 kept_ref, image_ref, charges_ref, table_ref, pieces_ref, sources_ref, total_ref):
    rhs, panels = image_ref.shape
    clusters = panels // cl
    span = clusters * rank
    fill_charges(pieces_ref, payload_ref, clusters, cl)
    fill_features(sources_ref, payload_ref, panels, cl)
    total_ref[...] = jnp.zeros_like(total_ref)
    build_list(2, pairs_ref, targets_ref, kept_ref, pieces_ref, sources_ref, total_ref)
    squared = correlation = jnp.zeros((rhs, cl), F32)
    for c in range(clusters):
        lanes = slice(c * cl, (c + 1) * cl)
        area = area_ref[c:c + 1, :]
        image = COULOMB * area * (start_ref[:, lanes] + folded(total_ref[c]))
        charges = area * image
        image_ref[:, lanes] = image
        charges_ref[:, lanes] = charges
        table_ref[:, c * rank:(c + 1) * rank] = moments_of(charges, basis_ref[:, lanes])
        krylov = krylov_ref[:, lanes]
        squared = squared + krylov * krylov
        correlation = correlation + krylov * image
    squared = jnp.sum(squared, axis=1, keepdims=True)
    correlation = jnp.sum(correlation, axis=1, keepdims=True)
    local = ratio(correlation, squared)
    energy = jnp.zeros((rhs, cl), F32)
    for c in range(clusters):
        lanes = slice(c * cl, (c + 1) * cl)
        residual = image_ref[:, lanes] - local * krylov_ref[:, lanes]
        energy = energy + residual * residual
    table_ref[:, span:] = in_lanes(squared, correlation, jnp.sum(energy, axis=1, keepdims=True), local)


def own_again_kernel(cl, pairs_ref, payload_ref, beside_ref, own_ref, kept_ref, near_out_ref, tail_ref, pieces_ref, total_ref):
    tail_ref[...] = beside_ref[:, beside_ref.shape[1] - LANES:]
    clusters = near_out_ref.shape[1] // cl
    fill_charges(pieces_ref, payload_ref, clusters, cl)
    for c in range(clusters):
        total_ref[c] = near_product(pieces_ref[c], own_ref.at[c], cl)
    apply_list(0, pairs_ref, kept_ref, pieces_ref, total_ref, cl)
    put_total(cl, total_ref, None, near_out_ref)


def neighbour_again_kernel(cl, which, pairs_ref, payload_ref, start_ref, kept_ref, near_out_ref, pieces_ref, total_ref):
    fill_charges(pieces_ref, payload_ref, near_out_ref.shape[1] // cl, cl)
    total_ref[...] = jnp.zeros_like(total_ref)
    apply_list(which, pairs_ref, kept_ref, pieces_ref, total_ref, cl)
    put_total(cl, total_ref, start_ref, near_out_ref)


def finish_kernel(cl, total, near_ref, area_ref, image_ref, krylov_ref, one_ref, two_ref, next_hbm, second_hbm, next_ref, second_ref, sems):
    panels = image_ref.shape[1]
    clusters = panels // cl
    squared, correlation, energy, local = merged([one_ref[...], two_ref[...]])
    projection = correlation / (squared + 1e-06)
    gap = projection - local
    scaling = 1.0 / jnp.sqrt((energy + gap * gap * squared) / total + 1e-06)
    moves = []
    parts = 4
    for h in range(parts):
        for c in range(h * clusters // parts, (h + 1) * clusters // parts):
            lanes = slice(c * cl, (c + 1) * cl)
            image = image_ref[:, lanes]
            next_ref[:, lanes] = (image - projection * krylov_ref[:, lanes]) * scaling
            second_ref[:, lanes] = (COULOMB * area_ref[c:c + 1, :] * near_ref[:, lanes] - projection * image) * scaling
        lanes = slice(h * panels // parts, (h + 1) * panels // parts)
        for held, hbm in ((next_ref, next_hbm), (second_ref, second_hbm)):
            moves.append(pltpu.make_async_copy(held.at[:, lanes], hbm.at[:, lanes], sems.at[len(moves)]))
            moves[-1].start()
    for move in moves:
        move.wait()


def load_window(tables, clusters, rank, pieces_ref, middle_ref):
    per = LANES // rank
    span = clusters * rank
    count = pieces_ref.shape[0] // per
    groups = span // LANES
    for at in range(count):
        (ref, first), g = tables[at // groups], at % groups
        tile = ref[:, first + g * LANES:first + (g + 1) * LANES]
        for s in range(per):
            pieces_ref[s * count + at] = stacked(pltpu.roll(tile, s * rank, 1) if s else tile)
        if middle_ref is not None:
            half = groups // 2
            row, lane = 8 * (g // half), first + span + g % half * LANES
            tile = ref[row:row + 8, lane:lane + LANES]
            for s in range(per):
                middle_ref[s * count + at] = pltpu.roll(tile, s * rank, 1) if s else tile


def six_tables(near_ref, far_ref, swapped_ref):
    width = near_ref.shape[1] // 2
    return (far_ref, 0), (far_ref, width), (near_ref, 0), (swapped_ref, width), (swapped_ref, 0), (swapped_ref, 3 * width)


def lane_masks(shape, rank, kind):
    lane = (lax.broadcasted_iota(jnp.int32, shape, 1) // rank).astype(kind)
    return [lane == jnp.asarray(u, kind) for u in range(LANES // rank)]


def pick(source_ref, at_ref, c, g, masks):
    row = None
    for u, mask in enumerate(masks):
        take = source_ref[at_ref[c, g * len(masks) + u]]
        row = take if row is None else jnp.where(mask, take, row)
    return row


def far_fields(gathered_ref, coupling_ref, fields_ref):
    for c in range(gathered_ref.shape[0]):
        field = quartered(dot_nt(gathered_ref[c], coupling_ref[c]))
        fields_ref[c] = stacked(jnp.concatenate([field, field], axis=1))


def far_potential(fields_ref, c, basis):
    return folded(dot_nn(fields_ref[c], basis))


def far_kernel(cl, rank, at_ref, near_pair_ref, far_pair_ref, swapped_ref, center_ref, near_ref, basis_ref, offsets_ref,
               out_ref, coupling_ref, pieces_ref, middle_ref, gathered_ref, fields_ref):
    clusters = near_ref.shape[1] // cl
    per = LANES // rank
    load_window(six_tables(near_pair_ref, far_pair_ref, swapped_ref), clusters, rank, pieces_ref, middle_ref)
    wide = lane_masks(middle_ref.shape[1:], rank, jnp.int32)
    masks = lane_masks(pieces_ref.shape[1:], rank, jnp.int16)
    for c in range(clusters):
        mine = [offsets_ref[3, k:k + 1, :] - center_ref[c:c + 1, k * LANES:(k + 1) * LANES] for k in range(3)]
        for g in range(at_ref.shape[1] // per):
            lanes = slice(g * LANES, (g + 1) * LANES)
            gathered_ref[c, :, lanes] = pick(pieces_ref, at_ref, c, g, masks)
            center = pick(middle_ref, at_ref, c, g, wide)
            gap = [(center[k:k + 1] + mine[k]) - offsets_ref[k] for k in range(3)]
            high, low = split(lax.rsqrt(gap[0] * gap[0] + gap[1] * gap[1] + gap[2] * gap[2] + SMOOTHING))
            coupling_ref[c, 0:rank, lanes] = high
            coupling_ref[c, rank:2 * rank, lanes] = low
    far_fields(gathered_ref, coupling_ref, fields_ref)
    for c in range(clusters):
        lanes = slice(c * cl, (c + 1) * cl)
        out_ref[:, lanes] = near_ref[:, lanes] + far_potential(fields_ref, c, basis_ref[:, lanes])


def far_again_kernel(cl, rank, at_ref, near_pair_ref, far_pair_ref, swapped_ref, near_ref, coupling_ref, basis_ref,
                     out_ref, pieces_ref, gathered_ref, fields_ref):
    clusters = near_ref.shape[1] // cl
    per = LANES // rank
    load_window(six_tables(near_pair_ref, far_pair_ref, swapped_ref), clusters, rank, pieces_ref, None)
    masks = lane_masks(pieces_ref.shape[1:], rank, jnp.int16)
    for c in range(clusters):
        for g in range(at_ref.shape[1] // per):
            gathered_ref[c, :, g * LANES:(g + 1) * LANES] = pick(pieces_ref, at_ref, c, g, masks)
    far_fields(gathered_ref, coupling_ref, fields_ref)
    for c in range(clusters):
        lanes = slice(c * cl, (c + 1) * cl)
        out_ref[:, lanes] = near_ref[:, lanes] + far_potential(fields_ref, c, basis_ref[:, lanes])


def ratio(correlation, squared):
    return jnp.where(squared > 0, correlation / jnp.where(squared > 0, squared, 1.0), 0.0)


def in_lanes(*columns):
    lane = lax.broadcasted_iota(jnp.int32, (columns[0].shape[0], LANES), 1)
    out = columns[-1]
    for i, column in enumerate(columns[:-1]):
        out = jnp.where(lane == i, column, out)
    return out


def merged(groups):
    squared = sum(group[:, 0:1] for group in groups)
    correlation = sum(group[:, 1:2] for group in groups)
    local = ratio(correlation, squared)
    energy = 0.0
    for group in groups:
        gap = local - group[:, 3:4]
        energy = energy + (group[:, 2:3] + gap * gap * group[:, 0:1])
    return squared, correlation, energy, local


def window_sums_kernel(payload_ref, partner_ref, near_pair_ref, far_pair_ref, swapped_ref, out_ref):
    width = near_pair_ref.shape[1] // 2
    ends = [(payload_ref, payload_ref.shape[1]), (partner_ref, partner_ref.shape[1])]
    ends += [(ref, end) for ref in (near_pair_ref, far_pair_ref, swapped_ref) for end in (width, 2 * width)]
    out_ref[...] = in_lanes(*merged([ref[:, end - LANES:end] for ref, end in ends]))


def merge_kernel(one_ref, two_ref, out_ref):
    out_ref[...] = in_lanes(*merged([one_ref[...], two_ref[...]]))


def call(kernel, outs, scratch, memory, *args, limit=10, us=1.0):
    spaces = {"s": pltpu.SMEM, "v": pltpu.VMEM, "p": pltpu.VMEM, "h": pltpu.HBM}
    ins, out_spaces = memory.split(">")
    pinned = {"h": pltpu.HBM, "p": pltpu.VMEM}
    return pl.pallas_call(
        kernel,
        out_shape=[pltpu.VMEM(*out) if m == "p" else jax.ShapeDtypeStruct(*out) for m, out in zip(out_spaces, outs)],
        in_specs=[pl.BlockSpec(memory_space=spaces[m]) for m in ins],
        out_specs=[pl.BlockSpec(memory_space=spaces[m]) for m in out_spaces],
        scratch_shapes=scratch,
        compiler_params=pltpu.CompilerParams(vmem_limit_bytes=limit * 2 ** 20),
        cost_estimate=pl.CostEstimate(flops=int(us * 5e8), bytes_accessed=int(us * 3.6e6), transcendentals=0),
    )(*(pltpu.with_memory_space_constraint(a, pinned[m]) if m in pinned else a for m, a in zip(ins, args)))


def body(vertices, panel_vertices, near_pairs, far_pairs, basis, krylov):
    clusters, slots = near_pairs.shape
    partners = far_pairs.shape[1]
    rhs, panels = krylov.shape
    rank = basis.shape[0]
    cl = panels // clusters
    vcl = vertices.shape[1] // clusters
    span = clusters * rank
    per = LANES // rank
    devices = lax.axis_size("clus")
    position = lax.axis_index("clus").reshape(1).astype(jnp.int32)
    offsets = proxy_offsets(rank)
    flat = np.concatenate([np.tile(offsets, (1, per)), np.zeros((rank - 3, LANES), np.float32)])
    offsets = jnp.asarray(np.concatenate([np.broadcast_to(offsets[:, :, None], (3, rank, LANES)), flat[None]]))
    width = span + span // 2
    pairing = [(i, i + 1 - 2 * (i % 2)) for i in range(devices)]
    bridging = [(i, i - 1 + 2 * (i % 2)) for i in range(1, devices - 1)] + [(0, 0), (devices - 1, devices - 1)]

    def move(value, pairs):
        return lax.ppermute(value, "clus", pairs)

    def outward(value, steps, wrap=True):
        moves = [(i, i + steps * (1 - 2 * (i % 2))) for i in range(devices)]
        return move(value, [(i, j % devices if wrap or 0 <= j < devices else i + 1 - 2 * (i % 2)) for i, j in moves])

    def exchange(payload, table, wrap):
        beside = move(table, pairing)
        pair = jnp.concatenate([table, beside], axis=1)
        near_pair, far_pair = outward(pair, 2, wrap), outward(pair, 4, wrap)
        sent = jnp.concatenate([payload, beside[:, beside.shape[1] - LANES:]], axis=1)
        return sent, beside, near_pair, far_pair, move(sent, bridging), move(payload, pairing)

    def swapped(near_pair, far_pair, tail):
        return move(jnp.concatenate([near_pair, far_pair, tail], axis=1), pairing)

    whole = ((rhs, panels), F32)
    payload, table, area, centers, at, pairs, basis, krylov, offsets = call(
        functools.partial(prepare_kernel, cl, vcl, rank),
        [
            ((rhs, panels + 3 * cl), F32), ((rhs, width), F32), ((clusters, cl), F32), ((clusters, 3 * LANES), F32),
            (far_pairs.shape, jnp.int32), ((8, LANES), jnp.int32), ((2 * rank, panels), BF16), whole, (offsets.shape, F32),
        ],
        [
            pltpu.VMEM(vertices.shape, F32),
            pltpu.VMEM(panel_vertices.shape, jnp.int32),
            pltpu.VMEM(basis.shape, F32),
            pltpu.VMEM(far_pairs.shape, jnp.int32),
            pltpu.VMEM((slots, clusters), jnp.int32),
            pltpu.VMEM((3 * clusters, vcl), F32),
            pltpu.VMEM((3 * panels // LANES, LANES), jnp.int32),
            pltpu.SemaphoreType.DMA((7,)),
        ],
        "shhhhhhh>vvvvvvppp",
        position, vertices, panel_vertices, krylov, basis, far_pairs, near_pairs.T, offsets,
        us=1.5,
    )
    sent, beside, near_pair, far_pair, other, partner = exchange(payload, table, False)
    group = 4
    own = ((clusters, 2 * cl, cl), BF16)
    kept = ((clusters * (slots - 1) // group, group, 2 * cl, cl), BF16)
    sums_shape = ((rhs, LANES), F32)
    total = pltpu.VMEM((clusters, 2 * rhs, cl), F32)
    pieces = pltpu.VMEM((clusters + 1, 2 * rhs, cl), BF16)
    sources = pltpu.VMEM((clusters + 1, FEATURES, cl), BF16)
    own_blocks, blocks, near, targets, tail = call(
        functools.partial(own_kernel, cl),
        [own, kept, whole, ((clusters, FEATURES, cl), BF16), sums_shape],
        [pieces, sources, total],
        "svv>ppvpv",
        pairs, sent, beside,
        us=8.0,
    )
    swap = swapped(near_pair, far_pair, tail)
    blocks_partner, near = call(
        functools.partial(partner_kernel, cl),
        [kept, whole],
        [pieces, sources, total],
        "svpv>pv",
        pairs, partner, targets, near,
        us=0.2,
    )
    tiles = 6 * per * span // LANES
    window = pltpu.VMEM((tiles, 2 * rhs, LANES), BF16)
    gathered = pltpu.VMEM((clusters, 2 * rhs, partners * rank), BF16)
    fields = pltpu.VMEM((clusters, 2 * rhs, 2 * rank), BF16)
    near, coupling = call(
        functools.partial(far_kernel, cl, rank),
        [whole, ((clusters, 2 * rank, partners * rank), BF16)],
        [window, pltpu.VMEM((tiles, 8, LANES), F32), gathered, fields],
        "svvvvvpp>vp",
        at, near_pair, far_pair, swap, centers, near, basis, offsets,
        us=0.2,
    )
    blocks_other, image, payload, table = call(
        functools.partial(image_kernel, cl, rank),
        [kept, whole, whole, ((rhs, span + LANES), F32)],
        [pieces, sources, total],
        "svpvvpp>pvvv",
        pairs, other, targets, near, area, krylov, basis,
        us=4.0,
    )
    sent, beside, near_pair, far_pair, other, partner = exchange(payload, table, True)
    near, tail = call(
        functools.partial(own_again_kernel, cl),
        [whole, sums_shape],
        [pieces, total],
        "svvpp>vv",
        pairs, sent, beside, own_blocks, blocks,
        us=8.0,
    )
    swap = swapped(near_pair, far_pair, tail)
    (near,) = call(
        functools.partial(neighbour_again_kernel, cl, 1),
        [whole],
        [pieces, total],
        "svvp>v",
        pairs, partner, near, blocks_partner,
        us=4.0,
    )
    (one,) = call(window_sums_kernel, [sums_shape], [], "vvvvv>v", table, beside, near_pair, far_pair, swap, us=0.3)
    size = 8
    many = outward(one, size)
    while 2 * size < devices:
        (one,) = call(merge_kernel, [sums_shape], [], "vv>v", one, many, us=0.3)
        size = 2 * size
        many = outward(one, size)
    (near,) = call(
        functools.partial(far_again_kernel, cl, rank),
        [whole],
        [window, gathered, fields],
        "svvvvpp>v",
        at, near_pair, far_pair, swap, near, coupling, basis,
        us=4.0,
    )
    (near,) = call(
        functools.partial(neighbour_again_kernel, cl, 2),
        [whole],
        [pieces, total],
        "svvp>v",
        pairs, other, near, blocks_other,
        us=1.5,
    )
    here = pltpu.VMEM((rhs, panels), F32)
    return tuple(call(
        functools.partial(finish_kernel, cl, panels * devices),
        [whole, whole],
        [here, here, pltpu.SemaphoreType.DMA((8,))],
        "vvvpvv>hh",
        near, area, image, krylov, one, many,
        us=1.0,
    ))


def solution(mesh):
    whole = P(None, ("jobs", "clus"))
    rows = P(("jobs", "clus"), None)
    return jax.shard_map(
        body,
        mesh=mesh,
        in_specs=(whole, whole, rows, rows, whole, whole),
        out_specs=(whole, whole),
        check_vma=False,
    )
```
